32 devices in a mesh: dp: 8 (over z, x), tensor: 4 (over y, core).
Axes of the slice: x: 2, y: 2, z: 4, core: 2. Of those that a mesh axis runs over, the one named last changes fastest.
Arguments:
- embeddings: bfloat16 [4096, 768], P('dp'), may hold values from -4 to 4
- replace_table: bfloat16 [32, 768], replicated, may hold values from -4 to 4
- replace_ids: int32 [4096], P('dp'), may hold values from 0 to 31
- masked: int32 [4096], P('dp'), may hold values 0 or 1
- padding: int32 [4096], P('dp'), may hold values from 0 to 1, as said below
- w_qkv: bfloat16 [2, 768, 2304], P(None, None, 'tensor'), may hold values from -4 to 4
- b_qv: bfloat16 [2, 1536], P(None, 'tensor'), may hold values from -2 to 2
- w_out: bfloat16 [2, 768, 768], P(None, 'tensor'), may hold values from -3.5 to 3.5
- b_out: bfloat16 [2, 768], replicated, may hold values from -3 to 3
- first_gain: bfloat16 [2, 768], replicated, may hold values from 0.25 to 1.75
- first_shift: bfloat16 [2, 768], replicated, may hold values from -3 to 3
- w_in: bfloat16 [2, 768, 3072], P(None, None, 'tensor'), may hold values from -0.21875 to 0.21875
- b_in: bfloat16 [2, 3072], P(None, 'tensor'), may hold values from -3 to 3
- w_down: bfloat16 [2, 3072, 768], P(None, 'tensor'), may hold values from -0.109375 to 0.109375
- b_down: bfloat16 [2, 768], replicated, may hold values from -3 to 3
- second_gain: bfloat16 [2, 768], replicated, may hold values from 0.25 to 1.75
- second_shift: bfloat16 [2, 768], replicated, may hold values from -3 to 3
- cotangent: bfloat16 [4096, 768], P('dp'), may hold values from -6 to 6
Outputs:
- hidden_out: bfloat16 [4096, 768], P('dp')
- grad_embeddings: bfloat16 [4096, 768], P('dp')
- grad_table: float32 [32, 768], replicated
- grad_w_qkv: float32 [2, 768, 2304], P(None, None, 'tensor')
- grad_b_qv: float32 [2, 1536], P(None, 'tensor')
- grad_w_out: float32 [2, 768, 768], P(None, 'tensor')
- grad_b_out: float32 [2, 768], replicated
- grad_first_gain: float32 [2, 768], replicated
- grad_first_shift: float32 [2, 768], replicated
- grad_w_in: float32 [2, 768, 3072], P(None, None, 'tensor')
- grad_b_in: float32 [2, 3072], P(None, 'tensor')
- grad_w_down: float32 [2, 3072, 768], P(None, 'tensor')
- grad_b_down: float32 [2, 768], replicated
- grad_second_gain: float32 [2, 768], replicated
- grad_second_shift: float32 [2, 768], replicated
The draws below stay inside these ranges and needn't reach their ends.
Inputs may be any that keep to these rules, and one draw needn't show every extreme that they name: `padding`: on each of the 8 pages of 512 tokens the real tokens come first and number 512 // 2 or more.
All inputs are finite; a program needn't handle non-finite values. No bound on the sum of `masked` on one device may be relied on, other than what follows from the above.
Results may differ from the reference program's by a relative error of at most 0.015.
Values sent between devices are 32-bit elements; how exact they have to be, the bound alone decides.
A program may use at most 128 MiB of HBM per device.

```python
import math
import jax
import jax.numpy as jnp
from jax import lax

D = 768
HEADS = 12
FF = 3072
HEAD_DIM = 64
LAYERS = 2
PAGE_LEN = 512
REPL = 32
PAGES = 8
TOKENS = 4096


def clipped_normal(key, shape, scale, limit):
    values = jax.random.normal(key, shape, jnp.float32)
    return jnp.clip(values, -limit, limit) * scale


def draw_embeddings(key, part):
    key = jax.random.fold_in(key, 21)
    return clipped_normal(key, (TOKENS, D), 1.0, 4.0).astype(jnp.bfloat16)


def draw_replace_table(key, part):
    key = jax.random.fold_in(key, 22)
    return clipped_normal(key, (REPL, D), 1.0, 4.0).astype(jnp.bfloat16)


def draw_w_qkv(key, part):
    key = jax.random.fold_in(key, 23)
    return clipped_normal(key, (LAYERS, D, 3 * D), D ** (-0.5), 4.0).astype(jnp.bfloat16)


def draw_b_qv(key, part):
    key = jax.random.fold_in(key, 24)
    return clipped_normal(key, (LAYERS, 2 * D), 0.5, 4.0).astype(jnp.bfloat16)


def draw_padding(key, part):
    key = jax.random.fold_in(key, 11)
    length_key, full_key = jax.random.split(key)
    lengths = jax.random.randint(length_key, (PAGES,), PAGE_LEN // 2, PAGE_LEN)
    full_page = jax.random.randint(full_key, (), 0, PAGES)
    lengths = jnp.where(jnp.arange(PAGES) == full_page, PAGE_LEN, lengths)
    positions = jnp.arange(PAGE_LEN)
    return (positions[None, :] < lengths[:, None]).astype(jnp.int32).reshape(PAGES * PAGE_LEN)


def set_ends(values, stream_key, low, top_value):
    spot = [jax.random.randint(jax.random.fold_in(stream_key, axis), (), 0, length) for axis, length in enumerate(values.shape)]
    main_axis = values.shape.index(max(values.shape))
    beside = spot[:main_axis] + [(spot[main_axis] + 1) % values.shape[main_axis]] + spot[main_axis + 1:]
    return values.at[tuple(spot)].set(low).at[tuple(beside)].set(top_value)


def raised(values, rng, source, target, shards_of, factor):
    owner, partner = [(jnp.arange(values.shape[position]) // (values.shape[position] // shards_of)).reshape([-1 if axis == position else 1 for axis in range(values.ndim)]) for position in (source, target)]
    chosen = jax.random.permutation(rng, shards_of)[partner]
    strong = (owner == chosen) | (owner == (partner + shards_of // 2) % shards_of)
    return jnp.where(strong, factor * values, values)


def block_scale(rng, dims, cuts, least, largest):
    def one(position, blocks):
        draws = jax.random.uniform(jax.random.fold_in(jax.random.fold_in(rng, 6), position), (blocks,), jnp.float32, least / len(cuts), largest / len(cuts))
        return jnp.repeat(jnp.exp(draws), dims[position] // blocks).reshape((-1,) + (1,) * (len(dims) - position - 1))

    level = one(*cuts[0])
    for cut in cuts[1:]:
        level = level * one(*cut)
    return level


def bell_draw(rng, dims, deviation, bound, cuts=(), kind=jnp.bfloat16):
    loudness = block_scale(rng, dims, cuts, -0.22, 0.18) if cuts else 1.0
    values = jax.random.normal(rng, dims, jnp.float32) * deviation * loudness
    return jnp.minimum(jnp.maximum(values, -bound), bound).astype(kind)


def gaussian_with(stream_key, extent, spread, most, pieces, heavy, kind=jnp.bfloat16):
    values = spread * jax.random.normal(stream_key, extent, jnp.float32)
    if pieces:
        values = values * block_scale(stream_key, extent, pieces, -0.22, 0.18)
    return jnp.clip(raised(values, jax.random.fold_in(stream_key, 3), *heavy), -most, most).astype(kind)


def setup_inputs(seed: int = 0) -> dict:
    arg_keys = jax.random.split(jax.random.key(seed), 19)
    embeddings = draw_embeddings(jax.random.fold_in(arg_keys[18], 71), 0)
    replace_table = draw_replace_table(jax.random.fold_in(arg_keys[18], 71), 0)
    replace_ids = set_ends(jax.random.randint(arg_keys[2], (TOKENS,), 0, REPL), jax.random.fold_in(arg_keys[2], 1), 0, REPL - 1).astype(jnp.int32)
    masked = set_ends((jax.random.randint(arg_keys[3], (TOKENS,), 0, 20) < 3).astype(jnp.int32), jax.random.fold_in(arg_keys[3], 1), 0, 1)
    padding = draw_padding(jax.random.fold_in(arg_keys[18], 71), 0)
    w_qkv = draw_w_qkv(jax.random.fold_in(arg_keys[18], 71), 0)
    b_qv = draw_b_qv(jax.random.fold_in(arg_keys[18], 71), 0)
    w_out = bell_draw(arg_keys[7], (LAYERS, D, D), (max(1, 2 * D // PAGE_LEN)) ** -0.5, 3.5, ((1, 4),))
    b_out = bell_draw(arg_keys[8], (LAYERS, D), 0.5, 3.0)
    first_gain = jnp.clip(1.0 + 0.15 * jax.random.normal(arg_keys[9], (LAYERS, D), jnp.float32), 0.25, 1.75).astype(jnp.bfloat16)
    first_shift = bell_draw(arg_keys[10], (LAYERS, D), 0.5, 3.0)
    w_in = bell_draw(arg_keys[11], (LAYERS, D, FF), D ** -0.5, 0.21875, ((2, 4),))
    b_in = bell_draw(arg_keys[12], (LAYERS, FF), 0.5, 3.0, ((1, 4),))
    w_down = bell_draw(arg_keys[13], (LAYERS, FF, D), FF ** -0.5, 0.109375, ((1, 4),))
    b_down = bell_draw(arg_keys[14], (LAYERS, D), 0.5, 3.0)
    second_gain = jnp.clip(1.0 + 0.15 * jax.random.normal(arg_keys[15], (LAYERS, D), jnp.float32), 0.25, 1.75).astype(jnp.bfloat16)
    second_shift = bell_draw(arg_keys[16], (LAYERS, D), 0.5, 3.0)
    cotangent = gaussian_with(arg_keys[17], (TOKENS, D), 1.0, 6.0, ((0, 8),), (0, 1, 8, 2.0))
    return dict(embeddings=embeddings, replace_table=replace_table, replace_ids=replace_ids, masked=masked, padding=padding, w_qkv=w_qkv, b_qv=b_qv, w_out=w_out, b_out=b_out, first_gain=first_gain, first_shift=first_shift, w_in=w_in, b_in=b_in, w_down=w_down, b_down=b_down, second_gain=second_gain, second_shift=second_shift, cotangent=cotangent)


@jax.custom_vjp
def low(v):
    return lax.optimization_barrier(v.astype(jnp.bfloat16)).astype(jnp.float32)

@jax.custom_vjp
def low_back(v):
    return v

def low_keep(v):
    return (low(v), None)

def low_pass(kept, grad):
    return (grad,)

def back_keep(v):
    return (v, None)

def back_low(kept, grad):
    return (low(grad),)
low.defvjp(low_keep, low_pass)
low_back.defvjp(back_keep, back_low)
EPSILON = 1e-12

def matmul_high(left, right):
    return jnp.dot(left, right, precision=lax.Precision.HIGHEST, preferred_element_type=jnp.float32)

def layer_norm(values, gain, shift):
    average = lax.optimization_barrier(jnp.mean(values, axis=-1, keepdims=True))
    centered = values - average
    variance = lax.optimization_barrier(jnp.mean(centered * centered, axis=-1, keepdims=True))
    return centered * lax.rsqrt(variance + EPSILON) * gain + shift

def attend_group(operands):
    block, bias_block = operands
    scores = jnp.einsum('gqhd,gkhd->ghqk', block[:, :, :, 0], block[:, :, :, 1], precision=lax.Precision.HIGHEST)
    scores = scores * HEAD_DIM ** (-0.5) + bias_block[:, None, None, :]
    scores = low_back(scores)
    probabilities = jax.nn.softmax(scores, axis=-1)
    return jnp.einsum('ghqk,gkhd->gqhd', low(probabilities), block[:, :, :, 2], precision=lax.Precision.HIGHEST)

def layer_forward(inputs, bias_rows, params):
    w_qkv, b_qv, w_out, b_out, gain_one, shift_one, w_in, b_in, w_down, b_down, gain_two, shift_two = params
    row_count = inputs.shape[0]
    inputs = low(inputs)
    bias_pair = b_qv.reshape(HEADS, 2, HEAD_DIM)
    bias_full = jnp.stack([bias_pair[:, 0], jnp.zeros_like(bias_pair[:, 0]), bias_pair[:, 1]], axis=1)
    projected = low_back(matmul_high(inputs, w_qkv)).reshape(row_count, HEADS, 3, HEAD_DIM)
    packed = low(projected + bias_full)
    group_pages = math.gcd(PAGES, 8)
    groups = PAGES // group_pages
    attended = lax.map(jax.checkpoint(attend_group), (packed.reshape(groups, group_pages, PAGE_LEN, HEADS, 3, HEAD_DIM), bias_rows.reshape(groups, group_pages, PAGE_LEN)))
    attended = low(low_back(attended.reshape(row_count, D)))
    before_one = inputs + (low_back(matmul_high(attended, w_out)) + b_out)
    normed_one = layer_norm(before_one, gain_one, shift_one)
    hidden = low_back(matmul_high(low(normed_one), w_in)) + b_in
    active = low(jax.nn.gelu(hidden, approximate=False))
    before_two = normed_one + (low_back(matmul_high(active, w_down)) + b_down)
    return layer_norm(before_two, gain_two, shift_two)

def reference(embeddings, replace_table, replace_ids, masked, padding, w_qkv, b_qv, w_out, b_out, first_gain, first_shift, w_in, b_in, w_down, b_down, second_gain, second_shift, cotangent):
    live_rows = (masked * padding).astype(jnp.float32)
    choose = (replace_ids[:, None] == jnp.arange(REPL, dtype=jnp.int32)[None, :]).astype(jnp.float32)
    bias_rows = ((padding.astype(jnp.float32) - 1.0) * 10000.0).reshape(PAGES, PAGE_LEN)
    floats = [operand.astype(jnp.float32) for operand in (embeddings, replace_table, w_qkv, b_qv, w_out, b_out, first_gain, first_shift, w_in, b_in, w_down, b_down, second_gain, second_shift)]

    def forward(embed_float, table_float, *weights):
        picked = matmul_high(choose, table_float)
        current = jnp.where(live_rows[:, None] > 0, picked, embed_float)
        for layer_index in range(LAYERS):
            current = layer_forward(current, bias_rows, tuple((stacked[layer_index] for stacked in weights)))
        return current
    result, pullback = jax.vjp(forward, *floats)
    gradients = pullback(cotangent.astype(jnp.float32) * live_rows[:, None])
    return (result.astype(jnp.bfloat16), gradients[0].astype(jnp.bfloat16), gradients[1], gradients[2], gradients[3], gradients[4], gradients[5], gradients[6], gradients[7], gradients[8], gradients[9], gradients[10], gradients[11], gradients[12], gradients[13])
```

```python
import functools

import jax
import jax.numpy as jnp
from jax import lax
from jax.experimental import pallas as pl
from jax.experimental.pallas import tpu as pltpu
from jax.sharding import PartitionSpec as P

MESH=pl.DeviceIdType.MESH

HEAD_DIM = 64
LAYERS = 2
PAGE_LEN = 512
REPL = 32


EPSILON = 1e-12


def layer_norm(values, gain, shift):
    average = jnp.mean(values, axis=-1, keepdims=True)
    centered = values - average
    variance = jnp.mean(centered * centered, axis=-1, keepdims=True)
    return centered * lax.rsqrt(variance + EPSILON) * gain + shift


def exact_gelu(values):
    return jax.nn.gelu(values, approximate=False)


def contract_rows(left, right):
    return lax.dot_general(
        left, right, (((0,), (0,)), ((), ())), preferred_element_type=jnp.float32
    )


def contract_cols(left, right):
    return lax.dot_general(
        left, right, (((1,), (1,)), ((), ())), preferred_element_type=jnp.float32
    )


def score_page(page_block, bias_row):
    scores = jnp.einsum(
        "qhd,khd->hqk", page_block[:, :, 0], page_block[:, :, 1], preferred_element_type=jnp.float32
    )
    return scores * HEAD_DIM ** (-0.5) + bias_row[None, None, :]


def page_forward(operands):
    page_block, bias_row = operands
    scores = score_page(page_block, bias_row)
    largest = jnp.max(scores, axis=-1, keepdims=True)
    weights = jnp.exp(scores - largest)
    totals = jnp.sum(weights, axis=-1, keepdims=True)
    probabilities = (weights / totals).astype(jnp.bfloat16)
    attended = jnp.einsum(
        "hqk,khd->qhd", probabilities, page_block[:, :, 2], preferred_element_type=jnp.float32
    )
    return (attended.astype(jnp.bfloat16), (largest + jnp.log(totals))[:, :, 0])


def page_backward(operands):
    page_block, bias_row, log_total, grad_heads = operands
    scores = score_page(page_block, bias_row)
    probabilities = jnp.exp(scores - log_total[:, :, None])
    grad_probs = jnp.einsum(
        "qhd,khd->hqk", grad_heads, page_block[:, :, 2], preferred_element_type=jnp.float32
    )
    grad_values = jnp.einsum(
        "hqk,qhd->khd",
        probabilities.astype(jnp.bfloat16),
        grad_heads,
        preferred_element_type=jnp.float32,
    )
    inner_sum = jnp.sum(probabilities * grad_probs, axis=-1, keepdims=True)
    grad_scores = (probabilities * (grad_probs - inner_sum)).astype(jnp.bfloat16)
    score_scale = HEAD_DIM ** (-0.5)
    grad_queries = (
        jnp.einsum(
            "hqk,khd->qhd", grad_scores, page_block[:, :, 1], preferred_element_type=jnp.float32
        )
        * score_scale
    )
    grad_keys = (
        jnp.einsum(
            "hqk,qhd->khd", grad_scores, page_block[:, :, 0], preferred_element_type=jnp.float32
        )
        * score_scale
    )
    return jnp.stack([grad_queries, grad_keys, grad_values], axis=2)


def forward_layer(inputs_low, bias_rows, params):
    (
        w_qkv,
        b_qv,
        w_out,
        b_out,
        gain_one,
        shift_one,
        w_in,
        b_in,
        w_down,
        b_down,
        gain_two,
        shift_two,
    ) = params
    row_count = inputs_low.shape[0]
    page_count = bias_rows.shape[0]
    local_heads = w_qkv.shape[1] // (3 * HEAD_DIM)
    projected = jnp.dot(inputs_low, w_qkv, preferred_element_type=jnp.float32).reshape(
        row_count, local_heads, 3, HEAD_DIM
    )
    bias_pair = b_qv.astype(jnp.float32).reshape(local_heads, 2, HEAD_DIM)
    bias_full = jnp.stack(
        [bias_pair[:, 0], jnp.zeros_like(bias_pair[:, 0]), bias_pair[:, 1]], axis=1
    )
    packed = (projected + bias_full).astype(jnp.bfloat16)
    attended_heads, log_total = lax.map(
        page_forward, (packed.reshape(page_count, PAGE_LEN, local_heads, 3, HEAD_DIM), bias_rows)
    )
    attended_heads = attended_heads.reshape(row_count, local_heads * HEAD_DIM)
    attended = lax.psum(
        jnp.dot(attended_heads, w_out, preferred_element_type=jnp.float32), "tensor"
    )
    before_one = inputs_low.astype(jnp.float32) + attended + b_out.astype(jnp.float32)
    normed_one = layer_norm(before_one, gain_one.astype(jnp.float32), shift_one.astype(jnp.float32))
    normed_low = normed_one.astype(jnp.bfloat16)
    hidden = jnp.dot(normed_low, w_in, preferred_element_type=jnp.float32) + b_in.astype(
        jnp.float32
    )
    active = exact_gelu(hidden).astype(jnp.bfloat16)
    lowered = lax.psum(jnp.dot(active, w_down, preferred_element_type=jnp.float32), "tensor")
    before_two = normed_one + lowered + b_down.astype(jnp.float32)
    result = layer_norm(before_two, gain_two.astype(jnp.float32), shift_two.astype(jnp.float32))
    return (
        result,
        (packed, attended_heads, log_total, before_one, normed_low, hidden, active, before_two),
    )


def backward_layer(inputs_low, bias_rows, params, saved, grad_result):
    (
        w_qkv,
        b_qv,
        w_out,
        b_out,
        gain_one,
        shift_one,
        w_in,
        b_in,
        w_down,
        b_down,
        gain_two,
        shift_two,
    ) = params
    packed, attended_heads, log_total, before_one, normed_low, hidden, active, before_two = saved
    row_count, local_heads = (packed.shape[0], packed.shape[1])
    page_count = bias_rows.shape[0]
    norm_values, norm_pull = jax.vjp(
        layer_norm, before_two, gain_two.astype(jnp.float32), shift_two.astype(jnp.float32)
    )
    grad_two, grad_gain_two, grad_shift_two = norm_pull(grad_result)
    grad_two_low = grad_two.astype(jnp.bfloat16)
    grad_w_down = contract_rows(active, grad_two_low)
    grad_active = contract_cols(grad_two_low, w_down)
    gelu_values, gelu_pull = jax.vjp(exact_gelu, hidden)
    grad_hidden = gelu_pull(grad_active)[0]
    grad_hidden_low = grad_hidden.astype(jnp.bfloat16)
    grad_w_in = contract_rows(normed_low, grad_hidden_low)
    grad_normed = grad_two + lax.psum(contract_cols(grad_hidden_low, w_in), "tensor")
    first_values, first_pull = jax.vjp(
        layer_norm, before_one, gain_one.astype(jnp.float32), shift_one.astype(jnp.float32)
    )
    grad_one, grad_gain_one, grad_shift_one = first_pull(grad_normed)
    grad_one_low = grad_one.astype(jnp.bfloat16)
    grad_w_out = contract_rows(attended_heads, grad_one_low)
    grad_heads = (
        contract_cols(grad_one_low, w_out)
        .astype(jnp.bfloat16)
        .reshape(page_count, PAGE_LEN, local_heads, HEAD_DIM)
    )
    grad_packed = lax.map(
        page_backward,
        (
            packed.reshape(page_count, PAGE_LEN, local_heads, 3, HEAD_DIM),
            bias_rows,
            log_total,
            grad_heads,
        ),
    )
    grad_packed = grad_packed.reshape(row_count, local_heads, 3, HEAD_DIM)
    grad_b_qv = jnp.sum(grad_packed[:, :, 0::2], axis=0).reshape(-1)
    grad_proj_low = grad_packed.reshape(row_count, -1).astype(jnp.bfloat16)
    grad_w_qkv = contract_rows(inputs_low, grad_proj_low)
    grad_inputs = grad_one + lax.psum(contract_cols(grad_proj_low, w_qkv), "tensor")
    gradients = (
        grad_w_qkv,
        grad_b_qv,
        grad_w_out,
        jnp.sum(grad_one, axis=0),
        grad_gain_one,
        grad_shift_one,
        grad_w_in,
        jnp.sum(grad_hidden, axis=0),
        grad_w_down,
        jnp.sum(grad_two, axis=0),
        grad_gain_two,
        grad_shift_two,
    )
    return (grad_inputs, gradients)


WIDTH=768
UNIT=16
CHUNK=4*UNIT
LAG=2
SLOTS=4*LAG
KINDS=12
(TX,TNEAR,TFAR,TA1,TA2,TQ1,TQ2,TTA,TTN,TTM,TTF,TG)=range(KINDS)

class Engine:
    def __init__(self, chunks, part, total, landing, send, recv, local):
        self.chunks=chunks; self.part=part; self.total=total; self.landing=landing
        self.send=send; self.recv=recv; self.local=local
        d=lax.axis_index("dp"); t=lax.axis_index("tensor")
        x=lax.rem(d,2); z=lax.rem(lax.div(d,2),4)
        self.x=x; self.z=z
        self.mid=jnp.logical_or(z==1,z==2)
        self.upper=lax.div(z,2)
        self.peer=(d+1-2*x,t)
        self.line=(d+2-4*lax.rem(z,2),t)
        self.cross=(jnp.where(z==1,d+2,d-2),t)
    def neighbours(self):
        return self.peer,self.line,self.cross
    def barrier(self, bar):
        def sig(dev): pl.semaphore_signal(bar,inc=1,device_id=dev,device_id_type=MESH)
        sig(self.peer); sig(self.line)
        pl.when(self.mid)(lambda: sig(self.cross))
        pl.semaphore_wait(bar,jnp.where(self.mid,3,2))
    def rows(self,j,unit):
        return pl.ds(pl.multiple_of(j*CHUNK+unit*UNIT,UNIT),UNIT)
    def copy(self,kind,j,src,dst,dev):
        slot=lax.rem(j,SLOTS)
        return pltpu.make_async_remote_copy(src_ref=src,dst_ref=dst,send_sem=self.send.at[kind,slot],recv_sem=self.recv.at[kind,slot],device_id=dev,device_id_type=MESH)
    def land(self,kind,j):
        return self.landing.at[kind,lax.rem(j,SLOTS)]
    def tick(self,t):
        K=self.chunks; part=self.part; total=self.total; mid=self.mid; end=jnp.logical_not(mid)
        mine=self.x; other=1-self.x; near=2+self.upper; far=3-self.upper
        def at(ref,j,u): return ref.at[self.rows(j,u)]
        def cx(j): return self.copy(TX,j,at(part,j,other),self.land(TX,j),self.peer)
        def cnear(j): return self.copy(TNEAR,j,at(part,j,near),self.land(TNEAR,j),self.line)
        def cfar(j): return self.copy(TFAR,j,at(part,j,far),self.land(TFAR,j),self.line)
        def ca1(j): return self.copy(TA1,j,at(part,j,mine),self.land(TA1,j),self.line)
        def ca2(j): return self.copy(TA2,j,at(part,j,mine),self.land(TA2,j),self.cross)
        def cq1(j): return self.copy(TQ1,j,at(part,j,far),self.land(TQ1,j),self.cross)
        def cq2(j): return self.copy(TQ2,j,at(part,j,near),self.land(TQ2,j),self.peer)
        def cta(j): return self.copy(TTA,j,at(part,j,mine),at(total,j,mine),self.line)
        def ctn(j): return self.copy(TTN,j,at(part,j,near),at(total,j,near),self.line)
        def ctm(j): return self.copy(TTM,j,at(part,j,near),at(total,j,near),self.cross)
        def ctf(j): return self.copy(TTF,j,at(total,j,far),at(total,j,far),self.line)
        def cg(j): return self.copy(TG,j,at(total,j,mine),at(total,j,mine),self.peer)
        def lc(k,j,u): return pltpu.make_async_copy(at(part,j,u),at(total,j,u),self.local.at[k,lax.rem(j,SLOTS)])
        def add(j,u,kind):
            r=self.rows(j,u)
            part[r,:]=part[r,:]+self.landing[kind,lax.rem(j,SLOTS)]
        def stage(s,f):
            j=t-s*LAG
            @pl.when(jnp.logical_and(j>=0,j<K))
            def _(): f(j)
        def s0(j):
            cx(j).start()
            @pl.when(end)
            def _():
                cnear(j).start(); cfar(j).start()
        def s1(j):
            cx(j).wait()
            add(j,mine,TX)
            @pl.when(end)
            def _():
                ca1(j).start()
                cnear(j).wait_send(); cfar(j).wait_send()
            @pl.when(mid)
            def _():
                cfar(j).wait_recv(); add(j,far,TFAR); cq1(j).start()
                cnear(j).wait_recv(); add(j,near,TNEAR)
        def s2(j):
            @pl.when(end)
            def _(): ca1(j).wait_send()
            @pl.when(mid)
            def _():
                ca1(j).wait_recv(); add(j,mine,TA1); ca2(j).start()
                cq1(j).wait(); add(j,near,TQ1); cq2(j).start()
        def s3(j):
            @pl.when(mid)
            def _():
                ca2(j).wait(); add(j,mine,TA2); cta(j).start(); lc(0,j,mine).start()
                cq2(j).wait(); add(j,near,TQ2); ctm(j).start(); ctn(j).start(); lc(1,j,near).start()
        def s4(j):
            @pl.when(mid)
            def _():
                cta(j).wait_send(); ctn(j).wait_send(); lc(0,j,mine).wait(); lc(1,j,near).wait()
                cg(j).start()
                ctm(j).wait(); ctf(j).start()
            @pl.when(end)
            def _():
                cta(j).wait_recv(); cg(j).start(); ctn(j).wait_recv()
        def s5(j):
            cg(j).wait()
            pl.when(mid)(lambda: ctf(j).wait_send())
            pl.when(end)(lambda: ctf(j).wait_recv())
        for s,f in ((5,s5),(4,s4),(3,s3),(2,s2),(1,s1),(0,s0)): stage(s,f)
def scratch():
    return [pltpu.VMEM((KINDS-5,SLOTS,UNIT,WIDTH),jnp.float32),pltpu.SemaphoreType.DMA((KINDS,SLOTS)),pltpu.SemaphoreType.DMA((KINDS,SLOTS)),pltpu.SemaphoreType.DMA((2,SLOTS))]
def ar_kernel(chunks,x_ref,o_ref,landing,send,recv,local,part=None):
    e=Engine(chunks,x_ref,o_ref,landing,send,recv,local)
    e.barrier(pltpu.get_barrier_semaphore())
    def body(t,c):
        e.tick(t); return c
    lax.fori_loop(0,chunks+5*LAG,body,0)
def allreduce(x,cid=0):
    chunks=x.shape[0]//CHUNK
    return pl.pallas_call(functools.partial(ar_kernel,chunks),name="dp_allreduce",
      out_shape=jax.ShapeDtypeStruct(x.shape,jnp.float32),
      in_specs=[pl.BlockSpec(memory_space=pltpu.VMEM)],out_specs=pl.BlockSpec(memory_space=pl.ANY),
      scratch_shapes=scratch(),
      compiler_params=pltpu.CompilerParams(collective_id=cid,has_side_effects=True,vmem_limit_bytes=60<<20))(x)


def sum_every(per_layer, table_term):
    pieces = []
    smalls = []
    for layer_index in reversed(range(LAYERS)):
        (w_qkv, b_qv, w_out, b_out, gain_one, shift_one, w_in, b_in, w_down, b_down, gain_two, shift_two) = per_layer[layer_index]
        pieces += [w_down, w_in, w_out, w_qkv.T]
        padded = jnp.pad(b_qv, (0, WIDTH - b_qv.shape[0]))
        smalls.append(jnp.stack([padded, b_out, gain_one, shift_one, b_in, b_down, gain_two, shift_two]))
    flat = jnp.concatenate(pieces + smalls + [table_term, jnp.zeros((16, WIDTH), jnp.float32)], axis=0)
    every = allreduce(flat)
    groups = lax.axis_size("dp") // 8
    if groups > 1:
        every = lax.psum(every, "dp", axis_index_groups=[[low + 8 * high for high in range(groups)] for low in range(8)])
    span = 2304
    def piece(start, rows):
        return jnp.stack([lax.slice_in_dim(every, start + span * (LAYERS - 1 - layer), start + span * (LAYERS - 1 - layer) + rows) for layer in range(LAYERS)])
    w_down = piece(0, 768); w_in = piece(768, 768); w_out = piece(1536, 192)
    w_qkv = jnp.swapaxes(piece(1728, 576), 1, 2)
    base = span * LAYERS
    small = jnp.stack([lax.slice_in_dim(every, base + 8 * (LAYERS - 1 - layer), base + 8 * (LAYERS - 1 - layer) + 8) for layer in range(LAYERS)])
    table = lax.slice_in_dim(every, base + 16, base + 48)
    return (w_qkv, small[:, 0, :384], w_out, small[:, 1], small[:, 2], small[:, 3], w_in, small[:, 4], w_down, small[:, 5], small[:, 6], small[:, 7], table)


def on_device(
    embeddings,
    replace_table,
    replace_ids,
    masked,
    padding,
    w_qkv,
    b_qv,
    w_out,
    b_out,
    first_gain,
    first_shift,
    w_in,
    b_in,
    w_down,
    b_down,
    second_gain,
    second_shift,
    cotangent,
):
    live_rows = (masked * padding).astype(jnp.float32)
    choose = (replace_ids[:, None] == jnp.arange(REPL, dtype=jnp.int32)[None, :]).astype(
        jnp.float32
    )
    picked = jnp.dot(
        choose.astype(jnp.bfloat16), replace_table, preferred_element_type=jnp.float32
    ).astype(jnp.bfloat16)
    layer_zero = jnp.where(live_rows[:, None] > 0, picked, embeddings)
    bias_rows = ((padding.astype(jnp.float32) - 1.0) * 10000.0).reshape(-1, PAGE_LEN)
    stacks = (
        w_qkv,
        b_qv,
        w_out,
        b_out,
        first_gain,
        first_shift,
        w_in,
        b_in,
        w_down,
        b_down,
        second_gain,
        second_shift,
    )
    inputs_list = [layer_zero]
    saved_list = []
    for layer_index in range(LAYERS):
        params = tuple((stacked[layer_index] for stacked in stacks))
        result, saved = forward_layer(inputs_list[-1], bias_rows, params)
        saved_list.append(saved)
        inputs_list.append(result.astype(jnp.bfloat16))
    hidden_out = inputs_list[-1]
    grad_inputs = cotangent.astype(jnp.float32) * live_rows[:, None]
    per_layer = [None] * LAYERS
    for layer_index in reversed(range(LAYERS)):
        params = tuple((stacked[layer_index] for stacked in stacks))
        saved = forward_layer(inputs_list[layer_index], bias_rows, params)[1]
        grad_inputs, gradients = backward_layer(
            inputs_list[layer_index], bias_rows, params, saved, grad_inputs
        )
        per_layer[layer_index] = gradients
    grad_embeddings = (grad_inputs * (1.0 - live_rows[:, None])).astype(jnp.bfloat16)
    table_term = lax.dot_general(
        choose,
        grad_inputs * live_rows[:, None],
        (((0,), (0,)), ((), ())),
        precision=lax.Precision.HIGHEST,
        preferred_element_type=jnp.float32,
    )
    every_result = sum_every(per_layer, table_term)
    merged = every_result[:12]
    grad_table = every_result[12]
    return (
        hidden_out,
        grad_embeddings,
        grad_table,
        merged[0],
        merged[1],
        merged[2],
        merged[3],
        merged[4],
        merged[5],
        merged[6],
        merged[7],
        merged[8],
        merged[9],
        merged[10],
        merged[11],
    )


def solution(mesh):
    placed = (
        P("dp", None),
        P(),
        P("dp"),
        P("dp"),
        P("dp"),
        P(None, None, "tensor"),
        P(None, "tensor"),
        P(None, "tensor", None),
        P(),
        P(),
        P(),
        P(None, None, "tensor"),
        P(None, "tensor"),
        P(None, "tensor", None),
        P(),
        P(),
        P(),
        P("dp", None),
    )
    return jax.shard_map(
        on_device,
        mesh=mesh,
        in_specs=placed,
        out_specs=(
            P("dp", None),
            P("dp", None),
            P(),
            P(None, None, "tensor"),
            P(None, "tensor"),
            P(None, "tensor", None),
            P(),
            P(),
            P(),
            P(None, None, "tensor"),
            P(None, "tensor"),
            P(None, "tensor", None),
            P(),
            P(),
            P(),
        ),
        check_vma=False,
    )
```

```python
import functools
import math

import jax
import jax.numpy as jnp
from jax import lax
from jax.experimental import pallas as pl
from jax.experimental.pallas import tpu as pltpu
from jax.sharding import PartitionSpec as P

HEAD_DIM = 64
LAYERS = 2
PAGE_LEN = 512
REPL = 32
EPSILON = 1e-12
SCALE = HEAD_DIM ** (-0.5)
MESH = pl.DeviceIdType.MESH

BLOCK = 128
OWN = BLOCK // 2
BLOCKS = PAGE_LEN // BLOCK

UNIT = 16
CHUNK = 4 * UNIT
LAG = 2
SLOTS = 4 * LAG
KINDS = 12
(TX, TNEAR, TFAR, TA1, TA2, TQ1, TQ2, TTA, TTN, TTM, TTF, TG) = range(KINDS)
LANDINGS = TTA
GROUP = 8


def contract_rows(left, right):
    return lax.dot_general(
        left, right, (((0,), (0,)), ((), ())), preferred_element_type=jnp.float32
    )


def contract_cols(left, right):
    return lax.dot_general(
        left, right, (((1,), (1,)), ((), ())), preferred_element_type=jnp.float32
    )


def matmul(left, right):
    return jnp.dot(left, right, preferred_element_type=jnp.float32)


def repeat(count, body):
    def step(index, carry):
        body(index)
        return carry

    lax.fori_loop(0, count, step, 0)


def normed(values):
    average = jnp.mean(values, axis=-1, keepdims=True)
    centered = values - average
    variance = jnp.mean(centered * centered, axis=-1, keepdims=True)
    scale = lax.rsqrt(variance + EPSILON)
    return centered * scale, scale


def norm_back(grad, zhat, scale, gain):
    scaled = grad * gain
    average = jnp.mean(scaled, axis=-1, keepdims=True)
    along = jnp.mean(scaled * zhat, axis=-1, keepdims=True)
    return scale * (scaled - average - zhat * along)


def normal_cdf(values):
    return 0.5 * (1.0 + lax.erf(values * math.sqrt(0.5)))


def column(row):
    return jnp.transpose(jnp.broadcast_to(row, (128, row.shape[1])))[:, :1]


class Place:
    def __init__(self):
        d = lax.axis_index("dp")
        t = lax.axis_index("tensor")
        self.core = lax.rem(t, 2)
        self.core_peer = (d, t + 1 - 2 * self.core)
        self.y_peer = (d, t + 2 - 4 * lax.div(t, 2))
        pair = lax.rem(d, 2)
        line = lax.rem(lax.div(d, 2), 4)
        self.pair = pair
        self.mid = jnp.logical_or(line == 1, line == 2)
        self.end = jnp.logical_not(self.mid)
        self.upper = lax.div(line, 2)
        self.peer = (d + 1 - 2 * pair, t)
        self.line = (d + 2 - 4 * lax.rem(line, 2), t)
        self.cross = (jnp.where(line == 1, d + 2, d - 2), t)


def greet(place, barrier):
    def signal(device):
        pl.semaphore_signal(barrier, inc=1, device_id=device, device_id_type=MESH)

    for device in (place.core_peer, place.y_peer, place.peer, place.line):
        signal(device)
    pl.when(place.mid)(lambda: signal(place.cross))


def meet(place, barrier):
    pl.semaphore_wait(barrier, jnp.where(place.mid, 5, 4))


class GradientSum:
    def __init__(self, place, chunks, part, total, landing, send, recv, local):
        self.place = place
        self.chunks = chunks
        self.part = part
        self.total = total
        self.landing = landing
        self.send = send
        self.recv = recv
        self.local = local

    def rows(self, j, unit):
        return pl.ds(pl.multiple_of(j * CHUNK + unit * UNIT, UNIT), UNIT)

    def tick(self, t):
        place, part, total, local = self.place, self.part, self.total, self.local
        mine, other = place.pair, 1 - place.pair
        near, far = 2 + place.upper, 3 - place.upper

        def at(ref, j, unit):
            return ref.at[self.rows(j, unit)]

        def copy(kind, j, source, target, device):
            slot = lax.rem(j, SLOTS)
            return pltpu.make_async_remote_copy(
                src_ref=source,
                dst_ref=target,
                send_sem=self.send.at[kind, slot],
                recv_sem=self.recv.at[kind, slot],
                device_id=device,
                device_id_type=MESH,
            )

        def partial(kind, j, unit, device):
            return copy(kind, j, at(part, j, unit), self.landing.at[kind, lax.rem(j, SLOTS)], device)

        def final(kind, j, unit, device, source=part):
            return copy(kind, j, at(source, j, unit), at(total, j, unit), device)

        def keep(index, j, unit):
            return pltpu.make_async_copy(
                at(part, j, unit), at(total, j, unit), local.at[index, lax.rem(j, SLOTS)]
            )

        def add(kind, j, unit):
            rows = self.rows(j, unit)
            part[rows, :] = part[rows, :] + self.landing[kind, lax.rem(j, SLOTS)]

        def pair_first(j):
            return partial(TX, j, other, place.peer)

        def near_in(j):
            return partial(TNEAR, j, near, place.line)

        def far_in(j):
            return partial(TFAR, j, far, place.line)

        def mine_in(j):
            return partial(TA1, j, mine, place.line)

        def mine_across(j):
            return partial(TA2, j, mine, place.cross)

        def far_across(j):
            return partial(TQ1, j, far, place.cross)

        def near_pair(j):
            return partial(TQ2, j, near, place.peer)

        def mine_out(j):
            return final(TTA, j, mine, place.line)

        def near_out(j):
            return final(TTN, j, near, place.line)

        def near_across(j):
            return final(TTM, j, near, place.cross)

        def far_out(j):
            return final(TTF, j, far, place.line, total)

        def pair_last(j):
            return final(TG, j, mine, place.peer, total)

        def stage_0(j):
            pair_first(j).start()

            @pl.when(place.end)
            def _():
                near_in(j).start()
                far_in(j).start()

        def stage_1(j):
            pair_first(j).wait()
            add(TX, j, mine)

            @pl.when(place.end)
            def _():
                mine_in(j).start()
                near_in(j).wait_send()
                far_in(j).wait_send()

            @pl.when(place.mid)
            def _():
                far_in(j).wait_recv()
                add(TFAR, j, far)
                far_across(j).start()
                near_in(j).wait_recv()
                add(TNEAR, j, near)

        def stage_2(j):
            @pl.when(place.end)
            def _():
                mine_in(j).wait_send()

            @pl.when(place.mid)
            def _():
                mine_in(j).wait_recv()
                add(TA1, j, mine)
                mine_across(j).start()
                far_across(j).wait()
                add(TQ1, j, near)
                near_pair(j).start()

        def stage_3(j):
            @pl.when(place.mid)
            def _():
                mine_across(j).wait()
                add(TA2, j, mine)
                mine_out(j).start()
                keep(0, j, mine).start()
                near_pair(j).wait()
                add(TQ2, j, near)
                near_across(j).start()
                near_out(j).start()
                keep(1, j, near).start()

        def stage_4(j):
            @pl.when(place.mid)
            def _():
                mine_out(j).wait_send()
                near_out(j).wait_send()
                keep(0, j, mine).wait()
                keep(1, j, near).wait()
                pair_last(j).start()
                near_across(j).wait()
                far_out(j).start()

            @pl.when(place.end)
            def _():
                mine_out(j).wait_recv()
                pair_last(j).start()
                near_out(j).wait_recv()

        def stage_5(j):
            pair_last(j).wait()
            pl.when(place.mid)(lambda: far_out(j).wait_send())
            pl.when(place.end)(lambda: far_out(j).wait_recv())

        stages = (stage_0, stage_1, stage_2, stage_3, stage_4, stage_5)
        for number in reversed(range(len(stages))):
            j = t - number * LAG
            pl.when(jnp.logical_and(j >= 0, j < self.chunks))(
                functools.partial(stages[number], j)
            )

    def ticks(self):
        return self.chunks + 5 * LAG


def page_kernel(
    sizes,
    embeddings,
    replace_table,
    replace_ids,
    masked,
    padding,
    w_qkv,
    b_qv,
    w_out,
    b_out,
    first_gain,
    first_shift,
    w_in,
    b_in,
    w_down,
    b_down,
    second_gain,
    second_shift,
    cotangent,
    hidden_out,
    grad_embeddings,
    total,
    inputs_low,
    queries,
    keys,
    values,
    log_total,
    heads,
    normed_low,
    hidden,
    active,
    zhat_one,
    scale_one,
    zhat_two,
    scale_two,
    columns,
    own_a,
    own_b,
    part,
    land_core,
    land_y,
    land_back,
    land_small,
    dz_low,
    du_low,
    dheads,
    dkeys,
    dvalues,
    dqkv_low,
    sums,
    local_sums,
    grads,
    landing,
    core_send,
    core_recv,
    y_send,
    y_recv,
    back_send,
    back_recv,
    small_send,
    small_recv,
    dp_send,
    dp_recv,
    dp_local,
):
    width, hidden_width, local_heads, span = sizes
    head_width = local_heads * HEAD_DIM
    place = Place()
    core = place.core
    barrier = pltpu.get_barrier_semaphore()
    greet(place, barrier)
    small_base = LAYERS * span
    chunks = grads.shape[0] // CHUNK
    grad_sum = GradientSum(place, chunks, grads, total, landing, dp_send, dp_recv, dp_local)
    tick = grad_sum.tick

    def vector(ref, layer):
        both = ref[...].astype(jnp.float32)
        return jnp.where(layer == 0, both[0:1], both[1:2])

    def block(b):
        return pl.ds(pl.multiple_of(b * BLOCK, BLOCK), BLOCK)

    def kept(b):
        return pl.ds(pl.multiple_of(b * BLOCK + core * OWN, OWN), OWN)

    def given(b):
        return pl.ds(pl.multiple_of(b * BLOCK + (1 - core) * OWN, OWN), OWN)

    def packed(b):
        return pl.ds(pl.multiple_of(b * OWN, OWN), OWN)

    def lanes(p, size=128):
        return pl.ds(pl.multiple_of(p * size, size), size)

    def remote(source, target, send, recv, device):
        return pltpu.make_async_remote_copy(
            src_ref=source,
            dst_ref=target,
            send_sem=send,
            recv_sem=recv,
            device_id=device,
            device_id_type=MESH,
        )

    def to_core(turn, b):
        return remote(
            part.at[given(b)],
            land_core.at[turn, b],
            core_send.at[turn, b],
            core_recv.at[turn, b],
            place.core_peer,
        )

    def over_y(turn, b):
        return remote(
            part.at[kept(b)],
            land_y.at[turn, b],
            y_send.at[turn, b],
            y_recv.at[turn, b],
            place.y_peer,
        )

    def to_other(turn, b, source):
        return remote(
            source.at[packed(b)],
            land_back.at[turn, b],
            back_send.at[turn, b],
            back_recv.at[turn, b],
            place.core_peer,
        )

    def send_y(turn, b):
        to_core(turn, b).wait()
        part[kept(b), :] = part[kept(b), :] + land_core[turn, b]
        over_y(turn, b).start()

    def summed(turn, b):
        over_y(turn, b).wait()
        return part[kept(b), :] + land_y[turn, b]

    pad_row = padding[...].astype(jnp.float32)
    live_row = masked[...].astype(jnp.float32) * pad_row
    bias_row = (pad_row - 1.0) * 10000.0
    columns[:, 0:1] = column(live_row)
    columns[:, 1:2] = column(replace_ids[...].astype(jnp.float32))
    grads[small_base:, :] = jnp.zeros((CHUNK, width), jnp.float32)

    def chosen(rows, count):
        spots = lax.broadcasted_iota(jnp.int32, (count, REPL), 1).astype(jnp.float32)
        return jnp.where(columns[rows, 1:2] == spots, 1.0, 0.0)

    def first_input(b):
        rows = block(b)
        picked = matmul(chosen(rows, BLOCK).astype(jnp.bfloat16), replace_table[...])
        taken = jnp.where(
            columns[rows, 0:1] > 0.0, picked, embeddings[rows, :].astype(jnp.float32)
        )
        inputs_low[0, rows, :] = taken.astype(jnp.bfloat16)

    repeat(BLOCKS, first_input)

    def scores_of(layer, h, rows):
        return contract_cols(queries[layer, h, rows, :], keys[layer, h]) * SCALE + bias_row

    def forward(layer):
        bias_pair = vector(b_qv, layer)

        def project(b):
            rows = block(b)
            projected = matmul(inputs_low[layer, rows, :], w_qkv[layer])
            for h in range(local_heads):
                base = 3 * HEAD_DIM * h
                bias = 2 * HEAD_DIM * h
                queries[layer, h, rows, :] = (
                    projected[:, base : base + HEAD_DIM] + bias_pair[:, bias : bias + HEAD_DIM]
                ).astype(jnp.bfloat16)
                keys[layer, h, rows, :] = projected[
                    :, base + HEAD_DIM : base + 2 * HEAD_DIM
                ].astype(jnp.bfloat16)
                values[layer, h, rows, :] = (
                    projected[:, base + 2 * HEAD_DIM : base + 3 * HEAD_DIM]
                    + bias_pair[:, bias + HEAD_DIM : bias + 2 * HEAD_DIM]
                ).astype(jnp.bfloat16)

        repeat(BLOCKS, project)
        pl.when(layer == 0)(lambda: meet(place, barrier))

        def attend(b):
            rows = block(b)
            outs = []
            for h in range(local_heads):
                scores = scores_of(layer, h, rows)
                largest = jnp.max(scores, axis=-1, keepdims=True)
                weights = jnp.exp(scores - largest)
                totals = jnp.sum(weights, axis=-1, keepdims=True)
                probs = (weights * (1.0 / totals)).astype(jnp.bfloat16)
                outs.append(matmul(probs, values[layer, h]).astype(jnp.bfloat16))
                log_total[layer, rows, h : h + 1] = largest + jnp.log(totals)
            joined = jnp.concatenate(outs, axis=1)
            heads[layer, rows, :] = joined
            part[rows, :] = matmul(joined, w_out[layer])
            to_core(0, b).start()
            pl.when(b >= 1)(lambda: send_y(0, b - 1))

        repeat(BLOCKS, attend)
        send_y(0, BLOCKS - 1)

        gain, shift, bias_out = vector(first_gain, layer), vector(first_shift, layer), vector(b_out, layer)
        bias_in = vector(b_in, layer)

        def feed(b):
            rows = block(b)
            before = (
                inputs_low[layer, kept(b), :].astype(jnp.float32) + summed(0, b) + bias_out
            )
            zhat, scale = normed(before)
            zhat_one[layer, packed(b), :] = zhat
            scale_one[layer, packed(b), :] = scale
            result = zhat * gain + shift
            own_a[packed(b), :] = result
            to_other(0, b, own_a).start()
            normed_low[layer, kept(b), :] = result.astype(jnp.bfloat16)
            pl.when(b >= 1)(lambda: send_y(1, b - 1))
            to_other(0, b, own_a).wait()
            normed_low[layer, given(b), :] = land_back[0, b].astype(jnp.bfloat16)
            u = matmul(normed_low[layer, rows, :], w_in[layer]) + bias_in
            hidden[layer, rows, :] = u
            g = (u * normal_cdf(u)).astype(jnp.bfloat16)
            active[layer, rows, :] = g
            part[rows, :] = matmul(g, w_down[layer])
            to_core(1, b).start()

        repeat(BLOCKS, feed)
        send_y(1, BLOCKS - 1)

        gain_two, shift_two, bias_down = (
            vector(second_gain, layer),
            vector(second_shift, layer),
            vector(b_down, layer),
        )

        def receive(b):
            to_other(1, b, own_b).wait()
            inputs_low[layer + 1, given(b), :] = land_back[1, b].astype(jnp.bfloat16)

        def finish(b):
            before = own_a[packed(b), :] + summed(1, b) + bias_down
            zhat, scale = normed(before)
            zhat_two[layer, packed(b), :] = zhat
            scale_two[layer, packed(b), :] = scale
            result = zhat * gain_two + shift_two
            own_b[packed(b), :] = result
            to_other(1, b, own_b).start()
            inputs_low[layer + 1, kept(b), :] = result.astype(jnp.bfloat16)
            pl.when(b >= 1)(lambda: receive(b - 1))

        repeat(BLOCKS, finish)
        receive(BLOCKS - 1)

    repeat(LAYERS, forward)
    hidden_out[...] = inputs_low[LAYERS]

    def first_grad(b):
        own_b[packed(b), :] = cotangent[kept(b), :].astype(jnp.float32) * columns[kept(b), 0:1]

    repeat(BLOCKS, first_grad)
    sums[...] = jnp.zeros_like(sums)
    local_sums[...] = jnp.zeros_like(local_sums)

    def backward(turn):
        layer = LAYERS - 1 - turn
        base = turn * span
        start = turn * (span // CHUNK)
        in_base = base + hidden_width
        out_base = in_base + width
        qkv_base = out_base + head_width

        def rows_at(first, count):
            return pl.ds(pl.multiple_of(first, 64), count)

        def total_row(index, amount):
            sums[turn, index : index + 1, :] = sums[turn, index : index + 1, :] + jnp.sum(
                amount, axis=0, keepdims=True
            )

        def receive(back, b, source):
            to_other(back, b, source).wait()
            dz_low[given(b), :] = land_back[back, b].astype(jnp.bfloat16)

        gain_two = vector(second_gain, layer)

        def norm_two(b):
            grad = own_b[packed(b), :]
            zhat = zhat_two[layer, packed(b), :]
            dz = norm_back(grad, zhat, scale_two[layer, packed(b), :], gain_two)
            own_a[packed(b), :] = dz
            to_other(0, b, own_a).start()
            dz_low[kept(b), :] = dz.astype(jnp.bfloat16)
            total_row(0, grad * zhat)
            total_row(1, grad)
            total_row(2, dz)

        repeat(BLOCKS, norm_two)
        repeat(BLOCKS, lambda b: receive(0, b, own_a))

        def down_piece(p):
            grads[rows_at(base + 128 * p, 128), :] = contract_rows(
                active[layer, :, lanes(p)], dz_low[...]
            )

        def in_piece(p):
            grads[rows_at(in_base + 128 * p, 128), :] = contract_rows(
                normed_low[layer, :, lanes(p)], du_low[...]
            )

        down_piece(0)
        tick(start)
        tick(start + 1)

        def feed(b):
            rows = block(b)
            dg = contract_cols(dz_low[rows, :], w_down[layer])
            u = hidden[layer, rows, :]
            density = jnp.exp(u * u * (-0.5)) * (1.0 / math.sqrt(2.0 * math.pi))
            du = dg * (normal_cdf(u) + u * density)
            du_low[rows, :] = du.astype(jnp.bfloat16)
            local_sums[turn, 0:1, :] = local_sums[turn, 0:1, :] + jnp.sum(
                du, axis=0, keepdims=True
            )
            down_piece(b + 1)
            tick(start + 2 + 2 * b)
            tick(start + 3 + 2 * b)

        repeat(BLOCKS, feed)
        down_piece(5)

        def feed_in(b):
            rows = block(b)
            part[rows, :] = contract_cols(du_low[rows, :], w_in[layer])
            to_core(0, b).start()
            in_piece(b)
            tick(start + 10 + 2 * b)
            send_y(0, b)
            tick(start + 11 + 2 * b)

        repeat(BLOCKS, feed_in)
        in_piece(4)
        tick(start + 18)
        in_piece(5)
        tick(start + 19)

        gain = vector(first_gain, layer)

        def norm_one(b):
            grad = own_a[packed(b), :] + summed(0, b)
            zhat = zhat_one[layer, packed(b), :]
            dz = norm_back(grad, zhat, scale_one[layer, packed(b), :], gain)
            own_b[packed(b), :] = dz
            to_other(1, b, own_b).start()
            dz_low[kept(b), :] = dz.astype(jnp.bfloat16)
            total_row(3, grad * zhat)
            total_row(4, grad)
            total_row(5, dz)
            tick(start + 20 + b)
            receive(1, b, own_b)

        repeat(BLOCKS, norm_one)
        grads[rows_at(out_base, head_width), :] = contract_rows(heads[layer], dz_low[...])
        dheads[...] = contract_cols(dz_low[...], w_out[layer]).astype(jnp.bfloat16)
        dkeys[...] = jnp.zeros_like(dkeys)
        dvalues[...] = jnp.zeros_like(dvalues)

        def attend(b):
            rows = block(b)
            for h in range(local_heads):
                side = HEAD_DIM * h
                probs = jnp.exp(scores_of(layer, h, rows) - log_total[layer, rows, h : h + 1])
                dhead = dheads[rows, side : side + HEAD_DIM]
                dprobs = contract_cols(dhead, values[layer, h])
                dvalues[h] = dvalues[h] + contract_rows(probs.astype(jnp.bfloat16), dhead)
                inner = jnp.sum(probs * dprobs, axis=-1, keepdims=True)
                ds = (probs * (dprobs - inner)).astype(jnp.bfloat16)
                dq = matmul(ds, keys[layer, h]) * SCALE
                dkeys[h] = dkeys[h] + contract_rows(ds, queries[layer, h, rows, :])
                dqkv_low[rows, 3 * side : 3 * side + HEAD_DIM] = dq.astype(jnp.bfloat16)
                local_sums[turn, 1:2, 2 * side : 2 * side + HEAD_DIM] = local_sums[
                    turn, 1:2, 2 * side : 2 * side + HEAD_DIM
                ] + jnp.sum(dq, axis=0, keepdims=True)
            pl.when(b < BLOCKS - 1)(lambda: tick(start + 24 + b))

        repeat(BLOCKS, attend)
        for h in range(local_heads):
            side = HEAD_DIM * h
            dqkv_low[:, 3 * side + HEAD_DIM : 3 * side + 2 * HEAD_DIM] = (
                dkeys[h] * SCALE
            ).astype(jnp.bfloat16)
            dv = dvalues[h]
            dqkv_low[:, 3 * side + 2 * HEAD_DIM : 3 * side + 3 * HEAD_DIM] = dv.astype(
                jnp.bfloat16
            )
            local_sums[turn, 1:2, 2 * side + HEAD_DIM : 2 * side + 2 * HEAD_DIM] = jnp.sum(
                dv, axis=0, keepdims=True
            )

        def project(b):
            rows = block(b)
            part[rows, :] = contract_cols(dqkv_low[rows, :], w_qkv[layer])
            to_core(1, b).start()
            pl.when(b >= 1)(lambda: send_y(1, b - 1))

        repeat(BLOCKS, project)
        send_y(1, BLOCKS - 1)

        def qkv_piece(p):
            grads[rows_at(qkv_base + 128 * p, 128), :] = contract_rows(
                dqkv_low[:, lanes(p)], inputs_low[layer]
            )
            tick(start + 27 + 2 * p)
            tick(start + 28 + 2 * p)

        repeat(4, qkv_piece)
        grads[rows_at(qkv_base + 512, 64), :] = contract_rows(
            dqkv_low[:, 512:], inputs_low[layer]
        )
        tick(start + 35)

        def pass_on(b):
            own_b[packed(b), :] = own_b[packed(b), :] + summed(1, b)

        repeat(BLOCKS, pass_on)

    repeat(LAYERS, backward)

    def last_grad(b):
        live = columns[kept(b), 0:1]
        grad = own_b[packed(b), :]
        masked_grad = grad * (1.0 - live)
        own_a[packed(b), :] = masked_grad
        to_other(0, b, own_a).start()
        grad_embeddings[kept(b), :] = masked_grad.astype(jnp.bfloat16)
        grads[small_base : small_base + REPL, :] = grads[
            small_base : small_base + REPL, :
        ] + lax.dot_general(
            chosen(kept(b), OWN),
            grad * live,
            (((0,), (0,)), ((), ())),
            precision=lax.Precision.HIGHEST,
            preferred_element_type=jnp.float32,
        )

    repeat(BLOCKS, last_grad)
    shared = REPL + 8 * LAYERS
    for turn in range(LAYERS):
        first = small_base + REPL + 8 * turn
        grads[first : first + 8, :] = sums[turn]
    grads[small_base + shared : small_base + shared + 8, :] = local_sums[...].reshape(8, width)
    short = remote(
        grads.at[pl.ds(small_base, shared)], land_small, small_send, small_recv, place.core_peer
    )
    short.start()

    def receive(b):
        to_other(0, b, own_a).wait()
        grad_embeddings[given(b), :] = land_back[0, b].astype(jnp.bfloat16)

    repeat(BLOCKS, receive)
    short.wait()
    grads[small_base : small_base + shared, :] = (
        grads[small_base : small_base + shared, :] + land_small[...]
    )
    done = LAYERS * (span // CHUNK)
    repeat(grad_sum.ticks() - done, lambda i: tick(done + i))


def run_pages(args, sizes):
    width, hidden_width, local_heads, span = sizes
    rows = PAGE_LEN
    flat = LAYERS * span + CHUNK
    half = rows // 2
    low, full = jnp.bfloat16, jnp.float32
    vmem, dma = pltpu.VMEM, pltpu.SemaphoreType.DMA
    head_width = local_heads * HEAD_DIM
    return pl.pallas_call(
        functools.partial(page_kernel, sizes),
        name="pages",
        out_shape=(
            jax.ShapeDtypeStruct((rows, width), low),
            jax.ShapeDtypeStruct((rows, width), low),
            jax.ShapeDtypeStruct((flat, width), full),
        ),
        in_specs=[pl.BlockSpec(memory_space=pltpu.VMEM)] * len(args),
        out_specs=(
            pl.BlockSpec(memory_space=pltpu.VMEM),
            pl.BlockSpec(memory_space=pltpu.VMEM),
            pl.BlockSpec(memory_space=pl.ANY),
        ),
        scratch_shapes=[
            vmem((LAYERS + 1, rows, width), low),
            vmem((LAYERS, local_heads, rows, HEAD_DIM), low),
            vmem((LAYERS, local_heads, rows, HEAD_DIM), low),
            vmem((LAYERS, local_heads, rows, HEAD_DIM), low),
            vmem((LAYERS, rows, 128), full),
            vmem((LAYERS, rows, head_width), low),
            vmem((LAYERS, rows, width), low),
            vmem((LAYERS, rows, hidden_width), full),
            vmem((LAYERS, rows, hidden_width), low),
            vmem((LAYERS, half, width), full),
            vmem((LAYERS, half, 1), full),
            vmem((LAYERS, half, width), full),
            vmem((LAYERS, half, 1), full),
            vmem((rows, 128), full),
            vmem((half, width), full),
            vmem((half, width), full),
            vmem((rows, width), full),
            vmem((2, BLOCKS, OWN, width), full),
            vmem((2, BLOCKS, OWN, width), full),
            vmem((2, BLOCKS, OWN, width), full),
            vmem((REPL + 8 * LAYERS, width), full),
            vmem((rows, width), low),
            vmem((rows, hidden_width), low),
            vmem((rows, head_width), low),
            vmem((local_heads, rows, HEAD_DIM), full),
            vmem((local_heads, rows, HEAD_DIM), full),
            vmem((rows, 3 * head_width), low),
            vmem((LAYERS, 8, width), full),
            vmem((LAYERS, 4, width), full),
            vmem((flat, width), full),
            vmem((LANDINGS, SLOTS, UNIT, width), full),
            dma((2, BLOCKS)),
            dma((2, BLOCKS)),
            dma((2, BLOCKS)),
            dma((2, BLOCKS)),
            dma((2, BLOCKS)),
            dma((2, BLOCKS)),
            dma,
            dma,
            dma((KINDS, SLOTS)),
            dma((KINDS, SLOTS)),
            dma((2, SLOTS)),
        ],
        compiler_params=pltpu.CompilerParams(
            collective_id=0, has_side_effects=True, vmem_limit_bytes=62 << 20
        ),
    )(*args)


def on_device(*args):
    (embeddings, replace_table, replace_ids, masked, padding, w_qkv, b_qv, *_) = args
    width = embeddings.shape[1]
    head_width = w_qkv.shape[2] // 3
    hidden_width = args[11].shape[2]
    span = 2 * hidden_width + 4 * head_width
    args = list(args)
    for index in (2, 3, 4):
        args[index] = args[index].reshape(1, PAGE_LEN)
    hidden_out, grad_embeddings, every = run_pages(
        args, (width, hidden_width, head_width // HEAD_DIM, span)
    )
    groups = lax.axis_size("dp") // GROUP
    if groups > 1:
        every = lax.psum(
            every,
            "dp",
            axis_index_groups=[
                [low + GROUP * high for high in range(groups)] for low in range(GROUP)
            ],
        )

    def piece(first, rows):
        return jnp.stack(
            [
                lax.slice_in_dim(every, start, start + rows)
                for start in [first + span * turn for turn in reversed(range(LAYERS))]
            ]
        )

    base = LAYERS * span

    def short(row, step):
        return jnp.stack([every[base + row + step * turn] for turn in reversed(range(LAYERS))])

    grad_w_down = piece(0, hidden_width)
    grad_w_in = piece(hidden_width, width)
    grad_w_out = piece(hidden_width + width, head_width)
    grad_w_qkv = jnp.swapaxes(piece(hidden_width + width + head_width, 3 * head_width), 1, 2)
    local = REPL + 8 * LAYERS
    return (
        hidden_out,
        grad_embeddings,
        lax.slice_in_dim(every, base, base + REPL),
        grad_w_qkv,
        short(local + 1, 4)[:, : 2 * head_width],
        grad_w_out,
        short(REPL + 5, 8),
        short(REPL + 3, 8),
        short(REPL + 4, 8),
        grad_w_in,
        short(local, 4),
        grad_w_down,
        short(REPL + 2, 8),
        short(REPL, 8),
        short(REPL + 1, 8),
    )


def solution(mesh):
    placed = (
        P("dp", None),
        P(),
        P("dp"),
        P("dp"),
        P("dp"),
        P(None, None, "tensor"),
        P(None, "tensor"),
        P(None, "tensor", None),
        P(),
        P(),
        P(),
        P(None, None, "tensor"),
        P(None, "tensor"),
        P(None, "tensor", None),
        P(),
        P(),
        P(),
        P("dp", None),
    )
    return jax.shard_map(
        on_device,
        mesh=mesh,
        in_specs=placed,
        out_specs=(
            P("dp", None),
            P("dp", None),
            P(),
            P(None, None, "tensor"),
            P(None, "tensor"),
            P(None, "tensor", None),
            P(),
            P(),
            P(),
            P(None, None, "tensor"),
            P(None, "tensor"),
            P(None, "tensor", None),
            P(),
            P(),
            P(),
        ),
        check_vma=False,
    )
```

```python
import functools
import math

import jax
import jax.numpy as jnp
from jax import lax
from jax.experimental import pallas as pl
from jax.experimental.pallas import tpu as pltpu
from jax.sharding import PartitionSpec as P

HEAD_DIM = 64
LAYERS = 2
PAGE_LEN = 512
REPL = 32
EPSILON = 1e-12
SCALE = HEAD_DIM ** (-0.5)
MESH = pl.DeviceIdType.MESH

BLOCK = 128
OWN = BLOCK // 2
BLOCKS = PAGE_LEN // BLOCK

UNIT = 16
CHUNK = 4 * UNIT
LAG = 2
SLOTS = 4 * LAG
KINDS = 12
(TX, TNEAR, TFAR, TA1, TA2, TQ1, TQ2, TTA, TTN, TTM, TTF, TG) = range(KINDS)
LANDINGS = TTA + 1
GROUP = 8
WEIGHTS = (5, 7, 11, 13)


def contract_rows(left, right):
    return lax.dot_general(
        left, right, (((0,), (0,)), ((), ())), preferred_element_type=jnp.float32
    )


def contract_cols(left, right):
    return lax.dot_general(
        left, right, (((1,), (1,)), ((), ())), preferred_element_type=jnp.float32
    )


def matmul(left, right):
    return jnp.dot(left, right, preferred_element_type=jnp.float32)


def repeat(count, body):
    def step(index, carry):
        body(index)
        return carry

    lax.fori_loop(0, count, step, 0)


def normed(values):
    average = jnp.mean(values, axis=-1, keepdims=True)
    centered = values - average
    variance = jnp.mean(centered * centered, axis=-1, keepdims=True)
    scale = lax.rsqrt(variance + EPSILON)
    return centered * scale, scale


def norm_back(grad, zhat, scale, gain):
    scaled = grad * gain
    average = jnp.mean(scaled, axis=-1, keepdims=True)
    along = jnp.mean(scaled * zhat, axis=-1, keepdims=True)
    return scale * (scaled - average - zhat * along)


def normal_cdf(values):
    return 0.5 * (1.0 + lax.erf(values * math.sqrt(0.5)))


def column(row):
    return jnp.transpose(jnp.broadcast_to(row, (128, row.shape[1])))[:, :1]


class Place:
    def __init__(self):
        d = lax.axis_index("dp")
        t = lax.axis_index("tensor")
        self.core = lax.rem(t, 2)
        self.core_peer = (d, t + 1 - 2 * self.core)
        self.y_peer = (d, t + 2 - 4 * lax.div(t, 2))
        pair = lax.rem(d, 2)
        line = lax.rem(lax.div(d, 2), 4)
        self.pair = pair
        self.mid = jnp.logical_or(line == 1, line == 2)
        self.end = jnp.logical_not(self.mid)
        self.upper = lax.div(line, 2)
        self.peer = (d + 1 - 2 * pair, t)
        self.line = (d + 2 - 4 * lax.rem(line, 2), t)
        self.cross = (jnp.where(line == 1, d + 2, d - 2), t)


def greet(place, barrier):
    def signal(device):
        pl.semaphore_signal(barrier, inc=1, device_id=device, device_id_type=MESH)

    for device in (place.core_peer, place.y_peer, place.peer, place.line):
        signal(device)
    pl.when(place.mid)(lambda: signal(place.cross))


def meet(place, barrier):
    pl.semaphore_wait(barrier, jnp.where(place.mid, 5, 4))


class GradientSum:
    def __init__(self, place, chunks, part, landing, send, recv):
        self.place = place
        self.chunks = chunks
        self.part = part
        self.landing = landing
        self.send = send
        self.recv = recv

    def rows(self, j, unit):
        return pl.ds(pl.multiple_of(j * CHUNK + unit * UNIT, UNIT), UNIT)

    def tick(self, t):
        place, part = self.place, self.part
        mine, other = place.pair, 1 - place.pair
        near, far = 2 + place.upper, 3 - place.upper

        def at(j, unit):
            return part.at[self.rows(j, unit)]

        def copy(kind, j, source, target, device):
            slot = lax.rem(j, SLOTS)
            return pltpu.make_async_remote_copy(
                src_ref=source,
                dst_ref=target,
                send_sem=self.send.at[kind, slot],
                recv_sem=self.recv.at[kind, slot],
                device_id=device,
                device_id_type=MESH,
            )

        def partial(kind, j, unit, device):
            return copy(kind, j, at(j, unit), self.landing.at[kind, lax.rem(j, SLOTS)], device)

        def final(kind, j, unit, device):
            return copy(kind, j, at(j, unit), at(j, unit), device)

        def add(kind, j, unit):
            rows = self.rows(j, unit)
            part[rows, :] = part[rows, :] + self.landing[kind, lax.rem(j, SLOTS)]

        def pair_first(j):
            return partial(TX, j, other, place.peer)

        def near_in(j):
            return partial(TNEAR, j, near, place.line)

        def far_in(j):
            return partial(TFAR, j, far, place.line)

        def mine_in(j):
            return partial(TA1, j, mine, place.line)

        def mine_across(j):
            return partial(TA2, j, mine, place.cross)

        def far_across(j):
            return partial(TQ1, j, far, place.cross)

        def near_pair(j):
            return partial(TQ2, j, near, place.peer)

        def mine_out(j):
            return partial(TTA, j, mine, place.line)

        def near_out(j):
            return final(TTN, j, near, place.line)

        def near_across(j):
            return final(TTM, j, near, place.cross)

        def far_out(j):
            return final(TTF, j, far, place.line)

        def pair_last(j):
            return final(TG, j, mine, place.peer)

        def stage_0(j):
            pair_first(j).start()

            @pl.when(place.end)
            def _():
                near_in(j).start()
                far_in(j).start()

        def stage_1(j):
            pair_first(j).wait()
            add(TX, j, mine)

            @pl.when(place.end)
            def _():
                near_in(j).wait_send()
                far_in(j).wait_send()
                mine_in(j).start()

            @pl.when(place.mid)
            def _():
                far_in(j).wait_recv()
                add(TFAR, j, far)
                far_across(j).start()
                near_in(j).wait_recv()
                add(TNEAR, j, near)

        def stage_2(j):
            @pl.when(place.end)
            def _():
                mine_in(j).wait_send()

            @pl.when(place.mid)
            def _():
                mine_in(j).wait_recv()
                far_across(j).wait()
                add(TA1, j, mine)
                mine_across(j).start()
                add(TQ1, j, near)
                near_pair(j).start()

        def stage_3(j):
            @pl.when(place.mid)
            def _():
                mine_across(j).wait()
                add(TA2, j, mine)
                mine_out(j).start()
                near_pair(j).wait()
                add(TQ2, j, near)
                near_across(j).start()
                near_out(j).start()

        def stage_4(j):
            @pl.when(place.mid)
            def _():
                mine_out(j).wait_send()
                near_out(j).wait_send()
                pair_last(j).start()
                near_across(j).wait()
                far_out(j).start()

            @pl.when(place.end)
            def _():
                mine_out(j).wait_recv()
                near_out(j).wait_recv()
                part[self.rows(j, mine), :] = self.landing[TTA, lax.rem(j, SLOTS)]
                pair_last(j).start()

        def stage_5(j):
            pair_last(j).wait()
            pl.when(place.mid)(lambda: far_out(j).wait_send())
            pl.when(place.end)(lambda: far_out(j).wait_recv())

        stages = (stage_0, stage_1, stage_2, stage_3, stage_4, stage_5)
        for number in reversed(range(len(stages))):
            j = t - number * LAG
            pl.when(jnp.logical_and(j >= 0, j < self.chunks))(
                functools.partial(stages[number], j)
            )

    def ticks(self):
        return self.chunks + 5 * LAG


def page_kernel(
    sizes,
    embeddings,
    replace_table,
    replace_ids,
    masked,
    padding,
    w_qkv_far,
    b_qv,
    w_out_far,
    b_out,
    first_gain,
    first_shift,
    w_in_far,
    b_in,
    w_down_far,
    b_down,
    second_gain,
    second_shift,
    cotangent,
    hidden_out,
    grad_embeddings,
    grads,
    inputs_low,
    queries,
    keys,
    values,
    log_total,
    heads,
    normed_low,
    hidden,
    active,
    zhat_one,
    scale_one,
    zhat_two,
    scale_two,
    w_qkv,
    w_out,
    w_in,
    w_down,
    columns,
    own_a,
    own_b,
    part,
    land_core,
    land_y,
    land_back,
    land_small,
    dz_low,
    du_low,
    dheads,
    dkeys,
    dvalues,
    dqkv_low,
    sums,
    local_sums,
    landing,
    core_send,
    core_recv,
    y_send,
    y_recv,
    back_send,
    back_recv,
    small_send,
    small_recv,
    dp_send,
    dp_recv,
    weight_sem,
):
    width, hidden_width, local_heads, span = sizes
    head_width = local_heads * HEAD_DIM
    place = Place()
    core = place.core
    barrier = pltpu.get_barrier_semaphore()
    greet(place, barrier)
    weights = ((w_qkv_far, w_qkv), (w_out_far, w_out), (w_in_far, w_in), (w_down_far, w_down))

    def weight(index, layer):
        source, target = weights[index]
        return pltpu.make_async_copy(
            source.at[layer], target.at[layer], weight_sem.at[index, layer]
        )

    for layer in range(LAYERS):
        for index in range(len(weights)):
            weight(index, layer).start()
    small_base = LAYERS * span
    chunks = grads.shape[0] // CHUNK
    grad_sum = GradientSum(place, chunks, grads, landing, dp_send, dp_recv)
    tick = grad_sum.tick

    def vector(ref, layer):
        both = ref[...].astype(jnp.float32)
        return jnp.where(layer == 0, both[0:1], both[1:2])

    def block(b):
        return pl.ds(pl.multiple_of(b * BLOCK, BLOCK), BLOCK)

    def kept(b):
        return pl.ds(pl.multiple_of(b * BLOCK + core * OWN, OWN), OWN)

    def given(b):
        return pl.ds(pl.multiple_of(b * BLOCK + (1 - core) * OWN, OWN), OWN)

    def packed(b):
        return pl.ds(pl.multiple_of(b * OWN, OWN), OWN)

    def lanes(p, size=128):
        return pl.ds(pl.multiple_of(p * size, size), size)

    def remote(source, target, send, recv, device):
        return pltpu.make_async_remote_copy(
            src_ref=source,
            dst_ref=target,
            send_sem=send,
            recv_sem=recv,
            device_id=device,
            device_id_type=MESH,
        )

    def to_core(turn, b):
        return remote(
            part.at[given(b)],
            land_core.at[turn, b],
            core_send.at[turn, b],
            core_recv.at[turn, b],
            place.core_peer,
        )

    def over_y(turn, b):
        return remote(
            part.at[kept(b)],
            land_y.at[turn, b],
            y_send.at[turn, b],
            y_recv.at[turn, b],
            place.y_peer,
        )

    def to_other(turn, b, source):
        return remote(
            source.at[packed(b)],
            land_back.at[turn, b],
            back_send.at[turn, b],
            back_recv.at[turn, b],
            place.core_peer,
        )

    def send_y(turn, b):
        to_core(turn, b).wait()
        part[kept(b), :] = part[kept(b), :] + land_core[turn, b]
        over_y(turn, b).start()

    def summed(turn, b):
        over_y(turn, b).wait()
        return part[kept(b), :] + land_y[turn, b]

    pad_row = padding[...].astype(jnp.float32)
    live_row = masked[...].astype(jnp.float32) * pad_row
    bias_row = (pad_row - 1.0) * 10000.0
    columns[:, 0:1] = column(live_row)
    columns[:, 1:2] = column(replace_ids[...].astype(jnp.float32))
    grads[small_base:, :] = jnp.zeros((CHUNK, width), jnp.float32)

    def chosen(rows, count):
        spots = lax.broadcasted_iota(jnp.int32, (count, REPL), 1).astype(jnp.float32)
        return jnp.where(columns[rows, 1:2] == spots, 1.0, 0.0)

    def first_input(b):
        rows = block(b)
        picked = matmul(chosen(rows, BLOCK).astype(jnp.bfloat16), replace_table[...])
        taken = jnp.where(
            columns[rows, 0:1] > 0.0, picked, embeddings[rows, :].astype(jnp.float32)
        )
        inputs_low[0, rows, :] = taken.astype(jnp.bfloat16)

    repeat(BLOCKS, first_input)

    def scores_of(layer, h, rows):
        return contract_cols(queries[layer, h, rows, :], keys[layer, h]) * SCALE + bias_row

    def forward(layer):
        bias_pair = vector(b_qv, layer)

        def project(b):
            rows = block(b)
            projected = contract_cols(inputs_low[layer, rows, :], w_qkv[layer])
            for h in range(local_heads):
                base = 3 * HEAD_DIM * h
                bias = 2 * HEAD_DIM * h
                queries[layer, h, rows, :] = (
                    projected[:, base : base + HEAD_DIM] + bias_pair[:, bias : bias + HEAD_DIM]
                ).astype(jnp.bfloat16)
                keys[layer, h, rows, :] = projected[
                    :, base + HEAD_DIM : base + 2 * HEAD_DIM
                ].astype(jnp.bfloat16)
                values[layer, h, rows, :] = (
                    projected[:, base + 2 * HEAD_DIM : base + 3 * HEAD_DIM]
                    + bias_pair[:, bias + HEAD_DIM : bias + 2 * HEAD_DIM]
                ).astype(jnp.bfloat16)

        weight(0, layer).wait()
        repeat(BLOCKS, project)
        pl.when(layer == 0)(lambda: meet(place, barrier))
        weight(1, layer).wait()

        def attend(b):
            rows = block(b)
            outs = []
            for h in range(local_heads):
                scores = scores_of(layer, h, rows)
                largest = jnp.max(scores, axis=-1, keepdims=True)
                weights = jnp.exp(scores - largest)
                totals = jnp.sum(weights, axis=-1, keepdims=True)
                probs = (weights * (1.0 / totals)).astype(jnp.bfloat16)
                outs.append(matmul(probs, values[layer, h]).astype(jnp.bfloat16))
                log_total[layer, rows, h : h + 1] = largest + jnp.log(totals)
            joined = jnp.concatenate(outs, axis=1)
            heads[layer, rows, :] = joined
            part[rows, :] = matmul(joined, w_out[layer])
            to_core(0, b).start()
            pl.when(b >= 1)(lambda: send_y(0, b - 1))

        repeat(BLOCKS, attend)
        send_y(0, BLOCKS - 1)

        gain, shift, bias_out = vector(first_gain, layer), vector(first_shift, layer), vector(b_out, layer)
        bias_in = vector(b_in, layer)

        def feed(b):
            rows = block(b)
            before = (
                inputs_low[layer, kept(b), :].astype(jnp.float32) + summed(0, b) + bias_out
            )
            zhat, scale = normed(before)
            zhat_one[layer, packed(b), :] = zhat
            scale_one[layer, packed(b), :] = scale
            result = zhat * gain + shift
            own_a[packed(b), :] = result
            to_other(0, b, own_a).start()
            normed_low[layer, kept(b), :] = result.astype(jnp.bfloat16)
            pl.when(b >= 1)(lambda: send_y(1, b - 1))
            to_other(0, b, own_a).wait()
            normed_low[layer, given(b), :] = land_back[0, b].astype(jnp.bfloat16)
            u = matmul(normed_low[layer, rows, :], w_in[layer]) + bias_in
            hidden[layer, rows, :] = u
            g = (u * normal_cdf(u)).astype(jnp.bfloat16)
            active[layer, rows, :] = g
            part[rows, :] = matmul(g, w_down[layer])
            to_core(1, b).start()

        weight(2, layer).wait()
        weight(3, layer).wait()
        repeat(BLOCKS, feed)
        send_y(1, BLOCKS - 1)

        gain_two, shift_two, bias_down = (
            vector(second_gain, layer),
            vector(second_shift, layer),
            vector(b_down, layer),
        )

        def receive(b):
            to_other(1, b, own_b).wait()
            inputs_low[layer + 1, given(b), :] = land_back[1, b].astype(jnp.bfloat16)

        def finish(b):
            before = own_a[packed(b), :] + summed(1, b) + bias_down
            zhat, scale = normed(before)
            zhat_two[layer, packed(b), :] = zhat
            scale_two[layer, packed(b), :] = scale
            result = zhat * gain_two + shift_two
            own_b[packed(b), :] = result
            to_other(1, b, own_b).start()
            inputs_low[layer + 1, kept(b), :] = result.astype(jnp.bfloat16)
            pl.when(b >= 1)(lambda: receive(b - 1))

        repeat(BLOCKS, finish)
        receive(BLOCKS - 1)

    repeat(LAYERS, forward)
    hidden_out[...] = inputs_low[LAYERS]

    def first_grad(b):
        own_b[packed(b), :] = cotangent[kept(b), :].astype(jnp.float32) * columns[kept(b), 0:1]

    repeat(BLOCKS, first_grad)
    sums[...] = jnp.zeros_like(sums)
    local_sums[...] = jnp.zeros_like(local_sums)

    def backward(turn):
        layer = LAYERS - 1 - turn
        base = turn * span
        start = turn * (span // CHUNK)
        in_base = base + hidden_width
        out_base = in_base + width
        qkv_base = out_base + head_width

        def rows_at(first, count):
            return pl.ds(pl.multiple_of(first, 64), count)

        def total_row(index, amount):
            sums[turn, index : index + 1, :] = sums[turn, index : index + 1, :] + jnp.sum(
                amount, axis=0, keepdims=True
            )

        def receive(back, b, source):
            to_other(back, b, source).wait()
            dz_low[given(b), :] = land_back[back, b].astype(jnp.bfloat16)

        gain_two = vector(second_gain, layer)

        def norm_two(b):
            grad = own_b[packed(b), :]
            zhat = zhat_two[layer, packed(b), :]
            dz = norm_back(grad, zhat, scale_two[layer, packed(b), :], gain_two)
            own_a[packed(b), :] = dz
            to_other(0, b, own_a).start()
            dz_low[kept(b), :] = dz.astype(jnp.bfloat16)
            total_row(0, grad * zhat)
            total_row(1, grad)
            total_row(2, dz)

        repeat(BLOCKS, norm_two)
        repeat(BLOCKS, lambda b: receive(0, b, own_a))

        def down_piece(p):
            grads[rows_at(base + 128 * p, 128), :] = contract_rows(
                active[layer, :, lanes(p)], dz_low[...]
            )

        def in_piece(p):
            grads[rows_at(in_base + 128 * p, 128), :] = contract_rows(
                normed_low[layer, :, lanes(p)], du_low[...]
            )

        down_piece(0)
        tick(start)
        tick(start + 1)

        def feed(b):
            rows = block(b)
            dg = contract_cols(dz_low[rows, :], w_down[layer])
            u = hidden[layer, rows, :]
            density = jnp.exp(u * u * (-0.5)) * (1.0 / math.sqrt(2.0 * math.pi))
            du = dg * (normal_cdf(u) + u * density)
            du_low[rows, :] = du.astype(jnp.bfloat16)
            local_sums[turn, 0:1, :] = local_sums[turn, 0:1, :] + jnp.sum(
                du, axis=0, keepdims=True
            )
            down_piece(b + 1)
            tick(start + 2 + 2 * b)
            tick(start + 3 + 2 * b)

        repeat(BLOCKS, feed)
        down_piece(5)

        def feed_in(b):
            rows = block(b)
            part[rows, :] = contract_cols(du_low[rows, :], w_in[layer])
            to_core(0, b).start()
            in_piece(b)
            tick(start + 10 + 2 * b)
            send_y(0, b)
            tick(start + 11 + 2 * b)

        repeat(BLOCKS, feed_in)
        in_piece(4)
        tick(start + 18)
        in_piece(5)
        tick(start + 19)

        gain = vector(first_gain, layer)

        def norm_one(b):
            grad = own_a[packed(b), :] + summed(0, b)
            zhat = zhat_one[layer, packed(b), :]
            dz = norm_back(grad, zhat, scale_one[layer, packed(b), :], gain)
            own_b[packed(b), :] = dz
            to_other(1, b, own_b).start()
            dz_low[kept(b), :] = dz.astype(jnp.bfloat16)
            total_row(3, grad * zhat)
            total_row(4, grad)
            total_row(5, dz)
            tick(start + 20 + b)
            receive(1, b, own_b)

        repeat(BLOCKS, norm_one)
        grads[rows_at(out_base, head_width), :] = contract_rows(heads[layer], dz_low[...])
        dheads[...] = contract_cols(dz_low[...], w_out[layer]).astype(jnp.bfloat16)
        dkeys[...] = jnp.zeros_like(dkeys)
        dvalues[...] = jnp.zeros_like(dvalues)

        def attend(b):
            rows = block(b)
            for h in range(local_heads):
                side = HEAD_DIM * h
                probs = jnp.exp(scores_of(layer, h, rows) - log_total[layer, rows, h : h + 1])
                dhead = dheads[rows, side : side + HEAD_DIM]
                dprobs = contract_cols(dhead, values[layer, h])
                dvalues[h] = dvalues[h] + contract_rows(probs.astype(jnp.bfloat16), dhead)
                inner = jnp.sum(probs * dprobs, axis=-1, keepdims=True)
                ds = (probs * (dprobs - inner)).astype(jnp.bfloat16)
                dq = matmul(ds, keys[layer, h]) * SCALE
                dkeys[h] = dkeys[h] + contract_rows(ds, queries[layer, h, rows, :])
                dqkv_low[rows, 3 * side : 3 * side + HEAD_DIM] = dq.astype(jnp.bfloat16)
                local_sums[turn, 1:2, 2 * side : 2 * side + HEAD_DIM] = local_sums[
                    turn, 1:2, 2 * side : 2 * side + HEAD_DIM
                ] + jnp.sum(dq, axis=0, keepdims=True)
            pl.when(b < BLOCKS - 1)(lambda: tick(start + 24 + b))

        repeat(BLOCKS, attend)
        for h in range(local_heads):
            side = HEAD_DIM * h
            dqkv_low[:, 3 * side + HEAD_DIM : 3 * side + 2 * HEAD_DIM] = (
                dkeys[h] * SCALE
            ).astype(jnp.bfloat16)
            dv = dvalues[h]
            dqkv_low[:, 3 * side + 2 * HEAD_DIM : 3 * side + 3 * HEAD_DIM] = dv.astype(
                jnp.bfloat16
            )
            local_sums[turn, 1:2, 2 * side + HEAD_DIM : 2 * side + 2 * HEAD_DIM] = jnp.sum(
                dv, axis=0, keepdims=True
            )

        def project(b):
            rows = block(b)
            part[rows, :] = matmul(dqkv_low[rows, :], w_qkv[layer])
            to_core(1, b).start()
            pl.when(b >= 1)(lambda: send_y(1, b - 1))

        repeat(BLOCKS, project)
        send_y(1, BLOCKS - 1)

        def qkv_piece(p):
            grads[rows_at(qkv_base + 128 * p, 128), :] = contract_rows(
                dqkv_low[:, lanes(p)], inputs_low[layer]
            )
            tick(start + 27 + 2 * p)
            tick(start + 28 + 2 * p)

        repeat(4, qkv_piece)
        grads[rows_at(qkv_base + 512, 64), :] = contract_rows(
            dqkv_low[:, 512:], inputs_low[layer]
        )
        tick(start + 35)

        def pass_on(b):
            own_b[packed(b), :] = own_b[packed(b), :] + summed(1, b)

        repeat(BLOCKS, pass_on)

    repeat(LAYERS, backward)

    def last_grad(b):
        live = columns[kept(b), 0:1]
        grad = own_b[packed(b), :]
        masked_grad = grad * (1.0 - live)
        own_a[packed(b), :] = masked_grad
        to_other(0, b, own_a).start()
        grad_embeddings[kept(b), :] = masked_grad.astype(jnp.bfloat16)
        grads[small_base : small_base + REPL, :] = grads[
            small_base : small_base + REPL, :
        ] + lax.dot_general(
            chosen(kept(b), OWN),
            grad * live,
            (((0,), (0,)), ((), ())),
            precision=lax.Precision.HIGHEST,
            preferred_element_type=jnp.float32,
        )

    repeat(BLOCKS, last_grad)
    shared = REPL + 8 * LAYERS
    for turn in range(LAYERS):
        first = small_base + REPL + 8 * turn
        grads[first : first + 8, :] = sums[turn]
    grads[small_base + shared : small_base + shared + 8, :] = local_sums[...].reshape(8, width)
    short = remote(
        grads.at[pl.ds(small_base, shared)], land_small, small_send, small_recv, place.core_peer
    )
    short.start()

    def receive(b):
        to_other(0, b, own_a).wait()
        grad_embeddings[given(b), :] = land_back[0, b].astype(jnp.bfloat16)

    repeat(BLOCKS, receive)
    short.wait()
    grads[small_base : small_base + shared, :] = (
        grads[small_base : small_base + shared, :] + land_small[...]
    )
    done = LAYERS * (span // CHUNK)
    repeat(grad_sum.ticks() - done, lambda i: tick(done + i))


def run_pages(args, sizes):
    width, hidden_width, local_heads, span = sizes
    rows = PAGE_LEN
    flat = LAYERS * span + CHUNK
    half = rows // 2
    low, full = jnp.bfloat16, jnp.float32
    vmem, dma = pltpu.VMEM, pltpu.SemaphoreType.DMA
    head_width = local_heads * HEAD_DIM
    return pl.pallas_call(
        functools.partial(page_kernel, sizes),
        name="pages",
        out_shape=(
            vmem((rows, width), low),
            vmem((rows, width), low),
            vmem((flat, width), full),
        ),
        in_specs=[
            pl.BlockSpec(memory_space=pl.ANY if index in WEIGHTS else pltpu.VMEM)
            for index in range(len(args))
        ],
        out_specs=(
            pl.BlockSpec(memory_space=pltpu.VMEM),
            pl.BlockSpec(memory_space=pltpu.VMEM),
            pl.BlockSpec(memory_space=pltpu.VMEM),
        ),
        scratch_shapes=[
            vmem((LAYERS + 1, rows, width), low),
            vmem((LAYERS, local_heads, rows, HEAD_DIM), low),
            vmem((LAYERS, local_heads, rows, HEAD_DIM), low),
            vmem((LAYERS, local_heads, rows, HEAD_DIM), low),
            vmem((LAYERS, rows, 128), full),
            vmem((LAYERS, rows, head_width), low),
            vmem((LAYERS, rows, width), low),
            vmem((LAYERS, rows, hidden_width), full),
            vmem((LAYERS, rows, hidden_width), low),
            vmem((LAYERS, half, width), full),
            vmem((LAYERS, half, 1), full),
            vmem((LAYERS, half, width), full),
            vmem((LAYERS, half, 1), full),
            vmem((LAYERS, 3 * head_width, width), low),
            vmem((LAYERS, head_width, width), low),
            vmem((LAYERS, width, hidden_width), low),
            vmem((LAYERS, hidden_width, width), low),
            vmem((rows, 128), full),
            vmem((half, width), full),
            vmem((half, width), full),
            vmem((rows, width), full),
            vmem((2, BLOCKS, OWN, width), full),
            vmem((2, BLOCKS, OWN, width), full),
            vmem((2, BLOCKS, OWN, width), full),
            vmem((REPL + 8 * LAYERS, width), full),
            vmem((rows, width), low),
            vmem((rows, hidden_width), low),
            vmem((rows, head_width), low),
            vmem((local_heads, rows, HEAD_DIM), full),
            vmem((local_heads, rows, HEAD_DIM), full),
            vmem((rows, 3 * head_width), low),
            vmem((LAYERS, 8, width), full),
            vmem((LAYERS, 4, width), full),
            vmem((LANDINGS, SLOTS, UNIT, width), full),
            dma((2, BLOCKS)),
            dma((2, BLOCKS)),
            dma((2, BLOCKS)),
            dma((2, BLOCKS)),
            dma((2, BLOCKS)),
            dma((2, BLOCKS)),
            dma,
            dma,
            dma((KINDS, SLOTS)),
            dma((KINDS, SLOTS)),
            dma((4, LAYERS)),
        ],
        compiler_params=pltpu.CompilerParams(
            collective_id=0, has_side_effects=True, vmem_limit_bytes=46 << 20
        ),
    )(*args)


def place_kernel(sizes, hidden_out, grad_embeddings, every, *refs):
    width, hidden_width, local_heads, span = sizes
    head_width = local_heads * HEAD_DIM
    (
        out_hidden,
        out_embeddings,
        out_table,
        out_w_qkv,
        out_b_qv,
        out_w_out,
        out_b_out,
        out_first_gain,
        out_first_shift,
        out_w_in,
        out_b_in,
        out_w_down,
        out_b_down,
        out_second_gain,
        out_second_shift,
        short,
        sems,
    ) = refs
    base = LAYERS * span
    pairs = [(every.at[pl.ds(base, CHUNK)], short), (every.at[pl.ds(base, REPL)], out_table)]
    pairs += [(hidden_out, out_hidden), (grad_embeddings, out_embeddings)]
    for turn in range(LAYERS):
        first = span * turn
        for ref, rows in (
            (out_w_down, hidden_width),
            (out_w_in, width),
            (out_w_out, head_width),
            (out_w_qkv, 3 * head_width),
        ):
            pairs.append((every.at[pl.ds(first, rows)], ref.at[LAYERS - 1 - turn]))
            first += rows
    copies = [
        pltpu.make_async_copy(source, target, sems.at[index])
        for index, (source, target) in enumerate(pairs)
    ]
    for copy in copies:
        copy.start()
    copies[0].wait()
    local = REPL + 8 * LAYERS
    for ref, row, step in (
        (out_second_gain, REPL, 8),
        (out_second_shift, REPL + 1, 8),
        (out_b_down, REPL + 2, 8),
        (out_first_gain, REPL + 3, 8),
        (out_first_shift, REPL + 4, 8),
        (out_b_out, REPL + 5, 8),
        (out_b_in, local, 4),
        (out_b_qv, local + 1, 4),
    ):
        for turn in range(LAYERS):
            layer = LAYERS - 1 - turn
            ref[layer : layer + 1, :] = short[
                row + step * turn : row + step * turn + 1, : ref.shape[1]
            ]
    for copy in copies[1:]:
        copy.wait()


def place_outputs(hidden_out, grad_embeddings, every, sizes):
    width, hidden_width, local_heads, span = sizes
    head_width = local_heads * HEAD_DIM
    low, full = jnp.bfloat16, jnp.float32
    rows = hidden_out.shape[0]
    shapes = (
        ((rows, width), low),
        ((rows, width), low),
        ((REPL, width), full),
        ((LAYERS, 3 * head_width, width), full),
        ((LAYERS, 2 * head_width), full),
        ((LAYERS, head_width, width), full),
        ((LAYERS, width), full),
        ((LAYERS, width), full),
        ((LAYERS, width), full),
        ((LAYERS, width, hidden_width), full),
        ((LAYERS, hidden_width), full),
        ((LAYERS, hidden_width, width), full),
        ((LAYERS, width), full),
        ((LAYERS, width), full),
        ((LAYERS, width), full),
    )
    far = pl.BlockSpec(memory_space=pl.ANY)
    close = pl.BlockSpec(memory_space=pltpu.VMEM)
    return pl.pallas_call(
        functools.partial(place_kernel, sizes),
        name="place_outputs",
        out_shape=[jax.ShapeDtypeStruct(shape, kind) for shape, kind in shapes],
        in_specs=[far] * 3,
        out_specs=[close if shape[0] == LAYERS and len(shape) == 2 else far for shape, _ in shapes],
        scratch_shapes=[
            pltpu.VMEM((CHUNK, width), full),
            pltpu.SemaphoreType.DMA((4 + 4 * LAYERS,)),
        ],
    )(hidden_out, grad_embeddings, every)


def moved(every):
    def kernel(source, target, sem):
        copy = pltpu.make_async_copy(source, target, sem)
        copy.start()
        copy.wait()

    far = pl.BlockSpec(memory_space=pl.ANY)
    return pl.pallas_call(
        kernel,
        name="moved",
        out_shape=jax.ShapeDtypeStruct(every.shape, every.dtype),
        in_specs=[far],
        out_specs=far,
        scratch_shapes=[pltpu.SemaphoreType.DMA],
    )(every)


def on_device(*args):
    (embeddings, replace_table, replace_ids, masked, padding, w_qkv, b_qv, *_) = args
    width = embeddings.shape[1]
    head_width = w_qkv.shape[2] // 3
    hidden_width = args[11].shape[2]
    span = 2 * hidden_width + 4 * head_width
    args = list(args)
    args[5] = jnp.swapaxes(args[5], 1, 2)
    for index in (2, 3, 4):
        args[index] = args[index].reshape(1, PAGE_LEN)
    sizes = (width, hidden_width, head_width // HEAD_DIM, span)
    hidden_out, grad_embeddings, every = run_pages(args, sizes)
    groups = lax.axis_size("dp") // GROUP
    if groups > 1:
        every = lax.psum(
            moved(every),
            "dp",
            axis_index_groups=[
                [low + GROUP * high for high in range(groups)] for low in range(GROUP)
            ],
        )

    results = place_outputs(hidden_out, grad_embeddings, every, sizes)
    return (*results[:3], jnp.swapaxes(results[3], 1, 2), *results[4:])


def solution(mesh):
    placed = (
        P("dp", None),
        P(),
        P("dp"),
        P("dp"),
        P("dp"),
        P(None, None, "tensor"),
        P(None, "tensor"),
        P(None, "tensor", None),
        P(),
        P(),
        P(),
        P(None, None, "tensor"),
        P(None, "tensor"),
        P(None, "tensor", None),
        P(),
        P(),
        P(),
        P("dp", None),
    )
    return jax.shard_map(
        on_device,
        mesh=mesh,
        in_specs=placed,
        out_specs=(
            P("dp", None),
            P("dp", None),
            P(),
            P(None, None, "tensor"),
            P(None, "tensor"),
            P(None, "tensor", None),
            P(),
            P(),
            P(),
            P(None, None, "tensor"),
            P(None, "tensor"),
            P(None, "tensor", None),
            P(),
            P(),
            P(),
        ),
        check_vma=False,
    )
```

```python
import functools
import math

import jax
import jax.numpy as jnp
from jax import lax
from jax.experimental import pallas as pl
from jax.experimental.pallas import tpu as pltpu
from jax.sharding import PartitionSpec as P

HEAD_DIM = 64
LAYERS = 2
PAGE_LEN = 512
REPL = 32
EPSILON = 1e-12
SCALE = HEAD_DIM ** (-0.5)
MESH = pl.DeviceIdType.MESH

BLOCK = 128
OWN = BLOCK // 2
BLOCKS = PAGE_LEN // BLOCK

UNIT = 16
CHUNK = 4 * UNIT
LAG = 2
SLOTS = 4 * LAG
KINDS = 12
(TX, TNEAR, TFAR, TA1, TA2, TQ1, TQ2, TTA, TTN, TTM, TTF, TG) = range(KINDS)
LANDINGS = TTA + 1
GROUP = 8
WEIGHTS = (5, 7, 11, 13)


def contract_rows(left, right):
    return lax.dot_general(
        left, right, (((0,), (0,)), ((), ())), preferred_element_type=jnp.float32
    )


def contract_cols(left, right):
    return lax.dot_general(
        left, right, (((1,), (1,)), ((), ())), preferred_element_type=jnp.float32
    )


def matmul(left, right):
    return jnp.dot(left, right, preferred_element_type=jnp.float32)


def repeat(count, body):
    def step(index, carry):
        body(index)
        return carry

    lax.fori_loop(0, count, step, 0)


def normed(values):
    average = jnp.mean(values, axis=-1, keepdims=True)
    centered = values - average
    variance = jnp.mean(centered * centered, axis=-1, keepdims=True)
    scale = lax.rsqrt(variance + EPSILON)
    return centered * scale, scale


def norm_back(grad, zhat, scale, gain):
    scaled = grad * gain
    average = jnp.mean(scaled, axis=-1, keepdims=True)
    along = jnp.mean(scaled * zhat, axis=-1, keepdims=True)
    return scale * (scaled - average - zhat * along)


def normal_cdf(values):
    return 0.5 * (1.0 + lax.erf(values * math.sqrt(0.5)))


def column(row):
    return jnp.transpose(jnp.broadcast_to(row, (128, row.shape[1])))[:, :1]


class Place:
    def __init__(self):
        d = lax.axis_index("dp")
        t = lax.axis_index("tensor")
        self.core = lax.rem(t, 2)
        self.core_peer = (d, t + 1 - 2 * self.core)
        self.y_peer = (d, t + 2 - 4 * lax.div(t, 2))
        pair = lax.rem(d, 2)
        line = lax.rem(lax.div(d, 2), 4)
        self.pair = pair
        self.mid = jnp.logical_or(line == 1, line == 2)
        self.end = jnp.logical_not(self.mid)
        self.upper = lax.div(line, 2)
        self.peer = (d + 1 - 2 * pair, t)
        self.line = (d + 2 - 4 * lax.rem(line, 2), t)
        self.cross = (jnp.where(line == 1, d + 2, d - 2), t)


def greet(place, barrier):
    def signal(device):
        pl.semaphore_signal(barrier, inc=1, device_id=device, device_id_type=MESH)

    for device in (place.core_peer, place.y_peer, place.peer, place.line):
        signal(device)
    pl.when(place.mid)(lambda: signal(place.cross))


def meet(place, barrier):
    pl.semaphore_wait(barrier, jnp.where(place.mid, 5, 4))


class GradientSum:
    def __init__(self, place, chunks, part, landing, send, recv):
        self.place = place
        self.chunks = chunks
        self.part = part
        self.landing = landing
        self.send = send
        self.recv = recv

    def rows(self, j, unit):
        return pl.ds(pl.multiple_of(j * CHUNK + unit * UNIT, UNIT), UNIT)

    def tick(self, t):
        place, part = self.place, self.part
        mine, other = place.pair, 1 - place.pair
        near, far = 2 + place.upper, 3 - place.upper

        def at(j, unit):
            return part.at[self.rows(j, unit)]

        def copy(kind, j, source, target, device):
            slot = lax.rem(j, SLOTS)
            return pltpu.make_async_remote_copy(
                src_ref=source,
                dst_ref=target,
                send_sem=self.send.at[kind, slot],
                recv_sem=self.recv.at[kind, slot],
                device_id=device,
                device_id_type=MESH,
            )

        def partial(kind, j, unit, device):
            return copy(kind, j, at(j, unit), self.landing.at[kind, lax.rem(j, SLOTS)], device)

        def final(kind, j, unit, device):
            return copy(kind, j, at(j, unit), at(j, unit), device)

        def add(kind, j, unit):
            rows = self.rows(j, unit)
            part[rows, :] = part[rows, :] + self.landing[kind, lax.rem(j, SLOTS)]

        def pair_first(j):
            return partial(TX, j, other, place.peer)

        def near_in(j):
            return partial(TNEAR, j, near, place.line)

        def far_in(j):
            return partial(TFAR, j, far, place.line)

        def mine_in(j):
            return partial(TA1, j, mine, place.line)

        def mine_across(j):
            return partial(TA2, j, mine, place.cross)

        def far_across(j):
            return partial(TQ1, j, far, place.cross)

        def near_pair(j):
            return partial(TQ2, j, near, place.peer)

        def mine_out(j):
            return partial(TTA, j, mine, place.line)

        def near_out(j):
            return final(TTN, j, near, place.line)

        def near_across(j):
            return final(TTM, j, near, place.cross)

        def far_out(j):
            return final(TTF, j, far, place.line)

        def pair_last(j):
            return final(TG, j, mine, place.peer)

        def stage_0(j):
            pair_first(j).start()

            @pl.when(place.end)
            def _():
                near_in(j).start()
                far_in(j).start()

        def stage_1(j):
            pair_first(j).wait()
            add(TX, j, mine)

            @pl.when(place.end)
            def _():
                near_in(j).wait_send()
                far_in(j).wait_send()
                mine_in(j).start()

            @pl.when(place.mid)
            def _():
                far_in(j).wait_recv()
                add(TFAR, j, far)
                far_across(j).start()
                near_in(j).wait_recv()
                add(TNEAR, j, near)

        def stage_2(j):
            @pl.when(place.end)
            def _():
                mine_in(j).wait_send()

            @pl.when(place.mid)
            def _():
                mine_in(j).wait_recv()
                far_across(j).wait()
                add(TA1, j, mine)
                mine_across(j).start()
                add(TQ1, j, near)
                near_pair(j).start()

        def stage_3(j):
            @pl.when(place.mid)
            def _():
                mine_across(j).wait()
                add(TA2, j, mine)
                mine_out(j).start()
                near_pair(j).wait()
                add(TQ2, j, near)
                near_across(j).start()
                near_out(j).start()

        def stage_4(j):
            @pl.when(place.mid)
            def _():
                mine_out(j).wait_send()
                near_out(j).wait_send()
                pair_last(j).start()
                near_across(j).wait()
                far_out(j).start()

            @pl.when(place.end)
            def _():
                mine_out(j).wait_recv()
                near_out(j).wait_recv()
                part[self.rows(j, mine), :] = self.landing[TTA, lax.rem(j, SLOTS)]
                pair_last(j).start()

        def stage_5(j):
            pair_last(j).wait()
            pl.when(place.mid)(lambda: far_out(j).wait_send())
            pl.when(place.end)(lambda: far_out(j).wait_recv())

        stages = (stage_0, stage_1, stage_2, stage_3, stage_4, stage_5)
        for number in reversed(range(len(stages))):
            j = t - number * LAG
            pl.when(jnp.logical_and(j >= 0, j < self.chunks))(
                functools.partial(stages[number], j)
            )

    def ticks(self):
        return self.chunks + 5 * LAG


def page_kernel(
    sizes,
    embeddings,
    replace_table,
    replace_ids,
    masked,
    padding,
    w_qkv_far,
    b_qv,
    w_out_far,
    b_out,
    first_gain,
    first_shift,
    w_in_far,
    b_in,
    w_down_far,
    b_down,
    second_gain,
    second_shift,
    cotangent,
    hidden_out,
    grad_embeddings,
    grads,
    inputs_low,
    queries,
    keys,
    values,
    log_total,
    heads,
    normed_low,
    hidden,
    active,
    zhat_one,
    scale_one,
    zhat_two,
    scale_two,
    w_qkv,
    w_out,
    w_in,
    w_down,
    columns,
    own_a,
    own_b,
    part,
    land_core,
    land_y,
    land_back,
    land_small,
    dz_low,
    du_low,
    dheads,
    dkeys,
    dvalues,
    dqkv_low,
    sums,
    local_sums,
    landing,
    core_send,
    core_recv,
    y_send,
    y_recv,
    back_send,
    back_recv,
    small_send,
    small_recv,
    dp_send,
    dp_recv,
    weight_sem,
):
    width, hidden_width, local_heads, span = sizes
    head_width = local_heads * HEAD_DIM
    place = Place()
    core = place.core
    barrier = pltpu.get_barrier_semaphore()
    greet(place, barrier)
    weights = ((w_qkv_far, w_qkv), (w_out_far, w_out), (w_in_far, w_in), (w_down_far, w_down))

    def weight(index, layer):
        source, target = weights[index]
        return pltpu.make_async_copy(
            source.at[layer], target.at[layer], weight_sem.at[index, layer]
        )

    for layer in range(LAYERS):
        for index in range(len(weights)):
            weight(index, layer).start()
    small_base = LAYERS * span
    chunks = grads.shape[0] // CHUNK
    grad_sum = GradientSum(place, chunks, grads, landing, dp_send, dp_recv)
    tick = grad_sum.tick

    def vector(ref, layer):
        both = ref[...].astype(jnp.float32)
        return jnp.where(layer == 0, both[0:1], both[1:2])

    def block(b):
        return pl.ds(pl.multiple_of(b * BLOCK, BLOCK), BLOCK)

    def kept(b):
        return pl.ds(pl.multiple_of(b * BLOCK + core * OWN, OWN), OWN)

    def given(b):
        return pl.ds(pl.multiple_of(b * BLOCK + (1 - core) * OWN, OWN), OWN)

    def packed(b):
        return pl.ds(pl.multiple_of(b * OWN, OWN), OWN)

    def lanes(p, size=128):
        return pl.ds(pl.multiple_of(p * size, size), size)

    def remote(source, target, send, recv, device):
        return pltpu.make_async_remote_copy(
            src_ref=source,
            dst_ref=target,
            send_sem=send,
            recv_sem=recv,
            device_id=device,
            device_id_type=MESH,
        )

    def to_core(turn, b):
        return remote(
            part.at[given(b)],
            land_core.at[turn, b],
            core_send.at[turn, b],
            core_recv.at[turn, b],
            place.core_peer,
        )

    def over_y(turn, b):
        return remote(
            part.at[kept(b)],
            land_y.at[turn, b],
            y_send.at[turn, b],
            y_recv.at[turn, b],
            place.y_peer,
        )

    def to_other(turn, b, source):
        return remote(
            source.at[packed(b)],
            land_back.at[turn, b],
            back_send.at[turn, b],
            back_recv.at[turn, b],
            place.core_peer,
        )

    def send_y(turn, b):
        to_core(turn, b).wait()
        part[kept(b), :] = part[kept(b), :] + land_core[turn, b]
        over_y(turn, b).start()

    def summed(turn, b):
        over_y(turn, b).wait()
        return part[kept(b), :] + land_y[turn, b]

    pad_row = padding[...].astype(jnp.float32)
    live_row = masked[...].astype(jnp.float32) * pad_row
    bias_row = (pad_row - 1.0) * 10000.0
    columns[:, 0:1] = column(live_row)
    columns[:, 1:2] = column(replace_ids[...].astype(jnp.float32))
    grads[small_base:, :] = jnp.zeros((CHUNK, width), jnp.float32)

    def chosen(rows, count):
        spots = lax.broadcasted_iota(jnp.int32, (count, REPL), 1).astype(jnp.float32)
        return jnp.where(columns[rows, 1:2] == spots, 1.0, 0.0)

    def first_input(b):
        rows = block(b)
        picked = matmul(chosen(rows, BLOCK).astype(jnp.bfloat16), replace_table[...])
        taken = jnp.where(
            columns[rows, 0:1] > 0.0, picked, embeddings[rows, :].astype(jnp.float32)
        )
        inputs_low[0, rows, :] = taken.astype(jnp.bfloat16)

    repeat(BLOCKS, first_input)

    def scores_of(layer, h, rows):
        return contract_cols(queries[layer, h, rows, :], keys[layer, h]) * SCALE + bias_row

    def forward(layer):
        bias_pair = vector(b_qv, layer)

        def project(b):
            rows = block(b)
            projected = contract_cols(inputs_low[layer, rows, :], w_qkv[layer])
            for h in range(local_heads):
                base = 3 * HEAD_DIM * h
                bias = 2 * HEAD_DIM * h
                queries[layer, h, rows, :] = (
                    projected[:, base : base + HEAD_DIM] + bias_pair[:, bias : bias + HEAD_DIM]
                ).astype(jnp.bfloat16)
                keys[layer, h, rows, :] = projected[
                    :, base + HEAD_DIM : base + 2 * HEAD_DIM
                ].astype(jnp.bfloat16)
                values[layer, h, rows, :] = (
                    projected[:, base + 2 * HEAD_DIM : base + 3 * HEAD_DIM]
                    + bias_pair[:, bias + HEAD_DIM : bias + 2 * HEAD_DIM]
                ).astype(jnp.bfloat16)

        weight(0, layer).wait()
        repeat(BLOCKS, project)
        pl.when(layer == 0)(lambda: meet(place, barrier))
        weight(1, layer).wait()

        def attend(b):
            rows = block(b)
            outs = []
            for h in range(local_heads):
                scores = scores_of(layer, h, rows)
                largest = jnp.max(scores, axis=-1, keepdims=True)
                weights = jnp.exp(scores - largest)
                totals = jnp.sum(weights, axis=-1, keepdims=True)
                probs = (weights * (1.0 / totals)).astype(jnp.bfloat16)
                outs.append(matmul(probs, values[layer, h]).astype(jnp.bfloat16))
                log_total[layer, rows, h : h + 1] = largest + jnp.log(totals)
            joined = jnp.concatenate(outs, axis=1)
            heads[layer, rows, :] = joined
            part[rows, :] = matmul(joined, w_out[layer])
            to_core(0, b).start()
            pl.when(b >= 1)(lambda: send_y(0, b - 1))

        repeat(BLOCKS, attend)
        send_y(0, BLOCKS - 1)

        gain, shift, bias_out = vector(first_gain, layer), vector(first_shift, layer), vector(b_out, layer)
        bias_in = vector(b_in, layer)

        def feed(b):
            rows = block(b)
            before = (
                inputs_low[layer, kept(b), :].astype(jnp.float32) + summed(0, b) + bias_out
            )
            zhat, scale = normed(before)
            zhat_one[layer, packed(b), :] = zhat
            scale_one[layer, packed(b), :] = scale
            result = zhat * gain + shift
            own_a[packed(b), :] = result
            to_other(0, b, own_a).start()
            normed_low[layer, kept(b), :] = result.astype(jnp.bfloat16)
            pl.when(b >= 1)(lambda: send_y(1, b - 1))
            to_other(0, b, own_a).wait()
            normed_low[layer, given(b), :] = land_back[0, b].astype(jnp.bfloat16)
            u = matmul(normed_low[layer, rows, :], w_in[layer]) + bias_in
            hidden[layer, rows, :] = u
            g = (u * normal_cdf(u)).astype(jnp.bfloat16)
            active[layer, rows, :] = g
            part[rows, :] = matmul(g, w_down[layer])
            to_core(1, b).start()

        weight(2, layer).wait()
        weight(3, layer).wait()
        repeat(BLOCKS, feed)
        send_y(1, BLOCKS - 1)

        gain_two, shift_two, bias_down = (
            vector(second_gain, layer),
            vector(second_shift, layer),
            vector(b_down, layer),
        )

        def receive(b):
            to_other(1, b, own_b).wait()
            inputs_low[layer + 1, given(b), :] = land_back[1, b].astype(jnp.bfloat16)

        def finish(b):
            before = own_a[packed(b), :] + summed(1, b) + bias_down
            zhat, scale = normed(before)
            zhat_two[layer, packed(b), :] = zhat
            scale_two[layer, packed(b), :] = scale
            result = zhat * gain_two + shift_two
            own_b[packed(b), :] = result
            to_other(1, b, own_b).start()
            inputs_low[layer + 1, kept(b), :] = result.astype(jnp.bfloat16)
            pl.when(b >= 1)(lambda: receive(b - 1))

        repeat(BLOCKS, finish)
        receive(BLOCKS - 1)

    repeat(LAYERS, forward)
    hidden_out[...] = inputs_low[LAYERS]

    def first_grad(b):
        own_b[packed(b), :] = cotangent[kept(b), :].astype(jnp.float32) * columns[kept(b), 0:1]

    repeat(BLOCKS, first_grad)
    sums[...] = jnp.zeros_like(sums)
    local_sums[...] = jnp.zeros_like(local_sums)

    def backward(turn):
        layer = LAYERS - 1 - turn
        base = turn * span
        start = turn * (span // CHUNK)
        in_base = base + hidden_width
        out_base = in_base + width
        qkv_base = out_base + head_width

        def rows_at(first, count):
            return pl.ds(pl.multiple_of(first, 64), count)

        def total_row(index, amount):
            sums[turn, index : index + 1, :] = sums[turn, index : index + 1, :] + jnp.sum(
                amount, axis=0, keepdims=True
            )

        def receive(back, b, source):
            to_other(back, b, source).wait()
            dz_low[given(b), :] = land_back[back, b].astype(jnp.bfloat16)

        gain_two = vector(second_gain, layer)

        def norm_two(b):
            grad = own_b[packed(b), :]
            zhat = zhat_two[layer, packed(b), :]
            dz = norm_back(grad, zhat, scale_two[layer, packed(b), :], gain_two)
            own_a[packed(b), :] = dz
            to_other(0, b, own_a).start()
            dz_low[kept(b), :] = dz.astype(jnp.bfloat16)
            total_row(0, grad * zhat)
            total_row(1, grad)
            total_row(2, dz)

        repeat(BLOCKS, norm_two)
        repeat(BLOCKS, lambda b: receive(0, b, own_a))

        def down_piece(p):
            grads[rows_at(base + 128 * p, 128), :] = contract_rows(
                active[layer, :, lanes(p)], dz_low[...]
            )

        def in_piece(p):
            grads[rows_at(in_base + 128 * p, 128), :] = contract_rows(
                normed_low[layer, :, lanes(p)], du_low[...]
            )

        down_piece(0)
        tick(start)
        tick(start + 1)

        def feed(b):
            rows = block(b)
            dg = contract_cols(dz_low[rows, :], w_down[layer])
            u = hidden[layer, rows, :]
            density = jnp.exp(u * u * (-0.5)) * (1.0 / math.sqrt(2.0 * math.pi))
            du = dg * (normal_cdf(u) + u * density)
            du_low[rows, :] = du.astype(jnp.bfloat16)
            local_sums[turn, 0:1, :] = local_sums[turn, 0:1, :] + jnp.sum(
                du, axis=0, keepdims=True
            )
            down_piece(b + 1)
            tick(start + 2 + 2 * b)
            tick(start + 3 + 2 * b)

        repeat(BLOCKS, feed)
        down_piece(5)

        def feed_in(b):
            rows = block(b)
            part[rows, :] = contract_cols(du_low[rows, :], w_in[layer])
            to_core(0, b).start()
            in_piece(b)
            tick(start + 10 + 2 * b)
            send_y(0, b)
            tick(start + 11 + 2 * b)

        repeat(BLOCKS, feed_in)
        in_piece(4)
        tick(start + 18)
        in_piece(5)
        tick(start + 19)

        gain = vector(first_gain, layer)

        def norm_one(b):
            grad = own_a[packed(b), :] + summed(0, b)
            zhat = zhat_one[layer, packed(b), :]
            dz = norm_back(grad, zhat, scale_one[layer, packed(b), :], gain)
            own_b[packed(b), :] = dz
            to_other(1, b, own_b).start()
            dz_low[kept(b), :] = dz.astype(jnp.bfloat16)
            total_row(3, grad * zhat)
            total_row(4, grad)
            total_row(5, dz)
            tick(start + 20 + b)
            receive(1, b, own_b)

        repeat(BLOCKS, norm_one)
        grads[rows_at(out_base, head_width), :] = contract_rows(heads[layer], dz_low[...])
        dheads[...] = contract_cols(dz_low[...], w_out[layer]).astype(jnp.bfloat16)
        dkeys[...] = jnp.zeros_like(dkeys)
        dvalues[...] = jnp.zeros_like(dvalues)

        def attend(b):
            rows = block(b)
            for h in range(local_heads):
                side = HEAD_DIM * h
                probs = jnp.exp(scores_of(layer, h, rows) - log_total[layer, rows, h : h + 1])
                dhead = dheads[rows, side : side + HEAD_DIM]
                dprobs = contract_cols(dhead, values[layer, h])
                dvalues[h] = dvalues[h] + contract_rows(probs.astype(jnp.bfloat16), dhead)
                inner = jnp.sum(probs * dprobs, axis=-1, keepdims=True)
                ds = (probs * (dprobs - inner)).astype(jnp.bfloat16)
                dq = matmul(ds, keys[layer, h]) * SCALE
                dkeys[h] = dkeys[h] + contract_rows(ds, queries[layer, h, rows, :])
                dqkv_low[rows, 3 * side : 3 * side + HEAD_DIM] = dq.astype(jnp.bfloat16)
                local_sums[turn, 1:2, 2 * side : 2 * side + HEAD_DIM] = local_sums[
                    turn, 1:2, 2 * side : 2 * side + HEAD_DIM
                ] + jnp.sum(dq, axis=0, keepdims=True)
            pl.when(b < BLOCKS - 1)(lambda: tick(start + 24 + b))

        repeat(BLOCKS, attend)
        for h in range(local_heads):
            side = HEAD_DIM * h
            dqkv_low[:, 3 * side + HEAD_DIM : 3 * side + 2 * HEAD_DIM] = (
                dkeys[h] * SCALE
            ).astype(jnp.bfloat16)
            dv = dvalues[h]
            dqkv_low[:, 3 * side + 2 * HEAD_DIM : 3 * side + 3 * HEAD_DIM] = dv.astype(
                jnp.bfloat16
            )
            local_sums[turn, 1:2, 2 * side + HEAD_DIM : 2 * side + 2 * HEAD_DIM] = jnp.sum(
                dv, axis=0, keepdims=True
            )

        def project(b):
            rows = block(b)
            part[rows, :] = matmul(dqkv_low[rows, :], w_qkv[layer])
            to_core(1, b).start()
            pl.when(b >= 1)(lambda: send_y(1, b - 1))

        repeat(BLOCKS, project)
        send_y(1, BLOCKS - 1)

        def qkv_piece(p):
            grads[rows_at(qkv_base + 128 * p, 128), :] = contract_rows(
                dqkv_low[:, lanes(p)], inputs_low[layer]
            )
            tick(start + 27 + 2 * p)
            tick(start + 28 + 2 * p)

        repeat(4, qkv_piece)
        grads[rows_at(qkv_base + 512, 64), :] = contract_rows(
            dqkv_low[:, 512:], inputs_low[layer]
        )
        tick(start + 35)

        def pass_on(b):
            own_b[packed(b), :] = own_b[packed(b), :] + summed(1, b)

        repeat(BLOCKS, pass_on)

    repeat(LAYERS, backward)

    def last_grad(b):
        live = columns[kept(b), 0:1]
        grad = own_b[packed(b), :]
        masked_grad = grad * (1.0 - live)
        own_a[packed(b), :] = masked_grad
        to_other(0, b, own_a).start()
        grad_embeddings[kept(b), :] = masked_grad.astype(jnp.bfloat16)
        grads[small_base : small_base + REPL, :] = grads[
            small_base : small_base + REPL, :
        ] + lax.dot_general(
            chosen(kept(b), OWN),
            grad * live,
            (((0,), (0,)), ((), ())),
            precision=lax.Precision.HIGHEST,
            preferred_element_type=jnp.float32,
        )

    repeat(BLOCKS, last_grad)
    shared = REPL + 8 * LAYERS
    for turn in range(LAYERS):
        first = small_base + REPL + 8 * turn
        grads[first : first + 8, :] = sums[turn]
    grads[small_base + shared : small_base + shared + 8, :] = local_sums[...].reshape(8, width)
    short = remote(
        grads.at[pl.ds(small_base, shared)], land_small, small_send, small_recv, place.core_peer
    )
    short.start()

    def receive(b):
        to_other(0, b, own_a).wait()
        grad_embeddings[given(b), :] = land_back[0, b].astype(jnp.bfloat16)

    repeat(BLOCKS, receive)
    short.wait()
    grads[small_base : small_base + shared, :] = (
        grads[small_base : small_base + shared, :] + land_small[...]
    )
    done = LAYERS * (span // CHUNK)
    repeat(grad_sum.ticks() - done, lambda i: tick(done + i))


def run_pages(args, sizes):
    width, hidden_width, local_heads, span = sizes
    rows = PAGE_LEN
    flat = LAYERS * span + CHUNK
    half = rows // 2
    low, full = jnp.bfloat16, jnp.float32
    vmem, dma = pltpu.VMEM, pltpu.SemaphoreType.DMA
    head_width = local_heads * HEAD_DIM
    return pl.pallas_call(
        functools.partial(page_kernel, sizes),
        name="pages",
        out_shape=(
            vmem((rows, width), low),
            vmem((rows, width), low),
            vmem((flat, width), full),
        ),
        in_specs=[
            pl.BlockSpec(memory_space=pl.ANY if index in WEIGHTS else pltpu.VMEM)
            for index in range(len(args))
        ],
        out_specs=(
            pl.BlockSpec(memory_space=pltpu.VMEM),
            pl.BlockSpec(memory_space=pltpu.VMEM),
            pl.BlockSpec(memory_space=pltpu.VMEM),
        ),
        scratch_shapes=[
            vmem((LAYERS + 1, rows, width), low),
            vmem((LAYERS, local_heads, rows, HEAD_DIM), low),
            vmem((LAYERS, local_heads, rows, HEAD_DIM), low),
            vmem((LAYERS, local_heads, rows, HEAD_DIM), low),
            vmem((LAYERS, rows, 128), full),
            vmem((LAYERS, rows, head_width), low),
            vmem((LAYERS, rows, width), low),
            vmem((LAYERS, rows, hidden_width), full),
            vmem((LAYERS, rows, hidden_width), low),
            vmem((LAYERS, half, width), full),
            vmem((LAYERS, half, 1), full),
            vmem((LAYERS, half, width), full),
            vmem((LAYERS, half, 1), full),
            vmem((LAYERS, 3 * head_width, width), low),
            vmem((LAYERS, head_width, width), low),
            vmem((LAYERS, width, hidden_width), low),
            vmem((LAYERS, hidden_width, width), low),
            vmem((rows, 128), full),
            vmem((half, width), full),
            vmem((half, width), full),
            vmem((rows, width), full),
            vmem((2, BLOCKS, OWN, width), full),
            vmem((2, BLOCKS, OWN, width), full),
            vmem((2, BLOCKS, OWN, width), full),
            vmem((REPL + 8 * LAYERS, width), full),
            vmem((rows, width), low),
            vmem((rows, hidden_width), low),
            vmem((rows, head_width), low),
            vmem((local_heads, rows, HEAD_DIM), full),
            vmem((local_heads, rows, HEAD_DIM), full),
            vmem((rows, 3 * head_width), low),
            vmem((LAYERS, 8, width), full),
            vmem((LAYERS, 4, width), full),
            vmem((LANDINGS, SLOTS, UNIT, width), full),
            dma((2, BLOCKS)),
            dma((2, BLOCKS)),
            dma((2, BLOCKS)),
            dma((2, BLOCKS)),
            dma((2, BLOCKS)),
            dma((2, BLOCKS)),
            dma,
            dma,
            dma((KINDS, SLOTS)),
            dma((KINDS, SLOTS)),
            dma((4, LAYERS)),
        ],
        compiler_params=pltpu.CompilerParams(
            collective_id=0, has_side_effects=True, vmem_limit_bytes=46 << 20
        ),
    )(*args)


def place_kernel(sizes, hidden_out, grad_embeddings, every, *refs):
    width, hidden_width, local_heads, span = sizes
    head_width = local_heads * HEAD_DIM
    (
        out_hidden,
        out_embeddings,
        out_table,
        out_w_qkv,
        out_b_qv,
        out_w_out,
        out_b_out,
        out_first_gain,
        out_first_shift,
        out_w_in,
        out_b_in,
        out_w_down,
        out_b_down,
        out_second_gain,
        out_second_shift,
        short,
        sems,
    ) = refs
    base = LAYERS * span
    pairs = [(every.at[pl.ds(base, CHUNK)], short), (every.at[pl.ds(base, REPL)], out_table)]
    pairs += [(hidden_out, out_hidden), (grad_embeddings, out_embeddings)]
    for turn in range(LAYERS):
        first = span * turn
        for ref, rows in (
            (out_w_down, hidden_width),
            (out_w_in, width),
            (out_w_out, head_width),
            (out_w_qkv, 3 * head_width),
        ):
            pairs.append((every.at[pl.ds(first, rows)], ref.at[LAYERS - 1 - turn]))
            first += rows
    copies = [
        pltpu.make_async_copy(source, target, sems.at[index])
        for index, (source, target) in enumerate(pairs)
    ]
    for copy in copies:
        copy.start()
    copies[0].wait()
    local = REPL + 8 * LAYERS
    for ref, row, step in (
        (out_second_gain, REPL, 8),
        (out_second_shift, REPL + 1, 8),
        (out_b_down, REPL + 2, 8),
        (out_first_gain, REPL + 3, 8),
        (out_first_shift, REPL + 4, 8),
        (out_b_out, REPL + 5, 8),
        (out_b_in, local, 4),
        (out_b_qv, local + 1, 4),
    ):
        for turn in range(LAYERS):
            layer = LAYERS - 1 - turn
            ref[layer : layer + 1, :] = short[
                row + step * turn : row + step * turn + 1, : ref.shape[1]
            ]
    for copy in copies[1:]:
        copy.wait()


def place_outputs(hidden_out, grad_embeddings, every, sizes):
    width, hidden_width, local_heads, span = sizes
    head_width = local_heads * HEAD_DIM
    low, full = jnp.bfloat16, jnp.float32
    rows = hidden_out.shape[0]
    shapes = (
        ((rows, width), low),
        ((rows, width), low),
        ((REPL, width), full),
        ((LAYERS, 3 * head_width, width), full),
        ((LAYERS, 2 * head_width), full),
        ((LAYERS, head_width, width), full),
        ((LAYERS, width), full),
        ((LAYERS, width), full),
        ((LAYERS, width), full),
        ((LAYERS, width, hidden_width), full),
        ((LAYERS, hidden_width), full),
        ((LAYERS, hidden_width, width), full),
        ((LAYERS, width), full),
        ((LAYERS, width), full),
        ((LAYERS, width), full),
    )
    far = pl.BlockSpec(memory_space=pl.ANY)
    close = pl.BlockSpec(memory_space=pltpu.VMEM)
    return pl.pallas_call(
        functools.partial(place_kernel, sizes),
        name="place_outputs",
        out_shape=[jax.ShapeDtypeStruct(shape, kind) for shape, kind in shapes],
        in_specs=[far] * 3,
        out_specs=[close if shape[0] == LAYERS and len(shape) == 2 else far for shape, _ in shapes],
        scratch_shapes=[
            pltpu.VMEM((CHUNK, width), full),
            pltpu.SemaphoreType.DMA((4 + 4 * LAYERS,)),
        ],
        compiler_params=pltpu.CompilerParams(vmem_limit_bytes=4 << 20),
    )(hidden_out, grad_embeddings, every)


def moved(every):
    def kernel(source, target, sem):
        copy = pltpu.make_async_copy(source, target, sem)
        copy.start()
        copy.wait()

    far = pl.BlockSpec(memory_space=pl.ANY)
    return pl.pallas_call(
        kernel,
        name="moved",
        out_shape=jax.ShapeDtypeStruct(every.shape, every.dtype),
        in_specs=[far],
        out_specs=far,
        scratch_shapes=[pltpu.SemaphoreType.DMA],
        compiler_params=pltpu.CompilerParams(vmem_limit_bytes=4 << 20),
    )(every)


def on_device(*args):
    (embeddings, replace_table, replace_ids, masked, padding, w_qkv, b_qv, *_) = args
    width = embeddings.shape[1]
    head_width = w_qkv.shape[2] // 3
    hidden_width = args[11].shape[2]
    span = 2 * hidden_width + 4 * head_width
    args = list(args)
    args[5] = jnp.swapaxes(args[5], 1, 2)
    for index in (2, 3, 4):
        args[index] = args[index].reshape(1, PAGE_LEN)
    sizes = (width, hidden_width, head_width // HEAD_DIM, span)
    hidden_out, grad_embeddings, every = run_pages(args, sizes)
    groups = lax.axis_size("dp") // GROUP
    if groups > 1:
        every = lax.psum(
            moved(every),
            "dp",
            axis_index_groups=[
                [low + GROUP * high for high in range(groups)] for low in range(GROUP)
            ],
        )

    results = place_outputs(hidden_out, grad_embeddings, every, sizes)
    return (*results[:3], jnp.swapaxes(results[3], 1, 2), *results[4:])


def solution(mesh):
    placed = (
        P("dp", None),
        P(),
        P("dp"),
        P("dp"),
        P("dp"),
        P(None, None, "tensor"),
        P(None, "tensor"),
        P(None, "tensor", None),
        P(),
        P(),
        P(),
        P(None, None, "tensor"),
        P(None, "tensor"),
        P(None, "tensor", None),
        P(),
        P(),
        P(),
        P("dp", None),
    )
    return jax.shard_map(
        on_device,
        mesh=mesh,
        in_specs=placed,
        out_specs=(
            P("dp", None),
            P("dp", None),
            P(),
            P(None, None, "tensor"),
            P(None, "tensor"),
            P(None, "tensor", None),
            P(),
            P(),
            P(),
            P(None, None, "tensor"),
            P(None, "tensor"),
            P(None, "tensor", None),
            P(),
            P(),
            P(),
        ),
        check_vma=False,
    )
```

```python
import functools
import math

import jax
import jax.numpy as jnp
from jax import lax
from jax.experimental import pallas as pl
from jax.experimental.pallas import tpu as pltpu
from jax.sharding import PartitionSpec as P

HEAD_DIM = 64
LAYERS = 2
PAGE_LEN = 512
REPL = 32
EPSILON = 1e-12
SCALE = HEAD_DIM ** (-0.5)
MESH = pl.DeviceIdType.MESH

HALF = PAGE_LEN // 2
SEG = 64
BLOCKS = HALF // SEG
BACK_SEG = 64
BACK_BLOCKS = HALF // BACK_SEG
BLOCK = 2 * BACK_SEG

UNIT = 16
CHUNK = 4 * UNIT
LAG = 2
SLOTS = 4 * LAG
KINDS = 12
(TX, TNEAR, TFAR, TA1, TA2, TQ1, TQ2, TTA, TTN, TTM, TTF, TG) = range(KINDS)
LANDINGS = TTA + 1
GROUP = 8
WEIGHTS = (5, 7, 11, 13)
DIRECT = (128, 0)


def contract_rows(left, right):
    return lax.dot_general(
        left, right, (((0,), (0,)), ((), ())), preferred_element_type=jnp.float32
    )


def contract_cols(left, right):
    return lax.dot_general(
        left, right, (((1,), (1,)), ((), ())), preferred_element_type=jnp.float32
    )


def matmul(left, right):
    return jnp.dot(left, right, preferred_element_type=jnp.float32)


def repeat(count, body):
    def step(index, carry):
        body(index)
        return carry

    lax.fori_loop(0, count, step, 0)


def normed(values):
    average = jnp.mean(values, axis=-1, keepdims=True)
    centered = values - average
    variance = jnp.mean(centered * centered, axis=-1, keepdims=True)
    scale = lax.rsqrt(variance + EPSILON)
    return centered * scale, scale


def norm_back(grad, zhat, scale, gain):
    scaled = grad * gain
    average = jnp.mean(scaled, axis=-1, keepdims=True)
    along = jnp.mean(scaled * zhat, axis=-1, keepdims=True)
    return scale * (scaled - average - zhat * along)


def normal_cdf(values):
    return 0.5 * (1.0 + lax.erf(values * math.sqrt(0.5)))


def column(row):
    return jnp.transpose(jnp.broadcast_to(row, (128, row.shape[1])))[:, :1]


class Place:
    def __init__(self):
        d = lax.axis_index("dp")
        t = lax.axis_index("tensor")
        self.core = lax.rem(t, 2)
        self.core_peer = (d, t + 1 - 2 * self.core)
        self.y_peer = (d, t + 2 - 4 * lax.div(t, 2))
        self.diagonal = (d, t + 3 - 2 * self.core - 4 * lax.div(t, 2))
        self.y = lax.div(t, 2)
        self.low = lax.rem(d, GROUP)
        self.others = [
            (d - self.low + lax.rem(self.low + k, GROUP), t) for k in range(1, GROUP)
        ]
        pair = lax.rem(d, 2)
        line = lax.rem(lax.div(d, 2), 4)
        self.pair = pair
        self.mid = jnp.logical_or(line == 1, line == 2)
        self.end = jnp.logical_not(self.mid)
        self.upper = lax.div(line, 2)
        self.peer = (d + 1 - 2 * pair, t)
        self.line = (d + 2 - 4 * lax.rem(line, 2), t)
        self.cross = (jnp.where(line == 1, d + 2, d - 2), t)


def greet(place, barrier):
    def signal(device):
        pl.semaphore_signal(barrier, inc=1, device_id=device, device_id_type=MESH)

    for device in (place.core_peer, place.y_peer, place.diagonal, *place.others):
        signal(device)


def meet(barrier):
    pl.semaphore_wait(barrier, 2 + GROUP)


class GradientSum:
    def __init__(self, place, chunks, part, landing, send, recv):
        self.place = place
        self.chunks = chunks
        self.part = part
        self.landing = landing
        self.send = send
        self.recv = recv

    def rows(self, j, unit):
        return pl.ds(pl.multiple_of(j * CHUNK + unit * UNIT, UNIT), UNIT)

    def tick(self, t):
        place, part = self.place, self.part
        mine, other = place.pair, 1 - place.pair
        near, far = 2 + place.upper, 3 - place.upper

        def at(j, unit):
            return part.at[self.rows(j, unit)]

        def copy(kind, j, source, target, device):
            slot = lax.rem(j, SLOTS)
            return pltpu.make_async_remote_copy(
                src_ref=source,
                dst_ref=target,
                send_sem=self.send.at[kind, slot],
                recv_sem=self.recv.at[kind, slot],
                device_id=device,
                device_id_type=MESH,
            )

        def partial(kind, j, unit, device):
            return copy(kind, j, at(j, unit), self.landing.at[kind, lax.rem(j, SLOTS)], device)

        def final(kind, j, unit, device):
            return copy(kind, j, at(j, unit), at(j, unit), device)

        def add(kind, j, unit):
            rows = self.rows(j, unit)
            part[rows, :] = part[rows, :] + self.landing[kind, lax.rem(j, SLOTS)]

        def pair_first(j):
            return partial(TX, j, other, place.peer)

        def near_in(j):
            return partial(TNEAR, j, near, place.line)

        def far_in(j):
            return partial(TFAR, j, far, place.line)

        def mine_in(j):
            return partial(TA1, j, mine, place.line)

        def mine_across(j):
            return partial(TA2, j, mine, place.cross)

        def far_across(j):
            return partial(TQ1, j, far, place.cross)

        def near_pair(j):
            return partial(TQ2, j, near, place.peer)

        def mine_out(j):
            return partial(TTA, j, mine, place.line)

        def near_out(j):
            return final(TTN, j, near, place.line)

        def near_across(j):
            return final(TTM, j, near, place.cross)

        def far_out(j):
            return final(TTF, j, far, place.line)

        def pair_last(j):
            return final(TG, j, mine, place.peer)

        def stage_0(j):
            pair_first(j).start()

            @pl.when(place.end)
            def _():
                near_in(j).start()
                far_in(j).start()

        def stage_1(j):
            pair_first(j).wait()
            add(TX, j, mine)

            @pl.when(place.end)
            def _():
                near_in(j).wait_send()
                far_in(j).wait_send()
                mine_in(j).start()

            @pl.when(place.mid)
            def _():
                far_in(j).wait_recv()
                add(TFAR, j, far)
                far_across(j).start()
                near_in(j).wait_recv()
                add(TNEAR, j, near)

        def stage_2(j):
            @pl.when(place.end)
            def _():
                mine_in(j).wait_send()

            @pl.when(place.mid)
            def _():
                mine_in(j).wait_recv()
                far_across(j).wait()
                add(TA1, j, mine)
                mine_across(j).start()
                add(TQ1, j, near)
                near_pair(j).start()

        def stage_3(j):
            @pl.when(place.mid)
            def _():
                mine_across(j).wait()
                add(TA2, j, mine)
                mine_out(j).start()
                near_pair(j).wait()
                add(TQ2, j, near)
                near_across(j).start()
                near_out(j).start()

        def stage_4(j):
            @pl.when(place.mid)
            def _():
                mine_out(j).wait_send()
                near_out(j).wait_send()
                pair_last(j).start()
                near_across(j).wait()
                far_out(j).start()

            @pl.when(place.end)
            def _():
                mine_out(j).wait_recv()
                near_out(j).wait_recv()
                part[self.rows(j, mine), :] = self.landing[TTA, lax.rem(j, SLOTS)]
                pair_last(j).start()

        def stage_5(j):
            pair_last(j).wait()
            pl.when(place.mid)(lambda: far_out(j).wait_send())
            pl.when(place.end)(lambda: far_out(j).wait_recv())

        stages = (stage_0, stage_1, stage_2, stage_3, stage_4, stage_5)
        for number in reversed(range(len(stages))):
            j = t - number * LAG
            pl.when(jnp.logical_and(j >= 0, j < self.chunks))(
                functools.partial(stages[number], j)
            )

    def ticks(self):
        return self.chunks + 5 * LAG


def page_kernel(
    sizes,
    embeddings,
    replace_table,
    replace_ids,
    masked,
    padding,
    w_qkv_far,
    b_qv,
    w_out_far,
    b_out,
    first_gain,
    first_shift,
    w_in_far,
    b_in,
    w_down_far,
    b_down,
    second_gain,
    second_shift,
    cotangent,
    hidden_out,
    grad_embeddings,
    grads,
    inputs_low,
    queries,
    keys,
    values,
    log_total,
    heads,
    normed_low,
    hidden,
    active,
    zhat_one,
    scale_one,
    zhat_two,
    scale_two,
    w_qkv,
    w_out,
    w_in,
    w_down,
    w_all,
    shared_heads,
    columns,
    own_a,
    own_b,
    part,
    land_core,
    land_y,
    land_back,
    land_small,
    dz_low,
    du_low,
    dheads,
    dkeys,
    dvalues,
    dqkv_low,
    sums,
    local_sums,
    landing,
    core_send,
    core_recv,
    y_send,
    y_recv,
    back_send,
    back_recv,
    small_send,
    small_recv,
    dp_send,
    dp_recv,
    weight_sem,
    gather_send,
    gather_recv,
    hand_send,
    hand_recv,
    heads_send,
    heads_recv,
):
    width, hidden_width, local_heads, span = sizes
    head_width = local_heads * HEAD_DIM
    place = Place()
    core = place.core
    barrier = pltpu.get_barrier_semaphore()
    greet(place, barrier)
    weights = ((w_qkv_far, w_qkv), (w_out_far, w_out), (w_in_far, w_in), (w_down_far, w_down))

    def weight(index, layer):
        source, target = weights[index]
        return pltpu.make_async_copy(
            source.at[layer], target.at[layer], weight_sem.at[index, layer]
        )

    for index, layer in ((0, 0), (1, 0), (1, 1), (2, 0), (3, 0), (0, 1), (2, 1), (3, 1)):
        weight(index, layer).start()
    small_base = LAYERS * span
    chunks = grads.shape[0] // CHUNK
    grad_sum = GradientSum(place, chunks, grads, landing, dp_send, dp_recv)
    tick = grad_sum.tick

    def vector(ref, layer):
        both = ref[...].astype(jnp.float32)
        return jnp.where(layer == 0, both[0:1], both[1:2])

    def block(b):
        return pl.ds(pl.multiple_of(b * BLOCK, BLOCK), BLOCK)

    def segment(b, size, half):
        return pl.ds(pl.multiple_of(half * HALF + b * size, size), size)

    def kept(b, size):
        return segment(b, size, core)

    def given(b, size):
        return segment(b, size, 1 - core)

    def packed(b, size):
        return segment(b, size, 0)

    def halves(b, size):
        return segment(b, size, 0), segment(b, size, 1)

    def lanes(p, size=128):
        return pl.ds(pl.multiple_of(p * size, size), size)

    def remote(source, target, send, recv, device):
        return pltpu.make_async_remote_copy(
            src_ref=source,
            dst_ref=target,
            send_sem=send,
            recv_sem=recv,
            device_id=device,
            device_id_type=MESH,
        )

    def to_core(turn, b, size):
        return remote(
            part.at[given(b, size)],
            land_core.at[turn, packed(b, size)],
            core_send.at[turn, b],
            core_recv.at[turn, b],
            place.core_peer,
        )

    def over_y(turn, b, size):
        return remote(
            part.at[kept(b, size)],
            land_y.at[turn, packed(b, size)],
            y_send.at[turn, b],
            y_recv.at[turn, b],
            place.y_peer,
        )

    def to_other(turn, b, size, source):
        return remote(
            source.at[packed(b, size)],
            land_back.at[turn, packed(b, size)],
            back_send.at[turn, b],
            back_recv.at[turn, b],
            place.core_peer,
        )

    def send_y(turn, b, size):
        to_core(turn, b, size).wait()
        rows = kept(b, size)
        part[rows, :] = part[rows, :] + land_core[turn, packed(b, size), :]
        over_y(turn, b, size).start()

    def summed(turn, b, size):
        over_y(turn, b, size).wait()
        return part[kept(b, size), :] + land_y[turn, packed(b, size), :]

    def received(turn, b, size, source):
        to_other(turn, b, size, source).wait()
        return land_back[turn, packed(b, size), :].astype(jnp.bfloat16)

    def shard(which, layer):
        return (which * LAYERS + layer) * head_width

    def direct(layer):
        return pl.ds(shard(0, layer), DIRECT[layer]), pl.ds(shard(2, layer), DIRECT[layer])

    def piece_rows(which, layer, owner):
        size = (head_width - DIRECT[layer]) // GROUP
        first = shard(which, layer) + DIRECT[layer] + owner * size
        return pl.ds(pl.multiple_of(first, 8), size)

    def moving(source, target, index, device):
        return remote(
            grads.at[source], grads.at[target], gather_send.at[index], gather_recv.at[index], device
        )

    def whole(which, layer):
        return pl.ds(shard(which, layer), head_width)

    def own_shard(layer):
        return moving(whole(0, layer), whole(1, layer), layer, place.core_peer)

    def other_shard(layer):
        return moving(whole(2, layer), whole(3, layer), LAYERS + layer, place.core_peer)

    def piece_over(layer):
        return moving(
            piece_rows(0, layer, place.low),
            piece_rows(2, layer, place.low),
            2 * LAYERS + layer,
            place.y_peer,
        )

    def rest_over(layer):
        return moving(*direct(layer), 3 * LAYERS + layer, place.y_peer)

    def handed(layer, k):
        rows = piece_rows(2, layer, place.low)
        return pltpu.make_async_remote_copy(
            src_ref=grads.at[rows],
            dst_ref=grads.at[rows],
            send_sem=hand_send.at[layer, k],
            recv_sem=hand_recv.at[layer, place.low],
            device_id=place.others[k],
            device_id_type=MESH,
        )

    def handed_in(layer, k):
        owner = lax.rem(place.low + 1 + k, GROUP)
        rows = piece_rows(2, layer, owner)
        return pltpu.make_async_remote_copy(
            src_ref=grads.at[rows],
            dst_ref=grads.at[rows],
            send_sem=hand_send.at[layer, k],
            recv_sem=hand_recv.at[layer, owner],
            device_id=place.others[k],
            device_id_type=MESH,
        )

    def gather_first(layer):
        weight(1, layer).wait()
        grads[whole(0, layer), :] = w_out[layer].astype(jnp.float32)
        piece_over(layer).start()
        if DIRECT[layer]:
            rest_over(layer).start()
        own_shard(layer).start()

    def gather_second(layer):
        piece_over(layer).wait()
        for k in range(GROUP - 1):
            handed(layer, k).start()

    def gather_third(layer):
        for k in range(GROUP - 1):
            handed(layer, k).wait_send()
            handed_in(layer, k).wait_recv()
        if DIRECT[layer]:
            rest_over(layer).wait()
        other_shard(layer).start()

    def gather_last(layer):
        own_shard(layer).wait()
        other_shard(layer).wait()
        pairs_width = 2 * HEAD_DIM
        for which in range(4):
            source = which // 2
            owner = 2 * (place.y + source - 2 * place.y * source) + (
                core + which % 2 - 2 * core * (which % 2)
            )
            low = grads[whole(which, layer), :].astype(jnp.bfloat16)
            first = pl.multiple_of(owner * pairs_width, pairs_width)
            w_all[layer, pl.ds(first, pairs_width), :] = low[:pairs_width]
            first = pl.multiple_of(4 * pairs_width + owner * HEAD_DIM, HEAD_DIM)
            w_all[layer, pl.ds(first, HEAD_DIM), :] = low[pairs_width:]

    def heads_out(b):
        mine, theirs = shared_heads.at[core, b], shared_heads.at[1 - core, b]
        return [
            remote(
                source,
                shared_heads.at[2 + index, b],
                heads_send.at[index, b],
                heads_recv.at[index, b],
                device,
            )
            for index, (source, device) in enumerate(
                (
                    (theirs, place.core_peer),
                    (mine, place.y_peer),
                    (theirs, place.diagonal),
                )
            )
        ]

    def pack_heads(rows):
        cut = 2 * HEAD_DIM
        return jnp.concatenate(
            [
                rows[:, :cut],
                jnp.concatenate([rows[: SEG // 2, cut:], rows[SEG // 2 :, cut:]], axis=1),
            ],
            axis=0,
        )

    def all_heads(b):
        pairs, thirds = [], []
        for owner in range(4):
            side, half = owner // 2, owner % 2
            apart = 2 * (place.y + side - 2 * place.y * side) + (core + half - 2 * core * half)
            slot = jnp.where(apart == 0, core, apart + 1)
            low = shared_heads[slot, b].astype(jnp.bfloat16)
            pairs.append(low[:SEG])
            tail = low[SEG:]
            thirds.append(jnp.concatenate([tail[:, :HEAD_DIM], tail[:, HEAD_DIM:]], axis=0))
        return jnp.concatenate(pairs + thirds, axis=1)

    pad_row = padding[...].astype(jnp.float32)
    live_row = masked[...].astype(jnp.float32) * pad_row
    bias_row = (pad_row - 1.0) * 10000.0
    columns[:, 0:1] = column(live_row)
    columns[:, 1:2] = column(replace_ids[...].astype(jnp.float32))
    grads[small_base:, :] = jnp.zeros((CHUNK, width), jnp.float32)

    def chosen(rows, count):
        spots = lax.broadcasted_iota(jnp.int32, (count, REPL), 1).astype(jnp.float32)
        return jnp.where(columns[rows, 1:2] == spots, 1.0, 0.0)

    def first_input(b):
        rows = block(b)
        picked = matmul(chosen(rows, BLOCK).astype(jnp.bfloat16), replace_table[...])
        taken = jnp.where(
            columns[rows, 0:1] > 0.0, picked, embeddings[rows, :].astype(jnp.float32)
        )
        inputs_low[0, rows, :] = taken.astype(jnp.bfloat16)

    sums[...] = jnp.zeros_like(sums)
    local_sums[...] = jnp.zeros_like(local_sums)

    def project(layer, spans):
        bias_pair = vector(b_qv, layer)
        inputs = jnp.concatenate([inputs_low[layer, rows, :] for rows in spans], axis=0)
        projected = contract_cols(inputs, w_qkv[layer])

        def split(ref, h, columns_of):
            low = columns_of.astype(jnp.bfloat16)
            first = 0
            for rows in spans:
                ref[layer, h, rows, :] = low[first : first + rows.size]
                first += rows.size

        for h in range(local_heads):
            base = 3 * HEAD_DIM * h
            bias = 2 * HEAD_DIM * h
            split(
                queries,
                h,
                projected[:, base : base + HEAD_DIM] + bias_pair[:, bias : bias + HEAD_DIM],
            )
            split(keys, h, projected[:, base + HEAD_DIM : base + 2 * HEAD_DIM])
            split(
                values,
                h,
                projected[:, base + 2 * HEAD_DIM : base + 3 * HEAD_DIM]
                + bias_pair[:, bias + HEAD_DIM : bias + 2 * HEAD_DIM],
            )

    def scores_of(layer, h, query):
        return contract_cols(query, keys[layer, h]) * SCALE + bias_row

    def total_row(turn, index, amount):
        sums[turn, index : index + 1, :] = sums[turn, index : index + 1, :] + jnp.sum(
            amount, axis=0, keepdims=True
        )

    def norm_two(turn, b, size, grad):
        layer = LAYERS - 1 - turn
        rows = packed(b, size)
        zhat = zhat_two[layer, rows, :]
        dz = norm_back(grad, zhat, scale_two[layer, rows, :], vector(second_gain, layer))
        own_a[rows, :] = dz
        to_other(0, b, size, own_a).start()
        dz_low[kept(b, size), :] = dz.astype(jnp.bfloat16)
        total_row(turn, 0, grad * zhat)
        total_row(turn, 1, grad)
        total_row(turn, 2, dz)

    def forward(layer):
        last = layer == LAYERS - 1

        def attend(b):
            spans = halves(b, SEG)
            outs, logs = [], []
            for h in range(local_heads):
                query = jnp.concatenate([queries[layer, h, rows, :] for rows in spans], axis=0)
                scores = scores_of(layer, h, query)
                largest = jnp.max(scores, axis=-1, keepdims=True)
                weights_of = jnp.exp(scores - largest)
                totals = jnp.sum(weights_of, axis=-1, keepdims=True)
                probs = (weights_of * (1.0 / totals)).astype(jnp.bfloat16)
                outs.append(matmul(probs, values[layer, h]).astype(jnp.bfloat16))
                logs.append(largest + jnp.log(totals))
            joined = jnp.concatenate(outs, axis=1)
            full = joined.astype(jnp.float32)
            for side in range(2):
                shared_heads[side, b] = pack_heads(full[side * SEG : (side + 1) * SEG])
            for copy in heads_out(b):
                copy.start()
            for side, rows in enumerate(spans):
                cut = slice(side * SEG, (side + 1) * SEG)
                heads[layer, rows, :] = joined[cut]
                for h in range(local_heads):
                    log_total[layer, rows, h : h + 1] = logs[h][cut]

        repeat(BLOCKS, attend)

        @pl.when(layer == 0)
        def _():
            gather_third(0)
            gather_second(1)
            gather_last(0)

        gain, shift, bias_out = (
            vector(first_gain, layer),
            vector(first_shift, layer),
            vector(b_out, layer),
        )
        bias_in = vector(b_in, layer)
        weight(2, layer).wait()
        weight(3, layer).wait()

        def feed_norm(b):
            rows = packed(b, SEG)
            for copy in heads_out(b):
                copy.wait()
            before = (
                inputs_low[layer, kept(b, SEG), :].astype(jnp.float32)
                + matmul(all_heads(b), w_all[layer])
                + bias_out
            )
            zhat, scale = normed(before)
            result = zhat * gain + shift
            own_a[rows, :] = result
            to_other(0, b, SEG, own_a).start()
            zhat_one[layer, rows, :] = zhat
            scale_one[layer, rows, :] = scale
            normed_low[layer, kept(b, SEG), :] = result.astype(jnp.bfloat16)

        def feed_main(b):
            spans = halves(b, SEG)
            normed_low[layer, given(b, SEG), :] = received(0, b, SEG, own_a)
            inputs = jnp.concatenate([normed_low[layer, rows, :] for rows in spans], axis=0)
            u = matmul(inputs, w_in[layer]) + bias_in
            g = (u * normal_cdf(u)).astype(jnp.bfloat16)
            lowered = matmul(g, w_down[layer])
            for side, rows in enumerate(spans):
                cut = slice(side * SEG, (side + 1) * SEG)
                part[rows, :] = lowered[cut]
                hidden[layer, rows, :] = u[cut]
                active[layer, rows, :] = g[cut]
            to_core(1, b, SEG).start()

        def feed(b):
            pl.when(b < BLOCKS)(lambda: feed_norm(b))
            pl.when(b >= 2)(lambda: send_y(1, b - 2, SEG))
            pl.when(b >= 1)(lambda: feed_main(b - 1))

        repeat(BLOCKS + 1, feed)
        pl.when(layer == 0)(lambda: gather_third(1))
        send_y(1, BLOCKS - 1, SEG)
        pl.when(layer == 0)(lambda: gather_last(1))

        gain_two, shift_two, bias_down = (
            vector(second_gain, layer),
            vector(second_shift, layer),
            vector(b_down, layer),
        )
        pl.when(jnp.logical_not(last))(lambda: weight(0, layer + 1).wait())

        def receive(b):
            inputs_low[layer + 1, given(b, SEG), :] = received(1, b, SEG, own_b)
            pl.when(jnp.logical_not(last))(lambda: project(layer + 1, halves(b, SEG)))

            @pl.when(last)
            def _():
                dz_low[given(b, SEG), :] = received(0, b, SEG, own_a)

        def finish(b):
            rows = packed(b, SEG)
            before = own_a[rows, :] + summed(1, b, SEG) + bias_down
            zhat, scale = normed(before)
            result = zhat * gain_two + shift_two
            own_b[rows, :] = result
            to_other(1, b, SEG, own_b).start()
            zhat_two[layer, rows, :] = zhat
            scale_two[layer, rows, :] = scale
            inputs_low[layer + 1, kept(b, SEG), :] = result.astype(jnp.bfloat16)

            @pl.when(last)
            def _():
                live = columns[kept(b, SEG), 0:1]
                norm_two(0, b, SEG, cotangent[kept(b, SEG), :].astype(jnp.float32) * live)

            pl.when(b >= 1)(lambda: receive(b - 1))

        repeat(BLOCKS, finish)
        receive(BLOCKS - 1)

    meet(barrier)
    gather_first(0)
    gather_first(1)
    repeat(BACK_BLOCKS, first_input)
    weight(0, 0).wait()
    repeat(BACK_BLOCKS, lambda b: project(0, (block(b),)))
    gather_second(0)
    repeat(LAYERS, forward)

    def backward(turn):
        layer = LAYERS - 1 - turn
        base = turn * span
        start = turn * (span // CHUNK)
        in_base = base + hidden_width
        out_base = in_base + width
        qkv_base = out_base + head_width

        def rows_at(first, count):
            return pl.ds(pl.multiple_of(first, 64), count)

        def down_piece(p):
            grads[rows_at(base + 128 * p, 128), :] = contract_rows(
                active[layer, :, lanes(p)], dz_low[...]
            )

        def in_piece(p):
            grads[rows_at(in_base + 128 * p, 128), :] = contract_rows(
                normed_low[layer, :, lanes(p)], du_low[...]
            )

        down_piece(0)
        tick(start)
        tick(start + 1)

        def feed(b):
            rows = block(b)
            dg = contract_cols(dz_low[rows, :], w_down[layer])
            u = hidden[layer, rows, :]
            density = jnp.exp(u * u * (-0.5)) * (1.0 / math.sqrt(2.0 * math.pi))
            du = dg * (normal_cdf(u) + u * density)
            du_low[rows, :] = du.astype(jnp.bfloat16)
            local_sums[turn, 0:1, :] = local_sums[turn, 0:1, :] + jnp.sum(
                du, axis=0, keepdims=True
            )
            down_piece(b + 1)
            tick(start + 2 + 2 * b)
            tick(start + 3 + 2 * b)

        repeat(BACK_BLOCKS, feed)
        down_piece(5)

        def feed_in(b):
            spans = halves(b, BACK_SEG)
            left = jnp.concatenate([du_low[rows, :] for rows in spans], axis=0)
            result = contract_cols(left, w_in[layer])
            for side, rows in enumerate(spans):
                part[rows, :] = result[side * BACK_SEG : (side + 1) * BACK_SEG]
            to_core(0, b, BACK_SEG).start()
            pl.when(b >= 1)(lambda: send_y(0, b - 1, BACK_SEG))
            in_piece(b)
            tick(start + 10 + 2 * b)
            tick(start + 11 + 2 * b)

        repeat(BACK_BLOCKS, feed_in)
        send_y(0, BACK_BLOCKS - 1, BACK_SEG)
        in_piece(4)
        tick(start + 18)
        in_piece(5)
        tick(start + 19)

        gain = vector(first_gain, layer)

        def norm_one(b):
            rows = packed(b, BACK_SEG)
            grad = own_a[rows, :] + summed(0, b, BACK_SEG)
            zhat = zhat_one[layer, rows, :]
            dz = norm_back(grad, zhat, scale_one[layer, rows, :], gain)
            own_b[rows, :] = dz
            to_other(1, b, BACK_SEG, own_b).start()
            dz_low[kept(b, BACK_SEG), :] = dz.astype(jnp.bfloat16)
            total_row(turn, 3, grad * zhat)
            total_row(turn, 4, grad)
            total_row(turn, 5, dz)
            tick(start + 20 + b)
            dz_low[given(b, BACK_SEG), :] = received(1, b, BACK_SEG, own_b)

        repeat(BACK_BLOCKS, norm_one)
        grads[rows_at(out_base, head_width), :] = contract_rows(heads[layer], dz_low[...])
        dheads[...] = contract_cols(dz_low[...], w_out[layer]).astype(jnp.bfloat16)
        dkeys[...] = jnp.zeros_like(dkeys)
        dvalues[...] = jnp.zeros_like(dvalues)

        def attend(b):
            rows = block(b)
            for h in range(local_heads):
                side = HEAD_DIM * h
                query = queries[layer, h, rows, :]
                probs = jnp.exp(scores_of(layer, h, query) - log_total[layer, rows, h : h + 1])
                dhead = dheads[rows, side : side + HEAD_DIM]
                dprobs = contract_cols(dhead, values[layer, h])
                dvalues[h] = dvalues[h] + contract_rows(probs.astype(jnp.bfloat16), dhead)
                inner = jnp.sum(probs * dprobs, axis=-1, keepdims=True)
                ds = (probs * (dprobs - inner)).astype(jnp.bfloat16)
                dq = matmul(ds, keys[layer, h]) * SCALE
                dkeys[h] = dkeys[h] + contract_rows(ds, query)
                dqkv_low[rows, 3 * side : 3 * side + HEAD_DIM] = dq.astype(jnp.bfloat16)
                local_sums[turn, 1:2, 2 * side : 2 * side + HEAD_DIM] = local_sums[
                    turn, 1:2, 2 * side : 2 * side + HEAD_DIM
                ] + jnp.sum(dq, axis=0, keepdims=True)
            pl.when(b < BACK_BLOCKS - 1)(lambda: tick(start + 24 + b))

        repeat(BACK_BLOCKS, attend)
        for h in range(local_heads):
            side = HEAD_DIM * h
            dqkv_low[:, 3 * side + HEAD_DIM : 3 * side + 2 * HEAD_DIM] = (
                dkeys[h] * SCALE
            ).astype(jnp.bfloat16)
            dv = dvalues[h]
            dqkv_low[:, 3 * side + 2 * HEAD_DIM : 3 * side + 3 * HEAD_DIM] = dv.astype(
                jnp.bfloat16
            )
            local_sums[turn, 1:2, 2 * side + HEAD_DIM : 2 * side + 2 * HEAD_DIM] = jnp.sum(
                dv, axis=0, keepdims=True
            )

        def back_project(b):
            spans = halves(b, BACK_SEG)
            left = jnp.concatenate([dqkv_low[rows, :] for rows in spans], axis=0)
            result = matmul(left, w_qkv[layer])
            for side, rows in enumerate(spans):
                part[rows, :] = result[side * BACK_SEG : (side + 1) * BACK_SEG]
            to_core(1, b, BACK_SEG).start()
            pl.when(b >= 1)(lambda: send_y(1, b - 1, BACK_SEG))

        repeat(BACK_BLOCKS, back_project)
        send_y(1, BACK_BLOCKS - 1, BACK_SEG)

        def qkv_piece(p):
            grads[rows_at(qkv_base + 128 * p, 128), :] = contract_rows(
                dqkv_low[:, lanes(p)], inputs_low[layer]
            )
            tick(start + 27 + 2 * p)
            tick(start + 28 + 2 * p)

        repeat(4, qkv_piece)
        grads[rows_at(qkv_base + 512, 64), :] = contract_rows(
            dqkv_low[:, 512:], inputs_low[layer]
        )
        tick(start + 35)

        def pass_on(b):
            rows = packed(b, BACK_SEG)
            grad = own_b[rows, :] + summed(1, b, BACK_SEG)
            own_b[rows, :] = grad
            pl.when(turn < LAYERS - 1)(lambda: norm_two(turn + 1, b, BACK_SEG, grad))

        repeat(BACK_BLOCKS, pass_on)

        def receive(b):
            dz_low[given(b, BACK_SEG), :] = received(0, b, BACK_SEG, own_a)

        pl.when(turn < LAYERS - 1)(lambda: repeat(BACK_BLOCKS, receive))

    repeat(LAYERS, backward)
    hidden_out[...] = inputs_low[LAYERS]

    def last_grad(b):
        rows = kept(b, BACK_SEG)
        live = columns[rows, 0:1]
        grad = own_b[packed(b, BACK_SEG), :]
        masked_grad = grad * (1.0 - live)
        own_a[packed(b, BACK_SEG), :] = masked_grad
        to_other(0, b, BACK_SEG, own_a).start()
        grad_embeddings[rows, :] = masked_grad.astype(jnp.bfloat16)
        grads[small_base : small_base + REPL, :] = grads[
            small_base : small_base + REPL, :
        ] + lax.dot_general(
            chosen(rows, BACK_SEG),
            grad * live,
            (((0,), (0,)), ((), ())),
            precision=lax.Precision.HIGHEST,
            preferred_element_type=jnp.float32,
        )

    repeat(BACK_BLOCKS, last_grad)
    shared = REPL + 8 * LAYERS
    for turn in range(LAYERS):
        first = small_base + REPL + 8 * turn
        grads[first : first + 8, :] = sums[turn]
    grads[small_base + shared : small_base + shared + 8, :] = local_sums[...].reshape(8, width)
    short = remote(
        grads.at[pl.ds(small_base, shared)], land_small, small_send, small_recv, place.core_peer
    )
    short.start()

    def receive_grad(b):
        grad_embeddings[given(b, BACK_SEG), :] = received(0, b, BACK_SEG, own_a)

    repeat(BACK_BLOCKS, receive_grad)
    short.wait()
    grads[small_base : small_base + shared, :] = (
        grads[small_base : small_base + shared, :] + land_small[...]
    )
    done = LAYERS * (span // CHUNK)
    repeat(grad_sum.ticks() - done, lambda i: tick(done + i))


def run_pages(args, sizes):
    width, hidden_width, local_heads, span = sizes
    rows = PAGE_LEN
    flat = LAYERS * span + CHUNK
    half = rows // 2
    low, full = jnp.bfloat16, jnp.float32
    vmem, dma = pltpu.VMEM, pltpu.SemaphoreType.DMA
    head_width = local_heads * HEAD_DIM
    return pl.pallas_call(
        functools.partial(page_kernel, sizes),
        name="pages",
        out_shape=(
            vmem((rows, width), low),
            vmem((rows, width), low),
            vmem((flat, width), full),
        ),
        in_specs=[
            pl.BlockSpec(memory_space=pl.ANY if index in WEIGHTS else pltpu.VMEM)
            for index in range(len(args))
        ],
        out_specs=(
            pl.BlockSpec(memory_space=pltpu.VMEM),
            pl.BlockSpec(memory_space=pltpu.VMEM),
            pl.BlockSpec(memory_space=pltpu.VMEM),
        ),
        scratch_shapes=[
            vmem((LAYERS + 1, rows, width), low),
            vmem((LAYERS, local_heads, rows, HEAD_DIM), low),
            vmem((LAYERS, local_heads, rows, HEAD_DIM), low),
            vmem((LAYERS, local_heads, rows, HEAD_DIM), low),
            vmem((LAYERS, rows, 128), full),
            vmem((LAYERS, rows, head_width), low),
            vmem((LAYERS, rows, width), low),
            vmem((LAYERS, rows, hidden_width), full),
            vmem((LAYERS, rows, hidden_width), low),
            vmem((LAYERS, half, width), full),
            vmem((LAYERS, half, 1), full),
            vmem((LAYERS, half, width), full),
            vmem((LAYERS, half, 1), full),
            vmem((LAYERS, 3 * head_width, width), low),
            vmem((LAYERS, head_width, width), low),
            vmem((LAYERS, width, hidden_width), low),
            vmem((LAYERS, hidden_width, width), low),
            vmem((LAYERS, 4 * head_width, width), low),
            vmem((5, BLOCKS, 3 * SEG // 2, 2 * HEAD_DIM), full),
            vmem((rows, 128), full),
            vmem((half, width), full),
            vmem((half, width), full),
            vmem((rows, width), full),
            vmem((2, half, width), full),
            vmem((2, half, width), full),
            vmem((2, half, width), full),
            vmem((REPL + 8 * LAYERS, width), full),
            vmem((rows, width), low),
            vmem((rows, hidden_width), low),
            vmem((rows, head_width), low),
            vmem((local_heads, rows, HEAD_DIM), full),
            vmem((local_heads, rows, HEAD_DIM), full),
            vmem((rows, 3 * head_width), low),
            vmem((LAYERS, 8, width), full),
            vmem((LAYERS, 4, width), full),
            vmem((LANDINGS, SLOTS, UNIT, width), full),
            dma((2, BLOCKS)),
            dma((2, BLOCKS)),
            dma((2, BLOCKS)),
            dma((2, BLOCKS)),
            dma((2, BLOCKS)),
            dma((2, BLOCKS)),
            dma,
            dma,
            dma((KINDS, SLOTS)),
            dma((KINDS, SLOTS)),
            dma((4, LAYERS)),
            dma((4 * LAYERS,)),
            dma((4 * LAYERS,)),
            dma((LAYERS, GROUP)),
            dma((LAYERS, GROUP)),
            dma((3, BLOCKS)),
            dma((3, BLOCKS)),
        ],
        compiler_params=pltpu.CompilerParams(
            collective_id=0, has_side_effects=True, vmem_limit_bytes=46 << 20
        ),
    )(*args)


def place_kernel(sizes, hidden_out, grad_embeddings, every, *refs):
    width, hidden_width, local_heads, span = sizes
    head_width = local_heads * HEAD_DIM
    (
        out_hidden,
        out_embeddings,
        out_table,
        out_w_qkv,
        out_b_qv,
        out_w_out,
        out_b_out,
        out_first_gain,
        out_first_shift,
        out_w_in,
        out_b_in,
        out_w_down,
        out_b_down,
        out_second_gain,
        out_second_shift,
        short,
        sems,
    ) = refs
    base = LAYERS * span
    pairs = [(every.at[pl.ds(base, CHUNK)], short), (every.at[pl.ds(base, REPL)], out_table)]
    pairs += [(hidden_out, out_hidden), (grad_embeddings, out_embeddings)]
    for turn in range(LAYERS):
        first = span * turn
        for ref, rows in (
            (out_w_down, hidden_width),
            (out_w_in, width),
            (out_w_out, head_width),
            (out_w_qkv, 3 * head_width),
        ):
            pairs.append((every.at[pl.ds(first, rows)], ref.at[LAYERS - 1 - turn]))
            first += rows
    copies = [
        pltpu.make_async_copy(source, target, sems.at[index])
        for index, (source, target) in enumerate(pairs)
    ]
    for copy in copies:
        copy.start()
    copies[0].wait()
    local = REPL + 8 * LAYERS
    for ref, row, step in (
        (out_second_gain, REPL, 8),
        (out_second_shift, REPL + 1, 8),
        (out_b_down, REPL + 2, 8),
        (out_first_gain, REPL + 3, 8),
        (out_first_shift, REPL + 4, 8),
        (out_b_out, REPL + 5, 8),
        (out_b_in, local, 4),
        (out_b_qv, local + 1, 4),
    ):
        for turn in range(LAYERS):
            layer = LAYERS - 1 - turn
            ref[layer : layer + 1, :] = short[
                row + step * turn : row + step * turn + 1, : ref.shape[1]
            ]
    for copy in copies[1:]:
        copy.wait()


def place_outputs(hidden_out, grad_embeddings, every, sizes):
    width, hidden_width, local_heads, span = sizes
    head_width = local_heads * HEAD_DIM
    low, full = jnp.bfloat16, jnp.float32
    rows = hidden_out.shape[0]
    shapes = (
        ((rows, width), low),
        ((rows, width), low),
        ((REPL, width), full),
        ((LAYERS, 3 * head_width, width), full),
        ((LAYERS, 2 * head_width), full),
        ((LAYERS, head_width, width), full),
        ((LAYERS, width), full),
        ((LAYERS, width), full),
        ((LAYERS, width), full),
        ((LAYERS, width, hidden_width), full),
        ((LAYERS, hidden_width), full),
        ((LAYERS, hidden_width, width), full),
        ((LAYERS, width), full),
        ((LAYERS, width), full),
        ((LAYERS, width), full),
    )
    far = pl.BlockSpec(memory_space=pl.ANY)
    close = pl.BlockSpec(memory_space=pltpu.VMEM)
    return pl.pallas_call(
        functools.partial(place_kernel, sizes),
        name="place_outputs",
        out_shape=[jax.ShapeDtypeStruct(shape, kind) for shape, kind in shapes],
        in_specs=[far] * 3,
        out_specs=[close if shape[0] == LAYERS and len(shape) == 2 else far for shape, _ in shapes],
        scratch_shapes=[
            pltpu.VMEM((CHUNK, width), full),
            pltpu.SemaphoreType.DMA((4 + 4 * LAYERS,)),
        ],
        compiler_params=pltpu.CompilerParams(vmem_limit_bytes=4 << 20),
    )(hidden_out, grad_embeddings, every)


def moved(every):
    def kernel(source, target, sem):
        copy = pltpu.make_async_copy(source, target, sem)
        copy.start()
        copy.wait()

    far = pl.BlockSpec(memory_space=pl.ANY)
    return pl.pallas_call(
        kernel,
        name="moved",
        out_shape=jax.ShapeDtypeStruct(every.shape, every.dtype),
        in_specs=[far],
        out_specs=far,
        scratch_shapes=[pltpu.SemaphoreType.DMA],
        compiler_params=pltpu.CompilerParams(vmem_limit_bytes=4 << 20),
    )(every)


def on_device(*args):
    (embeddings, replace_table, replace_ids, masked, padding, w_qkv, b_qv, *_) = args
    width = embeddings.shape[1]
    head_width = w_qkv.shape[2] // 3
    hidden_width = args[11].shape[2]
    span = 2 * hidden_width + 4 * head_width
    args = list(args)
    args[5] = jnp.swapaxes(args[5], 1, 2)
    for index in (2, 3, 4):
        args[index] = args[index].reshape(1, PAGE_LEN)
    sizes = (width, hidden_width, head_width // HEAD_DIM, span)
    hidden_out, grad_embeddings, every = run_pages(args, sizes)
    groups = lax.axis_size("dp") // GROUP
    if groups > 1:
        every = lax.psum(
            moved(every),
            "dp",
            axis_index_groups=[
                [low + GROUP * high for high in range(groups)] for low in range(GROUP)
            ],
        )

    results = place_outputs(hidden_out, grad_embeddings, every, sizes)
    return (*results[:3], jnp.swapaxes(results[3], 1, 2), *results[4:])


def solution(mesh):
    placed = (
        P("dp", None),
        P(),
        P("dp"),
        P("dp"),
        P("dp"),
        P(None, None, "tensor"),
        P(None, "tensor"),
        P(None, "tensor", None),
        P(),
        P(),
        P(),
        P(None, None, "tensor"),
        P(None, "tensor"),
        P(None, "tensor", None),
        P(),
        P(),
        P(),
        P("dp", None),
    )
    return jax.shard_map(
        on_device,
        mesh=mesh,
        in_specs=placed,
        out_specs=(
            P("dp", None),
            P("dp", None),
            P(),
            P(None, None, "tensor"),
            P(None, "tensor"),
            P(None, "tensor", None),
            P(),
            P(),
            P(),
            P(None, None, "tensor"),
            P(None, "tensor"),
            P(None, "tensor", None),
            P(),
            P(),
            P(),
        ),
        check_vma=False,
    )
```

```python
import functools
import math

import jax
import jax.numpy as jnp
from jax import lax
from jax.experimental import pallas as pl
from jax.experimental.pallas import tpu as pltpu
from jax.sharding import PartitionSpec as P

HEAD_DIM = 64
LAYERS = 2
PAGE_LEN = 512
REPL = 32
EPSILON = 1e-12
SCALE = HEAD_DIM ** (-0.5)
MESH = pl.DeviceIdType.MESH

HALF = PAGE_LEN // 2
SEG = 64
BLOCKS = HALF // SEG
BACK_SEG = 64
BACK_BLOCKS = HALF // BACK_SEG
BLOCK = 2 * BACK_SEG

UNIT = 16
CHUNK = 4 * UNIT
LAG = 2
SLOTS = 4 * LAG
KINDS = 12
(TX, TNEAR, TFAR, TA1, TA2, TQ1, TQ2, TTA, TTN, TTM, TTF, TG) = range(KINDS)
LANDINGS = TTA + 1
GROUP = 8
WEIGHTS = (5, 7, 11, 13)
DIRECT = (64, 0)


def contract_rows(left, right):
    return lax.dot_general(
        left, right, (((0,), (0,)), ((), ())), preferred_element_type=jnp.float32
    )


def contract_cols(left, right):
    return lax.dot_general(
        left, right, (((1,), (1,)), ((), ())), preferred_element_type=jnp.float32
    )


def matmul(left, right):
    return jnp.dot(left, right, preferred_element_type=jnp.float32)


def repeat(count, body):
    def step(index, carry):
        body(index)
        return carry

    lax.fori_loop(0, count, step, 0)


def normed(values):
    average = jnp.mean(values, axis=-1, keepdims=True)
    centered = values - average
    variance = jnp.mean(centered * centered, axis=-1, keepdims=True)
    scale = lax.rsqrt(variance + EPSILON)
    return centered * scale, scale


def norm_back(grad, zhat, scale, gain):
    scaled = grad * gain
    average = jnp.mean(scaled, axis=-1, keepdims=True)
    along = jnp.mean(scaled * zhat, axis=-1, keepdims=True)
    return scale * (scaled - average - zhat * along)


def normal_cdf(values):
    return 0.5 * (1.0 + lax.erf(values * math.sqrt(0.5)))


def column(row):
    return jnp.transpose(jnp.broadcast_to(row, (128, row.shape[1])))[:, :1]


class Place:
    def __init__(self):
        d = lax.axis_index("dp")
        t = lax.axis_index("tensor")
        self.core = lax.rem(t, 2)
        self.core_peer = (d, t + 1 - 2 * self.core)
        self.y_peer = (d, t + 2 - 4 * lax.div(t, 2))
        self.diagonal = (d, t + 3 - 2 * self.core - 4 * lax.div(t, 2))
        self.y = lax.div(t, 2)
        self.low = lax.rem(d, GROUP)
        self.others = [
            (d - self.low + lax.rem(self.low + k, GROUP), t) for k in range(1, GROUP)
        ]
        pair = lax.rem(d, 2)
        line = lax.rem(lax.div(d, 2), 4)
        self.pair = pair
        self.mid = jnp.logical_or(line == 1, line == 2)
        self.end = jnp.logical_not(self.mid)
        self.upper = lax.div(line, 2)
        self.peer = (d + 1 - 2 * pair, t)
        self.line = (d + 2 - 4 * lax.rem(line, 2), t)
        self.cross = (jnp.where(line == 1, d + 2, d - 2), t)


def greet(place, barrier):
    def signal(device):
        pl.semaphore_signal(barrier, inc=1, device_id=device, device_id_type=MESH)

    for device in (place.core_peer, place.y_peer, place.diagonal, *place.others):
        signal(device)


def meet(barrier):
    pl.semaphore_wait(barrier, 2 + GROUP)


class GradientSum:
    def __init__(self, place, chunks, part, landing, send, recv):
        self.place = place
        self.chunks = chunks
        self.part = part
        self.landing = landing
        self.send = send
        self.recv = recv

    def rows(self, j, unit):
        return pl.ds(pl.multiple_of(j * CHUNK + unit * UNIT, UNIT), UNIT)

    def tick(self, t):
        place, part = self.place, self.part
        mine, other = place.pair, 1 - place.pair
        near, far = 2 + place.upper, 3 - place.upper

        def at(j, unit):
            return part.at[self.rows(j, unit)]

        def copy(kind, j, source, target, device):
            slot = lax.rem(j, SLOTS)
            return pltpu.make_async_remote_copy(
                src_ref=source,
                dst_ref=target,
                send_sem=self.send.at[kind, slot],
                recv_sem=self.recv.at[kind, slot],
                device_id=device,
                device_id_type=MESH,
            )

        def partial(kind, j, unit, device):
            return copy(kind, j, at(j, unit), self.landing.at[kind, lax.rem(j, SLOTS)], device)

        def final(kind, j, unit, device):
            return copy(kind, j, at(j, unit), at(j, unit), device)

        def add(kind, j, unit):
            rows = self.rows(j, unit)
            part[rows, :] = part[rows, :] + self.landing[kind, lax.rem(j, SLOTS)]

        def pair_first(j):
            return partial(TX, j, other, place.peer)

        def near_in(j):
            return partial(TNEAR, j, near, place.line)

        def far_in(j):
            return partial(TFAR, j, far, place.line)

        def mine_in(j):
            return partial(TA1, j, mine, place.line)

        def mine_across(j):
            return partial(TA2, j, mine, place.cross)

        def far_across(j):
            return partial(TQ1, j, far, place.cross)

        def near_pair(j):
            return partial(TQ2, j, near, place.peer)

        def mine_out(j):
            return partial(TTA, j, mine, place.line)

        def near_out(j):
            return final(TTN, j, near, place.line)

        def near_across(j):
            return final(TTM, j, near, place.cross)

        def far_out(j):
            return final(TTF, j, far, place.line)

        def pair_last(j):
            return final(TG, j, mine, place.peer)

        def stage_0(j):
            pair_first(j).start()

            @pl.when(place.end)
            def _():
                near_in(j).start()
                far_in(j).start()

        def stage_1(j):
            pair_first(j).wait()
            add(TX, j, mine)

            @pl.when(place.end)
            def _():
                near_in(j).wait_send()
                far_in(j).wait_send()
                mine_in(j).start()

            @pl.when(place.mid)
            def _():
                far_in(j).wait_recv()
                add(TFAR, j, far)
                far_across(j).start()
                near_in(j).wait_recv()
                add(TNEAR, j, near)

        def stage_2(j):
            @pl.when(place.end)
            def _():
                mine_in(j).wait_send()

            @pl.when(place.mid)
            def _():
                mine_in(j).wait_recv()
                far_across(j).wait()
                add(TA1, j, mine)
                mine_across(j).start()
                add(TQ1, j, near)
                near_pair(j).start()

        def stage_3(j):
            @pl.when(place.mid)
            def _():
                mine_across(j).wait()
                add(TA2, j, mine)
                mine_out(j).start()
                near_pair(j).wait()
                add(TQ2, j, near)
                near_across(j).start()
                near_out(j).start()

        def stage_4(j):
            @pl.when(place.mid)
            def _():
                mine_out(j).wait_send()
                near_out(j).wait_send()
                pair_last(j).start()
                near_across(j).wait()
                far_out(j).start()

            @pl.when(place.end)
            def _():
                mine_out(j).wait_recv()
                near_out(j).wait_recv()
                part[self.rows(j, mine), :] = self.landing[TTA, lax.rem(j, SLOTS)]
                pair_last(j).start()

        def stage_5(j):
            pair_last(j).wait()
            pl.when(place.mid)(lambda: far_out(j).wait_send())
            pl.when(place.end)(lambda: far_out(j).wait_recv())

        stages = (stage_0, stage_1, stage_2, stage_3, stage_4, stage_5)
        for number in reversed(range(len(stages))):
            j = t - number * LAG
            pl.when(jnp.logical_and(j >= 0, j < self.chunks))(
                functools.partial(stages[number], j)
            )

    def ticks(self):
        return self.chunks + 5 * LAG


def page_kernel(
    sizes,
    embeddings,
    replace_table,
    replace_ids,
    masked,
    padding,
    w_qkv_far,
    b_qv,
    w_out_far,
    b_out,
    first_gain,
    first_shift,
    w_in_far,
    b_in,
    w_down_far,
    b_down,
    second_gain,
    second_shift,
    cotangent,
    hidden_out,
    grad_embeddings,
    grads,
    inputs_low,
    queries,
    keys,
    values,
    log_total,
    heads,
    normed_low,
    hidden,
    active,
    zhat_one,
    scale_one,
    zhat_two,
    scale_two,
    w_qkv,
    w_out,
    w_in,
    w_down,
    w_all,
    shared_heads,
    columns,
    own_a,
    own_b,
    part,
    land_core,
    land_y,
    land_back,
    land_small,
    dz_low,
    du_low,
    dheads,
    dkeys,
    dvalues,
    dqkv_low,
    sums,
    local_sums,
    landing,
    core_send,
    core_recv,
    y_send,
    y_recv,
    back_send,
    back_recv,
    small_send,
    small_recv,
    dp_send,
    dp_recv,
    weight_sem,
    gather_send,
    gather_recv,
    hand_send,
    hand_recv,
    heads_send,
    heads_recv,
):
    width, hidden_width, local_heads, span = sizes
    head_width = local_heads * HEAD_DIM
    place = Place()
    core = place.core
    barrier = pltpu.get_barrier_semaphore()
    greet(place, barrier)
    weights = ((w_qkv_far, w_qkv), (w_out_far, w_out), (w_in_far, w_in), (w_down_far, w_down))

    def weight(index, layer):
        source, target = weights[index]
        return pltpu.make_async_copy(
            source.at[layer], target.at[layer], weight_sem.at[index, layer]
        )

    for index, layer in ((0, 0), (1, 0), (1, 1), (2, 0), (3, 0), (0, 1), (2, 1), (3, 1)):
        weight(index, layer).start()
    small_base = LAYERS * span
    chunks = grads.shape[0] // CHUNK
    grad_sum = GradientSum(place, chunks, grads, landing, dp_send, dp_recv)
    tick = grad_sum.tick

    def vector(ref, layer):
        both = ref[...].astype(jnp.float32)
        return jnp.where(layer == 0, both[0:1], both[1:2])

    def block(b):
        return pl.ds(pl.multiple_of(b * BLOCK, BLOCK), BLOCK)

    def segment(b, size, half):
        return pl.ds(pl.multiple_of(half * HALF + b * size, size), size)

    def kept(b, size):
        return segment(b, size, core)

    def given(b, size):
        return segment(b, size, 1 - core)

    def packed(b, size):
        return segment(b, size, 0)

    def halves(b, size):
        return segment(b, size, 0), segment(b, size, 1)

    def lanes(p, size=128):
        return pl.ds(pl.multiple_of(p * size, size), size)

    def remote(source, target, send, recv, device):
        return pltpu.make_async_remote_copy(
            src_ref=source,
            dst_ref=target,
            send_sem=send,
            recv_sem=recv,
            device_id=device,
            device_id_type=MESH,
        )

    def to_core(turn, b, size):
        return remote(
            part.at[given(b, size)],
            land_core.at[turn, packed(b, size)],
            core_send.at[turn, b],
            core_recv.at[turn, b],
            place.core_peer,
        )

    def over_y(turn, b, size):
        return remote(
            part.at[kept(b, size)],
            land_y.at[turn, packed(b, size)],
            y_send.at[turn, b],
            y_recv.at[turn, b],
            place.y_peer,
        )

    def to_other(turn, b, size, source):
        return remote(
            source.at[packed(b, size)],
            land_back.at[turn, packed(b, size)],
            back_send.at[turn, b],
            back_recv.at[turn, b],
            place.core_peer,
        )

    def send_y(turn, b, size):
        to_core(turn, b, size).wait()
        rows = kept(b, size)
        part[rows, :] = part[rows, :] + land_core[turn, packed(b, size), :]
        over_y(turn, b, size).start()

    def summed(turn, b, size):
        over_y(turn, b, size).wait()
        return part[kept(b, size), :] + land_y[turn, packed(b, size), :]

    def received(turn, b, size, source):
        to_other(turn, b, size, source).wait()
        return land_back[turn, packed(b, size), :].astype(jnp.bfloat16)

    def shard(which, layer):
        return (which * LAYERS + layer) * head_width

    def direct(layer):
        return pl.ds(shard(0, layer), DIRECT[layer]), pl.ds(shard(2, layer), DIRECT[layer])

    def piece_rows(which, layer, owner):
        size = (head_width - DIRECT[layer]) // GROUP
        first = shard(which, layer) + DIRECT[layer] + owner * size
        return pl.ds(pl.multiple_of(first, 8), size)

    def moving(source, target, index, device):
        return remote(
            grads.at[source], grads.at[target], gather_send.at[index], gather_recv.at[index], device
        )

    def whole(which, layer):
        return pl.ds(shard(which, layer), head_width)

    def own_shard(layer):
        return moving(whole(0, layer), whole(1, layer), layer, place.core_peer)

    def other_shard(layer):
        return moving(whole(2, layer), whole(3, layer), LAYERS + layer, place.core_peer)

    def piece_over(layer):
        return moving(
            piece_rows(0, layer, place.low),
            piece_rows(2, layer, place.low),
            2 * LAYERS + layer,
            place.y_peer,
        )

    def rest_over(layer):
        return moving(*direct(layer), 3 * LAYERS + layer, place.y_peer)

    def handed(layer, k):
        rows = piece_rows(2, layer, place.low)
        return pltpu.make_async_remote_copy(
            src_ref=grads.at[rows],
            dst_ref=grads.at[rows],
            send_sem=hand_send.at[layer, k],
            recv_sem=hand_recv.at[layer, place.low],
            device_id=place.others[k],
            device_id_type=MESH,
        )

    def handed_in(layer, k):
        owner = lax.rem(place.low + 1 + k, GROUP)
        rows = piece_rows(2, layer, owner)
        return pltpu.make_async_remote_copy(
            src_ref=grads.at[rows],
            dst_ref=grads.at[rows],
            send_sem=hand_send.at[layer, k],
            recv_sem=hand_recv.at[layer, owner],
            device_id=place.others[k],
            device_id_type=MESH,
        )

    def gather_first(layer):
        weight(1, layer).wait()
        grads[whole(0, layer), :] = w_out[layer].astype(jnp.float32)
        piece_over(layer).start()
        if DIRECT[layer]:
            rest_over(layer).start()
        own_shard(layer).start()

    def gather_second(layer):
        piece_over(layer).wait()
        for k in range(GROUP - 1):
            handed(layer, k).start()

    def gather_third(layer):
        for k in range(GROUP - 1):
            handed(layer, k).wait_send()
            handed_in(layer, k).wait_recv()
        if DIRECT[layer]:
            rest_over(layer).wait()
        other_shard(layer).start()

    def gather_last(layer):
        own_shard(layer).wait()
        other_shard(layer).wait()
        pairs_width = 2 * HEAD_DIM
        for which in range(4):
            source = which // 2
            owner = 2 * (place.y + source - 2 * place.y * source) + (
                core + which % 2 - 2 * core * (which % 2)
            )
            low = grads[whole(which, layer), :].astype(jnp.bfloat16)
            first = pl.multiple_of(owner * pairs_width, pairs_width)
            w_all[layer, pl.ds(first, pairs_width), :] = low[:pairs_width]
            first = pl.multiple_of(4 * pairs_width + owner * HEAD_DIM, HEAD_DIM)
            w_all[layer, pl.ds(first, HEAD_DIM), :] = low[pairs_width:]

    def heads_out(b):
        mine, theirs = shared_heads.at[core, b], shared_heads.at[1 - core, b]
        return [
            remote(
                source,
                shared_heads.at[2 + index, b],
                heads_send.at[index, b],
                heads_recv.at[index, b],
                device,
            )
            for index, (source, device) in enumerate(
                (
                    (theirs, place.core_peer),
                    (mine, place.y_peer),
                    (theirs, place.diagonal),
                )
            )
        ]

    def pack_heads(rows):
        cut = 2 * HEAD_DIM
        return jnp.concatenate(
            [
                rows[:, :cut],
                jnp.concatenate([rows[: SEG // 2, cut:], rows[SEG // 2 :, cut:]], axis=1),
            ],
            axis=0,
        )

    def all_heads(b):
        pairs, thirds = [], []
        for owner in range(4):
            side, half = owner // 2, owner % 2
            apart = 2 * (place.y + side - 2 * place.y * side) + (core + half - 2 * core * half)
            slot = jnp.where(apart == 0, core, apart + 1)
            low = shared_heads[slot, b].astype(jnp.bfloat16)
            pairs.append(low[:SEG])
            tail = low[SEG:]
            thirds.append(jnp.concatenate([tail[:, :HEAD_DIM], tail[:, HEAD_DIM:]], axis=0))
        return jnp.concatenate(pairs + thirds, axis=1)

    pad_row = padding[...].astype(jnp.float32)
    live_row = masked[...].astype(jnp.float32) * pad_row
    bias_row = (pad_row - 1.0) * 10000.0
    columns[:, 0:1] = column(live_row)
    columns[:, 1:2] = column(replace_ids[...].astype(jnp.float32))
    grads[small_base:, :] = jnp.zeros((CHUNK, width), jnp.float32)

    def chosen(rows, count):
        spots = lax.broadcasted_iota(jnp.int32, (count, REPL), 1).astype(jnp.float32)
        return jnp.where(columns[rows, 1:2] == spots, 1.0, 0.0)

    def first_input(b):
        rows = block(b)
        picked = matmul(chosen(rows, BLOCK).astype(jnp.bfloat16), replace_table[...])
        taken = jnp.where(
            columns[rows, 0:1] > 0.0, picked, embeddings[rows, :].astype(jnp.float32)
        )
        inputs_low[0, rows, :] = taken.astype(jnp.bfloat16)

    sums[...] = jnp.zeros_like(sums)
    local_sums[...] = jnp.zeros_like(local_sums)

    def project(layer, spans):
        bias_pair = vector(b_qv, layer)
        inputs = jnp.concatenate([inputs_low[layer, rows, :] for rows in spans], axis=0)
        projected = contract_cols(inputs, w_qkv[layer])

        def split(ref, h, columns_of):
            low = columns_of.astype(jnp.bfloat16)
            first = 0
            for rows in spans:
                ref[layer, h, rows, :] = low[first : first + rows.size]
                first += rows.size

        for h in range(local_heads):
            base = 3 * HEAD_DIM * h
            bias = 2 * HEAD_DIM * h
            split(
                queries,
                h,
                projected[:, base : base + HEAD_DIM] + bias_pair[:, bias : bias + HEAD_DIM],
            )
            split(keys, h, projected[:, base + HEAD_DIM : base + 2 * HEAD_DIM])
            split(
                values,
                h,
                projected[:, base + 2 * HEAD_DIM : base + 3 * HEAD_DIM]
                + bias_pair[:, bias + HEAD_DIM : bias + 2 * HEAD_DIM],
            )

    def scores_of(layer, h, query):
        return contract_cols(query, keys[layer, h]) * SCALE + bias_row

    def total_row(turn, index, amount):
        sums[turn, index : index + 1, :] = sums[turn, index : index + 1, :] + jnp.sum(
            amount, axis=0, keepdims=True
        )

    def norm_two(turn, b, size, grad):
        layer = LAYERS - 1 - turn
        rows = packed(b, size)
        zhat = zhat_two[layer, rows, :]
        dz = norm_back(grad, zhat, scale_two[layer, rows, :], vector(second_gain, layer))
        own_a[rows, :] = dz
        to_other(0, b, size, own_a).start()
        dz_low[kept(b, size), :] = dz.astype(jnp.bfloat16)
        total_row(turn, 0, grad * zhat)
        total_row(turn, 1, grad)
        total_row(turn, 2, dz)

    def forward(layer):
        last = layer == LAYERS - 1

        def attend(b):
            spans = halves(b, SEG)
            outs, logs = [], []
            for h in range(local_heads):
                query = jnp.concatenate([queries[layer, h, rows, :] for rows in spans], axis=0)
                scores = scores_of(layer, h, query)
                largest = jnp.max(scores, axis=-1, keepdims=True)
                weights_of = jnp.exp(scores - largest)
                totals = jnp.sum(weights_of, axis=-1, keepdims=True)
                probs = (weights_of * (1.0 / totals)).astype(jnp.bfloat16)
                outs.append(matmul(probs, values[layer, h]).astype(jnp.bfloat16))
                logs.append(largest + jnp.log(totals))
            joined = jnp.concatenate(outs, axis=1)
            full = joined.astype(jnp.float32)
            for side in range(2):
                shared_heads[side, b] = pack_heads(full[side * SEG : (side + 1) * SEG])
            for copy in heads_out(b):
                copy.start()
            for side, rows in enumerate(spans):
                cut = slice(side * SEG, (side + 1) * SEG)
                heads[layer, rows, :] = joined[cut]
                for h in range(local_heads):
                    log_total[layer, rows, h : h + 1] = logs[h][cut]

        repeat(BLOCKS, attend)

        @pl.when(layer == 0)
        def _():
            gather_first(1)
            gather_third(0)
            gather_last(0)

        pl.when(layer == 1)(lambda: gather_last(1))

        gain, shift, bias_out = (
            vector(first_gain, layer),
            vector(first_shift, layer),
            vector(b_out, layer),
        )
        bias_in = vector(b_in, layer)
        weight(2, layer).wait()
        weight(3, layer).wait()

        def feed_norm(b):
            rows = packed(b, SEG)
            for copy in heads_out(b):
                copy.wait()
            before = (
                inputs_low[layer, kept(b, SEG), :].astype(jnp.float32)
                + matmul(all_heads(b), w_all[layer])
                + bias_out
            )
            zhat, scale = normed(before)
            result = zhat * gain + shift
            own_a[rows, :] = result
            to_other(0, b, SEG, own_a).start()
            zhat_one[layer, rows, :] = zhat
            scale_one[layer, rows, :] = scale
            normed_low[layer, kept(b, SEG), :] = result.astype(jnp.bfloat16)

        def feed_main(b):
            spans = halves(b, SEG)
            normed_low[layer, given(b, SEG), :] = received(0, b, SEG, own_a)
            inputs = jnp.concatenate([normed_low[layer, rows, :] for rows in spans], axis=0)
            u = matmul(inputs, w_in[layer]) + bias_in
            g = (u * normal_cdf(u)).astype(jnp.bfloat16)
            lowered = matmul(g, w_down[layer])
            for side, rows in enumerate(spans):
                cut = slice(side * SEG, (side + 1) * SEG)
                part[rows, :] = lowered[cut]
                hidden[layer, rows, :] = u[cut]
                active[layer, rows, :] = g[cut]
            to_core(1, b, SEG).start()

        def feed(b):
            pl.when(b < BLOCKS)(lambda: feed_norm(b))
            pl.when(b >= 2)(lambda: send_y(1, b - 2, SEG))
            pl.when(b >= 1)(lambda: feed_main(b - 1))
            pl.when(jnp.logical_and(layer == 0, b == 1))(lambda: gather_second(1))

        repeat(BLOCKS + 1, feed)
        send_y(1, BLOCKS - 1, SEG)

        gain_two, shift_two, bias_down = (
            vector(second_gain, layer),
            vector(second_shift, layer),
            vector(b_down, layer),
        )
        pl.when(jnp.logical_not(last))(lambda: weight(0, layer + 1).wait())

        def receive(b):
            inputs_low[layer + 1, given(b, SEG), :] = received(1, b, SEG, own_b)
            pl.when(jnp.logical_not(last))(lambda: project(layer + 1, halves(b, SEG)))

            @pl.when(last)
            def _():
                dz_low[given(b, SEG), :] = received(0, b, SEG, own_a)

        def finish(b):
            rows = packed(b, SEG)
            before = own_a[rows, :] + summed(1, b, SEG) + bias_down
            zhat, scale = normed(before)
            result = zhat * gain_two + shift_two
            own_b[rows, :] = result
            to_other(1, b, SEG, own_b).start()
            zhat_two[layer, rows, :] = zhat
            scale_two[layer, rows, :] = scale
            inputs_low[layer + 1, kept(b, SEG), :] = result.astype(jnp.bfloat16)

            @pl.when(last)
            def _():
                live = columns[kept(b, SEG), 0:1]
                norm_two(0, b, SEG, cotangent[kept(b, SEG), :].astype(jnp.float32) * live)

            pl.when(b >= 1)(lambda: receive(b - 1))

        repeat(BLOCKS, finish)
        receive(BLOCKS - 1)
        pl.when(layer == 0)(lambda: gather_third(1))

    meet(barrier)
    gather_first(0)
    repeat(BACK_BLOCKS, first_input)
    weight(0, 0).wait()
    project(0, (block(0),))
    gather_second(0)
    repeat(BACK_BLOCKS - 1, lambda b: project(0, (block(b + 1),)))
    repeat(LAYERS, forward)

    def last_grad(b, grad):
        rows = kept(b, BACK_SEG)
        live = columns[rows, 0:1]
        masked_grad = grad * (1.0 - live)
        own_a[packed(b, BACK_SEG), :] = masked_grad
        to_other(0, b, BACK_SEG, own_a).start()
        grad_embeddings[rows, :] = masked_grad.astype(jnp.bfloat16)
        grads[small_base : small_base + REPL, :] = grads[
            small_base : small_base + REPL, :
        ] + lax.dot_general(
            chosen(rows, BACK_SEG),
            grad * live,
            (((0,), (0,)), ((), ())),
            precision=lax.Precision.HIGHEST,
            preferred_element_type=jnp.float32,
        )

    def backward(turn):
        layer = LAYERS - 1 - turn
        base = turn * span
        start = turn * (span // CHUNK)
        in_base = base + hidden_width
        out_base = in_base + width
        qkv_base = out_base + head_width

        def rows_at(first, count):
            return pl.ds(pl.multiple_of(first, 64), count)

        def down_piece(p):
            grads[rows_at(base + 128 * p, 128), :] = contract_rows(
                active[layer, :, lanes(p)], dz_low[...]
            )

        def in_piece(p):
            grads[rows_at(in_base + 128 * p, 128), :] = contract_rows(
                normed_low[layer, :, lanes(p)], du_low[...]
            )

        down_piece(0)
        tick(start)
        tick(start + 1)

        def feed(b):
            rows = block(b)
            dg = contract_cols(dz_low[rows, :], w_down[layer])
            u = hidden[layer, rows, :]
            density = jnp.exp(u * u * (-0.5)) * (1.0 / math.sqrt(2.0 * math.pi))
            du = dg * (normal_cdf(u) + u * density)
            du_low[rows, :] = du.astype(jnp.bfloat16)
            local_sums[turn, 0:1, :] = local_sums[turn, 0:1, :] + jnp.sum(
                du, axis=0, keepdims=True
            )
            down_piece(b + 1)
            tick(start + 2 + b)

        repeat(BACK_BLOCKS, feed)
        down_piece(5)

        def feed_in(b):
            spans = halves(b, BACK_SEG)
            left = jnp.concatenate([du_low[rows, :] for rows in spans], axis=0)
            result = contract_cols(left, w_in[layer])
            for side, rows in enumerate(spans):
                part[rows, :] = result[side * BACK_SEG : (side + 1) * BACK_SEG]
            to_core(0, b, BACK_SEG).start()
            pl.when(b >= 1)(lambda: send_y(0, b - 1, BACK_SEG))
            tick(start + 6 + b)

        repeat(BACK_BLOCKS, feed_in)
        send_y(0, BACK_BLOCKS - 1, BACK_SEG)

        def early_piece(p):
            in_piece(p)
            tick(start + 10 + p)

        repeat(4, early_piece)

        gain = vector(first_gain, layer)

        def norm_one(b):
            rows = packed(b, BACK_SEG)
            grad = own_a[rows, :] + summed(0, b, BACK_SEG)
            zhat = zhat_one[layer, rows, :]
            dz = norm_back(grad, zhat, scale_one[layer, rows, :], gain)
            own_b[rows, :] = dz
            to_other(1, b, BACK_SEG, own_b).start()
            dz_low[kept(b, BACK_SEG), :] = dz.astype(jnp.bfloat16)
            total_row(turn, 3, grad * zhat)
            total_row(turn, 4, grad)
            total_row(turn, 5, dz)
            tick(start + 14 + b)
            dz_low[given(b, BACK_SEG), :] = received(1, b, BACK_SEG, own_b)

        repeat(BACK_BLOCKS, norm_one)
        grads[rows_at(out_base, head_width), :] = contract_rows(heads[layer], dz_low[...])
        dheads[...] = contract_cols(dz_low[...], w_out[layer]).astype(jnp.bfloat16)
        tick(start + 18)
        in_piece(4)
        in_piece(5)
        dkeys[...] = jnp.zeros_like(dkeys)
        dvalues[...] = jnp.zeros_like(dvalues)

        def attend(b):
            rows = block(b)
            for h in range(local_heads):
                side = HEAD_DIM * h
                query = queries[layer, h, rows, :]
                probs = jnp.exp(scores_of(layer, h, query) - log_total[layer, rows, h : h + 1])
                dhead = dheads[rows, side : side + HEAD_DIM]
                dprobs = contract_cols(dhead, values[layer, h])
                dvalues[h] = dvalues[h] + contract_rows(probs.astype(jnp.bfloat16), dhead)
                inner = jnp.sum(probs * dprobs, axis=-1, keepdims=True)
                ds = (probs * (dprobs - inner)).astype(jnp.bfloat16)
                dq = matmul(ds, keys[layer, h]) * SCALE
                dkeys[h] = dkeys[h] + contract_rows(ds, query)
                dqkv_low[rows, 3 * side : 3 * side + HEAD_DIM] = dq.astype(jnp.bfloat16)
                local_sums[turn, 1:2, 2 * side : 2 * side + HEAD_DIM] = local_sums[
                    turn, 1:2, 2 * side : 2 * side + HEAD_DIM
                ] + jnp.sum(dq, axis=0, keepdims=True)
            tick(start + 19 + b)

        repeat(BACK_BLOCKS, attend)
        for h in range(local_heads):
            side = HEAD_DIM * h
            dqkv_low[:, 3 * side + HEAD_DIM : 3 * side + 2 * HEAD_DIM] = (
                dkeys[h] * SCALE
            ).astype(jnp.bfloat16)
            dv = dvalues[h]
            dqkv_low[:, 3 * side + 2 * HEAD_DIM : 3 * side + 3 * HEAD_DIM] = dv.astype(
                jnp.bfloat16
            )
            local_sums[turn, 1:2, 2 * side + HEAD_DIM : 2 * side + 2 * HEAD_DIM] = jnp.sum(
                dv, axis=0, keepdims=True
            )

        def back_project(b):
            spans = halves(b, BACK_SEG)
            left = jnp.concatenate([dqkv_low[rows, :] for rows in spans], axis=0)
            result = matmul(left, w_qkv[layer])
            for side, rows in enumerate(spans):
                part[rows, :] = result[side * BACK_SEG : (side + 1) * BACK_SEG]
            to_core(1, b, BACK_SEG).start()
            pl.when(b >= 1)(lambda: send_y(1, b - 1, BACK_SEG))
            tick(start + 23 + b)

        repeat(BACK_BLOCKS, back_project)
        send_y(1, BACK_BLOCKS - 1, BACK_SEG)

        def qkv_piece(p):
            grads[rows_at(qkv_base + 128 * p, 128), :] = contract_rows(
                dqkv_low[:, lanes(p)], inputs_low[layer]
            )
            tick(start + 27 + p)

        repeat(4, qkv_piece)
        grads[rows_at(qkv_base + 512, 64), :] = contract_rows(
            dqkv_low[:, 512:], inputs_low[layer]
        )
        tick(start + 31)

        def pass_on(b):
            rows = packed(b, BACK_SEG)
            grad = own_b[rows, :] + summed(1, b, BACK_SEG)
            pl.when(turn < LAYERS - 1)(lambda: norm_two(turn + 1, b, BACK_SEG, grad))
            pl.when(turn == LAYERS - 1)(lambda: last_grad(b, grad))
            tick(start + 32 + b)

        repeat(BACK_BLOCKS, pass_on)

        def receive(b):
            dz_low[given(b, BACK_SEG), :] = received(0, b, BACK_SEG, own_a)

        pl.when(turn < LAYERS - 1)(lambda: repeat(BACK_BLOCKS, receive))

    repeat(LAYERS, backward)
    hidden_out[...] = inputs_low[LAYERS]

    shared = REPL + 8 * LAYERS
    for turn in range(LAYERS):
        first = small_base + REPL + 8 * turn
        grads[first : first + 8, :] = sums[turn]
    grads[small_base + shared : small_base + shared + 8, :] = local_sums[...].reshape(8, width)
    short = remote(
        grads.at[pl.ds(small_base, shared)], land_small, small_send, small_recv, place.core_peer
    )
    short.start()

    def receive_grad(b):
        grad_embeddings[given(b, BACK_SEG), :] = received(0, b, BACK_SEG, own_a)

    repeat(BACK_BLOCKS, receive_grad)
    short.wait()
    grads[small_base : small_base + shared, :] = (
        grads[small_base : small_base + shared, :] + land_small[...]
    )
    done = LAYERS * (span // CHUNK)
    repeat(grad_sum.ticks() - done, lambda i: tick(done + i))


def run_pages(args, sizes):
    width, hidden_width, local_heads, span = sizes
    rows = PAGE_LEN
    flat = LAYERS * span + CHUNK
    half = rows // 2
    low, full = jnp.bfloat16, jnp.float32
    vmem, dma = pltpu.VMEM, pltpu.SemaphoreType.DMA
    head_width = local_heads * HEAD_DIM
    return pl.pallas_call(
        functools.partial(page_kernel, sizes),
        name="pages",
        out_shape=(
            vmem((rows, width), low),
            vmem((rows, width), low),
            vmem((flat, width), full),
        ),
        in_specs=[
            pl.BlockSpec(memory_space=pl.ANY if index in WEIGHTS else pltpu.VMEM)
            for index in range(len(args))
        ],
        out_specs=(
            pl.BlockSpec(memory_space=pltpu.VMEM),
            pl.BlockSpec(memory_space=pltpu.VMEM),
            pl.BlockSpec(memory_space=pltpu.VMEM),
        ),
        scratch_shapes=[
            vmem((LAYERS + 1, rows, width), low),
            vmem((LAYERS, local_heads, rows, HEAD_DIM), low),
            vmem((LAYERS, local_heads, rows, HEAD_DIM), low),
            vmem((LAYERS, local_heads, rows, HEAD_DIM), low),
            vmem((LAYERS, rows, 128), full),
            vmem((LAYERS, rows, head_width), low),
            vmem((LAYERS, rows, width), low),
            vmem((LAYERS, rows, hidden_width), full),
            vmem((LAYERS, rows, hidden_width), low),
            vmem((LAYERS, half, width), full),
            vmem((LAYERS, half, 1), full),
            vmem((LAYERS, half, width), full),
            vmem((LAYERS, half, 1), full),
            vmem((LAYERS, 3 * head_width, width), low),
            vmem((LAYERS, head_width, width), low),
            vmem((LAYERS, width, hidden_width), low),
            vmem((LAYERS, hidden_width, width), low),
            vmem((LAYERS, 4 * head_width, width), low),
            vmem((5, BLOCKS, 3 * SEG // 2, 2 * HEAD_DIM), full),
            vmem((rows, 128), full),
            vmem((half, width), full),
            vmem((half, width), full),
            vmem((rows, width), full),
            vmem((2, half, width), full),
            vmem((2, half, width), full),
            vmem((2, half, width), full),
            vmem((REPL + 8 * LAYERS, width), full),
            vmem((rows, width), low),
            vmem((rows, hidden_width), low),
            vmem((rows, head_width), low),
            vmem((local_heads, rows, HEAD_DIM), full),
            vmem((local_heads, rows, HEAD_DIM), full),
            vmem((rows, 3 * head_width), low),
            vmem((LAYERS, 8, width), full),
            vmem((LAYERS, 4, width), full),
            vmem((LANDINGS, SLOTS, UNIT, width), full),
            dma((2, BLOCKS)),
            dma((2, BLOCKS)),
            dma((2, BLOCKS)),
            dma((2, BLOCKS)),
            dma((2, BLOCKS)),
            dma((2, BLOCKS)),
            dma,
            dma,
            dma((KINDS, SLOTS)),
            dma((KINDS, SLOTS)),
            dma((4, LAYERS)),
            dma((4 * LAYERS,)),
            dma((4 * LAYERS,)),
            dma((LAYERS, GROUP)),
            dma((LAYERS, GROUP)),
            dma((3, BLOCKS)),
            dma((3, BLOCKS)),
        ],
        compiler_params=pltpu.CompilerParams(
            collective_id=0, has_side_effects=True, vmem_limit_bytes=46 << 20
        ),
    )(*args)


def place_kernel(sizes, hidden_out, grad_embeddings, every, *refs):
    width, hidden_width, local_heads, span = sizes
    head_width = local_heads * HEAD_DIM
    (
        out_hidden,
        out_embeddings,
        out_table,
        out_w_qkv,
        out_b_qv,
        out_w_out,
        out_b_out,
        out_first_gain,
        out_first_shift,
        out_w_in,
        out_b_in,
        out_w_down,
        out_b_down,
        out_second_gain,
        out_second_shift,
        short,
        sems,
    ) = refs
    base = LAYERS * span
    pairs = [(every.at[pl.ds(base, CHUNK)], short), (every.at[pl.ds(base, REPL)], out_table)]
    pairs += [(hidden_out, out_hidden), (grad_embeddings, out_embeddings)]
    for turn in range(LAYERS):
        first = span * turn
        for ref, rows in (
            (out_w_down, hidden_width),
            (out_w_in, width),
            (out_w_out, head_width),
            (out_w_qkv, 3 * head_width),
        ):
            pairs.append((every.at[pl.ds(first, rows)], ref.at[LAYERS - 1 - turn]))
            first += rows
    copies = [
        pltpu.make_async_copy(source, target, sems.at[index])
        for index, (source, target) in enumerate(pairs)
    ]
    for copy in copies:
        copy.start()
    copies[0].wait()
    local = REPL + 8 * LAYERS
    for ref, row, step in (
        (out_second_gain, REPL, 8),
        (out_second_shift, REPL + 1, 8),
        (out_b_down, REPL + 2, 8),
        (out_first_gain, REPL + 3, 8),
        (out_first_shift, REPL + 4, 8),
        (out_b_out, REPL + 5, 8),
        (out_b_in, local, 4),
        (out_b_qv, local + 1, 4),
    ):
        for turn in range(LAYERS):
            layer = LAYERS - 1 - turn
            ref[layer : layer + 1, :] = short[
                row + step * turn : row + step * turn + 1, : ref.shape[1]
            ]
    for copy in copies[1:]:
        copy.wait()


def place_outputs(hidden_out, grad_embeddings, every, sizes):
    width, hidden_width, local_heads, span = sizes
    head_width = local_heads * HEAD_DIM
    low, full = jnp.bfloat16, jnp.float32
    rows = hidden_out.shape[0]
    shapes = (
        ((rows, width), low),
        ((rows, width), low),
        ((REPL, width), full),
        ((LAYERS, 3 * head_width, width), full),
        ((LAYERS, 2 * head_width), full),
        ((LAYERS, head_width, width), full),
        ((LAYERS, width), full),
        ((LAYERS, width), full),
        ((LAYERS, width), full),
        ((LAYERS, width, hidden_width), full),
        ((LAYERS, hidden_width), full),
        ((LAYERS, hidden_width, width), full),
        ((LAYERS, width), full),
        ((LAYERS, width), full),
        ((LAYERS, width), full),
    )
    far = pl.BlockSpec(memory_space=pl.ANY)
    close = pl.BlockSpec(memory_space=pltpu.VMEM)
    return pl.pallas_call(
        functools.partial(place_kernel, sizes),
        name="place_outputs",
        out_shape=[jax.ShapeDtypeStruct(shape, kind) for shape, kind in shapes],
        in_specs=[far] * 3,
        out_specs=[close if shape[0] == LAYERS and len(shape) == 2 else far for shape, _ in shapes],
        scratch_shapes=[
            pltpu.VMEM((CHUNK, width), full),
            pltpu.SemaphoreType.DMA((4 + 4 * LAYERS,)),
        ],
        compiler_params=pltpu.CompilerParams(vmem_limit_bytes=4 << 20),
    )(hidden_out, grad_embeddings, every)


def moved(every):
    def kernel(source, target, sem):
        copy = pltpu.make_async_copy(source, target, sem)
        copy.start()
        copy.wait()

    far = pl.BlockSpec(memory_space=pl.ANY)
    return pl.pallas_call(
        kernel,
        name="moved",
        out_shape=jax.ShapeDtypeStruct(every.shape, every.dtype),
        in_specs=[far],
        out_specs=far,
        scratch_shapes=[pltpu.SemaphoreType.DMA],
        compiler_params=pltpu.CompilerParams(vmem_limit_bytes=4 << 20),
    )(every)


def on_device(*args):
    (embeddings, replace_table, replace_ids, masked, padding, w_qkv, b_qv, *_) = args
    width = embeddings.shape[1]
    head_width = w_qkv.shape[2] // 3
    hidden_width = args[11].shape[2]
    span = 2 * hidden_width + 4 * head_width
    args = list(args)
    args[5] = jnp.swapaxes(args[5], 1, 2)
    for index in (2, 3, 4):
        args[index] = args[index].reshape(1, PAGE_LEN)
    sizes = (width, hidden_width, head_width // HEAD_DIM, span)
    hidden_out, grad_embeddings, every = run_pages(args, sizes)
    groups = lax.axis_size("dp") // GROUP
    if groups > 1:
        every = lax.psum(
            moved(every),
            "dp",
            axis_index_groups=[
                [low + GROUP * high for high in range(groups)] for low in range(GROUP)
            ],
        )

    results = place_outputs(hidden_out, grad_embeddings, every, sizes)
    return (*results[:3], jnp.swapaxes(results[3], 1, 2), *results[4:])


def solution(mesh):
    placed = (
        P("dp", None),
        P(),
        P("dp"),
        P("dp"),
        P("dp"),
        P(None, None, "tensor"),
        P(None, "tensor"),
        P(None, "tensor", None),
        P(),
        P(),
        P(),
        P(None, None, "tensor"),
        P(None, "tensor"),
        P(None, "tensor", None),
        P(),
        P(),
        P(),
        P("dp", None),
    )
    return jax.shard_map(
        on_device,
        mesh=mesh,
        in_specs=placed,
        out_specs=(
            P("dp", None),
            P("dp", None),
            P(),
            P(None, None, "tensor"),
            P(None, "tensor"),
            P(None, "tensor", None),
            P(),
            P(),
            P(),
            P(None, None, "tensor"),
            P(None, "tensor"),
            P(None, "tensor", None),
            P(),
            P(),
            P(),
        ),
        check_vma=False,
    )
```

```python
import functools
import math

import jax
import jax.numpy as jnp
from jax import lax
from jax.experimental import pallas as pl
from jax.experimental.pallas import tpu as pltpu
from jax.sharding import PartitionSpec as P

HEAD_DIM = 64
LAYERS = 2
PAGE_LEN = 512
REPL = 32
EPSILON = 1e-12
SCALE = HEAD_DIM ** (-0.5)
MESH = pl.DeviceIdType.MESH

HALF = PAGE_LEN // 2
SEG = 64
BLOCKS = HALF // SEG
BACK_SEG = 64
BACK_BLOCKS = HALF // BACK_SEG
BLOCK = 2 * BACK_SEG

WIDE = 24
NARROW = 8
CHUNK = 2 * WIDE + 4 * NARROW
HOLE = 2 * NARROW
SHORT_CHUNKS = 3
LAG = 2
SLOTS = 4 * LAG
KINDS = 18
(TX, TA1, TA2, TTA, TQ0, TQ1, TQ2, TR0, TR1, TR2, TR3, TTN, TTM, TTF, TG, TR4, TR5, TR6) = range(
    KINDS
)
WIDE_LANDINGS = (TX, TA1, TA2, TTA)
NARROW_LANDINGS = (TQ1, TQ2, TR0, TR1, TR2, TR3)
GROUP = 8
WEIGHTS = (5, 7, 11, 13)
DIRECT = (64, 0)


def contract_rows(left, right):
    return lax.dot_general(
        left, right, (((0,), (0,)), ((), ())), preferred_element_type=jnp.float32
    )


def contract_cols(left, right):
    return lax.dot_general(
        left, right, (((1,), (1,)), ((), ())), preferred_element_type=jnp.float32
    )


def matmul(left, right):
    return jnp.dot(left, right, preferred_element_type=jnp.float32)


def repeat(count, body):
    def step(index, carry):
        body(index)
        return carry

    lax.fori_loop(0, count, step, 0)


def normed(values):
    average = jnp.mean(values, axis=-1, keepdims=True)
    centered = values - average
    variance = jnp.mean(centered * centered, axis=-1, keepdims=True)
    scale = lax.rsqrt(variance + EPSILON)
    return centered * scale, scale


def norm_back(grad, zhat, scale, gain):
    scaled = grad * gain
    average = jnp.mean(scaled, axis=-1, keepdims=True)
    along = jnp.mean(scaled * zhat, axis=-1, keepdims=True)
    return scale * (scaled - average - zhat * along)


def normal_cdf(values):
    return 0.5 * (1.0 + lax.erf(values * math.sqrt(0.5)))


def column(row):
    return jnp.transpose(jnp.broadcast_to(row, (128, row.shape[1])))[:, :1]


class Place:
    def __init__(self):
        d = lax.axis_index("dp")
        t = lax.axis_index("tensor")
        self.core = lax.rem(t, 2)
        self.core_peer = (d, t + 1 - 2 * self.core)
        self.y_peer = (d, t + 2 - 4 * lax.div(t, 2))
        self.diagonal = (d, t + 3 - 2 * self.core - 4 * lax.div(t, 2))
        self.y = lax.div(t, 2)
        self.low = lax.rem(d, GROUP)
        self.others = [
            (d - self.low + lax.rem(self.low + k, GROUP), t) for k in range(1, GROUP)
        ]
        pair = lax.rem(d, 2)
        line = lax.rem(lax.div(d, 2), 4)
        self.pair = pair
        self.mid = jnp.logical_or(line == 1, line == 2)
        self.end = jnp.logical_not(self.mid)
        self.upper = lax.div(line, 2)
        self.peer = (d + 1 - 2 * pair, t)
        self.line = (d + 2 - 4 * lax.rem(line, 2), t)
        self.cross = (jnp.where(line == 1, d + 2, d - 2), t)


def greet(place, barrier):
    def signal(device):
        pl.semaphore_signal(barrier, inc=1, device_id=device, device_id_type=MESH)

    for device in (place.core_peer, place.y_peer, place.diagonal, *place.others):
        signal(device)


def meet(barrier):
    pl.semaphore_wait(barrier, 2 + GROUP)


class GradientSum:
    def __init__(self, place, chunks, part, wide, both, narrow, send, recv):
        self.place = place
        self.chunks = chunks
        self.part = part
        self.wide = wide
        self.both = both
        self.narrow = narrow
        self.send = send
        self.recv = recv

    def wide_rows(self, j, unit):
        return pl.ds(pl.multiple_of(j * CHUNK + unit * WIDE, NARROW), WIDE)

    def narrow_rows(self, j, unit, count=1):
        first = j * CHUNK + 2 * WIDE + unit * NARROW
        return pl.ds(pl.multiple_of(first, NARROW), count * NARROW)

    def tick(self, t):
        place, part = self.place, self.part
        mine, other = place.pair, 1 - place.pair
        near, far = place.upper, 1 - place.upper
        near_end, far_end = 2 + place.upper, 3 - place.upper

        def copy(kind, j, rows, target, device):
            slot = lax.rem(j, SLOTS)
            return pltpu.make_async_remote_copy(
                src_ref=part.at[rows],
                dst_ref=target,
                send_sem=self.send.at[kind, slot],
                recv_sem=self.recv.at[kind, slot],
                device_id=device,
                device_id_type=MESH,
            )

        def wide_slot(kind, j):
            return WIDE_LANDINGS.index(kind), lax.rem(j, SLOTS)

        def narrow_slot(kind, j):
            return NARROW_LANDINGS.index(kind), lax.rem(j, SLOTS)

        def wide_part(kind, j, unit, device):
            return copy(
                kind, j, self.wide_rows(j, unit), self.wide.at[wide_slot(kind, j)], device
            )

        def narrow_part(kind, j, unit, device):
            return copy(
                kind, j, self.narrow_rows(j, unit), self.narrow.at[narrow_slot(kind, j)], device
            )

        def final(kind, j, rows, device):
            return copy(kind, j, rows, part.at[rows], device)

        def add_wide(kind, j, unit):
            rows = self.wide_rows(j, unit)
            part[rows, :] = part[rows, :] + self.wide[wide_slot(kind, j)]

        def add_narrow(kind, j, unit):
            rows = self.narrow_rows(j, unit)
            part[rows, :] = part[rows, :] + self.narrow[narrow_slot(kind, j)]

        def pair_first(j):
            return wide_part(TX, j, other, place.peer)

        def mine_in(j):
            return wide_part(TA1, j, mine, place.line)

        def mine_across(j):
            return wide_part(TA2, j, mine, place.cross)

        def mine_out(j):
            return wide_part(TTA, j, mine, place.line)

        def pair_last(j):
            return final(TG, j, self.wide_rows(j, mine), place.peer)

        def both_in(j):
            rows = self.narrow_rows(j, 0, 2)
            return copy(TQ0, j, rows, self.both.at[lax.rem(j, SLOTS)], place.line)

        def far_across(j):
            return narrow_part(TQ1, j, far, place.cross)

        def near_pair(j):
            return narrow_part(TQ2, j, near, place.peer)

        def near_out(j):
            return final(TTN, j, self.narrow_rows(j, near), place.line)

        def near_across(j):
            return final(TTM, j, self.narrow_rows(j, near), place.cross)

        def far_out(j):
            return final(TTF, j, self.narrow_rows(j, far), place.line)

        def end_in(j):
            return narrow_part(TR0, j, far_end, place.line)

        def end_across(j):
            return narrow_part(TR1, j, far_end, place.cross)

        def end_up(j):
            return narrow_part(TR2, j, near_end, place.line)

        def end_pair(j):
            return narrow_part(TR3, j, near_end, place.peer)

        def end_down(j):
            return final(TR4, j, self.narrow_rows(j, near_end), place.line)

        def end_back(j):
            return final(TR5, j, self.narrow_rows(j, near_end), place.cross)

        def end_out(j):
            return final(TR6, j, self.narrow_rows(j, far_end), place.line)

        def ended(j, body):
            pl.when(j < self.chunks - SHORT_CHUNKS)(body)

        def stage_0(j):
            pair_first(j).start()

            @pl.when(place.end)
            def _():
                ended(j, lambda: end_in(j).start())
                both_in(j).start()

        def stage_1(j):
            pair_first(j).wait()

            @pl.when(place.end)
            def _():
                both_in(j).wait_send()
                ended(j, lambda: end_in(j).wait_send())
                add_wide(TX, j, mine)
                mine_in(j).start()

            @pl.when(place.mid)
            def _():
                def onward():
                    end_in(j).wait_recv()
                    add_narrow(TR0, j, far_end)
                    end_across(j).start()

                ended(j, onward)
                both_in(j).wait_recv()
                rows = self.narrow_rows(j, 0, 2)
                part[rows, :] = part[rows, :] + self.both[lax.rem(j, SLOTS)]
                far_across(j).start()
                add_wide(TX, j, mine)

        def stage_2(j):
            @pl.when(place.end)
            def _():
                mine_in(j).wait_send()

            @pl.when(place.mid)
            def _():
                mine_in(j).wait_recv()
                far_across(j).wait()

                def onward():
                    end_across(j).wait()
                    add_narrow(TR1, j, near_end)
                    end_up(j).start()

                ended(j, onward)
                add_narrow(TQ1, j, near)
                near_pair(j).start()
                add_wide(TA1, j, mine)
                mine_across(j).start()

        def stage_3(j):
            @pl.when(place.end)
            def _():
                def onward():
                    end_up(j).wait_recv()
                    add_narrow(TR2, j, near_end)
                    end_pair(j).start()

                ended(j, onward)

            @pl.when(place.mid)
            def _():
                ended(j, lambda: end_up(j).wait_send())
                mine_across(j).wait()
                near_pair(j).wait()
                add_narrow(TQ2, j, near)
                near_across(j).start()
                near_out(j).start()
                add_wide(TA2, j, mine)
                mine_out(j).start()

        def stage_4(j):
            @pl.when(place.mid)
            def _():
                near_across(j).wait()
                far_out(j).start()
                near_out(j).wait_send()
                mine_out(j).wait_send()
                pair_last(j).start()

            @pl.when(place.end)
            def _():
                mine_out(j).wait_recv()
                near_out(j).wait_recv()

                def onward():
                    end_pair(j).wait()
                    add_narrow(TR3, j, near_end)
                    end_down(j).start()

                ended(j, onward)
                part[self.wide_rows(j, mine), :] = self.wide[wide_slot(TTA, j)]
                pair_last(j).start()

        def stage_5(j):
            @pl.when(place.mid)
            def _():
                def onward():
                    end_down(j).wait_recv()
                    end_back(j).start()

                ended(j, onward)
                far_out(j).wait_send()

            @pl.when(place.end)
            def _():
                ended(j, lambda: end_down(j).wait_send())
                far_out(j).wait_recv()

            pair_last(j).wait()

        def stage_6(j):
            @pl.when(place.mid)
            def _():
                def onward():
                    end_back(j).wait()
                    end_out(j).start()

                ended(j, onward)

        def stage_7(j):
            pl.when(place.mid)(lambda: ended(j, lambda: end_out(j).wait_send()))
            pl.when(place.end)(lambda: ended(j, lambda: end_out(j).wait_recv()))

        stages = (stage_0, stage_1, stage_2, stage_3, stage_4, stage_5, stage_6, stage_7)
        for number in reversed(range(len(stages))):
            j = t - number * LAG
            pl.when(jnp.logical_and(j >= 0, j < self.chunks))(
                functools.partial(stages[number], j)
            )

    def ticks(self):
        return self.chunks + max(5 * LAG, 7 * LAG - SHORT_CHUNKS)


def page_kernel(
    sizes,
    embeddings,
    replace_table,
    replace_ids,
    masked,
    padding,
    w_qkv_far,
    b_qv,
    w_out_far,
    b_out,
    first_gain,
    first_shift,
    w_in_far,
    b_in,
    w_down_far,
    b_down,
    second_gain,
    second_shift,
    cotangent,
    hidden_out,
    grad_embeddings,
    grads,
    inputs_low,
    queries,
    keys,
    values,
    log_total,
    heads,
    normed_low,
    hidden,
    active,
    zhat_one,
    scale_one,
    zhat_two,
    scale_two,
    w_qkv,
    w_out,
    w_in,
    w_down,
    w_all,
    shared_heads,
    columns,
    own_a,
    own_b,
    part,
    land_core,
    land_y,
    land_back,
    land_small,
    dz_low,
    du_low,
    dheads,
    dkeys,
    dvalues,
    dqkv_low,
    sums,
    local_sums,
    land_wide,
    land_both,
    land_narrow,
    core_send,
    core_recv,
    y_send,
    y_recv,
    back_send,
    back_recv,
    small_send,
    small_recv,
    dp_send,
    dp_recv,
    weight_sem,
    gather_send,
    gather_recv,
    hand_send,
    hand_recv,
    heads_send,
    heads_recv,
):
    width, hidden_width, local_heads, span = sizes
    head_width = local_heads * HEAD_DIM
    place = Place()
    core = place.core
    barrier = pltpu.get_barrier_semaphore()
    greet(place, barrier)
    weights = ((w_qkv_far, w_qkv), (w_out_far, w_out), (w_in_far, w_in), (w_down_far, w_down))

    def weight(index, layer):
        source, target = weights[index]
        return pltpu.make_async_copy(
            source.at[layer], target.at[layer], weight_sem.at[index, layer]
        )

    for index, layer in ((0, 0), (1, 0), (1, 1), (2, 0), (3, 0), (0, 1), (2, 1), (3, 1)):
        weight(index, layer).start()
    tail_base = LAYERS * span - HEAD_DIM + HOLE
    small_base = tail_base + CHUNK
    assert tail_base % CHUNK == 0 and span % HEAD_DIM == 0
    chunks = grads.shape[0] // CHUNK
    grad_sum = GradientSum(place, chunks, grads, land_wide, land_both, land_narrow, dp_send, dp_recv)
    tick = grad_sum.tick

    def vector(ref, layer):
        both = ref[...].astype(jnp.float32)
        return jnp.where(layer == 0, both[0:1], both[1:2])

    def block(b):
        return pl.ds(pl.multiple_of(b * BLOCK, BLOCK), BLOCK)

    def segment(b, size, half):
        return pl.ds(pl.multiple_of(half * HALF + b * size, size), size)

    def kept(b, size):
        return segment(b, size, core)

    def given(b, size):
        return segment(b, size, 1 - core)

    def packed(b, size):
        return segment(b, size, 0)

    def halves(b, size):
        return segment(b, size, 0), segment(b, size, 1)

    def lanes(p, size=128):
        return pl.ds(pl.multiple_of(p * size, size), size)

    def remote(source, target, send, recv, device):
        return pltpu.make_async_remote_copy(
            src_ref=source,
            dst_ref=target,
            send_sem=send,
            recv_sem=recv,
            device_id=device,
            device_id_type=MESH,
        )

    def to_core(turn, b, size):
        return remote(
            part.at[given(b, size)],
            land_core.at[turn, packed(b, size)],
            core_send.at[turn, b],
            core_recv.at[turn, b],
            place.core_peer,
        )

    def over_y(turn, b, size):
        return remote(
            part.at[kept(b, size)],
            land_y.at[turn, packed(b, size)],
            y_send.at[turn, b],
            y_recv.at[turn, b],
            place.y_peer,
        )

    def to_other(turn, b, size, source):
        return remote(
            source.at[packed(b, size)],
            land_back.at[turn, packed(b, size)],
            back_send.at[turn, b],
            back_recv.at[turn, b],
            place.core_peer,
        )

    def send_y(turn, b, size):
        to_core(turn, b, size).wait()
        rows = kept(b, size)
        part[rows, :] = part[rows, :] + land_core[turn, packed(b, size), :]
        over_y(turn, b, size).start()

    def summed(turn, b, size):
        over_y(turn, b, size).wait()
        return part[kept(b, size), :] + land_y[turn, packed(b, size), :]

    def received(turn, b, size, source):
        to_other(turn, b, size, source).wait()
        return land_back[turn, packed(b, size), :].astype(jnp.bfloat16)

    def shard(which, layer):
        return (which * LAYERS + layer) * head_width

    def direct(layer):
        return pl.ds(shard(0, layer), DIRECT[layer]), pl.ds(shard(2, layer), DIRECT[layer])

    def piece_rows(which, layer, owner):
        size = (head_width - DIRECT[layer]) // GROUP
        first = shard(which, layer) + DIRECT[layer] + owner * size
        return pl.ds(pl.multiple_of(first, 8), size)

    def moving(source, target, index, device):
        return remote(
            grads.at[source], grads.at[target], gather_send.at[index], gather_recv.at[index], device
        )

    def whole(which, layer):
        return pl.ds(shard(which, layer), head_width)

    def own_shard(layer):
        return moving(whole(0, layer), whole(1, layer), layer, place.core_peer)

    def other_shard(layer):
        return moving(whole(2, layer), whole(3, layer), LAYERS + layer, place.core_peer)

    def piece_over(layer):
        return moving(
            piece_rows(0, layer, place.low),
            piece_rows(2, layer, place.low),
            2 * LAYERS + layer,
            place.y_peer,
        )

    def rest_over(layer):
        return moving(*direct(layer), 3 * LAYERS + layer, place.y_peer)

    def handed(layer, k):
        rows = piece_rows(2, layer, place.low)
        return pltpu.make_async_remote_copy(
            src_ref=grads.at[rows],
            dst_ref=grads.at[rows],
            send_sem=hand_send.at[layer, k],
            recv_sem=hand_recv.at[layer, place.low],
            device_id=place.others[k],
            device_id_type=MESH,
        )

    def handed_in(layer, k):
        owner = lax.rem(place.low + 1 + k, GROUP)
        rows = piece_rows(2, layer, owner)
        return pltpu.make_async_remote_copy(
            src_ref=grads.at[rows],
            dst_ref=grads.at[rows],
            send_sem=hand_send.at[layer, k],
            recv_sem=hand_recv.at[layer, owner],
            device_id=place.others[k],
            device_id_type=MESH,
        )

    def gather_first(layer):
        weight(1, layer).wait()
        grads[whole(0, layer), :] = w_out[layer].astype(jnp.float32)
        piece_over(layer).start()
        if DIRECT[layer]:
            rest_over(layer).start()
        own_shard(layer).start()

    def gather_second(layer):
        piece_over(layer).wait()
        for k in range(GROUP - 1):
            handed(layer, k).start()

    def gather_third(layer):
        for k in range(GROUP - 1):
            handed(layer, k).wait_send()
            handed_in(layer, k).wait_recv()
        if DIRECT[layer]:
            rest_over(layer).wait()
        other_shard(layer).start()

    def gather_last(layer):
        own_shard(layer).wait()
        other_shard(layer).wait()
        pairs_width = 2 * HEAD_DIM
        for which in range(4):
            source = which // 2
            owner = 2 * (place.y + source - 2 * place.y * source) + (
                core + which % 2 - 2 * core * (which % 2)
            )
            low = grads[whole(which, layer), :].astype(jnp.bfloat16)
            first = pl.multiple_of(owner * pairs_width, pairs_width)
            w_all[layer, pl.ds(first, pairs_width), :] = low[:pairs_width]
            first = pl.multiple_of(4 * pairs_width + owner * HEAD_DIM, HEAD_DIM)
            w_all[layer, pl.ds(first, HEAD_DIM), :] = low[pairs_width:]

    def heads_out(b):
        mine, theirs = shared_heads.at[core, b], shared_heads.at[1 - core, b]
        return [
            remote(
                source,
                shared_heads.at[2 + index, b],
                heads_send.at[index, b],
                heads_recv.at[index, b],
                device,
            )
            for index, (source, device) in enumerate(
                (
                    (theirs, place.core_peer),
                    (mine, place.y_peer),
                    (theirs, place.diagonal),
                )
            )
        ]

    def pack_heads(rows):
        cut = 2 * HEAD_DIM
        return jnp.concatenate(
            [
                rows[:, :cut],
                jnp.concatenate([rows[: SEG // 2, cut:], rows[SEG // 2 :, cut:]], axis=1),
            ],
            axis=0,
        )

    def all_heads(b):
        pairs, thirds = [], []
        for owner in range(4):
            side, half = owner // 2, owner % 2
            apart = 2 * (place.y + side - 2 * place.y * side) + (core + half - 2 * core * half)
            slot = jnp.where(apart == 0, core, apart + 1)
            low = shared_heads[slot, b].astype(jnp.bfloat16)
            pairs.append(low[:SEG])
            tail = low[SEG:]
            thirds.append(jnp.concatenate([tail[:, :HEAD_DIM], tail[:, HEAD_DIM:]], axis=0))
        return jnp.concatenate(pairs + thirds, axis=1)

    pad_row = padding[...].astype(jnp.float32)
    live_row = masked[...].astype(jnp.float32) * pad_row
    bias_row = (pad_row - 1.0) * 10000.0
    columns[:, 0:1] = column(live_row)
    columns[:, 1:2] = column(replace_ids[...].astype(jnp.float32))
    grads[small_base:, :] = jnp.zeros((CHUNK, width), jnp.float32)

    def chosen(rows, count):
        spots = lax.broadcasted_iota(jnp.int32, (count, REPL), 1).astype(jnp.float32)
        return jnp.where(columns[rows, 1:2] == spots, 1.0, 0.0)

    def first_input(b):
        rows = block(b)
        picked = matmul(chosen(rows, BLOCK).astype(jnp.bfloat16), replace_table[...])
        taken = jnp.where(
            columns[rows, 0:1] > 0.0, picked, embeddings[rows, :].astype(jnp.float32)
        )
        inputs_low[0, rows, :] = taken.astype(jnp.bfloat16)

    sums[...] = jnp.zeros_like(sums)
    local_sums[...] = jnp.zeros_like(local_sums)

    def project(layer, spans):
        bias_pair = vector(b_qv, layer)
        inputs = jnp.concatenate([inputs_low[layer, rows, :] for rows in spans], axis=0)
        projected = contract_cols(inputs, w_qkv[layer])

        def split(ref, h, columns_of):
            low = columns_of.astype(jnp.bfloat16)
            first = 0
            for rows in spans:
                ref[layer, h, rows, :] = low[first : first + rows.size]
                first += rows.size

        for h in range(local_heads):
            base = 3 * HEAD_DIM * h
            bias = 2 * HEAD_DIM * h
            split(
                queries,
                h,
                projected[:, base : base + HEAD_DIM] + bias_pair[:, bias : bias + HEAD_DIM],
            )
            split(keys, h, projected[:, base + HEAD_DIM : base + 2 * HEAD_DIM])
            split(
                values,
                h,
                projected[:, base + 2 * HEAD_DIM : base + 3 * HEAD_DIM]
                + bias_pair[:, bias + HEAD_DIM : bias + 2 * HEAD_DIM],
            )

    def scores_of(layer, h, query):
        return contract_cols(query, keys[layer, h]) * SCALE + bias_row

    def total_row(turn, index, amount):
        sums[turn, index : index + 1, :] = sums[turn, index : index + 1, :] + jnp.sum(
            amount, axis=0, keepdims=True
        )

    def norm_two(turn, b, size, grad):
        layer = LAYERS - 1 - turn
        rows = packed(b, size)
        zhat = zhat_two[layer, rows, :]
        dz = norm_back(grad, zhat, scale_two[layer, rows, :], vector(second_gain, layer))
        own_a[rows, :] = dz
        to_other(0, b, size, own_a).start()
        dz_low[kept(b, size), :] = dz.astype(jnp.bfloat16)
        total_row(turn, 0, grad * zhat)
        total_row(turn, 1, grad)
        total_row(turn, 2, dz)

    def forward(layer):
        last = layer == LAYERS - 1

        def attend(b):
            spans = halves(b, SEG)
            outs, logs = [], []
            for h in range(local_heads):
                query = jnp.concatenate([queries[layer, h, rows, :] for rows in spans], axis=0)
                scores = scores_of(layer, h, query)
                largest = jnp.max(scores, axis=-1, keepdims=True)
                weights_of = jnp.exp(scores - largest)
                totals = jnp.sum(weights_of, axis=-1, keepdims=True)
                probs = (weights_of * (1.0 / totals)).astype(jnp.bfloat16)
                outs.append(matmul(probs, values[layer, h]).astype(jnp.bfloat16))
                logs.append(largest + jnp.log(totals))
            joined = jnp.concatenate(outs, axis=1)
            full = joined.astype(jnp.float32)
            for side in range(2):
                shared_heads[side, b] = pack_heads(full[side * SEG : (side + 1) * SEG])
            for copy in heads_out(b):
                copy.start()
            for side, rows in enumerate(spans):
                cut = slice(side * SEG, (side + 1) * SEG)
                heads[layer, rows, :] = joined[cut]
                for h in range(local_heads):
                    log_total[layer, rows, h : h + 1] = logs[h][cut]

        repeat(BLOCKS, attend)

        @pl.when(layer == 0)
        def _():
            gather_first(1)
            gather_third(0)
            gather_last(0)

        pl.when(layer == 1)(lambda: gather_last(1))

        gain, shift, bias_out = (
            vector(first_gain, layer),
            vector(first_shift, layer),
            vector(b_out, layer),
        )
        bias_in = vector(b_in, layer)
        weight(2, layer).wait()
        weight(3, layer).wait()

        def feed_norm(b):
            rows = packed(b, SEG)
            for copy in heads_out(b):
                copy.wait()
            before = (
                inputs_low[layer, kept(b, SEG), :].astype(jnp.float32)
                + matmul(all_heads(b), w_all[layer])
                + bias_out
            )
            zhat, scale = normed(before)
            result = zhat * gain + shift
            own_a[rows, :] = result
            to_other(0, b, SEG, own_a).start()
            zhat_one[layer, rows, :] = zhat
            scale_one[layer, rows, :] = scale
            normed_low[layer, kept(b, SEG), :] = result.astype(jnp.bfloat16)

        def feed_main(b):
            spans = halves(b, SEG)
            normed_low[layer, given(b, SEG), :] = received(0, b, SEG, own_a)
            inputs = jnp.concatenate([normed_low[layer, rows, :] for rows in spans], axis=0)
            u = matmul(inputs, w_in[layer]) + bias_in
            g = (u * normal_cdf(u)).astype(jnp.bfloat16)
            lowered = matmul(g, w_down[layer])
            for side, rows in enumerate(spans):
                cut = slice(side * SEG, (side + 1) * SEG)
                part[rows, :] = lowered[cut]
                hidden[layer, rows, :] = u[cut]
                active[layer, rows, :] = g[cut]
            to_core(1, b, SEG).start()

        def feed(b):
            pl.when(b < BLOCKS)(lambda: feed_norm(b))
            pl.when(b >= 2)(lambda: send_y(1, b - 2, SEG))
            pl.when(b >= 1)(lambda: feed_main(b - 1))
            pl.when(jnp.logical_and(layer == 0, b == 1))(lambda: gather_second(1))

        repeat(BLOCKS + 1, feed)
        send_y(1, BLOCKS - 1, SEG)

        gain_two, shift_two, bias_down = (
            vector(second_gain, layer),
            vector(second_shift, layer),
            vector(b_down, layer),
        )
        pl.when(jnp.logical_not(last))(lambda: weight(0, layer + 1).wait())

        def receive(b):
            inputs_low[layer + 1, given(b, SEG), :] = received(1, b, SEG, own_b)
            pl.when(jnp.logical_not(last))(lambda: project(layer + 1, halves(b, SEG)))

            @pl.when(last)
            def _():
                dz_low[given(b, SEG), :] = received(0, b, SEG, own_a)

        def finish(b):
            rows = packed(b, SEG)
            before = own_a[rows, :] + summed(1, b, SEG) + bias_down
            zhat, scale = normed(before)
            result = zhat * gain_two + shift_two
            own_b[rows, :] = result
            to_other(1, b, SEG, own_b).start()
            zhat_two[layer, rows, :] = zhat
            scale_two[layer, rows, :] = scale
            inputs_low[layer + 1, kept(b, SEG), :] = result.astype(jnp.bfloat16)

            @pl.when(last)
            def _():
                live = columns[kept(b, SEG), 0:1]
                norm_two(0, b, SEG, cotangent[kept(b, SEG), :].astype(jnp.float32) * live)

            pl.when(b >= 1)(lambda: receive(b - 1))

        repeat(BLOCKS, finish)
        receive(BLOCKS - 1)
        pl.when(layer == 0)(lambda: gather_third(1))

    meet(barrier)
    gather_first(0)
    repeat(BACK_BLOCKS, first_input)
    weight(0, 0).wait()
    project(0, (block(0),))
    gather_second(0)
    repeat(BACK_BLOCKS - 1, lambda b: project(0, (block(b + 1),)))
    repeat(LAYERS, forward)

    def last_grad(b, grad):
        rows = kept(b, BACK_SEG)
        live = columns[rows, 0:1]
        masked_grad = grad * (1.0 - live)
        own_a[packed(b, BACK_SEG), :] = masked_grad
        to_other(0, b, BACK_SEG, own_a).start()
        grad_embeddings[rows, :] = masked_grad.astype(jnp.bfloat16)
        grads[small_base : small_base + REPL, :] = grads[
            small_base : small_base + REPL, :
        ] + lax.dot_general(
            chosen(rows, BACK_SEG),
            grad * live,
            (((0,), (0,)), ((), ())),
            precision=lax.Precision.HIGHEST,
            preferred_element_type=jnp.float32,
        )

    def backward(turn):
        layer = LAYERS - 1 - turn
        base = turn * span
        start = turn * (span // CHUNK)
        last = turn == LAYERS - 1
        in_base = base + hidden_width
        out_base = in_base + width
        qkv_base = out_base + head_width

        def rows_at(first, count):
            return pl.ds(pl.multiple_of(first, 16), count)

        def down_piece(p):
            grads[rows_at(base + 128 * p, 128), :] = contract_rows(
                active[layer, :, lanes(p)], dz_low[...]
            )

        def in_piece(p):
            grads[rows_at(in_base + 128 * p, 128), :] = contract_rows(
                normed_low[layer, :, lanes(p)], du_low[...]
            )

        down_piece(0)
        tick(start)

        def feed(b):
            rows = block(b)
            dg = contract_cols(dz_low[rows, :], w_down[layer])
            u = hidden[layer, rows, :]
            density = jnp.exp(u * u * (-0.5)) * (1.0 / math.sqrt(2.0 * math.pi))
            du = dg * (normal_cdf(u) + u * density)
            du_low[rows, :] = du.astype(jnp.bfloat16)
            local_sums[turn, 0:1, :] = local_sums[turn, 0:1, :] + jnp.sum(
                du, axis=0, keepdims=True
            )
            down_piece(b + 1)
            tick(start + 1 + b)

        repeat(BACK_BLOCKS, feed)
        down_piece(5)

        def feed_in(b):
            spans = halves(b, BACK_SEG)
            left = jnp.concatenate([du_low[rows, :] for rows in spans], axis=0)
            result = contract_cols(left, w_in[layer])
            for side, rows in enumerate(spans):
                part[rows, :] = result[side * BACK_SEG : (side + 1) * BACK_SEG]
            to_core(0, b, BACK_SEG).start()
            pl.when(b >= 1)(lambda: send_y(0, b - 1, BACK_SEG))
            tick(start + 5 + b)

        repeat(BACK_BLOCKS, feed_in)
        send_y(0, BACK_BLOCKS - 1, BACK_SEG)

        def early_piece(p):
            in_piece(p)
            tick(start + 9 + p)

        repeat(4, early_piece)
        in_piece(4)

        gain = vector(first_gain, layer)

        def norm_one(b):
            rows = packed(b, BACK_SEG)
            grad = own_a[rows, :] + summed(0, b, BACK_SEG)
            zhat = zhat_one[layer, rows, :]
            dz = norm_back(grad, zhat, scale_one[layer, rows, :], gain)
            own_b[rows, :] = dz
            to_other(1, b, BACK_SEG, own_b).start()
            dz_low[kept(b, BACK_SEG), :] = dz.astype(jnp.bfloat16)
            total_row(turn, 3, grad * zhat)
            total_row(turn, 4, grad)
            total_row(turn, 5, dz)
            tick(start + 13 + b)
            dz_low[given(b, BACK_SEG), :] = received(1, b, BACK_SEG, own_b)

        repeat(BACK_BLOCKS, norm_one)
        grads[rows_at(out_base, head_width), :] = contract_rows(heads[layer], dz_low[...])
        dheads[...] = contract_cols(dz_low[...], w_out[layer]).astype(jnp.bfloat16)
        in_piece(5)
        tick(start + 17)
        dkeys[...] = jnp.zeros_like(dkeys)
        dvalues[...] = jnp.zeros_like(dvalues)

        def attend(b):
            rows = block(b)
            for h in range(local_heads):
                side = HEAD_DIM * h
                query = queries[layer, h, rows, :]
                probs = jnp.exp(scores_of(layer, h, query) - log_total[layer, rows, h : h + 1])
                dhead = dheads[rows, side : side + HEAD_DIM]
                dprobs = contract_cols(dhead, values[layer, h])
                dvalues[h] = dvalues[h] + contract_rows(probs.astype(jnp.bfloat16), dhead)
                inner = jnp.sum(probs * dprobs, axis=-1, keepdims=True)
                ds = (probs * (dprobs - inner)).astype(jnp.bfloat16)
                dq = matmul(ds, keys[layer, h]) * SCALE
                dkeys[h] = dkeys[h] + contract_rows(ds, query)
                dqkv_low[rows, 3 * side : 3 * side + HEAD_DIM] = dq.astype(jnp.bfloat16)
                local_sums[turn, 1:2, 2 * side : 2 * side + HEAD_DIM] = local_sums[
                    turn, 1:2, 2 * side : 2 * side + HEAD_DIM
                ] + jnp.sum(dq, axis=0, keepdims=True)
            pl.when(b < BACK_BLOCKS - 1)(lambda: tick(start + 18 + b))

        repeat(BACK_BLOCKS, attend)
        for h in range(local_heads):
            side = HEAD_DIM * h
            dqkv_low[:, 3 * side + HEAD_DIM : 3 * side + 2 * HEAD_DIM] = (
                dkeys[h] * SCALE
            ).astype(jnp.bfloat16)
            dv = dvalues[h]
            dqkv_low[:, 3 * side + 2 * HEAD_DIM : 3 * side + 3 * HEAD_DIM] = dv.astype(
                jnp.bfloat16
            )
            local_sums[turn, 1:2, 2 * side + HEAD_DIM : 2 * side + 2 * HEAD_DIM] = jnp.sum(
                dv, axis=0, keepdims=True
            )

        def back_project(b):
            grads[rows_at(qkv_base + 128 * b, 128), :] = contract_rows(
                dqkv_low[:, lanes(b)], inputs_low[layer]
            )
            spans = halves(b, BACK_SEG)
            left = jnp.concatenate([dqkv_low[rows, :] for rows in spans], axis=0)
            result = matmul(left, w_qkv[layer])
            for side, rows in enumerate(spans):
                part[rows, :] = result[side * BACK_SEG : (side + 1) * BACK_SEG]
            to_core(1, b, BACK_SEG).start()
            pl.when(b >= 1)(lambda: send_y(1, b - 1, BACK_SEG))
            tick(start + 21 + b)

        repeat(BACK_BLOCKS, back_project)
        send_y(1, BACK_BLOCKS - 1, BACK_SEG)

        tail = jnp.where(last, HOLE, 0)
        grads[rows_at(qkv_base + 512 + tail, HEAD_DIM), :] = contract_rows(
            dqkv_low[:, 512:], inputs_low[layer]
        )
        tick(start + 25)

        def pass_on(b):
            rows = packed(b, BACK_SEG)
            grad = own_b[rows, :] + summed(1, b, BACK_SEG)
            pl.when(jnp.logical_not(last))(lambda: norm_two(turn + 1, b, BACK_SEG, grad))
            pl.when(last)(lambda: last_grad(b, grad))
            pl.when(jnp.logical_or(last, b < 2))(lambda: tick(start + 26 + b))

        repeat(BACK_BLOCKS, pass_on)

        def receive(b):
            dz_low[given(b, BACK_SEG), :] = received(0, b, BACK_SEG, own_a)

        pl.when(jnp.logical_not(last))(lambda: repeat(BACK_BLOCKS, receive))

    repeat(LAYERS, backward)
    hidden_out[...] = inputs_low[LAYERS]

    shared = REPL + 8 * LAYERS
    for turn in range(LAYERS):
        first = small_base + REPL + 8 * turn
        grads[first : first + 8, :] = sums[turn]
    grads[small_base + shared : small_base + shared + 8, :] = local_sums[...].reshape(8, width)
    short = remote(
        grads.at[pl.ds(small_base, shared)], land_small, small_send, small_recv, place.core_peer
    )
    short.start()

    def receive_grad(b):
        grad_embeddings[given(b, BACK_SEG), :] = received(0, b, BACK_SEG, own_a)

    repeat(BACK_BLOCKS, receive_grad)
    short.wait()
    grads[small_base : small_base + shared, :] = (
        grads[small_base : small_base + shared, :] + land_small[...]
    )
    done = chunks - 1
    repeat(grad_sum.ticks() - done, lambda i: tick(done + i))


def run_pages(args, sizes):
    width, hidden_width, local_heads, span = sizes
    rows = PAGE_LEN
    flat = LAYERS * span - HEAD_DIM + HOLE + 2 * CHUNK
    half = rows // 2
    low, full = jnp.bfloat16, jnp.float32
    vmem, dma = pltpu.VMEM, pltpu.SemaphoreType.DMA
    head_width = local_heads * HEAD_DIM
    return pl.pallas_call(
        functools.partial(page_kernel, sizes),
        name="pages",
        out_shape=(
            vmem((rows, width), low),
            vmem((rows, width), low),
            vmem((flat, width), full),
        ),
        in_specs=[
            pl.BlockSpec(memory_space=pl.ANY if index in WEIGHTS else pltpu.VMEM)
            for index in range(len(args))
        ],
        out_specs=(
            pl.BlockSpec(memory_space=pltpu.VMEM),
            pl.BlockSpec(memory_space=pltpu.VMEM),
            pl.BlockSpec(memory_space=pltpu.VMEM),
        ),
        scratch_shapes=[
            vmem((LAYERS + 1, rows, width), low),
            vmem((LAYERS, local_heads, rows, HEAD_DIM), low),
            vmem((LAYERS, local_heads, rows, HEAD_DIM), low),
            vmem((LAYERS, local_heads, rows, HEAD_DIM), low),
            vmem((LAYERS, rows, 128), full),
            vmem((LAYERS, rows, head_width), low),
            vmem((LAYERS, rows, width), low),
            vmem((LAYERS, rows, hidden_width), full),
            vmem((LAYERS, rows, hidden_width), low),
            vmem((LAYERS, half, width), full),
            vmem((LAYERS, half, 1), full),
            vmem((LAYERS, half, width), full),
            vmem((LAYERS, half, 1), full),
            vmem((LAYERS, 3 * head_width, width), low),
            vmem((LAYERS, head_width, width), low),
            vmem((LAYERS, width, hidden_width), low),
            vmem((LAYERS, hidden_width, width), low),
            vmem((LAYERS, 4 * head_width, width), low),
            vmem((5, BLOCKS, 3 * SEG // 2, 2 * HEAD_DIM), full),
            vmem((rows, 128), full),
            vmem((half, width), full),
            vmem((half, width), full),
            vmem((rows, width), full),
            vmem((2, half, width), full),
            vmem((2, half, width), full),
            vmem((2, half, width), full),
            vmem((REPL + 8 * LAYERS, width), full),
            vmem((rows, width), low),
            vmem((rows, hidden_width), low),
            vmem((rows, head_width), low),
            vmem((local_heads, rows, HEAD_DIM), full),
            vmem((local_heads, rows, HEAD_DIM), full),
            vmem((rows, 3 * head_width), low),
            vmem((LAYERS, 8, width), full),
            vmem((LAYERS, 4, width), full),
            vmem((len(WIDE_LANDINGS), SLOTS, WIDE, width), full),
            vmem((SLOTS, 2 * NARROW, width), full),
            vmem((len(NARROW_LANDINGS), SLOTS, NARROW, width), full),
            dma((2, BLOCKS)),
            dma((2, BLOCKS)),
            dma((2, BLOCKS)),
            dma((2, BLOCKS)),
            dma((2, BLOCKS)),
            dma((2, BLOCKS)),
            dma,
            dma,
            dma((KINDS, SLOTS)),
            dma((KINDS, SLOTS)),
            dma((4, LAYERS)),
            dma((4 * LAYERS,)),
            dma((4 * LAYERS,)),
            dma((LAYERS, GROUP)),
            dma((LAYERS, GROUP)),
            dma((3, BLOCKS)),
            dma((3, BLOCKS)),
        ],
        compiler_params=pltpu.CompilerParams(
            collective_id=0, has_side_effects=True, vmem_limit_bytes=46 << 20
        ),
    )(*args)


def place_kernel(sizes, hidden_out, grad_embeddings, every, *refs):
    width, hidden_width, local_heads, span = sizes
    head_width = local_heads * HEAD_DIM
    (
        out_hidden,
        out_embeddings,
        out_table,
        out_w_qkv,
        out_b_qv,
        out_w_out,
        out_b_out,
        out_first_gain,
        out_first_shift,
        out_w_in,
        out_b_in,
        out_w_down,
        out_b_down,
        out_second_gain,
        out_second_shift,
        short,
        sems,
    ) = refs
    tail = LAYERS * span - HEAD_DIM
    base = tail + HOLE + CHUNK
    pairs = [(every.at[pl.ds(base, CHUNK)], short), (every.at[pl.ds(base, REPL)], out_table)]
    pairs += [(hidden_out, out_hidden), (grad_embeddings, out_embeddings)]
    for turn in range(LAYERS):
        first = span * turn
        for ref, rows in (
            (out_w_down, hidden_width),
            (out_w_in, width),
            (out_w_out, head_width),
            (out_w_qkv, 3 * head_width),
        ):
            target = ref.at[LAYERS - 1 - turn]
            direct = min(rows, tail - first)
            pairs.append((every.at[pl.ds(first, direct)], target.at[pl.ds(0, direct)]))
            if direct < rows:
                pairs.append(
                    (
                        every.at[pl.ds(tail + HOLE, rows - direct)],
                        target.at[pl.ds(direct, rows - direct)],
                    )
                )
            first += rows
    copies = [
        pltpu.make_async_copy(source, target, sems.at[index])
        for index, (source, target) in enumerate(pairs)
    ]
    for copy in copies:
        copy.start()
    copies[0].wait()
    local = REPL + 8 * LAYERS
    for ref, row, step in (
        (out_second_gain, REPL, 8),
        (out_second_shift, REPL + 1, 8),
        (out_b_down, REPL + 2, 8),
        (out_first_gain, REPL + 3, 8),
        (out_first_shift, REPL + 4, 8),
        (out_b_out, REPL + 5, 8),
        (out_b_in, local, 4),
        (out_b_qv, local + 1, 4),
    ):
        for turn in range(LAYERS):
            layer = LAYERS - 1 - turn
            ref[layer : layer + 1, :] = short[
                row + step * turn : row + step * turn + 1, : ref.shape[1]
            ]
    for copy in copies[1:]:
        copy.wait()


def place_outputs(hidden_out, grad_embeddings, every, sizes):
    width, hidden_width, local_heads, span = sizes
    head_width = local_heads * HEAD_DIM
    low, full = jnp.bfloat16, jnp.float32
    rows = hidden_out.shape[0]
    shapes = (
        ((rows, width), low),
        ((rows, width), low),
        ((REPL, width), full),
        ((LAYERS, 3 * head_width, width), full),
        ((LAYERS, 2 * head_width), full),
        ((LAYERS, head_width, width), full),
        ((LAYERS, width), full),
        ((LAYERS, width), full),
        ((LAYERS, width), full),
        ((LAYERS, width, hidden_width), full),
        ((LAYERS, hidden_width), full),
        ((LAYERS, hidden_width, width), full),
        ((LAYERS, width), full),
        ((LAYERS, width), full),
        ((LAYERS, width), full),
    )
    far = pl.BlockSpec(memory_space=pl.ANY)
    close = pl.BlockSpec(memory_space=pltpu.VMEM)
    return pl.pallas_call(
        functools.partial(place_kernel, sizes),
        name="place_outputs",
        out_shape=[jax.ShapeDtypeStruct(shape, kind) for shape, kind in shapes],
        in_specs=[far] * 3,
        out_specs=[close if shape[0] == LAYERS and len(shape) == 2 else far for shape, _ in shapes],
        scratch_shapes=[
            pltpu.VMEM((CHUNK, width), full),
            pltpu.SemaphoreType.DMA((5 + 4 * LAYERS,)),
        ],
        compiler_params=pltpu.CompilerParams(vmem_limit_bytes=4 << 20),
    )(hidden_out, grad_embeddings, every)


def moved(every):
    def kernel(source, target, sem):
        copy = pltpu.make_async_copy(source, target, sem)
        copy.start()
        copy.wait()

    far = pl.BlockSpec(memory_space=pl.ANY)
    return pl.pallas_call(
        kernel,
        name="moved",
        out_shape=jax.ShapeDtypeStruct(every.shape, every.dtype),
        in_specs=[far],
        out_specs=far,
        scratch_shapes=[pltpu.SemaphoreType.DMA],
        compiler_params=pltpu.CompilerParams(vmem_limit_bytes=4 << 20),
    )(every)


def on_device(*args):
    (embeddings, replace_table, replace_ids, masked, padding, w_qkv, b_qv, *_) = args
    width = embeddings.shape[1]
    head_width = w_qkv.shape[2] // 3
    hidden_width = args[11].shape[2]
    span = 2 * hidden_width + 4 * head_width
    args = list(args)
    args[5] = jnp.swapaxes(args[5], 1, 2)
    for index in (2, 3, 4):
        args[index] = args[index].reshape(1, PAGE_LEN)
    sizes = (width, hidden_width, head_width // HEAD_DIM, span)
    hidden_out, grad_embeddings, every = run_pages(args, sizes)
    groups = lax.axis_size("dp") // GROUP
    if groups > 1:
        every = lax.psum(
            moved(every),
            "dp",
            axis_index_groups=[
                [low + GROUP * high for high in range(groups)] for low in range(GROUP)
            ],
        )

    results = place_outputs(hidden_out, grad_embeddings, every, sizes)
    return (*results[:3], jnp.swapaxes(results[3], 1, 2), *results[4:])


def solution(mesh):
    placed = (
        P("dp", None),
        P(),
        P("dp"),
        P("dp"),
        P("dp"),
        P(None, None, "tensor"),
        P(None, "tensor"),
        P(None, "tensor", None),
        P(),
        P(),
        P(),
        P(None, None, "tensor"),
        P(None, "tensor"),
        P(None, "tensor", None),
        P(),
        P(),
        P(),
        P("dp", None),
    )
    return jax.shard_map(
        on_device,
        mesh=mesh,
        in_specs=placed,
        out_specs=(
            P("dp", None),
            P("dp", None),
            P(),
            P(None, None, "tensor"),
            P(None, "tensor"),
            P(None, "tensor", None),
            P(),
            P(),
            P(),
            P(None, None, "tensor"),
            P(None, "tensor"),
            P(None, "tensor", None),
            P(),
            P(),
            P(),
        ),
        check_vma=False,
    )
```

```python
import functools
import math

import jax
import jax.numpy as jnp
from jax import lax
from jax.experimental import pallas as pl
from jax.experimental.pallas import tpu as pltpu
from jax.sharding import PartitionSpec as P

HEAD_DIM = 64
LAYERS = 2
PAGE_LEN = 512
REPL = 32
EPSILON = 1e-12
SCALE = HEAD_DIM ** (-0.5)
MESH = pl.DeviceIdType.MESH

HALF = PAGE_LEN // 2
SEG = 64
BLOCKS = HALF // SEG
BACK_SEG = 64
BACK_BLOCKS = HALF // BACK_SEG
BLOCK = 2 * BACK_SEG

WIDE = 24
NARROW = 8
CHUNK = 2 * WIDE + 4 * NARROW
HOLE = 2 * NARROW
SHORT_CHUNKS = 3
LAG = 2
SLOTS = 4 * LAG
EQUAL_SLOTS = 2 * LAG
EQUALS = (TX, TA2, TQ1, TQ2, TR1, TR3, TTM, TG, TR5) = range(9)
ONE_WAY = (TA1, TTA, TQ0, TR0, TR2, TTN, TTF, TR4, TR6) = range(9, 18)
WIDE_LANDINGS = (TX, TA1, TA2, TTA)
NARROW_LANDINGS = (TQ1, TQ2, TR0, TR1, TR2, TR3)
GROUP = 8
ARGS = 18
WEIGHTS = (5, 7, 11, 13)
SHORT_ARGS = tuple(index for index in range(1, ARGS - 1) if index not in WEIGHTS)
DIRECT = (64, 0)


def contract_rows(left, right):
    return lax.dot_general(
        left, right, (((0,), (0,)), ((), ())), preferred_element_type=jnp.float32
    )


def contract_cols(left, right):
    return lax.dot_general(
        left, right, (((1,), (1,)), ((), ())), preferred_element_type=jnp.float32
    )


def matmul(left, right):
    return jnp.dot(left, right, preferred_element_type=jnp.float32)


def repeat(count, body):
    def step(index, carry):
        body(index)
        return carry

    lax.fori_loop(0, count, step, 0)


def normed(values):
    average = jnp.mean(values, axis=-1, keepdims=True)
    centered = values - average
    variance = jnp.mean(centered * centered, axis=-1, keepdims=True)
    scale = lax.rsqrt(variance + EPSILON)
    return centered * scale, scale


def norm_back(grad, zhat, scale, gain):
    scaled = grad * gain
    average = jnp.mean(scaled, axis=-1, keepdims=True)
    along = jnp.mean(scaled * zhat, axis=-1, keepdims=True)
    return scale * (scaled - average - zhat * along)


def normal_cdf(values):
    return 0.5 * (1.0 + lax.erf(values * math.sqrt(0.5)))


def column(row):
    return jnp.transpose(jnp.broadcast_to(row, (128, row.shape[1])))[:, :1]


class Place:
    def __init__(self):
        d = lax.axis_index("dp")
        t = lax.axis_index("tensor")
        self.core = lax.rem(t, 2)
        self.core_peer = (d, t + 1 - 2 * self.core)
        self.y_peer = (d, t + 2 - 4 * lax.div(t, 2))
        self.diagonal = (d, t + 3 - 2 * self.core - 4 * lax.div(t, 2))
        self.y = lax.div(t, 2)
        self.low = lax.rem(d, GROUP)
        self.others = [
            (d - self.low + lax.rem(self.low + k, GROUP), t) for k in range(1, GROUP)
        ]
        pair = lax.rem(d, 2)
        line = lax.rem(lax.div(d, 2), 4)
        self.pair = pair
        self.mid = jnp.logical_or(line == 1, line == 2)
        self.end = jnp.logical_not(self.mid)
        self.upper = lax.div(line, 2)
        self.peer = (d + 1 - 2 * pair, t)
        self.line = (d + 2 - 4 * lax.rem(line, 2), t)
        self.cross = (jnp.where(line == 1, d + 2, d - 2), t)


def greet(place, barrier):
    def signal(device):
        pl.semaphore_signal(barrier, inc=1, device_id=device, device_id_type=MESH)

    for device in (place.core_peer, place.y_peer, place.diagonal, *place.others):
        signal(device)


def meet(barrier):
    pl.semaphore_wait(barrier, 2 + GROUP)


class GradientSum:
    def __init__(self, place, chunks, part, wide, both, narrow, send, recv, one_way):
        self.place = place
        self.chunks = chunks
        self.part = part
        self.wide = wide
        self.both = both
        self.narrow = narrow
        self.send = send
        self.recv = recv
        self.one_way = one_way

    def wide_rows(self, j, unit):
        return pl.ds(pl.multiple_of(j * CHUNK + unit * WIDE, NARROW), WIDE)

    def narrow_rows(self, j, unit, count=1):
        first = j * CHUNK + 2 * WIDE + unit * NARROW
        return pl.ds(pl.multiple_of(first, NARROW), count * NARROW)

    def tick(self, t):
        place, part = self.place, self.part
        mine, other = place.pair, 1 - place.pair
        near, far = place.upper, 1 - place.upper
        near_end, far_end = 2 + place.upper, 3 - place.upper

        def copy(kind, j, rows, target, device):
            if kind in EQUALS:
                slot = lax.rem(j, EQUAL_SLOTS)
                send, recv = self.send.at[kind, slot], self.recv.at[kind, slot]
            else:
                send = recv = self.one_way.at[kind - len(EQUALS), lax.rem(j, SLOTS)]
            return pltpu.make_async_remote_copy(
                src_ref=part.at[rows],
                dst_ref=target,
                send_sem=send,
                recv_sem=recv,
                device_id=device,
                device_id_type=MESH,
            )

        def wide_slot(kind, j):
            return WIDE_LANDINGS.index(kind), lax.rem(j, SLOTS)

        def narrow_slot(kind, j):
            return NARROW_LANDINGS.index(kind), lax.rem(j, SLOTS)

        def wide_part(kind, j, unit, device):
            return copy(
                kind, j, self.wide_rows(j, unit), self.wide.at[wide_slot(kind, j)], device
            )

        def narrow_part(kind, j, unit, device):
            return copy(
                kind, j, self.narrow_rows(j, unit), self.narrow.at[narrow_slot(kind, j)], device
            )

        def final(kind, j, rows, device):
            return copy(kind, j, rows, part.at[rows], device)

        def add_wide(kind, j, unit):
            rows = self.wide_rows(j, unit)
            part[rows, :] = part[rows, :] + self.wide[wide_slot(kind, j)]

        def add_narrow(kind, j, unit):
            rows = self.narrow_rows(j, unit)
            part[rows, :] = part[rows, :] + self.narrow[narrow_slot(kind, j)]

        def pair_first(j):
            return wide_part(TX, j, other, place.peer)

        def mine_in(j):
            return wide_part(TA1, j, mine, place.line)

        def mine_across(j):
            return wide_part(TA2, j, mine, place.cross)

        def mine_out(j):
            return wide_part(TTA, j, mine, place.line)

        def pair_last(j):
            return final(TG, j, self.wide_rows(j, mine), place.peer)

        def both_in(j):
            rows = self.narrow_rows(j, 0, 2)
            return copy(TQ0, j, rows, self.both.at[lax.rem(j, SLOTS)], place.line)

        def far_across(j):
            return narrow_part(TQ1, j, far, place.cross)

        def near_pair(j):
            return narrow_part(TQ2, j, near, place.peer)

        def near_out(j):
            return final(TTN, j, self.narrow_rows(j, near), place.line)

        def near_across(j):
            return final(TTM, j, self.narrow_rows(j, near), place.cross)

        def far_out(j):
            return final(TTF, j, self.narrow_rows(j, far), place.line)

        def end_in(j):
            return narrow_part(TR0, j, far_end, place.line)

        def end_across(j):
            return narrow_part(TR1, j, far_end, place.cross)

        def end_up(j):
            return narrow_part(TR2, j, near_end, place.line)

        def end_pair(j):
            return narrow_part(TR3, j, near_end, place.peer)

        def end_down(j):
            return final(TR4, j, self.narrow_rows(j, near_end), place.line)

        def end_back(j):
            return final(TR5, j, self.narrow_rows(j, near_end), place.cross)

        def end_out(j):
            return final(TR6, j, self.narrow_rows(j, far_end), place.line)

        def ended(j, body):
            pl.when(j < self.chunks - SHORT_CHUNKS)(body)

        def stage_0(j):
            pair_first(j).start()

            @pl.when(place.end)
            def _():
                ended(j, lambda: end_in(j).start())
                both_in(j).start()

        def stage_1(j):
            pair_first(j).wait()

            @pl.when(place.end)
            def _():
                both_in(j).wait_send()
                ended(j, lambda: end_in(j).wait_send())
                add_wide(TX, j, mine)
                mine_in(j).start()

            @pl.when(place.mid)
            def _():
                def onward():
                    end_in(j).wait_recv()
                    add_narrow(TR0, j, far_end)
                    end_across(j).start()

                ended(j, onward)
                both_in(j).wait_recv()
                rows = self.narrow_rows(j, 0, 2)
                part[rows, :] = part[rows, :] + self.both[lax.rem(j, SLOTS)]
                far_across(j).start()
                add_wide(TX, j, mine)

        def stage_2(j):
            @pl.when(place.end)
            def _():
                mine_in(j).wait_send()

            @pl.when(place.mid)
            def _():
                mine_in(j).wait_recv()
                far_across(j).wait()

                def onward():
                    end_across(j).wait()
                    add_narrow(TR1, j, near_end)
                    end_up(j).start()

                ended(j, onward)
                add_narrow(TQ1, j, near)
                near_pair(j).start()
                add_wide(TA1, j, mine)
                mine_across(j).start()

        def stage_3(j):
            @pl.when(place.end)
            def _():
                def onward():
                    end_up(j).wait_recv()
                    add_narrow(TR2, j, near_end)
                    end_pair(j).start()

                ended(j, onward)

            @pl.when(place.mid)
            def _():
                ended(j, lambda: end_up(j).wait_send())
                mine_across(j).wait()
                near_pair(j).wait()
                add_narrow(TQ2, j, near)
                near_across(j).start()
                near_out(j).start()
                add_wide(TA2, j, mine)
                mine_out(j).start()

        def stage_4(j):
            @pl.when(place.mid)
            def _():
                near_across(j).wait()
                far_out(j).start()
                near_out(j).wait_send()
                mine_out(j).wait_send()
                pair_last(j).start()

            @pl.when(place.end)
            def _():
                mine_out(j).wait_recv()
                near_out(j).wait_recv()

                def onward():
                    end_pair(j).wait()
                    add_narrow(TR3, j, near_end)
                    end_down(j).start()

                ended(j, onward)
                part[self.wide_rows(j, mine), :] = self.wide[wide_slot(TTA, j)]
                pair_last(j).start()

        def stage_5(j):
            @pl.when(place.mid)
            def _():
                def onward():
                    end_down(j).wait_recv()
                    end_back(j).start()

                ended(j, onward)
                far_out(j).wait_send()

            @pl.when(place.end)
            def _():
                ended(j, lambda: end_down(j).wait_send())
                far_out(j).wait_recv()

            pair_last(j).wait()

        def stage_6(j):
            @pl.when(place.mid)
            def _():
                def onward():
                    end_back(j).wait()
                    end_out(j).start()

                ended(j, onward)

        def stage_7(j):
            pl.when(place.mid)(lambda: ended(j, lambda: end_out(j).wait_send()))
            pl.when(place.end)(lambda: ended(j, lambda: end_out(j).wait_recv()))

        stages = (stage_0, stage_1, stage_2, stage_3, stage_4, stage_5, stage_6, stage_7)
        for number in reversed(range(len(stages))):
            j = t - number * LAG
            pl.when(jnp.logical_and(j >= 0, j < self.chunks))(
                functools.partial(stages[number], j)
            )

    def ticks(self):
        return self.chunks + max(5 * LAG, 7 * LAG - SHORT_CHUNKS)


def page_kernel(sizes, *refs):
    far, refs = refs[:ARGS], refs[ARGS:]
    (hidden_out, grad_embeddings, grads), refs = refs[:3], refs[3:]
    close, refs = refs[:ARGS], refs[ARGS:]
    (
        embeddings,
        replace_table,
        replace_ids,
        masked,
        padding,
        w_qkv,
        b_qv,
        w_out,
        b_out,
        first_gain,
        first_shift,
        w_in,
        b_in,
        w_down,
        b_down,
        second_gain,
        second_shift,
        cotangent,
    ) = close
    (
        inputs_low,
        queries,
        keys,
        values,
        log_total,
        heads,
        normed_low,
        hidden,
        active,
        zhat_one,
        scale_one,
        zhat_two,
        scale_two,
        w_all,
        shared_heads,
        columns,
        own_a,
        own_b,
        part,
        land_core,
        land_y,
        land_back,
        land_small,
        dz_low,
        du_low,
        dheads,
        dkeys,
        dvalues,
        dqkv_low,
        sums,
        local_sums,
        land_wide,
        land_both,
        land_narrow,
        core_send,
        core_recv,
        y_send,
        y_recv,
        back_send,
        back_recv,
        small_send,
        small_recv,
        dp_send,
        dp_recv,
        dp_one_way,
        gather_send,
        gather_recv,
        hand_send,
        hand_recv,
        heads_send,
        heads_recv,
        close_sem,
    ) = refs
    width, hidden_width, local_heads, span = sizes
    head_width = local_heads * HEAD_DIM
    place = Place()
    core = place.core
    barrier = pltpu.get_barrier_semaphore()
    greet(place, barrier)

    def fetch(index):
        return pltpu.make_async_copy(far[index], close[index], close_sem.at[index, 0])

    def weight(which, layer):
        index = WEIGHTS[which]
        return pltpu.make_async_copy(
            far[index].at[layer], close[index].at[layer], close_sem.at[index, layer]
        )

    weight(1, 0).start()
    fetch(0).start()
    weight(0, 0).start()
    for index in SHORT_ARGS:
        fetch(index).start()
    tail_base = LAYERS * span - HEAD_DIM + HOLE
    small_base = tail_base + CHUNK
    assert tail_base % CHUNK == 0 and span % HEAD_DIM == 0
    chunks = grads.shape[0] // CHUNK
    grad_sum = GradientSum(place, chunks, grads, land_wide, land_both, land_narrow, dp_send, dp_recv, dp_one_way)
    tick = grad_sum.tick

    def vector(ref, layer):
        both = ref[...].astype(jnp.float32)
        return jnp.where(layer == 0, both[0:1], both[1:2])

    def block(b):
        return pl.ds(pl.multiple_of(b * BLOCK, BLOCK), BLOCK)

    def segment(b, size, half):
        return pl.ds(pl.multiple_of(half * HALF + b * size, size), size)

    def kept(b, size):
        return segment(b, size, core)

    def given(b, size):
        return segment(b, size, 1 - core)

    def packed(b, size):
        return segment(b, size, 0)

    def halves(b, size):
        return segment(b, size, 0), segment(b, size, 1)

    def lanes(p, size=128):
        return pl.ds(pl.multiple_of(p * size, size), size)

    def remote(source, target, send, recv, device):
        return pltpu.make_async_remote_copy(
            src_ref=source,
            dst_ref=target,
            send_sem=send,
            recv_sem=recv,
            device_id=device,
            device_id_type=MESH,
        )

    def to_core(turn, b, size):
        return remote(
            part.at[given(b, size)],
            land_core.at[turn, packed(b, size)],
            core_send.at[turn, b],
            core_recv.at[turn, b],
            place.core_peer,
        )

    def over_y(turn, b, size):
        return remote(
            part.at[kept(b, size)],
            land_y.at[turn, packed(b, size)],
            y_send.at[turn, b],
            y_recv.at[turn, b],
            place.y_peer,
        )

    def to_other(turn, b, size, source):
        return remote(
            source.at[packed(b, size)],
            land_back.at[turn, packed(b, size)],
            back_send.at[turn, b],
            back_recv.at[turn, b],
            place.core_peer,
        )

    def send_y(turn, b, size):
        to_core(turn, b, size).wait()
        rows = kept(b, size)
        part[rows, :] = part[rows, :] + land_core[turn, packed(b, size), :]
        over_y(turn, b, size).start()

    def summed(turn, b, size):
        over_y(turn, b, size).wait()
        return part[kept(b, size), :] + land_y[turn, packed(b, size), :]

    def received(turn, b, size, source):
        to_other(turn, b, size, source).wait()
        return land_back[turn, packed(b, size), :].astype(jnp.bfloat16)

    def shard(which, layer):
        return (which * LAYERS + layer) * head_width

    def direct(layer):
        return pl.ds(shard(0, layer), DIRECT[layer]), pl.ds(shard(2, layer), DIRECT[layer])

    def piece_rows(which, layer, owner):
        size = (head_width - DIRECT[layer]) // GROUP
        first = shard(which, layer) + DIRECT[layer] + owner * size
        return pl.ds(pl.multiple_of(first, 8), size)

    def moving(source, target, index, device):
        return remote(
            grads.at[source], grads.at[target], gather_send.at[index], gather_recv.at[index], device
        )

    def whole(which, layer):
        return pl.ds(shard(which, layer), head_width)

    def own_shard(layer):
        return moving(whole(0, layer), whole(1, layer), layer, place.core_peer)

    def other_shard(layer):
        return moving(whole(2, layer), whole(3, layer), LAYERS + layer, place.core_peer)

    def piece_over(layer):
        return moving(
            piece_rows(0, layer, place.low),
            piece_rows(2, layer, place.low),
            2 * LAYERS + layer,
            place.y_peer,
        )

    def rest_over(layer):
        return moving(*direct(layer), 3 * LAYERS + layer, place.y_peer)

    def handed(layer, k):
        rows = piece_rows(2, layer, place.low)
        return pltpu.make_async_remote_copy(
            src_ref=grads.at[rows],
            dst_ref=grads.at[rows],
            send_sem=hand_send.at[layer, k],
            recv_sem=hand_recv.at[layer, place.low],
            device_id=place.others[k],
            device_id_type=MESH,
        )

    def handed_in(layer, k):
        owner = lax.rem(place.low + 1 + k, GROUP)
        rows = piece_rows(2, layer, owner)
        return pltpu.make_async_remote_copy(
            src_ref=grads.at[rows],
            dst_ref=grads.at[rows],
            send_sem=hand_send.at[layer, k],
            recv_sem=hand_recv.at[layer, owner],
            device_id=place.others[k],
            device_id_type=MESH,
        )

    def gather_first(layer):
        weight(1, layer).wait()
        grads[whole(0, layer), :] = w_out[layer].astype(jnp.float32)
        piece_over(layer).start()
        if DIRECT[layer]:
            rest_over(layer).start()
        own_shard(layer).start()

    def gather_second(layer):
        piece_over(layer).wait()
        for k in range(GROUP - 1):
            handed(layer, k).start()

    def gather_third(layer):
        for k in range(GROUP - 1):
            handed(layer, k).wait_send()
            handed_in(layer, k).wait_recv()
        if DIRECT[layer]:
            rest_over(layer).wait()
        other_shard(layer).start()

    def gather_last(layer):
        own_shard(layer).wait()
        other_shard(layer).wait()
        pairs_width = 2 * HEAD_DIM
        for which in range(4):
            source = which // 2
            owner = 2 * (place.y + source - 2 * place.y * source) + (
                core + which % 2 - 2 * core * (which % 2)
            )
            low = grads[whole(which, layer), :].astype(jnp.bfloat16)
            first = pl.multiple_of(owner * pairs_width, pairs_width)
            w_all[layer, pl.ds(first, pairs_width), :] = low[:pairs_width]
            first = pl.multiple_of(4 * pairs_width + owner * HEAD_DIM, HEAD_DIM)
            w_all[layer, pl.ds(first, HEAD_DIM), :] = low[pairs_width:]

    def heads_out(b):
        mine, theirs = shared_heads.at[core, b], shared_heads.at[1 - core, b]
        return [
            remote(
                source,
                shared_heads.at[2 + index, b],
                heads_send.at[index, b],
                heads_recv.at[index, b],
                device,
            )
            for index, (source, device) in enumerate(
                (
                    (theirs, place.core_peer),
                    (mine, place.y_peer),
                    (theirs, place.diagonal),
                )
            )
        ]

    def pack_heads(rows):
        cut = 2 * HEAD_DIM
        return jnp.concatenate(
            [
                rows[:, :cut],
                jnp.concatenate([rows[: SEG // 2, cut:], rows[SEG // 2 :, cut:]], axis=1),
            ],
            axis=0,
        )

    def all_heads(b):
        pairs, thirds = [], []
        for owner in range(4):
            side, half = owner // 2, owner % 2
            apart = 2 * (place.y + side - 2 * place.y * side) + (core + half - 2 * core * half)
            slot = jnp.where(apart == 0, core, apart + 1)
            low = shared_heads[slot, b].astype(jnp.bfloat16)
            pairs.append(low[:SEG])
            tail = low[SEG:]
            thirds.append(jnp.concatenate([tail[:, :HEAD_DIM], tail[:, HEAD_DIM:]], axis=0))
        return jnp.concatenate(pairs + thirds, axis=1)

    meet(barrier)
    gather_first(0)

    for index in SHORT_ARGS:
        fetch(index).wait()
    pad_row = padding[...].astype(jnp.float32)
    live_row = masked[...].astype(jnp.float32) * pad_row
    bias_row = (pad_row - 1.0) * 10000.0
    columns[:, 0:1] = column(live_row)
    columns[:, 1:2] = column(replace_ids[...].astype(jnp.float32))
    grads[small_base:, :] = jnp.zeros((CHUNK, width), jnp.float32)

    def chosen(rows, count):
        spots = lax.broadcasted_iota(jnp.int32, (count, REPL), 1).astype(jnp.float32)
        return jnp.where(columns[rows, 1:2] == spots, 1.0, 0.0)

    def first_input(b):
        rows = block(b)
        picked = matmul(chosen(rows, BLOCK).astype(jnp.bfloat16), replace_table[...])
        taken = jnp.where(
            columns[rows, 0:1] > 0.0, picked, embeddings[rows, :].astype(jnp.float32)
        )
        inputs_low[0, rows, :] = taken.astype(jnp.bfloat16)

    sums[...] = jnp.zeros_like(sums)
    local_sums[...] = jnp.zeros_like(local_sums)

    def project(layer, spans):
        bias_pair = vector(b_qv, layer)
        inputs = jnp.concatenate([inputs_low[layer, rows, :] for rows in spans], axis=0)
        projected = contract_cols(inputs, w_qkv[layer])

        def split(ref, h, columns_of):
            low = columns_of.astype(jnp.bfloat16)
            first = 0
            for rows in spans:
                ref[layer, h, rows, :] = low[first : first + rows.size]
                first += rows.size

        for h in range(local_heads):
            base = 3 * HEAD_DIM * h
            bias = 2 * HEAD_DIM * h
            split(
                queries,
                h,
                projected[:, base : base + HEAD_DIM] + bias_pair[:, bias : bias + HEAD_DIM],
            )
            split(keys, h, projected[:, base + HEAD_DIM : base + 2 * HEAD_DIM])
            split(
                values,
                h,
                projected[:, base + 2 * HEAD_DIM : base + 3 * HEAD_DIM]
                + bias_pair[:, bias + HEAD_DIM : bias + 2 * HEAD_DIM],
            )

    def scores_of(layer, h, query):
        return contract_cols(query, keys[layer, h]) * SCALE + bias_row

    def total_row(turn, index, amount):
        sums[turn, index : index + 1, :] = sums[turn, index : index + 1, :] + jnp.sum(
            amount, axis=0, keepdims=True
        )

    def norm_two(turn, b, size, grad):
        layer = LAYERS - 1 - turn
        rows = packed(b, size)
        zhat = zhat_two[layer, rows, :]
        dz = norm_back(grad, zhat, scale_two[layer, rows, :], vector(second_gain, layer))
        own_a[rows, :] = dz
        to_other(0, b, size, own_a).start()
        dz_low[kept(b, size), :] = dz.astype(jnp.bfloat16)
        total_row(turn, 0, grad * zhat)
        total_row(turn, 1, grad)
        total_row(turn, 2, dz)

    def forward(layer):
        last = layer == LAYERS - 1

        def attend(b):
            pl.when(jnp.logical_and(layer == 0, b == BLOCKS - 1))(lambda: gather_third(0))
            spans = halves(b, SEG)
            outs, logs = [], []
            for h in range(local_heads):
                query = jnp.concatenate([queries[layer, h, rows, :] for rows in spans], axis=0)
                scores = scores_of(layer, h, query)
                largest = jnp.max(scores, axis=-1, keepdims=True)
                weights_of = jnp.exp(scores - largest)
                totals = jnp.sum(weights_of, axis=-1, keepdims=True)
                probs = (weights_of * (1.0 / totals)).astype(jnp.bfloat16)
                outs.append(matmul(probs, values[layer, h]).astype(jnp.bfloat16))
                logs.append(largest + jnp.log(totals))
            joined = jnp.concatenate(outs, axis=1)
            full = joined.astype(jnp.float32)
            for side in range(2):
                shared_heads[side, b] = pack_heads(full[side * SEG : (side + 1) * SEG])
            for copy in heads_out(b):
                copy.start()
            for side, rows in enumerate(spans):
                cut = slice(side * SEG, (side + 1) * SEG)
                heads[layer, rows, :] = joined[cut]
                for h in range(local_heads):
                    log_total[layer, rows, h : h + 1] = logs[h][cut]

        repeat(BLOCKS, attend)

        @pl.when(layer == 0)
        def _():
            gather_first(1)
            gather_last(0)

        pl.when(layer == 1)(lambda: gather_last(1))

        gain, shift, bias_out = (
            vector(first_gain, layer),
            vector(first_shift, layer),
            vector(b_out, layer),
        )
        bias_in = vector(b_in, layer)
        weight(2, layer).wait()
        weight(3, layer).wait()

        def feed_norm(b):
            rows = packed(b, SEG)
            for copy in heads_out(b):
                copy.wait()
            before = (
                inputs_low[layer, kept(b, SEG), :].astype(jnp.float32)
                + matmul(all_heads(b), w_all[layer])
                + bias_out
            )
            zhat, scale = normed(before)
            result = zhat * gain + shift
            own_a[rows, :] = result
            to_other(0, b, SEG, own_a).start()
            zhat_one[layer, rows, :] = zhat
            scale_one[layer, rows, :] = scale
            normed_low[layer, kept(b, SEG), :] = result.astype(jnp.bfloat16)

        def feed_main(b):
            spans = halves(b, SEG)
            normed_low[layer, given(b, SEG), :] = received(0, b, SEG, own_a)
            inputs = jnp.concatenate([normed_low[layer, rows, :] for rows in spans], axis=0)
            u = matmul(inputs, w_in[layer]) + bias_in
            g = (u * normal_cdf(u)).astype(jnp.bfloat16)
            lowered = matmul(g, w_down[layer])
            for side, rows in enumerate(spans):
                cut = slice(side * SEG, (side + 1) * SEG)
                part[rows, :] = lowered[cut]
                hidden[layer, rows, :] = u[cut]
                active[layer, rows, :] = g[cut]
            to_core(1, b, SEG).start()

        def feed(b):
            feed_norm(b)
            pl.when(b >= 1)(lambda: send_y(1, b - 1, SEG))
            feed_main(b)
            pl.when(jnp.logical_and(layer == 0, b == 0))(lambda: gather_second(1))

        repeat(BLOCKS, feed)
        send_y(1, BLOCKS - 1, SEG)

        gain_two, shift_two, bias_down = (
            vector(second_gain, layer),
            vector(second_shift, layer),
            vector(b_down, layer),
        )
        pl.when(jnp.logical_not(last))(lambda: weight(0, layer + 1).wait())

        def receive(b):
            inputs_low[layer + 1, given(b, SEG), :] = received(1, b, SEG, own_b)
            pl.when(jnp.logical_not(last))(lambda: project(layer + 1, halves(b, SEG)))

            @pl.when(last)
            def _():
                dz_low[given(b, SEG), :] = received(0, b, SEG, own_a)

        def finish(b):
            rows = packed(b, SEG)
            before = own_a[rows, :] + summed(1, b, SEG) + bias_down
            zhat, scale = normed(before)
            result = zhat * gain_two + shift_two
            own_b[rows, :] = result
            to_other(1, b, SEG, own_b).start()
            zhat_two[layer, rows, :] = zhat
            scale_two[layer, rows, :] = scale
            inputs_low[layer + 1, kept(b, SEG), :] = result.astype(jnp.bfloat16)

            @pl.when(last)
            def _():
                live = columns[kept(b, SEG), 0:1]
                norm_two(0, b, SEG, cotangent[kept(b, SEG), :].astype(jnp.float32) * live)

            pl.when(b >= 1)(lambda: receive(b - 1))

        repeat(BLOCKS, finish)
        receive(BLOCKS - 1)
        pl.when(layer == 0)(lambda: gather_third(1))

    fetch(0).wait()
    repeat(BACK_BLOCKS, first_input)
    fetch(ARGS - 1).start()
    for index, layer in ((1, 1), (2, 0), (3, 0), (0, 1), (2, 1), (3, 1)):
        weight(index, layer).start()
    weight(0, 0).wait()
    project(0, (block(0),))
    gather_second(0)
    repeat(BACK_BLOCKS - 1, lambda b: project(0, (block(b + 1),)))
    fetch(ARGS - 1).wait()
    repeat(LAYERS, forward)

    def last_grad(b, grad):
        rows = kept(b, BACK_SEG)
        live = columns[rows, 0:1]
        masked_grad = grad * (1.0 - live)
        own_a[packed(b, BACK_SEG), :] = masked_grad
        to_other(0, b, BACK_SEG, own_a).start()
        grad_embeddings[rows, :] = masked_grad.astype(jnp.bfloat16)
        grads[small_base : small_base + REPL, :] = grads[
            small_base : small_base + REPL, :
        ] + lax.dot_general(
            chosen(rows, BACK_SEG),
            grad * live,
            (((0,), (0,)), ((), ())),
            precision=lax.Precision.HIGHEST,
            preferred_element_type=jnp.float32,
        )

    def backward(turn):
        layer = LAYERS - 1 - turn
        base = turn * span
        start = turn * (span // CHUNK)
        last = turn == LAYERS - 1
        in_base = base + hidden_width
        out_base = in_base + width
        qkv_base = out_base + head_width

        def rows_at(first, count):
            return pl.ds(pl.multiple_of(first, 16), count)

        def down_piece(p):
            grads[rows_at(base + 128 * p, 128), :] = contract_rows(
                active[layer, :, lanes(p)], dz_low[...]
            )

        def in_piece(p):
            grads[rows_at(in_base + 128 * p, 128), :] = contract_rows(
                normed_low[layer, :, lanes(p)], du_low[...]
            )

        down_piece(0)
        tick(start)

        def feed(b):
            rows = block(b)
            dg = contract_cols(dz_low[rows, :], w_down[layer])
            u = hidden[layer, rows, :]
            density = jnp.exp(u * u * (-0.5)) * (1.0 / math.sqrt(2.0 * math.pi))
            du = dg * (normal_cdf(u) + u * density)
            du_low[rows, :] = du.astype(jnp.bfloat16)
            local_sums[turn, 0:1, :] = local_sums[turn, 0:1, :] + jnp.sum(
                du, axis=0, keepdims=True
            )
            down_piece(b + 1)
            tick(start + 1 + b)

        repeat(BACK_BLOCKS, feed)
        down_piece(5)

        def feed_in(b):
            spans = halves(b, BACK_SEG)
            left = jnp.concatenate([du_low[rows, :] for rows in spans], axis=0)
            result = contract_cols(left, w_in[layer])
            for side, rows in enumerate(spans):
                part[rows, :] = result[side * BACK_SEG : (side + 1) * BACK_SEG]
            to_core(0, b, BACK_SEG).start()
            pl.when(b >= 1)(lambda: send_y(0, b - 1, BACK_SEG))
            tick(start + 5 + b)

        repeat(BACK_BLOCKS, feed_in)
        send_y(0, BACK_BLOCKS - 1, BACK_SEG)

        def early_piece(p):
            in_piece(p)
            tick(start + 9 + p)

        repeat(4, early_piece)
        in_piece(4)

        gain = vector(first_gain, layer)

        def norm_one(b):
            rows = packed(b, BACK_SEG)
            grad = own_a[rows, :] + summed(0, b, BACK_SEG)
            zhat = zhat_one[layer, rows, :]
            dz = norm_back(grad, zhat, scale_one[layer, rows, :], gain)
            own_b[rows, :] = dz
            to_other(1, b, BACK_SEG, own_b).start()
            dz_low[kept(b, BACK_SEG), :] = dz.astype(jnp.bfloat16)
            total_row(turn, 3, grad * zhat)
            total_row(turn, 4, grad)
            total_row(turn, 5, dz)
            tick(start + 13 + b)
            dz_low[given(b, BACK_SEG), :] = received(1, b, BACK_SEG, own_b)

        repeat(BACK_BLOCKS, norm_one)
        grads[rows_at(out_base, head_width), :] = contract_rows(heads[layer], dz_low[...])
        dheads[...] = contract_cols(dz_low[...], w_out[layer]).astype(jnp.bfloat16)
        in_piece(5)
        tick(start + 17)
        dkeys[...] = jnp.zeros_like(dkeys)
        dvalues[...] = jnp.zeros_like(dvalues)

        def attend(b):
            rows = block(b)
            for h in range(local_heads):
                side = HEAD_DIM * h
                query = queries[layer, h, rows, :]
                probs = jnp.exp(scores_of(layer, h, query) - log_total[layer, rows, h : h + 1])
                dhead = dheads[rows, side : side + HEAD_DIM]
                dprobs = contract_cols(dhead, values[layer, h])
                dvalues[h] = dvalues[h] + contract_rows(probs.astype(jnp.bfloat16), dhead)
                inner = jnp.sum(probs * dprobs, axis=-1, keepdims=True)
                ds = (probs * (dprobs - inner)).astype(jnp.bfloat16)
                dq = matmul(ds, keys[layer, h]) * SCALE
                dkeys[h] = dkeys[h] + contract_rows(ds, query)
                dqkv_low[rows, 3 * side : 3 * side + HEAD_DIM] = dq.astype(jnp.bfloat16)
                local_sums[turn, 1:2, 2 * side : 2 * side + HEAD_DIM] = local_sums[
                    turn, 1:2, 2 * side : 2 * side + HEAD_DIM
                ] + jnp.sum(dq, axis=0, keepdims=True)
            pl.when(b < BACK_BLOCKS - 1)(lambda: tick(start + 18 + b))

        repeat(BACK_BLOCKS, attend)
        for h in range(local_heads):
            side = HEAD_DIM * h
            dqkv_low[:, 3 * side + HEAD_DIM : 3 * side + 2 * HEAD_DIM] = (
                dkeys[h] * SCALE
            ).astype(jnp.bfloat16)
            dv = dvalues[h]
            dqkv_low[:, 3 * side + 2 * HEAD_DIM : 3 * side + 3 * HEAD_DIM] = dv.astype(
                jnp.bfloat16
            )
            local_sums[turn, 1:2, 2 * side + HEAD_DIM : 2 * side + 2 * HEAD_DIM] = jnp.sum(
                dv, axis=0, keepdims=True
            )

        def back_project(b):
            grads[rows_at(qkv_base + 128 * b, 128), :] = contract_rows(
                dqkv_low[:, lanes(b)], inputs_low[layer]
            )
            spans = halves(b, BACK_SEG)
            left = jnp.concatenate([dqkv_low[rows, :] for rows in spans], axis=0)
            result = matmul(left, w_qkv[layer])
            for side, rows in enumerate(spans):
                part[rows, :] = result[side * BACK_SEG : (side + 1) * BACK_SEG]
            to_core(1, b, BACK_SEG).start()
            pl.when(b >= 1)(lambda: send_y(1, b - 1, BACK_SEG))
            tick(start + 21 + b)

        repeat(BACK_BLOCKS, back_project)
        send_y(1, BACK_BLOCKS - 1, BACK_SEG)

        tail = jnp.where(last, HOLE, 0)
        grads[rows_at(qkv_base + 512 + tail, HEAD_DIM), :] = contract_rows(
            dqkv_low[:, 512:], inputs_low[layer]
        )
        tick(start + 25)

        def pass_on(b):
            rows = packed(b, BACK_SEG)
            grad = own_b[rows, :] + summed(1, b, BACK_SEG)
            pl.when(jnp.logical_not(last))(lambda: norm_two(turn + 1, b, BACK_SEG, grad))
            pl.when(last)(lambda: last_grad(b, grad))
            pl.when(jnp.logical_or(last, b < 2))(lambda: tick(start + 26 + b))

        repeat(BACK_BLOCKS, pass_on)

        def receive(b):
            dz_low[given(b, BACK_SEG), :] = received(0, b, BACK_SEG, own_a)

        pl.when(jnp.logical_not(last))(lambda: repeat(BACK_BLOCKS, receive))

    repeat(LAYERS, backward)
    hidden_out[...] = inputs_low[LAYERS]

    shared = REPL + 8 * LAYERS
    for turn in range(LAYERS):
        first = small_base + REPL + 8 * turn
        grads[first : first + 8, :] = sums[turn]
    grads[small_base + shared : small_base + shared + 8, :] = local_sums[...].reshape(8, width)
    short = remote(
        grads.at[pl.ds(small_base, shared)], land_small, small_send, small_recv, place.core_peer
    )
    short.start()

    def receive_grad(b):
        grad_embeddings[given(b, BACK_SEG), :] = received(0, b, BACK_SEG, own_a)

    repeat(BACK_BLOCKS, receive_grad)
    short.wait()
    grads[small_base : small_base + shared, :] = (
        grads[small_base : small_base + shared, :] + land_small[...]
    )
    done = chunks - 1
    repeat(grad_sum.ticks() - done, lambda i: tick(done + i))


def run_pages(args, sizes):
    width, hidden_width, local_heads, span = sizes
    rows = PAGE_LEN
    flat = LAYERS * span - HEAD_DIM + HOLE + 2 * CHUNK
    half = rows // 2
    low, full = jnp.bfloat16, jnp.float32
    vmem, dma = pltpu.VMEM, pltpu.SemaphoreType.DMA
    head_width = local_heads * HEAD_DIM
    return pl.pallas_call(
        functools.partial(page_kernel, sizes),
        name="pages",
        out_shape=(
            vmem((rows, width), low),
            vmem((rows, width), low),
            vmem((flat, width), full),
        ),
        in_specs=[pl.BlockSpec(memory_space=pl.ANY)] * ARGS,
        out_specs=(
            pl.BlockSpec(memory_space=pltpu.VMEM),
            pl.BlockSpec(memory_space=pltpu.VMEM),
            pl.BlockSpec(memory_space=pltpu.VMEM),
        ),
        scratch_shapes=[
            *[vmem(arg.shape, arg.dtype) for arg in args],
            vmem((LAYERS + 1, rows, width), low),
            vmem((LAYERS, local_heads, rows, HEAD_DIM), low),
            vmem((LAYERS, local_heads, rows, HEAD_DIM), low),
            vmem((LAYERS, local_heads, rows, HEAD_DIM), low),
            vmem((LAYERS, rows, 128), full),
            vmem((LAYERS, rows, head_width), low),
            vmem((LAYERS, rows, width), low),
            vmem((LAYERS, rows, hidden_width), full),
            vmem((LAYERS, rows, hidden_width), low),
            vmem((LAYERS, half, width), full),
            vmem((LAYERS, half, 1), full),
            vmem((LAYERS, half, width), full),
            vmem((LAYERS, half, 1), full),
            vmem((LAYERS, 4 * head_width, width), low),
            vmem((5, BLOCKS, 3 * SEG // 2, 2 * HEAD_DIM), full),
            vmem((rows, 128), full),
            vmem((half, width), full),
            vmem((half, width), full),
            vmem((rows, width), full),
            vmem((2, half, width), full),
            vmem((2, half, width), full),
            vmem((2, half, width), full),
            vmem((REPL + 8 * LAYERS, width), full),
            vmem((rows, width), low),
            vmem((rows, hidden_width), low),
            vmem((rows, head_width), low),
            vmem((local_heads, rows, HEAD_DIM), full),
            vmem((local_heads, rows, HEAD_DIM), full),
            vmem((rows, 3 * head_width), low),
            vmem((LAYERS, 8, width), full),
            vmem((LAYERS, 4, width), full),
            vmem((len(WIDE_LANDINGS), SLOTS, WIDE, width), full),
            vmem((SLOTS, 2 * NARROW, width), full),
            vmem((len(NARROW_LANDINGS), SLOTS, NARROW, width), full),
            dma((2, BLOCKS)),
            dma((2, BLOCKS)),
            dma((2, BLOCKS)),
            dma((2, BLOCKS)),
            dma((2, BLOCKS)),
            dma((2, BLOCKS)),
            dma,
            dma,
            dma((len(EQUALS), EQUAL_SLOTS)),
            dma((len(EQUALS), EQUAL_SLOTS)),
            dma((len(ONE_WAY), SLOTS)),
            dma((4 * LAYERS,)),
            dma((4 * LAYERS,)),
            dma((LAYERS, GROUP)),
            dma((LAYERS, GROUP)),
            dma((3, BLOCKS)),
            dma((3, BLOCKS)),
            dma((ARGS, LAYERS)),
        ],
        compiler_params=pltpu.CompilerParams(
            collective_id=0, has_side_effects=True, vmem_limit_bytes=46 << 20
        ),
    )(*args)


def place_kernel(sizes, hidden_out, grad_embeddings, every, *refs):
    width, hidden_width, local_heads, span = sizes
    head_width = local_heads * HEAD_DIM
    (
        out_hidden,
        out_embeddings,
        out_table,
        out_w_qkv,
        out_b_qv,
        out_w_out,
        out_b_out,
        out_first_gain,
        out_first_shift,
        out_w_in,
        out_b_in,
        out_w_down,
        out_b_down,
        out_second_gain,
        out_second_shift,
        short,
        shorts,
        sems,
    ) = refs
    tail = LAYERS * span - HEAD_DIM
    base = tail + HOLE + CHUNK
    pairs = [(every.at[pl.ds(base, CHUNK)], short), (every.at[pl.ds(base, REPL)], out_table)]
    pairs += [(hidden_out, out_hidden), (grad_embeddings, out_embeddings)]
    for turn in range(LAYERS):
        first = span * turn
        for ref, rows in (
            (out_w_down, hidden_width),
            (out_w_in, width),
            (out_w_out, head_width),
            (out_w_qkv, 3 * head_width),
        ):
            target = ref.at[LAYERS - 1 - turn]
            direct = min(rows, tail - first)
            pairs.append((every.at[pl.ds(first, direct)], target.at[pl.ds(0, direct)]))
            if direct < rows:
                pairs.append(
                    (
                        every.at[pl.ds(tail + HOLE, rows - direct)],
                        target.at[pl.ds(direct, rows - direct)],
                    )
                )
            first += rows
    copies = [
        pltpu.make_async_copy(source, target, sems.at[index])
        for index, (source, target) in enumerate(pairs)
    ]
    for copy in copies:
        copy.start()
    copies[0].wait()
    pieces = []
    local = REPL + 8 * LAYERS
    for index, (ref, row, step) in enumerate((
        (out_second_gain, REPL, 8),
        (out_second_shift, REPL + 1, 8),
        (out_b_down, REPL + 2, 8),
        (out_first_gain, REPL + 3, 8),
        (out_first_shift, REPL + 4, 8),
        (out_b_out, REPL + 5, 8),
        (out_b_in, local, 4),
        (out_b_qv, local + 1, 4),
    )):
        for turn in range(LAYERS):
            layer = LAYERS - 1 - turn
            shorts[index, layer : layer + 1, :] = short[
                row + step * turn : row + step * turn + 1, :
            ]
        piece = pltpu.make_async_copy(
            shorts.at[index, :, pl.ds(0, ref.shape[1])], ref, sems.at[len(copies) + index]
        )
        piece.start()
        pieces.append(piece)
    for copy in copies[1:] + pieces:
        copy.wait()


def place_outputs(hidden_out, grad_embeddings, every, sizes):
    width, hidden_width, local_heads, span = sizes
    head_width = local_heads * HEAD_DIM
    low, full = jnp.bfloat16, jnp.float32
    rows = hidden_out.shape[0]
    shapes = (
        ((rows, width), low),
        ((rows, width), low),
        ((REPL, width), full),
        ((LAYERS, 3 * head_width, width), full),
        ((LAYERS, 2 * head_width), full),
        ((LAYERS, head_width, width), full),
        ((LAYERS, width), full),
        ((LAYERS, width), full),
        ((LAYERS, width), full),
        ((LAYERS, width, hidden_width), full),
        ((LAYERS, hidden_width), full),
        ((LAYERS, hidden_width, width), full),
        ((LAYERS, width), full),
        ((LAYERS, width), full),
        ((LAYERS, width), full),
    )
    far = pl.BlockSpec(memory_space=pl.ANY)
    return pl.pallas_call(
        functools.partial(place_kernel, sizes),
        name="place_outputs",
        out_shape=[jax.ShapeDtypeStruct(shape, kind) for shape, kind in shapes],
        in_specs=[far] * 3,
        out_specs=[far] * len(shapes),
        scratch_shapes=[
            pltpu.VMEM((CHUNK, width), full),
            pltpu.VMEM((8, LAYERS, width), full),
            pltpu.SemaphoreType.DMA((13 + 4 * LAYERS,)),
        ],
        compiler_params=pltpu.CompilerParams(vmem_limit_bytes=4 << 20),
    )(hidden_out, grad_embeddings, every)


def moved(every):
    def kernel(source, target, sem):
        copy = pltpu.make_async_copy(source, target, sem)
        copy.start()
        copy.wait()

    far = pl.BlockSpec(memory_space=pl.ANY)
    return pl.pallas_call(
        kernel,
        name="moved",
        out_shape=jax.ShapeDtypeStruct(every.shape, every.dtype),
        in_specs=[far],
        out_specs=far,
        scratch_shapes=[pltpu.SemaphoreType.DMA],
        compiler_params=pltpu.CompilerParams(vmem_limit_bytes=4 << 20),
    )(every)


def on_device(*args):
    (embeddings, replace_table, replace_ids, masked, padding, w_qkv, b_qv, *_) = args
    width = embeddings.shape[1]
    head_width = w_qkv.shape[2] // 3
    hidden_width = args[11].shape[2]
    span = 2 * hidden_width + 4 * head_width
    args = list(args)
    args[5] = jnp.swapaxes(args[5], 1, 2)
    for index in (2, 3, 4):
        args[index] = args[index].reshape(1, PAGE_LEN)
    sizes = (width, hidden_width, head_width // HEAD_DIM, span)
    hidden_out, grad_embeddings, every = run_pages(args, sizes)
    groups = lax.axis_size("dp") // GROUP
    if groups > 1:
        every = lax.psum(
            moved(every),
            "dp",
            axis_index_groups=[
                [low + GROUP * high for high in range(groups)] for low in range(GROUP)
            ],
        )

    results = place_outputs(hidden_out, grad_embeddings, every, sizes)
    return (*results[:3], jnp.swapaxes(results[3], 1, 2), *results[4:])


def solution(mesh):
    placed = (
        P("dp", None),
        P(),
        P("dp"),
        P("dp"),
        P("dp"),
        P(None, None, "tensor"),
        P(None, "tensor"),
        P(None, "tensor", None),
        P(),
        P(),
        P(),
        P(None, None, "tensor"),
        P(None, "tensor"),
        P(None, "tensor", None),
        P(),
        P(),
        P(),
        P("dp", None),
    )
    return jax.shard_map(
        on_device,
        mesh=mesh,
        in_specs=placed,
        out_specs=(
            P("dp", None),
            P("dp", None),
            P(),
            P(None, None, "tensor"),
            P(None, "tensor"),
            P(None, "tensor", None),
            P(),
            P(),
            P(),
            P(None, None, "tensor"),
            P(None, "tensor"),
            P(None, "tensor", None),
            P(),
            P(),
            P(),
        ),
        check_vma=False,
    )
```

```python
import functools
import math

import jax
import jax.numpy as jnp
from jax import lax
from jax.experimental import pallas as pl
from jax.experimental.pallas import tpu as pltpu
from jax.sharding import PartitionSpec as P

HEAD_DIM = 64
LAYERS = 2
PAGE_LEN = 512
REPL = 32
EPSILON = 1e-12
SCALE = HEAD_DIM ** (-0.5)
MESH = pl.DeviceIdType.MESH

HALF = PAGE_LEN // 2
SEG = 64
BLOCKS = HALF // SEG
BACK_SEG = 64
BACK_BLOCKS = HALF // BACK_SEG
BLOCK = 2 * BACK_SEG

WIDE = 24
NARROW = 8
CHUNK = 2 * WIDE + 4 * NARROW
HOLE = 2 * NARROW
SHORT_CHUNKS = 3
LAG = 2
SLOTS = 4 * LAG
EQUAL_SLOTS = 3 * LAG
EQUALS = (TA2, TQ1, TQ2, TR1, TR3, TTM, TG, TR5) = range(8)
ONE_WAY = (TA1, TTA, TQ0, TR0, TTN, TR6) = range(8, 14)
SHORT_WAY = (TR2, TTF, TR4) = range(14, 17)
TX = 17
WIDE_LANDINGS = (TX, TA1, TA2, TTA)
NARROW_LANDINGS = (TQ1, TQ2, TR0, TR1, TR2, TR3)
GROUP = 8
ARGS = 18
WEIGHTS = (5, 7, 11, 13)
SHORT_ARGS = tuple(index for index in range(1, ARGS - 1) if index not in WEIGHTS)
DIRECT = (64, 0)


def contract_rows(left, right):
    return lax.dot_general(
        left, right, (((0,), (0,)), ((), ())), preferred_element_type=jnp.float32
    )


def contract_cols(left, right):
    return lax.dot_general(
        left, right, (((1,), (1,)), ((), ())), preferred_element_type=jnp.float32
    )


def matmul(left, right):
    return jnp.dot(left, right, preferred_element_type=jnp.float32)


def repeat(count, body):
    def step(index, carry):
        body(index)
        return carry

    lax.fori_loop(0, count, step, 0)


def normed(values):
    average = jnp.mean(values, axis=-1, keepdims=True)
    centered = values - average
    variance = jnp.mean(centered * centered, axis=-1, keepdims=True)
    scale = lax.rsqrt(variance + EPSILON)
    return centered * scale, scale


def norm_back(grad, zhat, scale, gain):
    scaled = grad * gain
    average = jnp.mean(scaled, axis=-1, keepdims=True)
    along = jnp.mean(scaled * zhat, axis=-1, keepdims=True)
    return scale * (scaled - average - zhat * along)


def normal_cdf(values):
    return 0.5 * (1.0 + lax.erf(values * math.sqrt(0.5)))


def column(row):
    return jnp.transpose(jnp.broadcast_to(row, (128, row.shape[1])))[:, :1]


class Place:
    def __init__(self):
        d = lax.axis_index("dp")
        t = lax.axis_index("tensor")
        self.core = lax.rem(t, 2)
        self.core_peer = (d, t + 1 - 2 * self.core)
        self.y_peer = (d, t + 2 - 4 * lax.div(t, 2))
        self.diagonal = (d, t + 3 - 2 * self.core - 4 * lax.div(t, 2))
        self.y = lax.div(t, 2)
        self.low = lax.rem(d, GROUP)
        self.others = [
            (d - self.low + lax.rem(self.low + k, GROUP), t) for k in range(1, GROUP)
        ]
        pair = lax.rem(d, 2)
        line = lax.rem(lax.div(d, 2), 4)
        self.pair = pair
        self.mid = jnp.logical_or(line == 1, line == 2)
        self.end = jnp.logical_not(self.mid)
        self.upper = lax.div(line, 2)
        self.peer = (d + 1 - 2 * pair, t)
        self.line = (d + 2 - 4 * lax.rem(line, 2), t)
        self.cross = (jnp.where(line == 1, d + 2, d - 2), t)


def greet(place, barrier):
    def signal(device):
        pl.semaphore_signal(barrier, inc=1, device_id=device, device_id_type=MESH)

    for device in (place.core_peer, place.y_peer, place.diagonal, *place.others):
        signal(device)


def meet(barrier):
    pl.semaphore_wait(barrier, 2 + GROUP)


class GradientSum:
    def __init__(self, place, chunks, part, wide, both, narrow, send, recv, one_way, short_way, first_send, first_recv):
        self.place = place
        self.chunks = chunks
        self.part = part
        self.wide = wide
        self.both = both
        self.narrow = narrow
        self.send = send
        self.recv = recv
        self.one_way = one_way
        self.short_way = short_way
        self.first_send = first_send
        self.first_recv = first_recv

    def wide_rows(self, j, unit):
        return pl.ds(pl.multiple_of(j * CHUNK + unit * WIDE, NARROW), WIDE)

    def narrow_rows(self, j, unit, count=1):
        first = j * CHUNK + 2 * WIDE + unit * NARROW
        return pl.ds(pl.multiple_of(first, NARROW), count * NARROW)

    def tick(self, t):
        place, part = self.place, self.part
        mine, other = place.pair, 1 - place.pair
        near, far = place.upper, 1 - place.upper
        near_end, far_end = 2 + place.upper, 3 - place.upper

        def copy(kind, j, rows, target, device):
            if kind == TX:
                slot = lax.rem(j, SLOTS)
                send, recv = self.first_send.at[slot], self.first_recv.at[slot]
            elif kind in EQUALS:
                slot = lax.rem(j, EQUAL_SLOTS)
                send, recv = self.send.at[kind, slot], self.recv.at[kind, slot]
            elif kind in ONE_WAY:
                send = recv = self.one_way.at[kind - len(EQUALS), lax.rem(j, SLOTS)]
            else:
                index = kind - len(EQUALS) - len(ONE_WAY)
                send = recv = self.short_way.at[index, lax.rem(j, EQUAL_SLOTS)]
            return pltpu.make_async_remote_copy(
                src_ref=part.at[rows],
                dst_ref=target,
                send_sem=send,
                recv_sem=recv,
                device_id=device,
                device_id_type=MESH,
            )

        def wide_slot(kind, j):
            return WIDE_LANDINGS.index(kind), lax.rem(j, SLOTS)

        def narrow_slot(kind, j):
            return NARROW_LANDINGS.index(kind), lax.rem(j, SLOTS)

        def wide_part(kind, j, unit, device):
            return copy(
                kind, j, self.wide_rows(j, unit), self.wide.at[wide_slot(kind, j)], device
            )

        def narrow_part(kind, j, unit, device):
            return copy(
                kind, j, self.narrow_rows(j, unit), self.narrow.at[narrow_slot(kind, j)], device
            )

        def final(kind, j, rows, device):
            return copy(kind, j, rows, part.at[rows], device)

        def add_wide(kind, j, unit):
            rows = self.wide_rows(j, unit)
            part[rows, :] = part[rows, :] + self.wide[wide_slot(kind, j)]

        def add_narrow(kind, j, unit):
            rows = self.narrow_rows(j, unit)
            part[rows, :] = part[rows, :] + self.narrow[narrow_slot(kind, j)]

        def pair_first(j):
            return wide_part(TX, j, other, place.peer)

        def mine_in(j):
            return wide_part(TA1, j, mine, place.line)

        def mine_across(j):
            return wide_part(TA2, j, mine, place.cross)

        def mine_out(j):
            return wide_part(TTA, j, mine, place.line)

        def pair_last(j):
            return final(TG, j, self.wide_rows(j, mine), place.peer)

        def both_in(j):
            rows = self.narrow_rows(j, 0, 2)
            return copy(TQ0, j, rows, self.both.at[lax.rem(j, SLOTS)], place.line)

        def far_across(j):
            return narrow_part(TQ1, j, far, place.cross)

        def near_pair(j):
            return narrow_part(TQ2, j, near, place.peer)

        def near_out(j):
            return final(TTN, j, self.narrow_rows(j, near), place.line)

        def near_across(j):
            return final(TTM, j, self.narrow_rows(j, near), place.cross)

        def far_out(j):
            return final(TTF, j, self.narrow_rows(j, far), place.line)

        def end_in(j):
            return narrow_part(TR0, j, far_end, place.line)

        def end_across(j):
            return narrow_part(TR1, j, far_end, place.cross)

        def end_up(j):
            return narrow_part(TR2, j, near_end, place.line)

        def end_pair(j):
            return narrow_part(TR3, j, near_end, place.peer)

        def end_down(j):
            return final(TR4, j, self.narrow_rows(j, near_end), place.line)

        def end_back(j):
            return final(TR5, j, self.narrow_rows(j, near_end), place.cross)

        def end_out(j):
            return final(TR6, j, self.narrow_rows(j, far_end), place.line)

        def ended(j, body):
            pl.when(j < self.chunks - SHORT_CHUNKS)(body)

        def stage_0(j):
            pair_first(j).start()

            @pl.when(place.end)
            def _():
                ended(j, lambda: end_in(j).start())
                both_in(j).start()

        def stage_1(j):
            pair_first(j).wait()

            @pl.when(place.end)
            def _():
                both_in(j).wait_send()
                ended(j, lambda: end_in(j).wait_send())
                add_wide(TX, j, mine)
                mine_in(j).start()

            @pl.when(place.mid)
            def _():
                def onward():
                    end_in(j).wait_recv()
                    add_narrow(TR0, j, far_end)
                    end_across(j).start()

                ended(j, onward)
                both_in(j).wait_recv()
                rows = self.narrow_rows(j, 0, 2)
                part[rows, :] = part[rows, :] + self.both[lax.rem(j, SLOTS)]
                far_across(j).start()
                add_wide(TX, j, mine)

        def stage_2(j):
            @pl.when(place.end)
            def _():
                mine_in(j).wait_send()

            @pl.when(place.mid)
            def _():
                mine_in(j).wait_recv()
                far_across(j).wait()

                def onward():
                    end_across(j).wait()
                    add_narrow(TR1, j, near_end)
                    end_up(j).start()

                ended(j, onward)
                add_narrow(TQ1, j, near)
                near_pair(j).start()
                add_wide(TA1, j, mine)
                mine_across(j).start()

        def stage_3(j):
            @pl.when(place.end)
            def _():
                def onward():
                    end_up(j).wait_recv()
                    add_narrow(TR2, j, near_end)
                    end_pair(j).start()

                ended(j, onward)

            @pl.when(place.mid)
            def _():
                ended(j, lambda: end_up(j).wait_send())
                mine_across(j).wait()
                near_pair(j).wait()
                add_narrow(TQ2, j, near)
                near_across(j).start()
                near_out(j).start()
                add_wide(TA2, j, mine)
                mine_out(j).start()

        def stage_4(j):
            @pl.when(place.mid)
            def _():
                near_across(j).wait()
                far_out(j).start()
                near_out(j).wait_send()
                mine_out(j).wait_send()
                pair_last(j).start()

            @pl.when(place.end)
            def _():
                mine_out(j).wait_recv()
                near_out(j).wait_recv()

                def onward():
                    end_pair(j).wait()
                    add_narrow(TR3, j, near_end)
                    end_down(j).start()

                ended(j, onward)
                part[self.wide_rows(j, mine), :] = self.wide[wide_slot(TTA, j)]
                pair_last(j).start()

        def stage_5(j):
            @pl.when(place.mid)
            def _():
                def onward():
                    end_down(j).wait_recv()
                    end_back(j).start()

                ended(j, onward)
                far_out(j).wait_send()

            @pl.when(place.end)
            def _():
                ended(j, lambda: end_down(j).wait_send())
                far_out(j).wait_recv()

            pair_last(j).wait()

        def stage_6(j):
            @pl.when(place.mid)
            def _():
                def onward():
                    end_back(j).wait()
                    end_out(j).start()

                ended(j, onward)

        def stage_7(j):
            pl.when(place.mid)(lambda: ended(j, lambda: end_out(j).wait_send()))
            pl.when(place.end)(lambda: ended(j, lambda: end_out(j).wait_recv()))

        stages = (stage_0, stage_1, stage_2, stage_3, stage_4, stage_5, stage_6, stage_7)
        for number in range(len(stages)):
            j = t - number * LAG
            pl.when(jnp.logical_and(j >= 0, j < self.chunks))(
                functools.partial(stages[number], j)
            )

    def ticks(self):
        return self.chunks + max(5 * LAG, 7 * LAG - SHORT_CHUNKS)


def page_kernel(sizes, *refs):
    far, refs = refs[:ARGS], refs[ARGS:]
    (hidden_out, grad_embeddings, grads), refs = refs[:3], refs[3:]
    close, refs = refs[:ARGS], refs[ARGS:]
    (
        embeddings,
        replace_table,
        replace_ids,
        masked,
        padding,
        w_qkv,
        b_qv,
        w_out,
        b_out,
        first_gain,
        first_shift,
        w_in,
        b_in,
        w_down,
        b_down,
        second_gain,
        second_shift,
        cotangent,
    ) = close
    (
        inputs_low,
        queries,
        keys,
        values,
        log_total,
        heads,
        normed_low,
        hidden,
        active,
        zhat_one,
        scale_one,
        zhat_two,
        scale_two,
        w_all,
        shared_heads,
        columns,
        own_a,
        own_b,
        part,
        land_core,
        land_y,
        land_back,
        land_small,
        dz_low,
        du_low,
        dheads,
        dkeys,
        dvalues,
        dqkv_low,
        sums,
        local_sums,
        land_wide,
        land_both,
        land_narrow,
        core_send,
        core_recv,
        y_send,
        y_recv,
        back_send,
        back_recv,
        small_send,
        small_recv,
        dp_send,
        dp_recv,
        dp_one_way,
        dp_short_way,
        dp_first_send,
        dp_first_recv,
        gather_send,
        gather_recv,
        hand_send,
        hand_recv,
        heads_send,
        heads_recv,
        close_sem,
    ) = refs
    width, hidden_width, local_heads, span = sizes
    head_width = local_heads * HEAD_DIM
    place = Place()
    core = place.core
    barrier = pltpu.get_barrier_semaphore()
    greet(place, barrier)

    def fetch(index):
        return pltpu.make_async_copy(far[index], close[index], close_sem.at[index])

    def weight(which, layer):
        index = WEIGHTS[which]
        return pltpu.make_async_copy(
            far[index].at[layer],
            close[index].at[layer],
            close_sem.at[index + layer * (ARGS - index) + layer * which],
        )

    weight(1, 0).start()
    fetch(0).start()
    weight(0, 0).start()
    for index in SHORT_ARGS:
        fetch(index).start()
    tail_base = LAYERS * span - HEAD_DIM + HOLE
    small_base = tail_base + CHUNK
    assert tail_base % CHUNK == 0 and span % HEAD_DIM == 0
    chunks = grads.shape[0] // CHUNK
    grad_sum = GradientSum(place, chunks, grads, land_wide, land_both, land_narrow, dp_send, dp_recv, dp_one_way, dp_short_way, dp_first_send, dp_first_recv)
    tick = grad_sum.tick

    def vector(ref, layer):
        both = ref[...].astype(jnp.float32)
        return jnp.where(layer == 0, both[0:1], both[1:2])

    def block(b):
        return pl.ds(pl.multiple_of(b * BLOCK, BLOCK), BLOCK)

    def segment(b, size, half):
        return pl.ds(pl.multiple_of(half * HALF + b * size, size), size)

    def kept(b, size):
        return segment(b, size, core)

    def given(b, size):
        return segment(b, size, 1 - core)

    def packed(b, size):
        return segment(b, size, 0)

    def halves(b, size):
        return segment(b, size, 0), segment(b, size, 1)

    def lanes(p, size=128):
        return pl.ds(pl.multiple_of(p * size, size), size)

    def remote(source, target, send, recv, device):
        return pltpu.make_async_remote_copy(
            src_ref=source,
            dst_ref=target,
            send_sem=send,
            recv_sem=recv,
            device_id=device,
            device_id_type=MESH,
        )

    def to_core(turn, b, size):
        return remote(
            part.at[given(b, size)],
            land_core.at[turn, packed(b, size)],
            core_send.at[turn, b],
            core_recv.at[turn, b],
            place.core_peer,
        )

    def over_y(turn, b, size):
        return remote(
            part.at[kept(b, size)],
            land_y.at[turn, packed(b, size)],
            y_send.at[turn, b],
            y_recv.at[turn, b],
            place.y_peer,
        )

    def to_other(turn, b, size, source):
        return remote(
            source.at[packed(b, size)],
            land_back.at[turn, packed(b, size)],
            back_send.at[turn, b],
            back_recv.at[turn, b],
            place.core_peer,
        )

    def send_y(turn, b, size):
        to_core(turn, b, size).wait()
        rows = kept(b, size)
        part[rows, :] = part[rows, :] + land_core[turn, packed(b, size), :]
        over_y(turn, b, size).start()

    def summed(turn, b, size):
        over_y(turn, b, size).wait()
        return part[kept(b, size), :] + land_y[turn, packed(b, size), :]

    def received(turn, b, size, source):
        to_other(turn, b, size, source).wait()
        return land_back[turn, packed(b, size), :].astype(jnp.bfloat16)

    def shard(which, layer):
        return (which * LAYERS + layer) * head_width

    def direct(layer):
        return pl.ds(shard(0, layer), DIRECT[layer]), pl.ds(shard(2, layer), DIRECT[layer])

    def piece_rows(which, layer, owner):
        size = (head_width - DIRECT[layer]) // GROUP
        first = shard(which, layer) + DIRECT[layer] + owner * size
        return pl.ds(pl.multiple_of(first, 8), size)

    def moving(source, target, index, device):
        return remote(
            grads.at[source], grads.at[target], gather_send.at[index], gather_recv.at[index], device
        )

    def whole(which, layer):
        return pl.ds(shard(which, layer), head_width)

    def own_shard(layer):
        return moving(whole(0, layer), whole(1, layer), layer, place.core_peer)

    def other_shard(layer):
        return moving(whole(2, layer), whole(3, layer), LAYERS + layer, place.core_peer)

    def piece_over(layer):
        return moving(
            piece_rows(0, layer, place.low),
            piece_rows(2, layer, place.low),
            2 * LAYERS + layer,
            place.y_peer,
        )

    def rest_over(layer):
        return moving(*direct(layer), 3 * LAYERS + layer, place.y_peer)

    def handed(layer, k):
        rows = piece_rows(2, layer, place.low)
        return pltpu.make_async_remote_copy(
            src_ref=grads.at[rows],
            dst_ref=grads.at[rows],
            send_sem=hand_send.at[layer, k],
            recv_sem=hand_recv.at[layer, place.low],
            device_id=place.others[k],
            device_id_type=MESH,
        )

    def handed_in(layer, k):
        owner = lax.rem(place.low + 1 + k, GROUP)
        rows = piece_rows(2, layer, owner)
        return pltpu.make_async_remote_copy(
            src_ref=grads.at[rows],
            dst_ref=grads.at[rows],
            send_sem=hand_send.at[layer, k],
            recv_sem=hand_recv.at[layer, owner],
            device_id=place.others[k],
            device_id_type=MESH,
        )

    def gather_first(layer):
        weight(1, layer).wait()
        grads[whole(0, layer), :] = w_out[layer].astype(jnp.float32)
        piece_over(layer).start()
        if DIRECT[layer]:
            rest_over(layer).start()
        own_shard(layer).start()

    def gather_second(layer):
        piece_over(layer).wait()
        for k in range(GROUP - 1):
            handed(layer, k).start()

    def gather_third(layer):
        for k in range(GROUP - 1):
            handed(layer, k).wait_send()
            handed_in(layer, k).wait_recv()
        if DIRECT[layer]:
            rest_over(layer).wait()
        other_shard(layer).start()

    def gather_last(layer):
        own_shard(layer).wait()
        other_shard(layer).wait()
        pairs_width = 2 * HEAD_DIM
        for which in range(4):
            source = which // 2
            owner = 2 * (place.y + source - 2 * place.y * source) + (
                core + which % 2 - 2 * core * (which % 2)
            )
            low = grads[whole(which, layer), :].astype(jnp.bfloat16)
            first = pl.multiple_of(owner * pairs_width, pairs_width)
            w_all[layer, pl.ds(first, pairs_width), :] = low[:pairs_width]
            first = pl.multiple_of(4 * pairs_width + owner * HEAD_DIM, HEAD_DIM)
            w_all[layer, pl.ds(first, HEAD_DIM), :] = low[pairs_width:]

    def heads_out(b):
        mine, theirs = shared_heads.at[core, b], shared_heads.at[1 - core, b]
        return [
            remote(
                source,
                shared_heads.at[2 + index, b],
                heads_send.at[index, b],
                heads_recv.at[index, b],
                device,
            )
            for index, (source, device) in enumerate(
                (
                    (theirs, place.core_peer),
                    (mine, place.y_peer),
                    (theirs, place.diagonal),
                )
            )
        ]

    def pack_heads(rows):
        cut = 2 * HEAD_DIM
        return jnp.concatenate(
            [
                rows[:, :cut],
                jnp.concatenate([rows[: SEG // 2, cut:], rows[SEG // 2 :, cut:]], axis=1),
            ],
            axis=0,
        )

    def all_heads(b):
        pairs, thirds = [], []
        for owner in range(4):
            side, half = owner // 2, owner % 2
            apart = 2 * (place.y + side - 2 * place.y * side) + (core + half - 2 * core * half)
            slot = jnp.where(apart == 0, core, apart + 1)
            low = shared_heads[slot, b].astype(jnp.bfloat16)
            pairs.append(low[:SEG])
            tail = low[SEG:]
            thirds.append(jnp.concatenate([tail[:, :HEAD_DIM], tail[:, HEAD_DIM:]], axis=0))
        return jnp.concatenate(pairs + thirds, axis=1)

    meet(barrier)
    gather_first(0)

    for index in SHORT_ARGS:
        fetch(index).wait()
    pad_row = padding[...].astype(jnp.float32)
    live_row = masked[...].astype(jnp.float32) * pad_row
    bias_row = (pad_row - 1.0) * 10000.0
    columns[:, 0:1] = column(live_row)
    columns[:, 1:2] = column(replace_ids[...].astype(jnp.float32))
    grads[small_base:, :] = jnp.zeros((CHUNK, width), jnp.float32)

    def chosen(rows, count):
        spots = lax.broadcasted_iota(jnp.int32, (count, REPL), 1).astype(jnp.float32)
        return jnp.where(columns[rows, 1:2] == spots, 1.0, 0.0)

    def first_input(b):
        rows = block(b)
        picked = matmul(chosen(rows, BLOCK).astype(jnp.bfloat16), replace_table[...])
        taken = jnp.where(
            columns[rows, 0:1] > 0.0, picked, embeddings[rows, :].astype(jnp.float32)
        )
        inputs_low[0, rows, :] = taken.astype(jnp.bfloat16)

    sums[...] = jnp.zeros_like(sums)
    local_sums[...] = jnp.zeros_like(local_sums)

    def project(layer, spans):
        bias_pair = vector(b_qv, layer)
        inputs = jnp.concatenate([inputs_low[layer, rows, :] for rows in spans], axis=0)
        projected = contract_cols(inputs, w_qkv[layer])

        def split(ref, h, columns_of):
            low = columns_of.astype(jnp.bfloat16)
            first = 0
            for rows in spans:
                ref[layer, h, rows, :] = low[first : first + rows.size]
                first += rows.size

        for h in range(local_heads):
            base = 3 * HEAD_DIM * h
            bias = 2 * HEAD_DIM * h
            split(
                queries,
                h,
                projected[:, base : base + HEAD_DIM] + bias_pair[:, bias : bias + HEAD_DIM],
            )
            split(keys, h, projected[:, base + HEAD_DIM : base + 2 * HEAD_DIM])
            split(
                values,
                h,
                projected[:, base + 2 * HEAD_DIM : base + 3 * HEAD_DIM]
                + bias_pair[:, bias + HEAD_DIM : bias + 2 * HEAD_DIM],
            )

    def scores_of(layer, h, query):
        return contract_cols(query, keys[layer, h]) * SCALE + bias_row

    def total_row(turn, index, amount):
        sums[turn, index : index + 1, :] = sums[turn, index : index + 1, :] + jnp.sum(
            amount, axis=0, keepdims=True
        )

    def norm_two(turn, b, size, grad):
        layer = LAYERS - 1 - turn
        rows = packed(b, size)
        zhat = zhat_two[layer, rows, :]
        dz = norm_back(grad, zhat, scale_two[layer, rows, :], vector(second_gain, layer))
        own_a[rows, :] = dz
        to_other(0, b, size, own_a).start()
        dz_low[kept(b, size), :] = dz.astype(jnp.bfloat16)
        total_row(turn, 0, grad * zhat)
        total_row(turn, 1, grad)
        total_row(turn, 2, dz)

    def forward(layer):
        last = layer == LAYERS - 1

        def attend(b):
            pl.when(jnp.logical_and(layer == 0, b == BLOCKS - 1))(lambda: gather_third(0))
            spans = halves(b, SEG)
            outs, logs = [], []
            for h in range(local_heads):
                query = jnp.concatenate([queries[layer, h, rows, :] for rows in spans], axis=0)
                scores = scores_of(layer, h, query)
                largest = jnp.max(scores, axis=-1, keepdims=True)
                weights_of = jnp.exp(scores - largest)
                totals = jnp.sum(weights_of, axis=-1, keepdims=True)
                probs = (weights_of * (1.0 / totals)).astype(jnp.bfloat16)
                outs.append(matmul(probs, values[layer, h]).astype(jnp.bfloat16))
                logs.append(largest + jnp.log(totals))
            joined = jnp.concatenate(outs, axis=1)
            full = joined.astype(jnp.float32)
            for side in range(2):
                shared_heads[side, b] = pack_heads(full[side * SEG : (side + 1) * SEG])
            for copy in heads_out(b):
                copy.start()
            for side, rows in enumerate(spans):
                cut = slice(side * SEG, (side + 1) * SEG)
                heads[layer, rows, :] = joined[cut]
                for h in range(local_heads):
                    log_total[layer, rows, h : h + 1] = logs[h][cut]

        repeat(BLOCKS, attend)

        @pl.when(layer == 0)
        def _():
            gather_first(1)
            gather_last(0)

        pl.when(layer == 1)(lambda: gather_last(1))

        gain, shift, bias_out = (
            vector(first_gain, layer),
            vector(first_shift, layer),
            vector(b_out, layer),
        )
        bias_in = vector(b_in, layer)
        weight(2, layer).wait()
        weight(3, layer).wait()

        def feed_norm(b):
            rows = packed(b, SEG)
            for copy in heads_out(b):
                copy.wait()
            before = (
                inputs_low[layer, kept(b, SEG), :].astype(jnp.float32)
                + matmul(all_heads(b), w_all[layer])
                + bias_out
            )
            zhat, scale = normed(before)
            result = zhat * gain + shift
            own_a[rows, :] = result
            to_other(0, b, SEG, own_a).start()
            zhat_one[layer, rows, :] = zhat
            scale_one[layer, rows, :] = scale
            normed_low[layer, kept(b, SEG), :] = result.astype(jnp.bfloat16)

        def feed_main(b):
            spans = halves(b, SEG)
            normed_low[layer, given(b, SEG), :] = received(0, b, SEG, own_a)
            inputs = jnp.concatenate([normed_low[layer, rows, :] for rows in spans], axis=0)
            u = matmul(inputs, w_in[layer]) + bias_in
            g = (u * normal_cdf(u)).astype(jnp.bfloat16)
            lowered = matmul(g, w_down[layer])
            for side, rows in enumerate(spans):
                cut = slice(side * SEG, (side + 1) * SEG)
                part[rows, :] = lowered[cut]
                hidden[layer, rows, :] = u[cut]
                active[layer, rows, :] = g[cut]
            to_core(1, b, SEG).start()

        def feed(b):
            feed_norm(b)
            pl.when(b >= 1)(lambda: send_y(1, b - 1, SEG))
            feed_main(b)
            pl.when(jnp.logical_and(layer == 0, b == 0))(lambda: gather_second(1))

        repeat(BLOCKS, feed)
        send_y(1, BLOCKS - 1, SEG)

        gain_two, shift_two, bias_down = (
            vector(second_gain, layer),
            vector(second_shift, layer),
            vector(b_down, layer),
        )
        pl.when(jnp.logical_not(last))(lambda: weight(0, layer + 1).wait())

        def receive(b):
            inputs_low[layer + 1, given(b, SEG), :] = received(1, b, SEG, own_b)
            pl.when(jnp.logical_not(last))(lambda: project(layer + 1, halves(b, SEG)))

            @pl.when(last)
            def _():
                dz_low[given(b, SEG), :] = received(0, b, SEG, own_a)

        def finish(b):
            rows = packed(b, SEG)
            before = own_a[rows, :] + summed(1, b, SEG) + bias_down
            zhat, scale = normed(before)
            result = zhat * gain_two + shift_two
            own_b[rows, :] = result
            to_other(1, b, SEG, own_b).start()
            zhat_two[layer, rows, :] = zhat
            scale_two[layer, rows, :] = scale
            inputs_low[layer + 1, kept(b, SEG), :] = result.astype(jnp.bfloat16)

            @pl.when(last)
            def _():
                live = columns[kept(b, SEG), 0:1]
                norm_two(0, b, SEG, cotangent[kept(b, SEG), :].astype(jnp.float32) * live)

            pl.when(b >= 1)(lambda: receive(b - 1))

        repeat(BLOCKS, finish)
        receive(BLOCKS - 1)
        pl.when(layer == 0)(lambda: gather_third(1))

    fetch(0).wait()
    repeat(BACK_BLOCKS, first_input)
    fetch(ARGS - 1).start()
    for index, layer in ((1, 1), (2, 0), (3, 0), (0, 1), (2, 1), (3, 1)):
        weight(index, layer).start()
    weight(0, 0).wait()
    project(0, (block(0),))
    gather_second(0)
    repeat(BACK_BLOCKS - 1, lambda b: project(0, (block(b + 1),)))
    fetch(ARGS - 1).wait()
    repeat(LAYERS, forward)

    def last_grad(b, grad):
        rows = kept(b, BACK_SEG)
        live = columns[rows, 0:1]
        masked_grad = grad * (1.0 - live)
        own_a[packed(b, BACK_SEG), :] = masked_grad
        to_other(0, b, BACK_SEG, own_a).start()
        grad_embeddings[rows, :] = masked_grad.astype(jnp.bfloat16)
        grads[small_base : small_base + REPL, :] = grads[
            small_base : small_base + REPL, :
        ] + lax.dot_general(
            chosen(rows, BACK_SEG),
            grad * live,
            (((0,), (0,)), ((), ())),
            precision=lax.Precision.HIGHEST,
            preferred_element_type=jnp.float32,
        )

    def backward(turn):
        layer = LAYERS - 1 - turn
        base = turn * span
        start = turn * (span // CHUNK)
        last = turn == LAYERS - 1
        in_base = base + hidden_width
        out_base = in_base + width
        qkv_base = out_base + head_width

        def rows_at(first, count):
            return pl.ds(pl.multiple_of(first, 16), count)

        def down_piece(p):
            grads[rows_at(base + 128 * p, 128), :] = contract_rows(
                active[layer, :, lanes(p)], dz_low[...]
            )

        def in_piece(p):
            grads[rows_at(in_base + 128 * p, 128), :] = contract_rows(
                normed_low[layer, :, lanes(p)], du_low[...]
            )

        down_piece(0)
        tick(start)

        def feed(b):
            rows = block(b)
            dg = contract_cols(dz_low[rows, :], w_down[layer])
            u = hidden[layer, rows, :]
            density = jnp.exp(u * u * (-0.5)) * (1.0 / math.sqrt(2.0 * math.pi))
            du = dg * (normal_cdf(u) + u * density)
            du_low[rows, :] = du.astype(jnp.bfloat16)
            local_sums[turn, 0:1, :] = local_sums[turn, 0:1, :] + jnp.sum(
                du, axis=0, keepdims=True
            )
            down_piece(b + 1)
            tick(start + 1 + b)

        repeat(BACK_BLOCKS, feed)
        down_piece(5)

        def feed_in(b):
            spans = halves(b, BACK_SEG)
            left = jnp.concatenate([du_low[rows, :] for rows in spans], axis=0)
            result = contract_cols(left, w_in[layer])
            for side, rows in enumerate(spans):
                part[rows, :] = result[side * BACK_SEG : (side + 1) * BACK_SEG]
            to_core(0, b, BACK_SEG).start()
            pl.when(b >= 1)(lambda: send_y(0, b - 1, BACK_SEG))
            tick(start + 5 + b)

        repeat(BACK_BLOCKS, feed_in)
        send_y(0, BACK_BLOCKS - 1, BACK_SEG)

        def early_piece(p):
            in_piece(p)
            tick(start + 9 + p)

        repeat(4, early_piece)
        in_piece(4)

        gain = vector(first_gain, layer)

        def norm_one(b):
            rows = packed(b, BACK_SEG)
            grad = own_a[rows, :] + summed(0, b, BACK_SEG)
            zhat = zhat_one[layer, rows, :]
            dz = norm_back(grad, zhat, scale_one[layer, rows, :], gain)
            own_b[rows, :] = dz
            to_other(1, b, BACK_SEG, own_b).start()
            dz_low[kept(b, BACK_SEG), :] = dz.astype(jnp.bfloat16)
            total_row(turn, 3, grad * zhat)
            total_row(turn, 4, grad)
            total_row(turn, 5, dz)
            tick(start + 13 + b)
            dz_low[given(b, BACK_SEG), :] = received(1, b, BACK_SEG, own_b)

        repeat(BACK_BLOCKS, norm_one)
        grads[rows_at(out_base, head_width), :] = contract_rows(heads[layer], dz_low[...])
        dheads[...] = contract_cols(dz_low[...], w_out[layer]).astype(jnp.bfloat16)
        in_piece(5)
        tick(start + 17)
        dkeys[...] = jnp.zeros_like(dkeys)
        dvalues[...] = jnp.zeros_like(dvalues)

        def attend(b):
            rows = block(b)
            for h in range(local_heads):
                side = HEAD_DIM * h
                query = queries[layer, h, rows, :]
                probs = jnp.exp(scores_of(layer, h, query) - log_total[layer, rows, h : h + 1])
                dhead = dheads[rows, side : side + HEAD_DIM]
                dprobs = contract_cols(dhead, values[layer, h])
                dvalues[h] = dvalues[h] + contract_rows(probs.astype(jnp.bfloat16), dhead)
                inner = jnp.sum(probs * dprobs, axis=-1, keepdims=True)
                ds = (probs * (dprobs - inner)).astype(jnp.bfloat16)
                dq = matmul(ds, keys[layer, h]) * SCALE
                dkeys[h] = dkeys[h] + contract_rows(ds, query)
                dqkv_low[rows, 3 * side : 3 * side + HEAD_DIM] = dq.astype(jnp.bfloat16)
                local_sums[turn, 1:2, 2 * side : 2 * side + HEAD_DIM] = local_sums[
                    turn, 1:2, 2 * side : 2 * side + HEAD_DIM
                ] + jnp.sum(dq, axis=0, keepdims=True)
            pl.when(b < BACK_BLOCKS - 1)(lambda: tick(start + 18 + b))

        repeat(BACK_BLOCKS, attend)
        for h in range(local_heads):
            side = HEAD_DIM * h
            dqkv_low[:, 3 * side + HEAD_DIM : 3 * side + 2 * HEAD_DIM] = (
                dkeys[h] * SCALE
            ).astype(jnp.bfloat16)
            dv = dvalues[h]
            dqkv_low[:, 3 * side + 2 * HEAD_DIM : 3 * side + 3 * HEAD_DIM] = dv.astype(
                jnp.bfloat16
            )
            local_sums[turn, 1:2, 2 * side + HEAD_DIM : 2 * side + 2 * HEAD_DIM] = jnp.sum(
                dv, axis=0, keepdims=True
            )

        def back_project(b):
            grads[rows_at(qkv_base + 128 * b, 128), :] = contract_rows(
                dqkv_low[:, lanes(b)], inputs_low[layer]
            )
            spans = halves(b, BACK_SEG)
            left = jnp.concatenate([dqkv_low[rows, :] for rows in spans], axis=0)
            result = matmul(left, w_qkv[layer])
            for side, rows in enumerate(spans):
                part[rows, :] = result[side * BACK_SEG : (side + 1) * BACK_SEG]
            to_core(1, b, BACK_SEG).start()
            pl.when(b >= 1)(lambda: send_y(1, b - 1, BACK_SEG))
            tick(start + 21 + b)

        repeat(BACK_BLOCKS, back_project)
        send_y(1, BACK_BLOCKS - 1, BACK_SEG)

        tail = jnp.where(last, HOLE, 0)
        grads[rows_at(qkv_base + 512 + tail, HEAD_DIM), :] = contract_rows(
            dqkv_low[:, 512:], inputs_low[layer]
        )
        tick(start + 25)

        def pass_on(b):
            rows = packed(b, BACK_SEG)
            grad = own_b[rows, :] + summed(1, b, BACK_SEG)
            pl.when(jnp.logical_not(last))(lambda: norm_two(turn + 1, b, BACK_SEG, grad))
            pl.when(last)(lambda: last_grad(b, grad))
            pl.when(jnp.logical_or(last, b < 2))(lambda: tick(start + 26 + b))

        repeat(BACK_BLOCKS, pass_on)

        def receive(b):
            dz_low[given(b, BACK_SEG), :] = received(0, b, BACK_SEG, own_a)

        pl.when(jnp.logical_not(last))(lambda: repeat(BACK_BLOCKS, receive))

    repeat(LAYERS, backward)
    hidden_out[...] = inputs_low[LAYERS]

    shared = REPL + 8 * LAYERS
    for turn in range(LAYERS):
        first = small_base + REPL + 8 * turn
        grads[first : first + 8, :] = sums[turn]
    grads[small_base + shared : small_base + shared + 8, :] = local_sums[...].reshape(8, width)
    short = remote(
        grads.at[pl.ds(small_base, shared)], land_small, small_send, small_recv, place.core_peer
    )
    short.start()

    def receive_grad(b):
        grad_embeddings[given(b, BACK_SEG), :] = received(0, b, BACK_SEG, own_a)

    repeat(BACK_BLOCKS, receive_grad)
    short.wait()
    grads[small_base : small_base + shared, :] = (
        grads[small_base : small_base + shared, :] + land_small[...]
    )
    done = chunks - 1
    repeat(grad_sum.ticks() - done, lambda i: tick(done + i))


def run_pages(args, sizes):
    width, hidden_width, local_heads, span = sizes
    rows = PAGE_LEN
    flat = LAYERS * span - HEAD_DIM + HOLE + 2 * CHUNK
    half = rows // 2
    low, full = jnp.bfloat16, jnp.float32
    vmem, dma = pltpu.VMEM, pltpu.SemaphoreType.DMA
    head_width = local_heads * HEAD_DIM
    return pl.pallas_call(
        functools.partial(page_kernel, sizes),
        name="pages",
        out_shape=(
            vmem((rows, width), low),
            vmem((rows, width), low),
            vmem((flat, width), full),
        ),
        in_specs=[pl.BlockSpec(memory_space=pl.ANY)] * ARGS,
        out_specs=(
            pl.BlockSpec(memory_space=pltpu.VMEM),
            pl.BlockSpec(memory_space=pltpu.VMEM),
            pl.BlockSpec(memory_space=pltpu.VMEM),
        ),
        scratch_shapes=[
            *[vmem(arg.shape, arg.dtype) for arg in args],
            vmem((LAYERS + 1, rows, width), low),
            vmem((LAYERS, local_heads, rows, HEAD_DIM), low),
            vmem((LAYERS, local_heads, rows, HEAD_DIM), low),
            vmem((LAYERS, local_heads, rows, HEAD_DIM), low),
            vmem((LAYERS, rows, 128), full),
            vmem((LAYERS, rows, head_width), low),
            vmem((LAYERS, rows, width), low),
            vmem((LAYERS, rows, hidden_width), full),
            vmem((LAYERS, rows, hidden_width), low),
            vmem((LAYERS, half, width), full),
            vmem((LAYERS, half, 1), full),
            vmem((LAYERS, half, width), full),
            vmem((LAYERS, half, 1), full),
            vmem((LAYERS, 4 * head_width, width), low),
            vmem((5, BLOCKS, 3 * SEG // 2, 2 * HEAD_DIM), full),
            vmem((rows, 128), full),
            vmem((half, width), full),
            vmem((half, width), full),
            vmem((rows, width), full),
            vmem((2, half, width), full),
            vmem((2, half, width), full),
            vmem((2, half, width), full),
            vmem((REPL + 8 * LAYERS, width), full),
            vmem((rows, width), low),
            vmem((rows, hidden_width), low),
            vmem((rows, head_width), low),
            vmem((local_heads, rows, HEAD_DIM), full),
            vmem((local_heads, rows, HEAD_DIM), full),
            vmem((rows, 3 * head_width), low),
            vmem((LAYERS, 8, width), full),
            vmem((LAYERS, 4, width), full),
            vmem((len(WIDE_LANDINGS), SLOTS, WIDE, width), full),
            vmem((SLOTS, 2 * NARROW, width), full),
            vmem((len(NARROW_LANDINGS), SLOTS, NARROW, width), full),
            dma((2, BLOCKS)),
            dma((2, BLOCKS)),
            dma((2, BLOCKS)),
            dma((2, BLOCKS)),
            dma((2, BLOCKS)),
            dma((2, BLOCKS)),
            dma,
            dma,
            dma((len(EQUALS), EQUAL_SLOTS)),
            dma((len(EQUALS), EQUAL_SLOTS)),
            dma((len(ONE_WAY), SLOTS)),
            dma((len(SHORT_WAY), EQUAL_SLOTS)),
            dma((SLOTS,)),
            dma((SLOTS,)),
            dma((4 * LAYERS,)),
            dma((4 * LAYERS,)),
            dma((LAYERS, GROUP)),
            dma((LAYERS, GROUP)),
            dma((3, BLOCKS)),
            dma((3, BLOCKS)),
            dma((ARGS + (LAYERS - 1) * len(WEIGHTS),)),
        ],
        compiler_params=pltpu.CompilerParams(
            collective_id=0, has_side_effects=True, vmem_limit_bytes=46 << 20
        ),
    )(*args)


def place_kernel(sizes, hidden_out, grad_embeddings, every, *refs):
    width, hidden_width, local_heads, span = sizes
    head_width = local_heads * HEAD_DIM
    (
        out_hidden,
        out_embeddings,
        out_table,
        out_w_qkv,
        out_b_qv,
        out_w_out,
        out_b_out,
        out_first_gain,
        out_first_shift,
        out_w_in,
        out_b_in,
        out_w_down,
        out_b_down,
        out_second_gain,
        out_second_shift,
        short,
        shorts,
        sems,
    ) = refs
    tail = LAYERS * span - HEAD_DIM
    base = tail + HOLE + CHUNK
    pairs = [(every.at[pl.ds(base, CHUNK)], short), (every.at[pl.ds(base, REPL)], out_table)]
    pairs += [(hidden_out, out_hidden), (grad_embeddings, out_embeddings)]
    for turn in range(LAYERS):
        first = span * turn
        for ref, rows in (
            (out_w_down, hidden_width),
            (out_w_in, width),
            (out_w_out, head_width),
            (out_w_qkv, 3 * head_width),
        ):
            target = ref.at[LAYERS - 1 - turn]
            direct = min(rows, tail - first)
            pairs.append((every.at[pl.ds(first, direct)], target.at[pl.ds(0, direct)]))
            if direct < rows:
                pairs.append(
                    (
                        every.at[pl.ds(tail + HOLE, rows - direct)],
                        target.at[pl.ds(direct, rows - direct)],
                    )
                )
            first += rows
    copies = [
        pltpu.make_async_copy(source, target, sems.at[index])
        for index, (source, target) in enumerate(pairs)
    ]
    for copy in copies:
        copy.start()
    copies[0].wait()
    pieces = []
    local = REPL + 8 * LAYERS
    for index, (ref, row, step) in enumerate((
        (out_second_gain, REPL, 8),
        (out_second_shift, REPL + 1, 8),
        (out_b_down, REPL + 2, 8),
        (out_first_gain, REPL + 3, 8),
        (out_first_shift, REPL + 4, 8),
        (out_b_out, REPL + 5, 8),
        (out_b_in, local, 4),
        (out_b_qv, local + 1, 4),
    )):
        for turn in range(LAYERS):
            layer = LAYERS - 1 - turn
            shorts[index, layer : layer + 1, :] = short[
                row + step * turn : row + step * turn + 1, :
            ]
        piece = pltpu.make_async_copy(
            shorts.at[index, :, pl.ds(0, ref.shape[1])], ref, sems.at[len(copies) + index]
        )
        piece.start()
        pieces.append(piece)
    for copy in copies[1:] + pieces:
        copy.wait()


def place_outputs(hidden_out, grad_embeddings, every, sizes):
    width, hidden_width, local_heads, span = sizes
    head_width = local_heads * HEAD_DIM
    low, full = jnp.bfloat16, jnp.float32
    rows = hidden_out.shape[0]
    shapes = (
        ((rows, width), low),
        ((rows, width), low),
        ((REPL, width), full),
        ((LAYERS, 3 * head_width, width), full),
        ((LAYERS, 2 * head_width), full),
        ((LAYERS, head_width, width), full),
        ((LAYERS, width), full),
        ((LAYERS, width), full),
        ((LAYERS, width), full),
        ((LAYERS, width, hidden_width), full),
        ((LAYERS, hidden_width), full),
        ((LAYERS, hidden_width, width), full),
        ((LAYERS, width), full),
        ((LAYERS, width), full),
        ((LAYERS, width), full),
    )
    far = pl.BlockSpec(memory_space=pl.ANY)
    return pl.pallas_call(
        functools.partial(place_kernel, sizes),
        name="place_outputs",
        out_shape=[jax.ShapeDtypeStruct(shape, kind) for shape, kind in shapes],
        in_specs=[far] * 3,
        out_specs=[far] * len(shapes),
        scratch_shapes=[
            pltpu.VMEM((CHUNK, width), full),
            pltpu.VMEM((8, LAYERS, width), full),
            pltpu.SemaphoreType.DMA((13 + 4 * LAYERS,)),
        ],
        compiler_params=pltpu.CompilerParams(vmem_limit_bytes=4 << 20),
    )(hidden_out, grad_embeddings, every)


def moved(every):
    def kernel(source, target, sem):
        copy = pltpu.make_async_copy(source, target, sem)
        copy.start()
        copy.wait()

    far = pl.BlockSpec(memory_space=pl.ANY)
    return pl.pallas_call(
        kernel,
        name="moved",
        out_shape=jax.ShapeDtypeStruct(every.shape, every.dtype),
        in_specs=[far],
        out_specs=far,
        scratch_shapes=[pltpu.SemaphoreType.DMA],
        compiler_params=pltpu.CompilerParams(vmem_limit_bytes=4 << 20),
    )(every)


def on_device(*args):
    (embeddings, replace_table, replace_ids, masked, padding, w_qkv, b_qv, *_) = args
    width = embeddings.shape[1]
    head_width = w_qkv.shape[2] // 3
    hidden_width = args[11].shape[2]
    span = 2 * hidden_width + 4 * head_width
    args = list(args)
    args[5] = jnp.swapaxes(args[5], 1, 2)
    for index in (2, 3, 4):
        args[index] = args[index].reshape(1, PAGE_LEN)
    sizes = (width, hidden_width, head_width // HEAD_DIM, span)
    hidden_out, grad_embeddings, every = run_pages(args, sizes)
    groups = lax.axis_size("dp") // GROUP
    if groups > 1:
        every = lax.psum(
            moved(every),
            "dp",
            axis_index_groups=[
                [low + GROUP * high for high in range(groups)] for low in range(GROUP)
            ],
        )

    results = place_outputs(hidden_out, grad_embeddings, every, sizes)
    return (*results[:3], jnp.swapaxes(results[3], 1, 2), *results[4:])


def solution(mesh):
    placed = (
        P("dp", None),
        P(),
        P("dp"),
        P("dp"),
        P("dp"),
        P(None, None, "tensor"),
        P(None, "tensor"),
        P(None, "tensor", None),
        P(),
        P(),
        P(),
        P(None, None, "tensor"),
        P(None, "tensor"),
        P(None, "tensor", None),
        P(),
        P(),
        P(),
        P("dp", None),
    )
    return jax.shard_map(
        on_device,
        mesh=mesh,
        in_specs=placed,
        out_specs=(
            P("dp", None),
            P("dp", None),
            P(),
            P(None, None, "tensor"),
            P(None, "tensor"),
            P(None, "tensor", None),
            P(),
            P(),
            P(),
            P(None, None, "tensor"),
            P(None, "tensor"),
            P(None, "tensor", None),
            P(),
            P(),
            P(),
        ),
        check_vma=False,
    )
```

```python
import functools
import math

import jax
import jax.numpy as jnp
from jax import lax
from jax.experimental import pallas as pl
from jax.experimental.pallas import tpu as pltpu
from jax.sharding import PartitionSpec as P

HEAD_DIM = 64
LAYERS = 2
PAGE_LEN = 512
REPL = 32
EPSILON = 1e-12
SCALE = HEAD_DIM ** (-0.5)
MESH = pl.DeviceIdType.MESH

HALF = PAGE_LEN // 2
SEG = 64
BLOCKS = HALF // SEG
BACK_SEG = 64
BACK_BLOCKS = HALF // BACK_SEG
BLOCK = 2 * BACK_SEG

WIDE = 24
NARROW = 8
CHUNK = 2 * WIDE + 4 * NARROW
HOLE = 2 * NARROW
SHORT_CHUNKS = 3
LAG = 2
SLOTS = 4 * LAG
EQUAL_SLOTS = 3 * LAG
EQUALS = (TA2, TQ1, TQ2, TR1, TTM, TG, TR5) = range(7)
ONE_WAY = (TA1, TTA, TQ0, TR0, TTN, TR6) = range(7, 13)
SHORT_WAY = (TR2, TTF, TR4) = range(13, 16)
TX, TR3 = 16, 17
WIDE_LANDINGS = (TX, TA1, TA2, TTA)
NARROW_LANDINGS = (TQ1, TQ2, TR0, TR1, TR2, TR3)
GROUP = 8
ARGS = 18
WEIGHTS = (5, 7, 11, 13)
SHORT_ARGS = tuple(index for index in range(1, ARGS - 1) if index not in WEIGHTS)
DIRECT = (64, 0)


def contract_rows(left, right):
    return lax.dot_general(
        left, right, (((0,), (0,)), ((), ())), preferred_element_type=jnp.float32
    )


def contract_cols(left, right):
    return lax.dot_general(
        left, right, (((1,), (1,)), ((), ())), preferred_element_type=jnp.float32
    )


def matmul(left, right):
    return jnp.dot(left, right, preferred_element_type=jnp.float32)


def repeat(count, body):
    def step(index, carry):
        body(index)
        return carry

    lax.fori_loop(0, count, step, 0)


def normed(values):
    average = jnp.mean(values, axis=-1, keepdims=True)
    centered = values - average
    variance = jnp.mean(centered * centered, axis=-1, keepdims=True)
    scale = lax.rsqrt(variance + EPSILON)
    return centered * scale, scale


def norm_back(grad, zhat, scale, gain):
    scaled = grad * gain
    average = jnp.mean(scaled, axis=-1, keepdims=True)
    along = jnp.mean(scaled * zhat, axis=-1, keepdims=True)
    return scale * (scaled - average - zhat * along)


def normal_cdf(values):
    return 0.5 * (1.0 + lax.erf(values * math.sqrt(0.5)))


def column(row):
    return jnp.transpose(jnp.broadcast_to(row, (128, row.shape[1])))[:, :1]


class Place:
    def __init__(self):
        d = lax.axis_index("dp")
        t = lax.axis_index("tensor")
        self.core = lax.rem(t, 2)
        self.core_peer = (d, t + 1 - 2 * self.core)
        self.y_peer = (d, t + 2 - 4 * lax.div(t, 2))
        self.diagonal = (d, t + 3 - 2 * self.core - 4 * lax.div(t, 2))
        self.y = lax.div(t, 2)
        self.low = lax.rem(d, GROUP)
        self.others = [
            (d - self.low + lax.rem(self.low + k, GROUP), t) for k in range(1, GROUP)
        ]
        pair = lax.rem(d, 2)
        line = lax.rem(lax.div(d, 2), 4)
        self.pair = pair
        self.mid = jnp.logical_or(line == 1, line == 2)
        self.end = jnp.logical_not(self.mid)
        self.upper = lax.div(line, 2)
        self.peer = (d + 1 - 2 * pair, t)
        self.line = (d + 2 - 4 * lax.rem(line, 2), t)
        self.cross = (jnp.where(line == 1, d + 2, d - 2), t)


def greet(place, barrier):
    def signal(device):
        pl.semaphore_signal(barrier, inc=1, device_id=device, device_id_type=MESH)

    for device in (place.core_peer, place.y_peer, place.diagonal, *place.others):
        signal(device)


def meet(barrier):
    pl.semaphore_wait(barrier, 2 + GROUP)


class GradientSum:
    def __init__(self, place, chunks, part, wide, both, narrow, send, recv, one_way, short_way, first_send, first_recv):
        self.place = place
        self.chunks = chunks
        self.part = part
        self.wide = wide
        self.both = both
        self.narrow = narrow
        self.send = send
        self.recv = recv
        self.one_way = one_way
        self.short_way = short_way
        self.first_send = first_send
        self.first_recv = first_recv

    def wide_rows(self, j, unit):
        return pl.ds(pl.multiple_of(j * CHUNK + unit * WIDE, NARROW), WIDE)

    def narrow_rows(self, j, unit, count=1):
        first = j * CHUNK + 2 * WIDE + unit * NARROW
        return pl.ds(pl.multiple_of(first, NARROW), count * NARROW)

    def tick(self, t):
        place, part = self.place, self.part
        mine, other = place.pair, 1 - place.pair
        near, far = place.upper, 1 - place.upper
        near_end, far_end = 2 + place.upper, 3 - place.upper

        def copy(kind, j, rows, target, device):
            if kind == TX:
                slot = lax.rem(j, SLOTS)
                send, recv = self.first_send.at[slot], self.first_recv.at[slot]
            elif kind in EQUALS or kind == TR3:
                slot, index = lax.rem(j, EQUAL_SLOTS), TQ2 if kind == TR3 else kind
                send, recv = self.send.at[index, slot], self.recv.at[index, slot]
            elif kind in ONE_WAY:
                send = recv = self.one_way.at[kind - len(EQUALS), lax.rem(j, SLOTS)]
            else:
                index = kind - len(EQUALS) - len(ONE_WAY)
                send = recv = self.short_way.at[index, lax.rem(j, EQUAL_SLOTS)]
            return pltpu.make_async_remote_copy(
                src_ref=part.at[rows],
                dst_ref=target,
                send_sem=send,
                recv_sem=recv,
                device_id=device,
                device_id_type=MESH,
            )

        def wide_slot(kind, j):
            return WIDE_LANDINGS.index(kind), lax.rem(j, SLOTS)

        def narrow_slot(kind, j):
            return NARROW_LANDINGS.index(kind), lax.rem(j, SLOTS)

        def wide_part(kind, j, unit, device):
            return copy(
                kind, j, self.wide_rows(j, unit), self.wide.at[wide_slot(kind, j)], device
            )

        def narrow_part(kind, j, unit, device):
            return copy(
                kind, j, self.narrow_rows(j, unit), self.narrow.at[narrow_slot(kind, j)], device
            )

        def final(kind, j, rows, device):
            return copy(kind, j, rows, part.at[rows], device)

        def add_wide(kind, j, unit):
            rows = self.wide_rows(j, unit)
            part[rows, :] = part[rows, :] + self.wide[wide_slot(kind, j)]

        def add_narrow(kind, j, unit):
            rows = self.narrow_rows(j, unit)
            part[rows, :] = part[rows, :] + self.narrow[narrow_slot(kind, j)]

        def pair_first(j):
            return wide_part(TX, j, other, place.peer)

        def mine_in(j):
            return wide_part(TA1, j, mine, place.line)

        def mine_across(j):
            return wide_part(TA2, j, mine, place.cross)

        def mine_out(j):
            return wide_part(TTA, j, mine, place.line)

        def pair_last(j):
            return final(TG, j, self.wide_rows(j, mine), place.peer)

        def both_in(j):
            rows = self.narrow_rows(j, 0, 2)
            return copy(TQ0, j, rows, self.both.at[lax.rem(j, SLOTS)], place.line)

        def far_across(j):
            return narrow_part(TQ1, j, far, place.cross)

        def near_pair(j):
            return narrow_part(TQ2, j, near, place.peer)

        def near_out(j):
            return final(TTN, j, self.narrow_rows(j, near), place.line)

        def near_across(j):
            return final(TTM, j, self.narrow_rows(j, near), place.cross)

        def far_out(j):
            return final(TTF, j, self.narrow_rows(j, far), place.line)

        def end_in(j):
            return narrow_part(TR0, j, far_end, place.line)

        def end_across(j):
            return narrow_part(TR1, j, far_end, place.cross)

        def end_up(j):
            return narrow_part(TR2, j, near_end, place.line)

        def end_pair(j):
            return narrow_part(TR3, j, near_end, place.peer)

        def end_down(j):
            return final(TR4, j, self.narrow_rows(j, near_end), place.line)

        def end_back(j):
            return final(TR5, j, self.narrow_rows(j, near_end), place.cross)

        def end_out(j):
            return final(TR6, j, self.narrow_rows(j, far_end), place.line)

        def ended(j, body):
            pl.when(j < self.chunks - SHORT_CHUNKS)(body)

        def stage_0(j):
            pair_first(j).start()

            @pl.when(place.end)
            def _():
                ended(j, lambda: end_in(j).start())
                both_in(j).start()

        def stage_1(j):
            pair_first(j).wait()

            @pl.when(place.end)
            def _():
                both_in(j).wait_send()
                ended(j, lambda: end_in(j).wait_send())
                add_wide(TX, j, mine)
                mine_in(j).start()

            @pl.when(place.mid)
            def _():
                def onward():
                    end_in(j).wait_recv()
                    add_narrow(TR0, j, far_end)
                    end_across(j).start()

                ended(j, onward)
                both_in(j).wait_recv()
                rows = self.narrow_rows(j, 0, 2)
                part[rows, :] = part[rows, :] + self.both[lax.rem(j, SLOTS)]
                far_across(j).start()
                add_wide(TX, j, mine)

        def stage_2(j):
            @pl.when(place.end)
            def _():
                mine_in(j).wait_send()

            @pl.when(place.mid)
            def _():
                mine_in(j).wait_recv()
                far_across(j).wait()

                def onward():
                    end_across(j).wait()
                    add_narrow(TR1, j, near_end)
                    end_up(j).start()

                ended(j, onward)
                add_narrow(TQ1, j, near)
                near_pair(j).start()
                add_wide(TA1, j, mine)
                mine_across(j).start()

        def stage_3(j):
            @pl.when(place.end)
            def _():
                def onward():
                    end_up(j).wait_recv()
                    add_narrow(TR2, j, near_end)
                    end_pair(j).start()

                ended(j, onward)

            @pl.when(place.mid)
            def _():
                ended(j, lambda: end_up(j).wait_send())
                mine_across(j).wait()
                near_pair(j).wait()
                add_narrow(TQ2, j, near)
                near_across(j).start()
                near_out(j).start()
                add_wide(TA2, j, mine)
                mine_out(j).start()

        def stage_4(j):
            @pl.when(place.mid)
            def _():
                near_across(j).wait()
                far_out(j).start()
                near_out(j).wait_send()
                mine_out(j).wait_send()
                pair_last(j).start()

            @pl.when(place.end)
            def _():
                mine_out(j).wait_recv()
                near_out(j).wait_recv()

                def onward():
                    end_pair(j).wait()
                    add_narrow(TR3, j, near_end)
                    end_down(j).start()

                ended(j, onward)
                part[self.wide_rows(j, mine), :] = self.wide[wide_slot(TTA, j)]
                pair_last(j).start()

        def stage_5(j):
            @pl.when(place.mid)
            def _():
                def onward():
                    end_down(j).wait_recv()
                    end_back(j).start()

                ended(j, onward)
                far_out(j).wait_send()

            @pl.when(place.end)
            def _():
                ended(j, lambda: end_down(j).wait_send())
                far_out(j).wait_recv()

            pair_last(j).wait()

        def stage_6(j):
            @pl.when(place.mid)
            def _():
                def onward():
                    end_back(j).wait()
                    end_out(j).start()

                ended(j, onward)

        def stage_7(j):
            pl.when(place.mid)(lambda: ended(j, lambda: end_out(j).wait_send()))
            pl.when(place.end)(lambda: ended(j, lambda: end_out(j).wait_recv()))

        stages = (stage_0, stage_1, stage_2, stage_3, stage_4, stage_5, stage_6, stage_7)
        for number in range(len(stages)):
            j = t - number * LAG
            pl.when(jnp.logical_and(j >= 0, j < self.chunks))(
                functools.partial(stages[number], j)
            )

    def ticks(self):
        return self.chunks + max(5 * LAG, 7 * LAG - SHORT_CHUNKS)


def page_kernel(sizes, *refs):
    far, refs = refs[:ARGS], refs[ARGS:]
    (hidden_out, grad_embeddings, grads), refs = refs[:3], refs[3:]
    close, refs = refs[:ARGS], refs[ARGS:]
    (
        embeddings,
        replace_table,
        replace_ids,
        masked,
        padding,
        w_qkv,
        b_qv,
        w_out,
        b_out,
        first_gain,
        first_shift,
        w_in,
        b_in,
        w_down,
        b_down,
        second_gain,
        second_shift,
        cotangent,
    ) = close
    (
        inputs_low,
        queries,
        keys,
        values,
        log_total,
        heads,
        normed_low,
        hidden,
        active,
        zhat_one,
        scale_one,
        zhat_two,
        scale_two,
        w_all,
        shared_heads,
        columns,
        own_a,
        own_b,
        part,
        land_core,
        land_y,
        land_back,
        land_small,
        dz_low,
        du_low,
        dheads,
        dkeys,
        dvalues,
        dqkv_low,
        sums,
        local_sums,
        land_wide,
        land_both,
        land_narrow,
        core_send,
        core_recv,
        y_send,
        y_recv,
        back_send,
        back_recv,
        small_send,
        small_recv,
        dp_send,
        dp_recv,
        dp_one_way,
        dp_short_way,
        dp_first_send,
        dp_first_recv,
        gather_send,
        gather_recv,
        hand_send,
        hand_recv,
        heads_send,
        heads_recv,
        close_sem,
    ) = refs
    width, hidden_width, local_heads, span = sizes
    head_width = local_heads * HEAD_DIM
    place = Place()
    core = place.core
    barrier = pltpu.get_barrier_semaphore()
    greet(place, barrier)

    def fetch(index):
        return pltpu.make_async_copy(far[index], close[index], close_sem.at[index])

    def weight(which, layer):
        index = WEIGHTS[which]
        return pltpu.make_async_copy(
            far[index].at[layer],
            close[index].at[layer],
            close_sem.at[index + layer * (ARGS - index) + layer * which],
        )

    weight(1, 0).start()
    fetch(0).start()
    weight(0, 0).start()
    for index in SHORT_ARGS:
        fetch(index).start()
    tail_base = LAYERS * span - HEAD_DIM + HOLE
    small_base = tail_base + CHUNK
    assert tail_base % CHUNK == 0 and span % HEAD_DIM == 0
    chunks = grads.shape[0] // CHUNK
    grad_sum = GradientSum(place, chunks, grads, land_wide, land_both, land_narrow, dp_send, dp_recv, dp_one_way, dp_short_way, dp_first_send, dp_first_recv)
    tick = grad_sum.tick

    def vector(ref, layer):
        both = ref[...].astype(jnp.float32)
        return jnp.where(layer == 0, both[0:1], both[1:2])

    def block(b):
        return pl.ds(pl.multiple_of(b * BLOCK, BLOCK), BLOCK)

    def segment(b, size, half):
        return pl.ds(pl.multiple_of(half * HALF + b * size, size), size)

    def kept(b, size):
        return segment(b, size, core)

    def given(b, size):
        return segment(b, size, 1 - core)

    def packed(b, size):
        return segment(b, size, 0)

    def halves(b, size):
        return segment(b, size, 0), segment(b, size, 1)

    def lanes(p, size=128):
        return pl.ds(pl.multiple_of(p * size, size), size)

    def remote(source, target, send, recv, device):
        return pltpu.make_async_remote_copy(
            src_ref=source,
            dst_ref=target,
            send_sem=send,
            recv_sem=recv,
            device_id=device,
            device_id_type=MESH,
        )

    def to_core(turn, b, size):
        return remote(
            part.at[given(b, size)],
            land_core.at[turn, packed(b, size)],
            core_send.at[turn, b],
            core_recv.at[turn, b],
            place.core_peer,
        )

    def over_y(turn, b, size):
        return remote(
            part.at[kept(b, size)],
            land_y.at[turn, packed(b, size)],
            y_send.at[turn, b],
            y_recv.at[turn, b],
            place.y_peer,
        )

    def to_other(turn, b, size, source):
        return remote(
            source.at[packed(b, size)],
            land_back.at[turn, packed(b, size)],
            back_send.at[turn, b],
            back_recv.at[turn, b],
            place.core_peer,
        )

    def send_y(turn, b, size):
        to_core(turn, b, size).wait()
        rows = kept(b, size)
        part[rows, :] = part[rows, :] + land_core[turn, packed(b, size), :]
        over_y(turn, b, size).start()

    def summed(turn, b, size):
        over_y(turn, b, size).wait()
        return part[kept(b, size), :] + land_y[turn, packed(b, size), :]

    def received(turn, b, size, source):
        to_other(turn, b, size, source).wait()
        return land_back[turn, packed(b, size), :].astype(jnp.bfloat16)

    def shard(which, layer):
        return (which * LAYERS + layer) * head_width

    def direct(layer):
        return pl.ds(shard(0, layer), DIRECT[layer]), pl.ds(shard(2, layer), DIRECT[layer])

    def piece_rows(which, layer, owner):
        size = (head_width - DIRECT[layer]) // GROUP
        first = shard(which, layer) + DIRECT[layer] + owner * size
        return pl.ds(pl.multiple_of(first, 8), size)

    def moving(source, target, index, device):
        return remote(
            grads.at[source], grads.at[target], gather_send.at[index], gather_recv.at[index], device
        )

    def whole(which, layer):
        return pl.ds(shard(which, layer), head_width)

    def own_shard(layer):
        return moving(whole(0, layer), whole(1, layer), layer, place.core_peer)

    def other_shard(layer):
        return moving(whole(2, layer), whole(3, layer), LAYERS + layer, place.core_peer)

    def piece_over(layer):
        return moving(
            piece_rows(0, layer, place.low),
            piece_rows(2, layer, place.low),
            2 * LAYERS + layer,
            place.y_peer,
        )

    def rest_over(layer):
        return moving(*direct(layer), 3 * LAYERS + layer, place.y_peer)

    def handed(layer, k):
        rows = piece_rows(2, layer, place.low)
        return pltpu.make_async_remote_copy(
            src_ref=grads.at[rows],
            dst_ref=grads.at[rows],
            send_sem=hand_send.at[layer, k],
            recv_sem=hand_recv.at[layer, place.low],
            device_id=place.others[k],
            device_id_type=MESH,
        )

    def handed_in(layer, k):
        owner = lax.rem(place.low + 1 + k, GROUP)
        rows = piece_rows(2, layer, owner)
        return pltpu.make_async_remote_copy(
            src_ref=grads.at[rows],
            dst_ref=grads.at[rows],
            send_sem=hand_send.at[layer, k],
            recv_sem=hand_recv.at[layer, owner],
            device_id=place.others[k],
            device_id_type=MESH,
        )

    def gather_first(layer):
        weight(1, layer).wait()
        grads[whole(0, layer), :] = w_out[layer].astype(jnp.float32)
        piece_over(layer).start()
        if DIRECT[layer]:
            rest_over(layer).start()
        own_shard(layer).start()

    def gather_second(layer):
        piece_over(layer).wait()
        for k in range(GROUP - 1):
            handed(layer, k).start()

    def gather_third(layer):
        for k in range(GROUP - 1):
            handed(layer, k).wait_send()
            handed_in(layer, k).wait_recv()
        if DIRECT[layer]:
            rest_over(layer).wait()
        other_shard(layer).start()

    def gather_last(layer):
        own_shard(layer).wait()
        other_shard(layer).wait()
        pairs_width = 2 * HEAD_DIM
        for which in range(4):
            source = which // 2
            owner = 2 * (place.y + source - 2 * place.y * source) + (
                core + which % 2 - 2 * core * (which % 2)
            )
            low = grads[whole(which, layer), :].astype(jnp.bfloat16)
            first = pl.multiple_of(owner * pairs_width, pairs_width)
            w_all[layer, pl.ds(first, pairs_width), :] = low[:pairs_width]
            first = pl.multiple_of(4 * pairs_width + owner * HEAD_DIM, HEAD_DIM)
            w_all[layer, pl.ds(first, HEAD_DIM), :] = low[pairs_width:]

    def heads_out(b):
        mine, theirs = shared_heads.at[core, b], shared_heads.at[1 - core, b]
        return [
            remote(
                source,
                shared_heads.at[2 + index, b],
                heads_send.at[index, b],
                heads_recv.at[index, b],
                device,
            )
            for index, (source, device) in enumerate(
                (
                    (theirs, place.core_peer),
                    (mine, place.y_peer),
                    (theirs, place.diagonal),
                )
            )
        ]

    def pack_heads(rows):
        cut = 2 * HEAD_DIM
        return jnp.concatenate(
            [
                rows[:, :cut],
                jnp.concatenate([rows[: SEG // 2, cut:], rows[SEG // 2 :, cut:]], axis=1),
            ],
            axis=0,
        )

    def all_heads(b):
        pairs, thirds = [], []
        for owner in range(4):
            side, half = owner // 2, owner % 2
            apart = 2 * (place.y + side - 2 * place.y * side) + (core + half - 2 * core * half)
            slot = jnp.where(apart == 0, core, apart + 1)
            low = shared_heads[slot, b].astype(jnp.bfloat16)
            pairs.append(low[:SEG])
            tail = low[SEG:]
            thirds.append(jnp.concatenate([tail[:, :HEAD_DIM], tail[:, HEAD_DIM:]], axis=0))
        return jnp.concatenate(pairs + thirds, axis=1)

    meet(barrier)
    gather_first(0)

    for index in SHORT_ARGS:
        fetch(index).wait()
    pad_row = padding[...].astype(jnp.float32)
    live_row = masked[...].astype(jnp.float32) * pad_row
    bias_row = (pad_row - 1.0) * 10000.0
    columns[:, 0:1] = column(live_row)
    columns[:, 1:2] = column(replace_ids[...].astype(jnp.float32))
    grads[small_base:, :] = jnp.zeros((CHUNK, width), jnp.float32)

    def chosen(rows, count):
        spots = lax.broadcasted_iota(jnp.int32, (count, REPL), 1).astype(jnp.float32)
        return jnp.where(columns[rows, 1:2] == spots, 1.0, 0.0)

    def first_input(b):
        rows = block(b)
        picked = matmul(chosen(rows, BLOCK).astype(jnp.bfloat16), replace_table[...])
        taken = jnp.where(
            columns[rows, 0:1] > 0.0, picked, embeddings[rows, :].astype(jnp.float32)
        )
        inputs_low[0, rows, :] = taken.astype(jnp.bfloat16)

    sums[...] = jnp.zeros_like(sums)
    local_sums[...] = jnp.zeros_like(local_sums)

    def project(layer, spans):
        bias_pair = vector(b_qv, layer)
        inputs = jnp.concatenate([inputs_low[layer, rows, :] for rows in spans], axis=0)
        projected = contract_cols(inputs, w_qkv[layer])

        def split(ref, h, columns_of):
            low = columns_of.astype(jnp.bfloat16)
            first = 0
            for rows in spans:
                ref[layer, h, rows, :] = low[first : first + rows.size]
                first += rows.size

        for h in range(local_heads):
            base = 3 * HEAD_DIM * h
            bias = 2 * HEAD_DIM * h
            split(
                queries,
                h,
                projected[:, base : base + HEAD_DIM] + bias_pair[:, bias : bias + HEAD_DIM],
            )
            split(keys, h, projected[:, base + HEAD_DIM : base + 2 * HEAD_DIM])
            split(
                values,
                h,
                projected[:, base + 2 * HEAD_DIM : base + 3 * HEAD_DIM]
                + bias_pair[:, bias + HEAD_DIM : bias + 2 * HEAD_DIM],
            )

    def scores_of(layer, h, query):
        return contract_cols(query, keys[layer, h]) * SCALE + bias_row

    def total_row(turn, index, amount):
        sums[turn, index : index + 1, :] = sums[turn, index : index + 1, :] + jnp.sum(
            amount, axis=0, keepdims=True
        )

    def norm_two(turn, b, size, grad):
        layer = LAYERS - 1 - turn
        rows = packed(b, size)
        zhat = zhat_two[layer, rows, :]
        dz = norm_back(grad, zhat, scale_two[layer, rows, :], vector(second_gain, layer))
        own_a[rows, :] = dz
        to_other(0, b, size, own_a).start()
        dz_low[kept(b, size), :] = dz.astype(jnp.bfloat16)
        total_row(turn, 0, grad * zhat)
        total_row(turn, 1, grad)
        total_row(turn, 2, dz)

    def forward(layer):
        last = layer == LAYERS - 1

        def attend(b):
            pl.when(jnp.logical_and(layer == 0, b == BLOCKS - 1))(lambda: gather_third(0))
            spans = halves(b, SEG)
            outs, logs = [], []
            all_scores = [
                scores_of(
                    layer,
                    h,
                    jnp.concatenate([queries[layer, h, rows, :] for rows in spans], axis=0),
                )
                for h in range(local_heads)
            ]
            all_probs = []
            for scores in all_scores:
                largest = jnp.max(scores, axis=-1, keepdims=True)
                weights_of = jnp.exp(scores - largest)
                totals = jnp.sum(weights_of, axis=-1, keepdims=True)
                all_probs.append((weights_of * (1.0 / totals)).astype(jnp.bfloat16))
                logs.append(largest + jnp.log(totals))
            for h, probs in enumerate(all_probs):
                outs.append(matmul(probs, values[layer, h]).astype(jnp.bfloat16))
            joined = jnp.concatenate(outs, axis=1)
            full = joined.astype(jnp.float32)
            for side in range(2):
                shared_heads[side, b] = pack_heads(full[side * SEG : (side + 1) * SEG])
            for copy in heads_out(b):
                copy.start()
            for side, rows in enumerate(spans):
                cut = slice(side * SEG, (side + 1) * SEG)
                heads[layer, rows, :] = joined[cut]
                for h in range(local_heads):
                    log_total[layer, rows, h : h + 1] = logs[h][cut]

        repeat(BLOCKS, attend)

        @pl.when(layer == 0)
        def _():
            gather_first(1)
            gather_last(0)

        pl.when(layer == 1)(lambda: gather_last(1))

        gain, shift, bias_out = (
            vector(first_gain, layer),
            vector(first_shift, layer),
            vector(b_out, layer),
        )
        bias_in = vector(b_in, layer)
        weight(2, layer).wait()
        weight(3, layer).wait()

        def feed_norm(b):
            rows = packed(b, SEG)
            for copy in heads_out(b):
                copy.wait()
            before = (
                inputs_low[layer, kept(b, SEG), :].astype(jnp.float32)
                + matmul(all_heads(b), w_all[layer])
                + bias_out
            )
            zhat, scale = normed(before)
            result = zhat * gain + shift
            own_a[rows, :] = result
            to_other(0, b, SEG, own_a).start()
            zhat_one[layer, rows, :] = zhat
            scale_one[layer, rows, :] = scale
            normed_low[layer, kept(b, SEG), :] = result.astype(jnp.bfloat16)

        def feed_main(b):
            spans = halves(b, SEG)
            normed_low[layer, given(b, SEG), :] = received(0, b, SEG, own_a)
            inputs = jnp.concatenate([normed_low[layer, rows, :] for rows in spans], axis=0)
            u = matmul(inputs, w_in[layer]) + bias_in
            g = (u * normal_cdf(u)).astype(jnp.bfloat16)
            lowered = matmul(g, w_down[layer])
            for side, rows in enumerate(spans):
                cut = slice(side * SEG, (side + 1) * SEG)
                part[rows, :] = lowered[cut]
                hidden[layer, rows, :] = u[cut]
                active[layer, rows, :] = g[cut]
            to_core(1, b, SEG).start()

        def feed(b):
            feed_norm(b)
            pl.when(b >= 1)(lambda: send_y(1, b - 1, SEG))
            feed_main(b)
            pl.when(jnp.logical_and(layer == 0, b == 0))(lambda: gather_second(1))

        repeat(BLOCKS, feed)
        send_y(1, BLOCKS - 1, SEG)

        gain_two, shift_two, bias_down = (
            vector(second_gain, layer),
            vector(second_shift, layer),
            vector(b_down, layer),
        )
        pl.when(jnp.logical_not(last))(lambda: weight(0, layer + 1).wait())

        def receive(b):
            inputs_low[layer + 1, given(b, SEG), :] = received(1, b, SEG, own_b)
            pl.when(jnp.logical_not(last))(lambda: project(layer + 1, halves(b, SEG)))

            @pl.when(last)
            def _():
                dz_low[given(b, SEG), :] = received(0, b, SEG, own_a)

        def finish(b):
            rows = packed(b, SEG)
            before = own_a[rows, :] + summed(1, b, SEG) + bias_down
            zhat, scale = normed(before)
            result = zhat * gain_two + shift_two
            own_b[rows, :] = result
            to_other(1, b, SEG, own_b).start()
            zhat_two[layer, rows, :] = zhat
            scale_two[layer, rows, :] = scale
            inputs_low[layer + 1, kept(b, SEG), :] = result.astype(jnp.bfloat16)

            @pl.when(last)
            def _():
                live = columns[kept(b, SEG), 0:1]
                norm_two(0, b, SEG, cotangent[kept(b, SEG), :].astype(jnp.float32) * live)

            pl.when(b >= 1)(lambda: receive(b - 1))

        repeat(BLOCKS, finish)
        receive(BLOCKS - 1)
        pl.when(layer == 0)(lambda: gather_third(1))

    fetch(0).wait()
    repeat(BACK_BLOCKS, first_input)
    fetch(ARGS - 1).start()
    for index, layer in ((1, 1), (2, 0), (3, 0), (0, 1), (2, 1), (3, 1)):
        weight(index, layer).start()
    weight(0, 0).wait()
    project(0, (block(0),))
    gather_second(0)
    repeat(BACK_BLOCKS - 1, lambda b: project(0, (block(b + 1),)))
    fetch(ARGS - 1).wait()
    repeat(LAYERS, forward)

    def last_grad(b, grad):
        rows = kept(b, BACK_SEG)
        live = columns[rows, 0:1]
        masked_grad = grad * (1.0 - live)
        own_a[packed(b, BACK_SEG), :] = masked_grad
        to_other(0, b, BACK_SEG, own_a).start()
        grad_embeddings[rows, :] = masked_grad.astype(jnp.bfloat16)
        grads[small_base : small_base + REPL, :] = grads[
            small_base : small_base + REPL, :
        ] + lax.dot_general(
            chosen(rows, BACK_SEG),
            grad * live,
            (((0,), (0,)), ((), ())),
            precision=lax.Precision.HIGHEST,
            preferred_element_type=jnp.float32,
        )

    def backward(turn):
        layer = LAYERS - 1 - turn
        base = turn * span
        start = turn * (span // CHUNK)
        last = turn == LAYERS - 1
        in_base = base + hidden_width
        out_base = in_base + width
        qkv_base = out_base + head_width

        def rows_at(first, count):
            return pl.ds(pl.multiple_of(first, 16), count)

        def down_piece(p):
            grads[rows_at(base + 128 * p, 128), :] = contract_rows(
                active[layer, :, lanes(p)], dz_low[...]
            )

        def in_piece(p):
            grads[rows_at(in_base + 128 * p, 128), :] = contract_rows(
                normed_low[layer, :, lanes(p)], du_low[...]
            )

        down_piece(0)
        tick(start)

        def feed(b):
            rows = block(b)
            dg = contract_cols(dz_low[rows, :], w_down[layer])
            u = hidden[layer, rows, :]
            density = jnp.exp(u * u * (-0.5)) * (1.0 / math.sqrt(2.0 * math.pi))
            du = dg * (normal_cdf(u) + u * density)
            du_low[rows, :] = du.astype(jnp.bfloat16)
            local_sums[turn, 0:1, :] = local_sums[turn, 0:1, :] + jnp.sum(
                du, axis=0, keepdims=True
            )
            down_piece(b + 1)
            tick(start + 1 + b)

        repeat(BACK_BLOCKS, feed)
        down_piece(5)

        def feed_in(b):
            spans = halves(b, BACK_SEG)
            left = jnp.concatenate([du_low[rows, :] for rows in spans], axis=0)
            result = contract_cols(left, w_in[layer])
            for side, rows in enumerate(spans):
                part[rows, :] = result[side * BACK_SEG : (side + 1) * BACK_SEG]
            to_core(0, b, BACK_SEG).start()
            pl.when(b >= 1)(lambda: send_y(0, b - 1, BACK_SEG))
            tick(start + 5 + b)

        repeat(BACK_BLOCKS, feed_in)
        send_y(0, BACK_BLOCKS - 1, BACK_SEG)

        def early_piece(p):
            in_piece(p)
            tick(start + 9 + p)

        repeat(4, early_piece)
        in_piece(4)

        gain = vector(first_gain, layer)

        def norm_one(b):
            rows = packed(b, BACK_SEG)
            grad = own_a[rows, :] + summed(0, b, BACK_SEG)
            zhat = zhat_one[layer, rows, :]
            dz = norm_back(grad, zhat, scale_one[layer, rows, :], gain)
            own_b[rows, :] = dz
            to_other(1, b, BACK_SEG, own_b).start()
            dz_low[kept(b, BACK_SEG), :] = dz.astype(jnp.bfloat16)
            total_row(turn, 3, grad * zhat)
            total_row(turn, 4, grad)
            total_row(turn, 5, dz)
            tick(start + 13 + b)
            dz_low[given(b, BACK_SEG), :] = received(1, b, BACK_SEG, own_b)

        repeat(BACK_BLOCKS, norm_one)
        grads[rows_at(out_base, head_width), :] = contract_rows(heads[layer], dz_low[...])
        dheads[...] = contract_cols(dz_low[...], w_out[layer]).astype(jnp.bfloat16)
        in_piece(5)
        tick(start + 17)
        dkeys[...] = jnp.zeros_like(dkeys)
        dvalues[...] = jnp.zeros_like(dvalues)

        def attend(b):
            rows = block(b)
            for h in range(local_heads):
                side = HEAD_DIM * h
                query = queries[layer, h, rows, :]
                probs = jnp.exp(scores_of(layer, h, query) - log_total[layer, rows, h : h + 1])
                dhead = dheads[rows, side : side + HEAD_DIM]
                dprobs = contract_cols(dhead, values[layer, h])
                dvalues[h] = dvalues[h] + contract_rows(probs.astype(jnp.bfloat16), dhead)
                inner = jnp.sum(probs * dprobs, axis=-1, keepdims=True)
                ds = (probs * (dprobs - inner)).astype(jnp.bfloat16)
                dq = matmul(ds, keys[layer, h]) * SCALE
                dkeys[h] = dkeys[h] + contract_rows(ds, query)
                dqkv_low[rows, 3 * side : 3 * side + HEAD_DIM] = dq.astype(jnp.bfloat16)
                local_sums[turn, 1:2, 2 * side : 2 * side + HEAD_DIM] = local_sums[
                    turn, 1:2, 2 * side : 2 * side + HEAD_DIM
                ] + jnp.sum(dq, axis=0, keepdims=True)
            pl.when(b < BACK_BLOCKS - 1)(lambda: tick(start + 18 + b))

        repeat(BACK_BLOCKS, attend)
        for h in range(local_heads):
            side = HEAD_DIM * h
            dqkv_low[:, 3 * side + HEAD_DIM : 3 * side + 2 * HEAD_DIM] = (
                dkeys[h] * SCALE
            ).astype(jnp.bfloat16)
            dv = dvalues[h]
            dqkv_low[:, 3 * side + 2 * HEAD_DIM : 3 * side + 3 * HEAD_DIM] = dv.astype(
                jnp.bfloat16
            )
            local_sums[turn, 1:2, 2 * side + HEAD_DIM : 2 * side + 2 * HEAD_DIM] = jnp.sum(
                dv, axis=0, keepdims=True
            )

        def back_project(b):
            grads[rows_at(qkv_base + 128 * b, 128), :] = contract_rows(
                dqkv_low[:, lanes(b)], inputs_low[layer]
            )
            spans = halves(b, BACK_SEG)
            left = jnp.concatenate([dqkv_low[rows, :] for rows in spans], axis=0)
            result = matmul(left, w_qkv[layer])
            for side, rows in enumerate(spans):
                part[rows, :] = result[side * BACK_SEG : (side + 1) * BACK_SEG]
            to_core(1, b, BACK_SEG).start()
            pl.when(b >= 1)(lambda: send_y(1, b - 1, BACK_SEG))
            tick(start + 21 + b)

        repeat(BACK_BLOCKS, back_project)
        send_y(1, BACK_BLOCKS - 1, BACK_SEG)

        tail = jnp.where(last, HOLE, 0)
        grads[rows_at(qkv_base + 512 + tail, HEAD_DIM), :] = contract_rows(
            dqkv_low[:, 512:], inputs_low[layer]
        )
        tick(start + 25)

        def pass_on(b):
            rows = packed(b, BACK_SEG)
            grad = own_b[rows, :] + summed(1, b, BACK_SEG)
            pl.when(jnp.logical_not(last))(lambda: norm_two(turn + 1, b, BACK_SEG, grad))
            pl.when(last)(lambda: last_grad(b, grad))
            pl.when(jnp.logical_or(last, b < 2))(lambda: tick(start + 26 + b))

        repeat(BACK_BLOCKS, pass_on)

        def receive(b):
            dz_low[given(b, BACK_SEG), :] = received(0, b, BACK_SEG, own_a)

        pl.when(jnp.logical_not(last))(lambda: repeat(BACK_BLOCKS, receive))

    repeat(LAYERS, backward)
    hidden_out[...] = inputs_low[LAYERS]

    shared = REPL + 8 * LAYERS
    for turn in range(LAYERS):
        first = small_base + REPL + 8 * turn
        grads[first : first + 8, :] = sums[turn]
    grads[small_base + shared : small_base + shared + 8, :] = local_sums[...].reshape(8, width)
    short = remote(
        grads.at[pl.ds(small_base, shared)], land_small, small_send, small_recv, place.core_peer
    )
    short.start()

    def receive_grad(b):
        grad_embeddings[given(b, BACK_SEG), :] = received(0, b, BACK_SEG, own_a)

    repeat(BACK_BLOCKS, receive_grad)
    short.wait()
    grads[small_base : small_base + shared, :] = (
        grads[small_base : small_base + shared, :] + land_small[...]
    )
    done = chunks - 1
    repeat(grad_sum.ticks() - done, lambda i: tick(done + i))


def run_pages(args, sizes):
    width, hidden_width, local_heads, span = sizes
    rows = PAGE_LEN
    flat = LAYERS * span - HEAD_DIM + HOLE + 2 * CHUNK
    half = rows // 2
    low, full = jnp.bfloat16, jnp.float32
    vmem, dma = pltpu.VMEM, pltpu.SemaphoreType.DMA
    head_width = local_heads * HEAD_DIM
    return pl.pallas_call(
        functools.partial(page_kernel, sizes),
        name="pages",
        out_shape=(
            vmem((rows, width), low),
            vmem((rows, width), low),
            vmem((flat, width), full),
        ),
        in_specs=[pl.BlockSpec(memory_space=pl.ANY)] * ARGS,
        out_specs=(
            pl.BlockSpec(memory_space=pltpu.VMEM),
            pl.BlockSpec(memory_space=pltpu.VMEM),
            pl.BlockSpec(memory_space=pltpu.VMEM),
        ),
        scratch_shapes=[
            *[vmem(arg.shape, arg.dtype) for arg in args],
            vmem((LAYERS + 1, rows, width), low),
            vmem((LAYERS, local_heads, rows, HEAD_DIM), low),
            vmem((LAYERS, local_heads, rows, HEAD_DIM), low),
            vmem((LAYERS, local_heads, rows, HEAD_DIM), low),
            vmem((LAYERS, rows, 128), full),
            vmem((LAYERS, rows, head_width), low),
            vmem((LAYERS, rows, width), low),
            vmem((LAYERS, rows, hidden_width), full),
            vmem((LAYERS, rows, hidden_width), low),
            vmem((LAYERS, half, width), full),
            vmem((LAYERS, half, 1), full),
            vmem((LAYERS, half, width), full),
            vmem((LAYERS, half, 1), full),
            vmem((LAYERS, 4 * head_width, width), low),
            vmem((5, BLOCKS, 3 * SEG // 2, 2 * HEAD_DIM), full),
            vmem((rows, 128), full),
            vmem((half, width), full),
            vmem((half, width), full),
            vmem((rows, width), full),
            vmem((2, half, width), full),
            vmem((2, half, width), full),
            vmem((2, half, width), full),
            vmem((REPL + 8 * LAYERS, width), full),
            vmem((rows, width), low),
            vmem((rows, hidden_width), low),
            vmem((rows, head_width), low),
            vmem((local_heads, rows, HEAD_DIM), full),
            vmem((local_heads, rows, HEAD_DIM), full),
            vmem((rows, 3 * head_width), low),
            vmem((LAYERS, 8, width), full),
            vmem((LAYERS, 4, width), full),
            vmem((len(WIDE_LANDINGS), SLOTS, WIDE, width), full),
            vmem((SLOTS, 2 * NARROW, width), full),
            vmem((len(NARROW_LANDINGS), SLOTS, NARROW, width), full),
            dma((2, BLOCKS)),
            dma((2, BLOCKS)),
            dma((2, BLOCKS)),
            dma((2, BLOCKS)),
            dma((2, BLOCKS)),
            dma((2, BLOCKS)),
            dma,
            dma,
            dma((len(EQUALS), EQUAL_SLOTS)),
            dma((len(EQUALS), EQUAL_SLOTS)),
            dma((len(ONE_WAY), SLOTS)),
            dma((len(SHORT_WAY), EQUAL_SLOTS)),
            dma((SLOTS,)),
            dma((SLOTS,)),
            dma((4 * LAYERS,)),
            dma((4 * LAYERS,)),
            dma((LAYERS, GROUP)),
            dma((LAYERS, GROUP)),
            dma((3, BLOCKS)),
            dma((3, BLOCKS)),
            dma((ARGS + (LAYERS - 1) * len(WEIGHTS),)),
        ],
        compiler_params=pltpu.CompilerParams(
            collective_id=0, has_side_effects=True, vmem_limit_bytes=46 << 20
        ),
    )(*args)


def place_kernel(sizes, hidden_out, grad_embeddings, every, *refs):
    width, hidden_width, local_heads, span = sizes
    head_width = local_heads * HEAD_DIM
    (
        out_hidden,
        out_embeddings,
        out_table,
        out_w_qkv,
        out_b_qv,
        out_w_out,
        out_b_out,
        out_first_gain,
        out_first_shift,
        out_w_in,
        out_b_in,
        out_w_down,
        out_b_down,
        out_second_gain,
        out_second_shift,
        short,
        shorts,
        sems,
    ) = refs
    tail = LAYERS * span - HEAD_DIM
    base = tail + HOLE + CHUNK
    pairs = [(every.at[pl.ds(base, CHUNK)], short), (every.at[pl.ds(base, REPL)], out_table)]
    pairs += [(hidden_out, out_hidden), (grad_embeddings, out_embeddings)]
    for turn in range(LAYERS):
        first = span * turn
        for ref, rows in (
            (out_w_down, hidden_width),
            (out_w_in, width),
            (out_w_out, head_width),
            (out_w_qkv, 3 * head_width),
        ):
            target = ref.at[LAYERS - 1 - turn]
            direct = min(rows, tail - first)
            pairs.append((every.at[pl.ds(first, direct)], target.at[pl.ds(0, direct)]))
            if direct < rows:
                pairs.append(
                    (
                        every.at[pl.ds(tail + HOLE, rows - direct)],
                        target.at[pl.ds(direct, rows - direct)],
                    )
                )
            first += rows
    copies = [
        pltpu.make_async_copy(source, target, sems.at[index])
        for index, (source, target) in enumerate(pairs)
    ]
    for copy in copies:
        copy.start()
    copies[0].wait()
    pieces = []
    local = REPL + 8 * LAYERS
    for index, (ref, row, step) in enumerate((
        (out_second_gain, REPL, 8),
        (out_second_shift, REPL + 1, 8),
        (out_b_down, REPL + 2, 8),
        (out_first_gain, REPL + 3, 8),
        (out_first_shift, REPL + 4, 8),
        (out_b_out, REPL + 5, 8),
        (out_b_in, local, 4),
        (out_b_qv, local + 1, 4),
    )):
        for turn in range(LAYERS):
            layer = LAYERS - 1 - turn
            shorts[index, layer : layer + 1, :] = short[
                row + step * turn : row + step * turn + 1, :
            ]
        piece = pltpu.make_async_copy(
            shorts.at[index, :, pl.ds(0, ref.shape[1])], ref, sems.at[len(copies) + index]
        )
        piece.start()
        pieces.append(piece)
    for copy in copies[1:] + pieces:
        copy.wait()


def place_outputs(hidden_out, grad_embeddings, every, sizes):
    width, hidden_width, local_heads, span = sizes
    head_width = local_heads * HEAD_DIM
    low, full = jnp.bfloat16, jnp.float32
    rows = hidden_out.shape[0]
    shapes = (
        ((rows, width), low),
        ((rows, width), low),
        ((REPL, width), full),
        ((LAYERS, 3 * head_width, width), full),
        ((LAYERS, 2 * head_width), full),
        ((LAYERS, head_width, width), full),
        ((LAYERS, width), full),
        ((LAYERS, width), full),
        ((LAYERS, width), full),
        ((LAYERS, width, hidden_width), full),
        ((LAYERS, hidden_width), full),
        ((LAYERS, hidden_width, width), full),
        ((LAYERS, width), full),
        ((LAYERS, width), full),
        ((LAYERS, width), full),
    )
    far = pl.BlockSpec(memory_space=pl.ANY)
    return pl.pallas_call(
        functools.partial(place_kernel, sizes),
        name="place_outputs",
        out_shape=[jax.ShapeDtypeStruct(shape, kind) for shape, kind in shapes],
        in_specs=[far] * 3,
        out_specs=[far] * len(shapes),
        scratch_shapes=[
            pltpu.VMEM((CHUNK, width), full),
            pltpu.VMEM((8, LAYERS, width), full),
            pltpu.SemaphoreType.DMA((13 + 4 * LAYERS,)),
        ],
        compiler_params=pltpu.CompilerParams(vmem_limit_bytes=4 << 20),
    )(hidden_out, grad_embeddings, every)


def moved(every):
    def kernel(source, target, sem):
        copy = pltpu.make_async_copy(source, target, sem)
        copy.start()
        copy.wait()

    far = pl.BlockSpec(memory_space=pl.ANY)
    return pl.pallas_call(
        kernel,
        name="moved",
        out_shape=jax.ShapeDtypeStruct(every.shape, every.dtype),
        in_specs=[far],
        out_specs=far,
        scratch_shapes=[pltpu.SemaphoreType.DMA],
        compiler_params=pltpu.CompilerParams(vmem_limit_bytes=4 << 20),
    )(every)


def on_device(*args):
    (embeddings, replace_table, replace_ids, masked, padding, w_qkv, b_qv, *_) = args
    width = embeddings.shape[1]
    head_width = w_qkv.shape[2] // 3
    hidden_width = args[11].shape[2]
    span = 2 * hidden_width + 4 * head_width
    args = list(args)
    args[5] = jnp.swapaxes(args[5], 1, 2)
    for index in (2, 3, 4):
        args[index] = args[index].reshape(1, PAGE_LEN)
    sizes = (width, hidden_width, head_width // HEAD_DIM, span)
    hidden_out, grad_embeddings, every = run_pages(args, sizes)
    groups = lax.axis_size("dp") // GROUP
    if groups > 1:
        every = lax.psum(
            moved(every),
            "dp",
            axis_index_groups=[
                [low + GROUP * high for high in range(groups)] for low in range(GROUP)
            ],
        )

    results = place_outputs(hidden_out, grad_embeddings, every, sizes)
    return (*results[:3], jnp.swapaxes(results[3], 1, 2), *results[4:])


def solution(mesh):
    placed = (
        P("dp", None),
        P(),
        P("dp"),
        P("dp"),
        P("dp"),
        P(None, None, "tensor"),
        P(None, "tensor"),
        P(None, "tensor", None),
        P(),
        P(),
        P(),
        P(None, None, "tensor"),
        P(None, "tensor"),
        P(None, "tensor", None),
        P(),
        P(),
        P(),
        P("dp", None),
    )
    return jax.shard_map(
        on_device,
        mesh=mesh,
        in_specs=placed,
        out_specs=(
            P("dp", None),
            P("dp", None),
            P(),
            P(None, None, "tensor"),
            P(None, "tensor"),
            P(None, "tensor", None),
            P(),
            P(),
            P(),
            P(None, None, "tensor"),
            P(None, "tensor"),
            P(None, "tensor", None),
            P(),
            P(),
            P(),
        ),
        check_vma=False,
    )
```

```python
import functools
import math

import jax
import jax.numpy as jnp
from jax import lax
from jax.experimental import pallas as pl
from jax.experimental.pallas import tpu as pltpu
from jax.sharding import PartitionSpec as P

HEAD_DIM = 64
LAYERS = 2
PAGE_LEN = 512
REPL = 32
EPSILON = 1e-12
SCALE = HEAD_DIM ** (-0.5)
MESH = pl.DeviceIdType.MESH

HALF = PAGE_LEN // 2
SEG = 64
BLOCKS = HALF // SEG
BACK_SEG = 64
BACK_BLOCKS = HALF // BACK_SEG
BLOCK = 2 * BACK_SEG

WIDE = 24
NARROW = 8
CHUNK = 2 * WIDE + 4 * NARROW
HOLE = 2 * NARROW
SHORT_CHUNKS = 3
LAG = 2
SLOTS = 4 * LAG
EQUAL_SLOTS = 3 * LAG
EQUALS = (TA2, TQ1, TQ2, TR1, TTM, TG, TR5) = range(7)
ONE_WAY = (TA1, TTA, TQ0, TR0, TTN, TR6) = range(7, 13)
SHORT_WAY = (TR2, TTF, TR4) = range(13, 16)
TX, TR3 = 16, 17
WIDE_LANDINGS = (TX, TA1, TA2, TTA)
NARROW_LANDINGS = (TQ1, TQ2, TR0, TR1, TR2, TR3)
GROUP = 8
ARGS = 18
WEIGHTS = (5, 7, 11, 13)
SHORT_ARGS = tuple(index for index in range(1, ARGS - 1) if index not in WEIGHTS)
DIRECT = (64, 0)


def contract_rows(left, right):
    return lax.dot_general(
        left, right, (((0,), (0,)), ((), ())), preferred_element_type=jnp.float32
    )


def contract_cols(left, right):
    return lax.dot_general(
        left, right, (((1,), (1,)), ((), ())), preferred_element_type=jnp.float32
    )


def matmul(left, right):
    return jnp.dot(left, right, preferred_element_type=jnp.float32)


def repeat(count, body):
    def step(index, carry):
        body(index)
        return carry

    lax.fori_loop(0, count, step, 0)


def normed(values):
    average = jnp.mean(values, axis=-1, keepdims=True)
    centered = values - average
    variance = jnp.mean(centered * centered, axis=-1, keepdims=True)
    scale = lax.rsqrt(variance + EPSILON)
    return centered * scale, scale


def norm_back(grad, zhat, scale, gain):
    scaled = grad * gain
    average = jnp.mean(scaled, axis=-1, keepdims=True)
    along = jnp.mean(scaled * zhat, axis=-1, keepdims=True)
    return scale * (scaled - average - zhat * along)


def normal_cdf(values):
    return 0.5 * (1.0 + lax.erf(values * math.sqrt(0.5)))


def column(row):
    return jnp.transpose(jnp.broadcast_to(row, (128, row.shape[1])))[:, :1]


class Place:
    def __init__(self):
        d = lax.axis_index("dp")
        t = lax.axis_index("tensor")
        self.core = lax.rem(t, 2)
        self.core_peer = (d, t + 1 - 2 * self.core)
        self.y_peer = (d, t + 2 - 4 * lax.div(t, 2))
        self.diagonal = (d, t + 3 - 2 * self.core - 4 * lax.div(t, 2))
        self.y = lax.div(t, 2)
        self.low = lax.rem(d, GROUP)
        self.others = [
            (d - self.low + lax.rem(self.low + k, GROUP), t) for k in range(1, GROUP)
        ]
        pair = lax.rem(d, 2)
        line = lax.rem(lax.div(d, 2), 4)
        self.pair = pair
        self.mid = jnp.logical_or(line == 1, line == 2)
        self.end = jnp.logical_not(self.mid)
        self.upper = lax.div(line, 2)
        self.peer = (d + 1 - 2 * pair, t)
        self.line = (d + 2 - 4 * lax.rem(line, 2), t)
        self.cross = (jnp.where(line == 1, d + 2, d - 2), t)


def greet(place, barrier):
    def signal(device):
        pl.semaphore_signal(barrier, inc=1, device_id=device, device_id_type=MESH)

    for device in (place.core_peer, place.y_peer, place.diagonal, *place.others):
        signal(device)


def meet(barrier):
    pl.semaphore_wait(barrier, 2 + GROUP)


class GradientSum:
    def __init__(self, place, chunks, part, wide, both, narrow, send, recv, one_way, short_way, first_send, first_recv):
        self.place = place
        self.chunks = chunks
        self.part = part
        self.wide = wide
        self.both = both
        self.narrow = narrow
        self.send = send
        self.recv = recv
        self.one_way = one_way
        self.short_way = short_way
        self.first_send = first_send
        self.first_recv = first_recv

    def wide_rows(self, j, unit):
        return pl.ds(pl.multiple_of(j * CHUNK + unit * WIDE, NARROW), WIDE)

    def narrow_rows(self, j, unit, count=1):
        first = j * CHUNK + 2 * WIDE + unit * NARROW
        return pl.ds(pl.multiple_of(first, NARROW), count * NARROW)

    def tick(self, t):
        place, part = self.place, self.part
        mine, other = place.pair, 1 - place.pair
        near, far = place.upper, 1 - place.upper
        near_end, far_end = 2 + place.upper, 3 - place.upper

        def copy(kind, j, rows, target, device):
            if kind == TX:
                slot = lax.rem(j, SLOTS)
                send, recv = self.first_send.at[slot], self.first_recv.at[slot]
            elif kind in EQUALS or kind == TR3:
                slot, index = lax.rem(j, EQUAL_SLOTS), TQ2 if kind == TR3 else kind
                send, recv = self.send.at[index, slot], self.recv.at[index, slot]
            elif kind in ONE_WAY:
                send = recv = self.one_way.at[kind - len(EQUALS), lax.rem(j, SLOTS)]
            else:
                index = kind - len(EQUALS) - len(ONE_WAY)
                send = recv = self.short_way.at[index, lax.rem(j, EQUAL_SLOTS)]
            return pltpu.make_async_remote_copy(
                src_ref=part.at[rows],
                dst_ref=target,
                send_sem=send,
                recv_sem=recv,
                device_id=device,
                device_id_type=MESH,
            )

        def wide_slot(kind, j):
            return WIDE_LANDINGS.index(kind), lax.rem(j, SLOTS)

        def narrow_slot(kind, j):
            return NARROW_LANDINGS.index(kind), lax.rem(j, SLOTS)

        def wide_part(kind, j, unit, device):
            return copy(
                kind, j, self.wide_rows(j, unit), self.wide.at[wide_slot(kind, j)], device
            )

        def narrow_part(kind, j, unit, device):
            return copy(
                kind, j, self.narrow_rows(j, unit), self.narrow.at[narrow_slot(kind, j)], device
            )

        def final(kind, j, rows, device):
            return copy(kind, j, rows, part.at[rows], device)

        def add_wide(kind, j, unit):
            rows = self.wide_rows(j, unit)
            part[rows, :] = part[rows, :] + self.wide[wide_slot(kind, j)]

        def add_narrow(kind, j, unit):
            rows = self.narrow_rows(j, unit)
            part[rows, :] = part[rows, :] + self.narrow[narrow_slot(kind, j)]

        def pair_first(j):
            return wide_part(TX, j, other, place.peer)

        def mine_in(j):
            return wide_part(TA1, j, mine, place.line)

        def mine_across(j):
            return wide_part(TA2, j, mine, place.cross)

        def mine_out(j):
            return wide_part(TTA, j, mine, place.line)

        def pair_last(j):
            return final(TG, j, self.wide_rows(j, mine), place.peer)

        def both_in(j):
            rows = self.narrow_rows(j, 0, 2)
            return copy(TQ0, j, rows, self.both.at[lax.rem(j, SLOTS)], place.line)

        def far_across(j):
            return narrow_part(TQ1, j, far, place.cross)

        def near_pair(j):
            return narrow_part(TQ2, j, near, place.peer)

        def near_out(j):
            return final(TTN, j, self.narrow_rows(j, near), place.line)

        def near_across(j):
            return final(TTM, j, self.narrow_rows(j, near), place.cross)

        def far_out(j):
            return final(TTF, j, self.narrow_rows(j, far), place.line)

        def end_in(j):
            return narrow_part(TR0, j, far_end, place.line)

        def end_across(j):
            return narrow_part(TR1, j, far_end, place.cross)

        def end_up(j):
            return narrow_part(TR2, j, near_end, place.line)

        def end_pair(j):
            return narrow_part(TR3, j, near_end, place.peer)

        def end_down(j):
            return final(TR4, j, self.narrow_rows(j, near_end), place.line)

        def end_back(j):
            return final(TR5, j, self.narrow_rows(j, near_end), place.cross)

        def end_out(j):
            return final(TR6, j, self.narrow_rows(j, far_end), place.line)

        def ended(j, body):
            pl.when(j < self.chunks - SHORT_CHUNKS)(body)

        def stage_0(j):
            pair_first(j).start()

            @pl.when(place.end)
            def _():
                ended(j, lambda: end_in(j).start())
                both_in(j).start()

        def stage_1(j):
            pair_first(j).wait()

            @pl.when(place.end)
            def _():
                both_in(j).wait_send()
                ended(j, lambda: end_in(j).wait_send())
                add_wide(TX, j, mine)
                mine_in(j).start()

            @pl.when(place.mid)
            def _():
                def onward():
                    end_in(j).wait_recv()
                    add_narrow(TR0, j, far_end)
                    end_across(j).start()

                ended(j, onward)
                both_in(j).wait_recv()
                rows = self.narrow_rows(j, 0, 2)
                part[rows, :] = part[rows, :] + self.both[lax.rem(j, SLOTS)]
                far_across(j).start()
                add_wide(TX, j, mine)

        def stage_2(j):
            @pl.when(place.end)
            def _():
                mine_in(j).wait_send()

            @pl.when(place.mid)
            def _():
                mine_in(j).wait_recv()
                far_across(j).wait()

                def onward():
                    end_across(j).wait()
                    add_narrow(TR1, j, near_end)
                    end_up(j).start()

                ended(j, onward)
                add_narrow(TQ1, j, near)
                near_pair(j).start()
                add_wide(TA1, j, mine)
                mine_across(j).start()

        def stage_3(j):
            @pl.when(place.end)
            def _():
                def onward():
                    end_up(j).wait_recv()
                    add_narrow(TR2, j, near_end)
                    end_pair(j).start()

                ended(j, onward)

            @pl.when(place.mid)
            def _():
                ended(j, lambda: end_up(j).wait_send())
                mine_across(j).wait()
                add_wide(TA2, j, mine)
                mine_out(j).start()
                near_pair(j).wait()
                add_narrow(TQ2, j, near)
                near_across(j).start()
                near_out(j).start()

        def stage_4(j):
            @pl.when(place.mid)
            def _():
                near_across(j).wait()
                far_out(j).start()
                near_out(j).wait_send()
                mine_out(j).wait_send()
                pair_last(j).start()

            @pl.when(place.end)
            def _():
                mine_out(j).wait_recv()
                near_out(j).wait_recv()

                def onward():
                    end_pair(j).wait()
                    add_narrow(TR3, j, near_end)
                    end_down(j).start()

                ended(j, onward)
                part[self.wide_rows(j, mine), :] = self.wide[wide_slot(TTA, j)]
                pair_last(j).start()

        def stage_5(j):
            @pl.when(place.mid)
            def _():
                def onward():
                    end_down(j).wait_recv()
                    end_back(j).start()

                ended(j, onward)
                far_out(j).wait_send()

            @pl.when(place.end)
            def _():
                ended(j, lambda: end_down(j).wait_send())
                far_out(j).wait_recv()

            pair_last(j).wait()

        def stage_6(j):
            @pl.when(place.mid)
            def _():
                def onward():
                    end_back(j).wait()
                    end_out(j).start()

                ended(j, onward)

        def stage_7(j):
            pl.when(place.mid)(lambda: ended(j, lambda: end_out(j).wait_send()))
            pl.when(place.end)(lambda: ended(j, lambda: end_out(j).wait_recv()))

        stages = (stage_0, stage_1, stage_2, stage_3, stage_4, stage_5, stage_6, stage_7)
        for number in range(len(stages)):
            j = t - number * LAG
            pl.when(jnp.logical_and(j >= 0, j < self.chunks))(
                functools.partial(stages[number], j)
            )

    def ticks(self):
        return self.chunks + max(5 * LAG, 7 * LAG - SHORT_CHUNKS)


def page_kernel(sizes, *refs):
    far, refs = refs[:ARGS], refs[ARGS:]
    (hidden_out, grad_embeddings, grads), refs = refs[:3], refs[3:]
    close, refs = refs[:ARGS], refs[ARGS:]
    (
        embeddings,
        replace_table,
        replace_ids,
        masked,
        padding,
        w_qkv,
        b_qv,
        w_out,
        b_out,
        first_gain,
        first_shift,
        w_in,
        b_in,
        w_down,
        b_down,
        second_gain,
        second_shift,
        cotangent,
    ) = close
    (
        inputs_low,
        queries,
        keys,
        values,
        log_total,
        heads,
        normed_low,
        hidden,
        active,
        zhat_one,
        scale_one,
        zhat_two,
        scale_two,
        w_all,
        shared_heads,
        columns,
        own_a,
        own_b,
        part,
        land_core,
        land_y,
        land_back,
        land_small,
        dz_low,
        du_low,
        dheads,
        dkeys,
        dvalues,
        dqkv_low,
        sums,
        local_sums,
        land_wide,
        land_both,
        land_narrow,
        core_send,
        core_recv,
        y_send,
        y_recv,
        back_send,
        back_recv,
        small_send,
        small_recv,
        dp_send,
        dp_recv,
        dp_one_way,
        dp_short_way,
        dp_first_send,
        dp_first_recv,
        gather_send,
        gather_recv,
        hand_send,
        hand_recv,
        heads_send,
        heads_recv,
        close_sem,
    ) = refs
    width, hidden_width, local_heads, span = sizes
    head_width = local_heads * HEAD_DIM
    place = Place()
    core = place.core
    barrier = pltpu.get_barrier_semaphore()
    greet(place, barrier)

    def fetch(index):
        return pltpu.make_async_copy(far[index], close[index], close_sem.at[index])

    def weight(which, layer):
        index = WEIGHTS[which]
        return pltpu.make_async_copy(
            far[index].at[layer],
            close[index].at[layer],
            close_sem.at[index + layer * (ARGS - index) + layer * which],
        )

    weight(1, 0).start()
    fetch(0).start()
    weight(0, 0).start()
    for index in SHORT_ARGS:
        fetch(index).start()
    tail_base = LAYERS * span - HEAD_DIM + HOLE
    small_base = tail_base + CHUNK
    assert tail_base % CHUNK == 0 and span % HEAD_DIM == 0
    chunks = grads.shape[0] // CHUNK
    grad_sum = GradientSum(place, chunks, grads, land_wide, land_both, land_narrow, dp_send, dp_recv, dp_one_way, dp_short_way, dp_first_send, dp_first_recv)
    tick = grad_sum.tick

    def vector(ref, layer):
        both = ref[...].astype(jnp.float32)
        return jnp.where(layer == 0, both[0:1], both[1:2])

    def block(b):
        return pl.ds(pl.multiple_of(b * BLOCK, BLOCK), BLOCK)

    def segment(b, size, half):
        return pl.ds(pl.multiple_of(half * HALF + b * size, size), size)

    def kept(b, size):
        return segment(b, size, core)

    def given(b, size):
        return segment(b, size, 1 - core)

    def packed(b, size):
        return segment(b, size, 0)

    def halves(b, size):
        return segment(b, size, 0), segment(b, size, 1)

    def lanes(p, size=128):
        return pl.ds(pl.multiple_of(p * size, size), size)

    def remote(source, target, send, recv, device):
        return pltpu.make_async_remote_copy(
            src_ref=source,
            dst_ref=target,
            send_sem=send,
            recv_sem=recv,
            device_id=device,
            device_id_type=MESH,
        )

    def to_core(turn, b, size):
        return remote(
            part.at[given(b, size)],
            land_core.at[turn, packed(b, size)],
            core_send.at[turn, b],
            core_recv.at[turn, b],
            place.core_peer,
        )

    def over_y(turn, b, size):
        return remote(
            part.at[kept(b, size)],
            land_y.at[turn, packed(b, size)],
            y_send.at[turn, b],
            y_recv.at[turn, b],
            place.y_peer,
        )

    def to_other(turn, b, size, source):
        return remote(
            source.at[packed(b, size)],
            land_back.at[turn, packed(b, size)],
            back_send.at[turn, b],
            back_recv.at[turn, b],
            place.core_peer,
        )

    def send_y(turn, b, size):
        to_core(turn, b, size).wait()
        rows = kept(b, size)
        part[rows, :] = part[rows, :] + land_core[turn, packed(b, size), :]
        over_y(turn, b, size).start()

    def summed(turn, b, size):
        over_y(turn, b, size).wait()
        return part[kept(b, size), :] + land_y[turn, packed(b, size), :]

    def received(turn, b, size, source):
        to_other(turn, b, size, source).wait()
        return land_back[turn, packed(b, size), :].astype(jnp.bfloat16)

    def shard(which, layer):
        return (which * LAYERS + layer) * head_width

    def direct(layer):
        return pl.ds(shard(0, layer), DIRECT[layer]), pl.ds(shard(2, layer), DIRECT[layer])

    def piece_rows(which, layer, owner):
        size = (head_width - DIRECT[layer]) // GROUP
        first = shard(which, layer) + DIRECT[layer] + owner * size
        return pl.ds(pl.multiple_of(first, 8), size)

    def moving(source, target, index, device):
        return remote(
            grads.at[source], grads.at[target], gather_send.at[index], gather_recv.at[index], device
        )

    def whole(which, layer):
        return pl.ds(shard(which, layer), head_width)

    def own_shard(layer):
        return moving(whole(0, layer), whole(1, layer), layer, place.core_peer)

    def other_shard(layer):
        return moving(whole(2, layer), whole(3, layer), LAYERS + layer, place.core_peer)

    def piece_over(layer):
        return moving(
            piece_rows(0, layer, place.low),
            piece_rows(2, layer, place.low),
            2 * LAYERS + layer,
            place.y_peer,
        )

    def rest_over(layer):
        return moving(*direct(layer), 3 * LAYERS + layer, place.y_peer)

    def handed(layer, k):
        rows = piece_rows(2, layer, place.low)
        return pltpu.make_async_remote_copy(
            src_ref=grads.at[rows],
            dst_ref=grads.at[rows],
            send_sem=hand_send.at[layer, k],
            recv_sem=hand_recv.at[layer, place.low],
            device_id=place.others[k],
            device_id_type=MESH,
        )

    def handed_in(layer, k):
        owner = lax.rem(place.low + 1 + k, GROUP)
        rows = piece_rows(2, layer, owner)
        return pltpu.make_async_remote_copy(
            src_ref=grads.at[rows],
            dst_ref=grads.at[rows],
            send_sem=hand_send.at[layer, k],
            recv_sem=hand_recv.at[layer, owner],
            device_id=place.others[k],
            device_id_type=MESH,
        )

    def gather_first(layer):
        weight(1, layer).wait()
        grads[whole(0, layer), :] = w_out[layer].astype(jnp.float32)
        piece_over(layer).start()
        if DIRECT[layer]:
            rest_over(layer).start()
        own_shard(layer).start()

    def gather_second(layer):
        piece_over(layer).wait()
        for k in range(GROUP - 1):
            handed(layer, k).start()

    def gather_third(layer):
        for k in range(GROUP - 1):
            handed(layer, k).wait_send()
            handed_in(layer, k).wait_recv()
        if DIRECT[layer]:
            rest_over(layer).wait()
        other_shard(layer).start()

    def gather_last(layer):
        own_shard(layer).wait()
        other_shard(layer).wait()
        pairs_width = 2 * HEAD_DIM
        for which in range(4):
            source = which // 2
            owner = 2 * (place.y + source - 2 * place.y * source) + (
                core + which % 2 - 2 * core * (which % 2)
            )
            low = grads[whole(which, layer), :].astype(jnp.bfloat16)
            first = pl.multiple_of(owner * pairs_width, pairs_width)
            w_all[layer, pl.ds(first, pairs_width), :] = low[:pairs_width]
            first = pl.multiple_of(4 * pairs_width + owner * HEAD_DIM, HEAD_DIM)
            w_all[layer, pl.ds(first, HEAD_DIM), :] = low[pairs_width:]

    def heads_out(b):
        mine, theirs = shared_heads.at[core, b], shared_heads.at[1 - core, b]
        return [
            remote(
                source,
                shared_heads.at[2 + index, b],
                heads_send.at[index, b],
                heads_recv.at[index, b],
                device,
            )
            for index, (source, device) in enumerate(
                (
                    (theirs, place.core_peer),
                    (mine, place.y_peer),
                    (theirs, place.diagonal),
                )
            )
        ]

    def pack_heads(rows):
        cut = 2 * HEAD_DIM
        return jnp.concatenate(
            [
                rows[:, :cut],
                jnp.concatenate([rows[: SEG // 2, cut:], rows[SEG // 2 :, cut:]], axis=1),
            ],
            axis=0,
        )

    def all_heads(b):
        pairs, thirds = [], []
        for owner in range(4):
            side, half = owner // 2, owner % 2
            apart = 2 * (place.y + side - 2 * place.y * side) + (core + half - 2 * core * half)
            slot = jnp.where(apart == 0, core, apart + 1)
            low = shared_heads[slot, b].astype(jnp.bfloat16)
            pairs.append(low[:SEG])
            tail = low[SEG:]
            thirds.append(jnp.concatenate([tail[:, :HEAD_DIM], tail[:, HEAD_DIM:]], axis=0))
        return jnp.concatenate(pairs + thirds, axis=1)

    meet(barrier)
    gather_first(0)

    for index in SHORT_ARGS:
        fetch(index).wait()
    pad_row = padding[...].astype(jnp.float32)
    live_row = masked[...].astype(jnp.float32) * pad_row
    bias_row = (pad_row - 1.0) * 10000.0
    columns[:, 0:1] = column(live_row)
    columns[:, 1:2] = column(replace_ids[...].astype(jnp.float32))
    grads[small_base:, :] = jnp.zeros((CHUNK, width), jnp.float32)

    def chosen(rows, count):
        spots = lax.broadcasted_iota(jnp.int32, (count, REPL), 1).astype(jnp.float32)
        return jnp.where(columns[rows, 1:2] == spots, 1.0, 0.0)

    def first_input(b):
        rows = block(b)
        picked = matmul(chosen(rows, BLOCK).astype(jnp.bfloat16), replace_table[...])
        taken = jnp.where(
            columns[rows, 0:1] > 0.0, picked, embeddings[rows, :].astype(jnp.float32)
        )
        inputs_low[0, rows, :] = taken.astype(jnp.bfloat16)

    sums[...] = jnp.zeros_like(sums)
    local_sums[...] = jnp.zeros_like(local_sums)

    def project(layer, spans):
        bias_pair = vector(b_qv, layer)
        inputs = jnp.concatenate([inputs_low[layer, rows, :] for rows in spans], axis=0)
        projected = contract_cols(inputs, w_qkv[layer])

        def split(ref, h, columns_of):
            low = columns_of.astype(jnp.bfloat16)
            first = 0
            for rows in spans:
                ref[layer, h, rows, :] = low[first : first + rows.size]
                first += rows.size

        for h in range(local_heads):
            base = 3 * HEAD_DIM * h
            bias = 2 * HEAD_DIM * h
            split(
                queries,
                h,
                projected[:, base : base + HEAD_DIM] + bias_pair[:, bias : bias + HEAD_DIM],
            )
            split(keys, h, projected[:, base + HEAD_DIM : base + 2 * HEAD_DIM])
            split(
                values,
                h,
                projected[:, base + 2 * HEAD_DIM : base + 3 * HEAD_DIM]
                + bias_pair[:, bias + HEAD_DIM : bias + 2 * HEAD_DIM],
            )

    def scores_of(layer, h, query):
        return contract_cols(query, keys[layer, h]) * SCALE + bias_row

    def total_row(turn, index, amount):
        sums[turn, index : index + 1, :] = sums[turn, index : index + 1, :] + jnp.sum(
            amount, axis=0, keepdims=True
        )

    def norm_two(turn, b, size, grad):
        layer = LAYERS - 1 - turn
        rows = packed(b, size)
        zhat = zhat_two[layer, rows, :]
        dz = norm_back(grad, zhat, scale_two[layer, rows, :], vector(second_gain, layer))
        own_a[rows, :] = dz
        to_other(0, b, size, own_a).start()
        dz_low[kept(b, size), :] = dz.astype(jnp.bfloat16)
        total_row(turn, 0, grad * zhat)
        total_row(turn, 1, grad)
        total_row(turn, 2, dz)

    def forward(layer):
        last = layer == LAYERS - 1

        def attend(b):
            pl.when(jnp.logical_and(layer == 0, b == BLOCKS - 1))(lambda: gather_third(0))
            spans = halves(b, SEG)
            outs, logs = [], []
            all_scores = [
                scores_of(
                    layer,
                    h,
                    jnp.concatenate([queries[layer, h, rows, :] for rows in spans], axis=0),
                )
                for h in range(local_heads)
            ]
            all_probs = []
            for scores in all_scores:
                largest = jnp.max(scores, axis=-1, keepdims=True)
                weights_of = jnp.exp(scores - largest)
                totals = jnp.sum(weights_of, axis=-1, keepdims=True)
                all_probs.append((weights_of * (1.0 / totals)).astype(jnp.bfloat16))
                logs.append(largest + jnp.log(totals))
            for h, probs in enumerate(all_probs):
                outs.append(matmul(probs, values[layer, h]).astype(jnp.bfloat16))
            joined = jnp.concatenate(outs, axis=1)
            full = joined.astype(jnp.float32)
            for side in range(2):
                shared_heads[side, b] = pack_heads(full[side * SEG : (side + 1) * SEG])
            for copy in heads_out(b):
                copy.start()
            for side, rows in enumerate(spans):
                cut = slice(side * SEG, (side + 1) * SEG)
                heads[layer, rows, :] = joined[cut]
                for h in range(local_heads):
                    log_total[layer, rows, h : h + 1] = logs[h][cut]

        repeat(BLOCKS, attend)

        @pl.when(layer == 0)
        def _():
            gather_first(1)
            gather_last(0)

        pl.when(layer == 1)(lambda: gather_last(1))

        gain, shift, bias_out = (
            vector(first_gain, layer),
            vector(first_shift, layer),
            vector(b_out, layer),
        )
        bias_in = vector(b_in, layer)
        weight(2, layer).wait()
        weight(3, layer).wait()

        def feed_norm(b):
            rows = packed(b, SEG)
            for copy in heads_out(b):
                copy.wait()
            before = (
                inputs_low[layer, kept(b, SEG), :].astype(jnp.float32)
                + matmul(all_heads(b), w_all[layer])
                + bias_out
            )
            zhat, scale = normed(before)
            result = zhat * gain + shift
            own_a[rows, :] = result
            to_other(0, b, SEG, own_a).start()
            zhat_one[layer, rows, :] = zhat
            scale_one[layer, rows, :] = scale
            normed_low[layer, kept(b, SEG), :] = result.astype(jnp.bfloat16)

        def feed_main(b):
            spans = halves(b, SEG)
            normed_low[layer, given(b, SEG), :] = received(0, b, SEG, own_a)
            inputs = jnp.concatenate([normed_low[layer, rows, :] for rows in spans], axis=0)
            u = matmul(inputs, w_in[layer]) + bias_in
            g = (u * normal_cdf(u)).astype(jnp.bfloat16)
            lowered = matmul(g, w_down[layer])
            for side, rows in enumerate(spans):
                cut = slice(side * SEG, (side + 1) * SEG)
                part[rows, :] = lowered[cut]
                hidden[layer, rows, :] = u[cut]
                active[layer, rows, :] = g[cut]
            to_core(1, b, SEG).start()

        def feed(b):
            feed_norm(b)
            pl.when(b >= 1)(lambda: send_y(1, b - 1, SEG))
            feed_main(b)
            pl.when(jnp.logical_and(layer == 0, b == 0))(lambda: gather_second(1))

        repeat(BLOCKS, feed)
        send_y(1, BLOCKS - 1, SEG)

        gain_two, shift_two, bias_down = (
            vector(second_gain, layer),
            vector(second_shift, layer),
            vector(b_down, layer),
        )
        pl.when(jnp.logical_not(last))(lambda: weight(0, layer + 1).wait())

        def receive(b):
            inputs_low[layer + 1, given(b, SEG), :] = received(1, b, SEG, own_b)
            pl.when(jnp.logical_not(last))(lambda: project(layer + 1, halves(b, SEG)))

            @pl.when(last)
            def _():
                dz_low[given(b, SEG), :] = received(0, b, SEG, own_a)

        def finish(b):
            rows = packed(b, SEG)
            before = own_a[rows, :] + summed(1, b, SEG) + bias_down
            zhat, scale = normed(before)
            result = zhat * gain_two + shift_two
            own_b[rows, :] = result
            to_other(1, b, SEG, own_b).start()
            zhat_two[layer, rows, :] = zhat
            scale_two[layer, rows, :] = scale
            inputs_low[layer + 1, kept(b, SEG), :] = result.astype(jnp.bfloat16)

            @pl.when(last)
            def _():
                live = columns[kept(b, SEG), 0:1]
                norm_two(0, b, SEG, cotangent[kept(b, SEG), :].astype(jnp.float32) * live)

            pl.when(b >= 1)(lambda: receive(b - 1))

        repeat(BLOCKS, finish)
        receive(BLOCKS - 1)
        pl.when(layer == 0)(lambda: gather_third(1))

    fetch(0).wait()
    repeat(BACK_BLOCKS, first_input)
    fetch(ARGS - 1).start()
    for index, layer in ((1, 1), (2, 0), (3, 0), (0, 1), (2, 1), (3, 1)):
        weight(index, layer).start()
    weight(0, 0).wait()
    project(0, (block(0),))
    gather_second(0)
    repeat(BACK_BLOCKS - 1, lambda b: project(0, (block(b + 1),)))
    fetch(ARGS - 1).wait()
    repeat(LAYERS, forward)

    def last_grad(b, grad):
        rows = kept(b, BACK_SEG)
        live = columns[rows, 0:1]
        masked_grad = grad * (1.0 - live)
        own_a[packed(b, BACK_SEG), :] = masked_grad
        to_other(0, b, BACK_SEG, own_a).start()
        grad_embeddings[rows, :] = masked_grad.astype(jnp.bfloat16)
        grads[small_base : small_base + REPL, :] = grads[
            small_base : small_base + REPL, :
        ] + lax.dot_general(
            chosen(rows, BACK_SEG),
            grad * live,
            (((0,), (0,)), ((), ())),
            precision=lax.Precision.HIGHEST,
            preferred_element_type=jnp.float32,
        )

    def backward(turn):
        layer = LAYERS - 1 - turn
        base = turn * span
        start = turn * (span // CHUNK)
        last = turn == LAYERS - 1
        in_base = base + hidden_width
        out_base = in_base + width
        qkv_base = out_base + head_width

        def rows_at(first, count):
            return pl.ds(pl.multiple_of(first, 16), count)

        def down_piece(p):
            grads[rows_at(base + 128 * p, 128), :] = contract_rows(
                active[layer, :, lanes(p)], dz_low[...]
            )

        def in_piece(p):
            grads[rows_at(in_base + 128 * p, 128), :] = contract_rows(
                normed_low[layer, :, lanes(p)], du_low[...]
            )

        down_piece(0)
        tick(start)

        def feed(b):
            rows = block(b)
            dg = contract_cols(dz_low[rows, :], w_down[layer])
            u = hidden[layer, rows, :]
            density = jnp.exp(u * u * (-0.5)) * (1.0 / math.sqrt(2.0 * math.pi))
            du = dg * (normal_cdf(u) + u * density)
            du_low[rows, :] = du.astype(jnp.bfloat16)
            local_sums[turn, 0:1, :] = local_sums[turn, 0:1, :] + jnp.sum(
                du, axis=0, keepdims=True
            )
            down_piece(b + 1)
            tick(start + 1 + b)

        repeat(BACK_BLOCKS, feed)
        down_piece(5)

        def feed_in(b):
            spans = halves(b, BACK_SEG)
            left = jnp.concatenate([du_low[rows, :] for rows in spans], axis=0)
            result = contract_cols(left, w_in[layer])
            for side, rows in enumerate(spans):
                part[rows, :] = result[side * BACK_SEG : (side + 1) * BACK_SEG]
            to_core(0, b, BACK_SEG).start()
            pl.when(b >= 1)(lambda: send_y(0, b - 1, BACK_SEG))
            tick(start + 5 + b)

        repeat(BACK_BLOCKS, feed_in)
        send_y(0, BACK_BLOCKS - 1, BACK_SEG)

        def early_piece(p):
            in_piece(p)
            tick(start + 9 + p)

        repeat(4, early_piece)
        in_piece(4)

        gain = vector(first_gain, layer)

        def norm_one(b):
            rows = packed(b, BACK_SEG)
            grad = own_a[rows, :] + summed(0, b, BACK_SEG)
            zhat = zhat_one[layer, rows, :]
            dz = norm_back(grad, zhat, scale_one[layer, rows, :], gain)
            own_b[rows, :] = dz
            to_other(1, b, BACK_SEG, own_b).start()
            dz_low[kept(b, BACK_SEG), :] = dz.astype(jnp.bfloat16)
            total_row(turn, 3, grad * zhat)
            total_row(turn, 4, grad)
            total_row(turn, 5, dz)
            tick(start + 13 + b)
            dz_low[given(b, BACK_SEG), :] = received(1, b, BACK_SEG, own_b)

        repeat(BACK_BLOCKS, norm_one)
        grads[rows_at(out_base, head_width), :] = contract_rows(heads[layer], dz_low[...])
        dheads[...] = contract_cols(dz_low[...], w_out[layer]).astype(jnp.bfloat16)
        in_piece(5)
        tick(start + 17)
        dkeys[...] = jnp.zeros_like(dkeys)
        dvalues[...] = jnp.zeros_like(dvalues)

        def attend(b):
            rows = block(b)
            for h in range(local_heads):
                side = HEAD_DIM * h
                query = queries[layer, h, rows, :]
                probs = jnp.exp(scores_of(layer, h, query) - log_total[layer, rows, h : h + 1])
                dhead = dheads[rows, side : side + HEAD_DIM]
                dprobs = contract_cols(dhead, values[layer, h])
                dvalues[h] = dvalues[h] + contract_rows(probs.astype(jnp.bfloat16), dhead)
                inner = jnp.sum(probs * dprobs, axis=-1, keepdims=True)
                ds = (probs * (dprobs - inner)).astype(jnp.bfloat16)
                dq = matmul(ds, keys[layer, h]) * SCALE
                dkeys[h] = dkeys[h] + contract_rows(ds, query)
                dqkv_low[rows, 3 * side : 3 * side + HEAD_DIM] = dq.astype(jnp.bfloat16)
                local_sums[turn, 1:2, 2 * side : 2 * side + HEAD_DIM] = local_sums[
                    turn, 1:2, 2 * side : 2 * side + HEAD_DIM
                ] + jnp.sum(dq, axis=0, keepdims=True)
            pl.when(b < BACK_BLOCKS - 1)(lambda: tick(start + 18 + b))

        repeat(BACK_BLOCKS, attend)
        for h in range(local_heads):
            side = HEAD_DIM * h
            dqkv_low[:, 3 * side + HEAD_DIM : 3 * side + 2 * HEAD_DIM] = (
                dkeys[h] * SCALE
            ).astype(jnp.bfloat16)
            dv = dvalues[h]
            dqkv_low[:, 3 * side + 2 * HEAD_DIM : 3 * side + 3 * HEAD_DIM] = dv.astype(
                jnp.bfloat16
            )
            local_sums[turn, 1:2, 2 * side + HEAD_DIM : 2 * side + 2 * HEAD_DIM] = jnp.sum(
                dv, axis=0, keepdims=True
            )

        def back_project(b):
            grads[rows_at(qkv_base + 128 * b, 128), :] = contract_rows(
                dqkv_low[:, lanes(b)], inputs_low[layer]
            )
            spans = halves(b, BACK_SEG)
            left = jnp.concatenate([dqkv_low[rows, :] for rows in spans], axis=0)
            result = matmul(left, w_qkv[layer])
            for side, rows in enumerate(spans):
                part[rows, :] = result[side * BACK_SEG : (side + 1) * BACK_SEG]
            to_core(1, b, BACK_SEG).start()
            pl.when(b >= 1)(lambda: send_y(1, b - 1, BACK_SEG))
            tick(start + 21 + b)

        repeat(BACK_BLOCKS, back_project)
        send_y(1, BACK_BLOCKS - 1, BACK_SEG)

        tail = jnp.where(last, HOLE, 0)
        grads[rows_at(qkv_base + 512 + tail, HEAD_DIM), :] = contract_rows(
            dqkv_low[:, 512:], inputs_low[layer]
        )
        tick(start + 25)

        def pass_on(b):
            rows = packed(b, BACK_SEG)
            grad = own_b[rows, :] + summed(1, b, BACK_SEG)
            pl.when(jnp.logical_not(last))(lambda: norm_two(turn + 1, b, BACK_SEG, grad))
            pl.when(last)(lambda: last_grad(b, grad))
            pl.when(jnp.logical_or(last, b < 2))(lambda: tick(start + 26 + b))

        repeat(BACK_BLOCKS, pass_on)

        def receive(b):
            dz_low[given(b, BACK_SEG), :] = received(0, b, BACK_SEG, own_a)

        pl.when(jnp.logical_not(last))(lambda: repeat(BACK_BLOCKS, receive))

    repeat(LAYERS, backward)
    hidden_out[...] = inputs_low[LAYERS]

    shared = REPL + 8 * LAYERS
    for turn in range(LAYERS):
        first = small_base + REPL + 8 * turn
        grads[first : first + 8, :] = sums[turn]
    grads[small_base + shared : small_base + shared + 8, :] = local_sums[...].reshape(8, width)
    short = remote(
        grads.at[pl.ds(small_base, shared)], land_small, small_send, small_recv, place.core_peer
    )
    short.start()

    def receive_grad(b):
        grad_embeddings[given(b, BACK_SEG), :] = received(0, b, BACK_SEG, own_a)

    repeat(BACK_BLOCKS, receive_grad)
    short.wait()
    grads[small_base : small_base + shared, :] = (
        grads[small_base : small_base + shared, :] + land_small[...]
    )
    done = chunks - 1
    repeat(grad_sum.ticks() - done, lambda i: tick(done + i))


def run_pages(args, sizes):
    width, hidden_width, local_heads, span = sizes
    rows = PAGE_LEN
    flat = LAYERS * span - HEAD_DIM + HOLE + 2 * CHUNK
    half = rows // 2
    low, full = jnp.bfloat16, jnp.float32
    vmem, dma = pltpu.VMEM, pltpu.SemaphoreType.DMA
    head_width = local_heads * HEAD_DIM
    return pl.pallas_call(
        functools.partial(page_kernel, sizes),
        name="pages",
        out_shape=(
            vmem((rows, width), low),
            vmem((rows, width), low),
            vmem((flat, width), full),
        ),
        in_specs=[pl.BlockSpec(memory_space=pl.ANY)] * ARGS,
        out_specs=(
            pl.BlockSpec(memory_space=pltpu.VMEM),
            pl.BlockSpec(memory_space=pltpu.VMEM),
            pl.BlockSpec(memory_space=pltpu.VMEM),
        ),
        scratch_shapes=[
            *[vmem(arg.shape, arg.dtype) for arg in args],
            vmem((LAYERS + 1, rows, width), low),
            vmem((LAYERS, local_heads, rows, HEAD_DIM), low),
            vmem((LAYERS, local_heads, rows, HEAD_DIM), low),
            vmem((LAYERS, local_heads, rows, HEAD_DIM), low),
            vmem((LAYERS, rows, 128), full),
            vmem((LAYERS, rows, head_width), low),
            vmem((LAYERS, rows, width), low),
            vmem((LAYERS, rows, hidden_width), full),
            vmem((LAYERS, rows, hidden_width), low),
            vmem((LAYERS, half, width), full),
            vmem((LAYERS, half, 1), full),
            vmem((LAYERS, half, width), full),
            vmem((LAYERS, half, 1), full),
            vmem((LAYERS, 4 * head_width, width), low),
            vmem((5, BLOCKS, 3 * SEG // 2, 2 * HEAD_DIM), full),
            vmem((rows, 128), full),
            vmem((half, width), full),
            vmem((half, width), full),
            vmem((rows, width), full),
            vmem((2, half, width), full),
            vmem((2, half, width), full),
            vmem((2, half, width), full),
            vmem((REPL + 8 * LAYERS, width), full),
            vmem((rows, width), low),
            vmem((rows, hidden_width), low),
            vmem((rows, head_width), low),
            vmem((local_heads, rows, HEAD_DIM), full),
            vmem((local_heads, rows, HEAD_DIM), full),
            vmem((rows, 3 * head_width), low),
            vmem((LAYERS, 8, width), full),
            vmem((LAYERS, 4, width), full),
            vmem((len(WIDE_LANDINGS), SLOTS, WIDE, width), full),
            vmem((SLOTS, 2 * NARROW, width), full),
            vmem((len(NARROW_LANDINGS), SLOTS, NARROW, width), full),
            dma((2, BLOCKS)),
            dma((2, BLOCKS)),
            dma((2, BLOCKS)),
            dma((2, BLOCKS)),
            dma((2, BLOCKS)),
            dma((2, BLOCKS)),
            dma,
            dma,
            dma((len(EQUALS), EQUAL_SLOTS)),
            dma((len(EQUALS), EQUAL_SLOTS)),
            dma((len(ONE_WAY), SLOTS)),
            dma((len(SHORT_WAY), EQUAL_SLOTS)),
            dma((SLOTS,)),
            dma((SLOTS,)),
            dma((4 * LAYERS,)),
            dma((4 * LAYERS,)),
            dma((LAYERS, GROUP)),
            dma((LAYERS, GROUP)),
            dma((3, BLOCKS)),
            dma((3, BLOCKS)),
            dma((ARGS + (LAYERS - 1) * len(WEIGHTS),)),
        ],
        compiler_params=pltpu.CompilerParams(
            collective_id=0, has_side_effects=True, vmem_limit_bytes=46 << 20
        ),
    )(*args)


def place_kernel(sizes, hidden_out, grad_embeddings, every, *refs):
    width, hidden_width, local_heads, span = sizes
    head_width = local_heads * HEAD_DIM
    (
        out_hidden,
        out_embeddings,
        out_table,
        out_w_qkv,
        out_b_qv,
        out_w_out,
        out_b_out,
        out_first_gain,
        out_first_shift,
        out_w_in,
        out_b_in,
        out_w_down,
        out_b_down,
        out_second_gain,
        out_second_shift,
        short,
        shorts,
        sems,
    ) = refs
    tail = LAYERS * span - HEAD_DIM
    base = tail + HOLE + CHUNK
    pairs = [(every.at[pl.ds(base, CHUNK)], short), (every.at[pl.ds(base, REPL)], out_table)]
    pairs += [(hidden_out, out_hidden), (grad_embeddings, out_embeddings)]
    for turn in range(LAYERS):
        first = span * turn
        for ref, rows in (
            (out_w_down, hidden_width),
            (out_w_in, width),
            (out_w_out, head_width),
            (out_w_qkv, 3 * head_width),
        ):
            target = ref.at[LAYERS - 1 - turn]
            direct = min(rows, tail - first)
            pairs.append((every.at[pl.ds(first, direct)], target.at[pl.ds(0, direct)]))
            if direct < rows:
                pairs.append(
                    (
                        every.at[pl.ds(tail + HOLE, rows - direct)],
                        target.at[pl.ds(direct, rows - direct)],
                    )
                )
            first += rows
    copies = [
        pltpu.make_async_copy(source, target, sems.at[index])
        for index, (source, target) in enumerate(pairs)
    ]
    for copy in copies:
        copy.start()
    copies[0].wait()
    pieces = []
    local = REPL + 8 * LAYERS
    for index, (ref, row, step) in enumerate((
        (out_second_gain, REPL, 8),
        (out_second_shift, REPL + 1, 8),
        (out_b_down, REPL + 2, 8),
        (out_first_gain, REPL + 3, 8),
        (out_first_shift, REPL + 4, 8),
        (out_b_out, REPL + 5, 8),
        (out_b_in, local, 4),
        (out_b_qv, local + 1, 4),
    )):
        for turn in range(LAYERS):
            layer = LAYERS - 1 - turn
            shorts[index, layer : layer + 1, :] = short[
                row + step * turn : row + step * turn + 1, :
            ]
        piece = pltpu.make_async_copy(
            shorts.at[index, :, pl.ds(0, ref.shape[1])], ref, sems.at[len(copies) + index]
        )
        piece.start()
        pieces.append(piece)
    for copy in copies[1:] + pieces:
        copy.wait()


def place_outputs(hidden_out, grad_embeddings, every, sizes):
    width, hidden_width, local_heads, span = sizes
    head_width = local_heads * HEAD_DIM
    low, full = jnp.bfloat16, jnp.float32
    rows = hidden_out.shape[0]
    shapes = (
        ((rows, width), low),
        ((rows, width), low),
        ((REPL, width), full),
        ((LAYERS, 3 * head_width, width), full),
        ((LAYERS, 2 * head_width), full),
        ((LAYERS, head_width, width), full),
        ((LAYERS, width), full),
        ((LAYERS, width), full),
        ((LAYERS, width), full),
        ((LAYERS, width, hidden_width), full),
        ((LAYERS, hidden_width), full),
        ((LAYERS, hidden_width, width), full),
        ((LAYERS, width), full),
        ((LAYERS, width), full),
        ((LAYERS, width), full),
    )
    far = pl.BlockSpec(memory_space=pl.ANY)
    return pl.pallas_call(
        functools.partial(place_kernel, sizes),
        name="place_outputs",
        out_shape=[jax.ShapeDtypeStruct(shape, kind) for shape, kind in shapes],
        in_specs=[far] * 3,
        out_specs=[far] * len(shapes),
        scratch_shapes=[
            pltpu.VMEM((CHUNK, width), full),
            pltpu.VMEM((8, LAYERS, width), full),
            pltpu.SemaphoreType.DMA((13 + 4 * LAYERS,)),
        ],
        compiler_params=pltpu.CompilerParams(vmem_limit_bytes=4 << 20),
    )(hidden_out, grad_embeddings, every)


def moved(every):
    def kernel(source, target, sem):
        copy = pltpu.make_async_copy(source, target, sem)
        copy.start()
        copy.wait()

    far = pl.BlockSpec(memory_space=pl.ANY)
    return pl.pallas_call(
        kernel,
        name="moved",
        out_shape=jax.ShapeDtypeStruct(every.shape, every.dtype),
        in_specs=[far],
        out_specs=far,
        scratch_shapes=[pltpu.SemaphoreType.DMA],
        compiler_params=pltpu.CompilerParams(vmem_limit_bytes=4 << 20),
    )(every)


def on_device(*args):
    (embeddings, replace_table, replace_ids, masked, padding, w_qkv, b_qv, *_) = args
    width = embeddings.shape[1]
    head_width = w_qkv.shape[2] // 3
    hidden_width = args[11].shape[2]
    span = 2 * hidden_width + 4 * head_width
    args = list(args)
    args[5] = jnp.swapaxes(args[5], 1, 2)
    for index in (2, 3, 4):
        args[index] = args[index].reshape(1, PAGE_LEN)
    sizes = (width, hidden_width, head_width // HEAD_DIM, span)
    hidden_out, grad_embeddings, every = run_pages(args, sizes)
    groups = lax.axis_size("dp") // GROUP
    if groups > 1:
        every = lax.psum(
            moved(every),
            "dp",
            axis_index_groups=[
                [low + GROUP * high for high in range(groups)] for low in range(GROUP)
            ],
        )

    results = place_outputs(hidden_out, grad_embeddings, every, sizes)
    return (*results[:3], jnp.swapaxes(results[3], 1, 2), *results[4:])


def solution(mesh):
    placed = (
        P("dp", None),
        P(),
        P("dp"),
        P("dp"),
        P("dp"),
        P(None, None, "tensor"),
        P(None, "tensor"),
        P(None, "tensor", None),
        P(),
        P(),
        P(),
        P(None, None, "tensor"),
        P(None, "tensor"),
        P(None, "tensor", None),
        P(),
        P(),
        P(),
        P("dp", None),
    )
    return jax.shard_map(
        on_device,
        mesh=mesh,
        in_specs=placed,
        out_specs=(
            P("dp", None),
            P("dp", None),
            P(),
            P(None, None, "tensor"),
            P(None, "tensor"),
            P(None, "tensor", None),
            P(),
            P(),
            P(),
            P(None, None, "tensor"),
            P(None, "tensor"),
            P(None, "tensor", None),
            P(),
            P(),
            P(),
        ),
        check_vma=False,
    )
```
